32 devices in a mesh: dp: 2 (over core), ctx: 8 (over z, x), tp: 2 (over y).
Axes of the slice: x: 2, y: 2, z: 4, core: 2. Of those that a mesh axis runs over, the one named last changes fastest.
Arguments:
- tokens: bfloat16 [8, 16, 256, 1152], P('dp', 'ctx', 'tp'), may hold values from -6 to 6
- condition: bfloat16 [8, 1152], P('dp'), may hold values from -6 to 6
- micro_ids: int32 [8], P('dp'), may hold values from 0 to 2, as said below
- w_qkv: float32 [2, 3, 1152, 1152], P(None, None, ('dp', 'ctx'), 'tp'), may hold values from -0.1875 to 0.1875
- w_out: float32 [2, 1152, 1152], P(None, 'tp', ('dp', 'ctx')), may hold values from -1 to 1
- w_up: float32 [2, 1152, 4608], P(None, ('dp', 'ctx'), 'tp'), may hold values from -0.1875 to 0.1875
- w_down: float32 [2, 4608, 1152], P(None, 'tp', ('dp', 'ctx')), may hold values from -0.09375 to 0.09375
- w_ada: float32 [2, 1152, 6912], P(None, ('dp', 'ctx'), 'tp'), may hold values from -0.1875 to 0.1875
- cotangent: bfloat16 [8, 16, 256, 1152], P('dp', 'ctx', 'tp'), may hold values from -6 to 6
Outputs:
- output: bfloat16 [8, 16, 256, 1152], P('dp', 'ctx', 'tp')
- grad_tokens: float32 [8, 16, 256, 1152], P('dp', 'ctx', 'tp')
- grad_condition: float32 [8, 1152], P('dp')
- grad_qkv: float32 [2, 3, 1152, 1152], P(None, None, ('dp', 'ctx'), 'tp')
- grad_out: float32 [2, 1152, 1152], P(None, 'tp', ('dp', 'ctx'))
- grad_up: float32 [2, 1152, 4608], P(None, ('dp', 'ctx'), 'tp')
- grad_down: float32 [2, 4608, 1152], P(None, 'tp', ('dp', 'ctx'))
- grad_ada: float32 [2, 1152, 6912], P(None, ('dp', 'ctx'), 'tp')
The draws below stay inside these ranges and needn't reach their ends.
Inputs may be any that keep to these rules, and one draw needn't show every extreme that they name: `micro_ids`: in each aligned block of 4 clips (one data group) one micro-batch id is held by exactly two clips and every other id of 0 to 2 by exactly one clip.
All inputs are finite; a program needn't handle non-finite values.
Results may differ from the reference program's by a relative error of at most 0.02125.
The reference program's roundings to bfloat16 on the way count: a program that leaves them out, or rounds other values in their place, can miss the bound.
Values may be sent and summed in bfloat16 or wider, within the bound.
No kernel may reach another device: no remote copies, remote signals or barrier semaphores. Data moves between devices by JAX's collectives and lax.ppermute only.
A program may use at most 640 MiB of HBM per device.

```python
import jax
import jax.numpy as jnp
from jax import lax

D = 1152
HEADS = 16
HEAD_DIM = 72
FF = 4608
PATCHES = 256
LAYERS = 2
MICRO = 3
CLIPS_DP = 4
CLIPS = 8
FRAMES = 16


def one_group(group_key):
    labels = jax.random.permutation(jax.random.fold_in(group_key, 1), MICRO)
    shuffle = jax.random.permutation(jax.random.fold_in(group_key, 2), CLIPS_DP)
    pair_base = jnp.maximum(jnp.arange(CLIPS_DP, dtype=jnp.int32) - 1, 0)
    return labels[pair_base][shuffle].astype(jnp.int32)


def draw_micro_ids(key, part):
    group_keys = jax.random.split(jax.random.fold_in(key, 7), CLIPS // CLIPS_DP)
    return jax.vmap(one_group)(group_keys).reshape(CLIPS)


def shard_levels(key, extent, cuts, least, largest):
    factor_of, own = 1.0, jax.random.fold_in(key, 6)
    for position, shards_of in cuts:
        steps = jnp.exp(jax.random.uniform(jax.random.fold_in(own, position), (shards_of,), jnp.float32, least / len(cuts), largest / len(cuts)))
        factor_of = factor_of * jnp.repeat(steps, extent[position] // shards_of).reshape([-1 if axis == position else 1 for axis in range(len(extent))])
    return factor_of


def scatter_about(rng, extent, deviation, reach, cuts=(), held_as=jnp.bfloat16):
    gain = shard_levels(rng, extent, cuts, -0.22, 0.18) if cuts else 1.0
    values = jax.random.normal(rng, extent, jnp.float32) * deviation * gain
    return jnp.minimum(jnp.maximum(values, -reach), reach).astype(held_as)


def setup_inputs(seed: int = 0) -> dict:
    key_of = jax.random.split(jax.random.key(seed), 10)
    tokens = scatter_about(key_of[0], (CLIPS, FRAMES, PATCHES, D), 1.0, 6.0, ((0, 2), (1, 8), (2, 2)))
    condition = scatter_about(key_of[1], (CLIPS, D), 1.0, 6.0, ((0, 2),))
    micro_ids = draw_micro_ids(jax.random.fold_in(key_of[9], 71), 0)
    w_qkv = scatter_about(key_of[3], (LAYERS, 3, D, D), D ** -0.5, 0.1875, ((2, 16), (3, 2)), jnp.float32)
    w_out = scatter_about(key_of[4], (LAYERS, D, D), (max(D // 32, 8)) ** -0.5, 1.0, ((1, 2), (2, 16)), jnp.float32)
    w_up = scatter_about(key_of[5], (LAYERS, D, FF), D ** -0.5, 0.1875, ((1, 16), (2, 2)), jnp.float32)
    w_down = scatter_about(key_of[6], (LAYERS, FF, D), FF ** -0.5, 0.09375, ((1, 2), (2, 16)), jnp.float32)
    w_ada = scatter_about(key_of[7], (LAYERS, D, 6 * D), D ** -0.5, 0.1875, ((1, 16), (2, 2)), jnp.float32)
    cotangent = scatter_about(key_of[8], (CLIPS, FRAMES, PATCHES, D), 1.0, 6.0, ((0, 2), (1, 8), (2, 2)))
    return dict(tokens=tokens, condition=condition, micro_ids=micro_ids, w_qkv=w_qkv, w_out=w_out, w_up=w_up, w_down=w_down, w_ada=w_ada, cotangent=cotangent)


@jax.custom_vjp
def low(v):
    return lax.optimization_barrier(v.astype(jnp.bfloat16)).astype(jnp.float32)

@jax.custom_vjp
def low_back(v):
    return v

def low_keep(v):
    return (low(v), None)

def low_pass(kept, grad):
    return (grad,)

def back_keep(v):
    return (v, None)

def back_low(kept, grad):
    return (low(grad),)
low.defvjp(low_keep, low_pass)
low_back.defvjp(back_keep, back_low)
eps_norm = 1e-06
highest = lax.Precision.HIGHEST

def layer_norm(values):
    centred = values - lax.optimization_barrier(jnp.mean(values, axis=-1, keepdims=True))
    spread_sq = lax.optimization_barrier(jnp.mean(centred * centred, axis=-1, keepdims=True))
    return centred * lax.rsqrt(spread_sq + eps_norm)

def modulate(values, shifts, scales):
    return layer_norm(values) * (1.0 + scales) + shifts

def attend(queries, key_rows, values, form_scores, form_out):
    scores = low_back(jnp.einsum(form_scores, queries, key_rows, precision=highest) * HEAD_DIM ** (-0.5))
    chances = jax.nn.softmax(scores, axis=-1)
    return jnp.einsum(form_out, low(chances), values, precision=highest)

def clip_forward(residual, cond_in, w_qkv, w_out, w_up, w_down, w_ada):
    frames = residual.shape[0]
    patches = residual.shape[1]
    cond_low = low(jax.nn.silu(cond_in))
    for level_id in range(LAYERS):
        modulation = jnp.dot(cond_low, low(w_ada[level_id]), precision=highest)
        shift_a, scale_a, gate_a, shift_m, scale_m, gate_m = jnp.split(modulation, 6)
        normed = low(modulate(residual, shift_a, scale_a))
        projected = jnp.einsum('fsd,kde->kfse', normed, low(w_qkv[level_id]), precision=highest)
        queries = low(low_back(projected[0])).reshape(frames, patches, HEADS, HEAD_DIM)
        key_rows = low(low_back(projected[1])).reshape(frames, patches, HEADS, HEAD_DIM)
        values = low(low_back(projected[2])).reshape(frames, patches, HEADS, HEAD_DIM)
        if level_id % 2 == 0:
            result = attend(queries, key_rows, values, 'fqhe,fkhe->fhqk', 'fhqk,fkhe->fqhe')
        else:
            result = attend(queries, key_rows, values, 'qshe,kshe->shqk', 'shqk,kshe->qshe')
        out_low = low(low_back(result.reshape(frames, patches, D)))
        branch = low_back(jnp.einsum('fsh,hd->fsd', out_low, low(w_out[level_id]), precision=highest))
        middle = residual + gate_a * branch
        normed_mlp = low(modulate(middle, shift_m, scale_m))
        pre_act = low_back(jnp.einsum('fsd,dh->fsh', normed_mlp, low(w_up[level_id]), precision=highest))
        activated = low(jax.nn.gelu(pre_act, approximate=True))
        branch_mlp = low_back(jnp.einsum('fsh,hd->fsd', activated, low(w_down[level_id]), precision=highest))
        residual = middle + gate_m * branch_mlp
    return residual

def reference(tokens, condition, micro_ids, w_qkv, w_out, w_up, w_down, w_ada, cotangent):
    groups = jnp.arange(CLIPS, dtype=jnp.int32) // CLIPS_DP
    matched = (micro_ids[:, None] == micro_ids[None, :]) & (groups[:, None] == groups[None, :])
    shares = 1.0 / lax.optimization_barrier(jnp.sum(matched.astype(jnp.float32), axis=1))
    params = (w_qkv, w_out, w_up, w_down, w_ada)
    empty_sums = tuple((jnp.zeros_like(entry_w) for entry_w in params))

    def one_clip(totals, inputs_now):
        clip_in, cond_in, cot_in, weight = inputs_now
        result, pullback = jax.vjp(clip_forward, clip_in.astype(jnp.float32), cond_in.astype(jnp.float32), *params)
        gradients = pullback(cot_in.astype(jnp.float32) * weight)
        totals = jax.tree.map(jnp.add, totals, tuple(gradients[2:]))
        return (totals, (result.astype(jnp.bfloat16), gradients[0], gradients[1]))
    totals, outputs = lax.scan(one_clip, empty_sums, (tokens, condition, cotangent, shares))
    return (outputs[0], outputs[1], outputs[2], totals[0], totals[1], totals[2], totals[3], totals[4])
```

```python
import functools

import jax
import jax.numpy as jnp
from jax import lax
from jax.experimental import pallas as pl
from jax.experimental.pallas import tpu as pltpu
from jax.sharding import PartitionSpec as P

HEAD_DIM = 72
LAYERS = 2
LANES = 128
EPS = 1e-06
SCALE = HEAD_DIM ** (-0.5)
HIGHEST = lax.Precision.HIGHEST
BF16 = jnp.bfloat16
F32 = jnp.float32

NN = (((1,), (0,)), ((), ()))
NT = (((1,), (1,)), ((), ()))
TN = (((0,), (0,)), ((), ()))


def dot(a, b, dims=NN):
    return lax.dot_general(a, b, dims, preferred_element_type=F32)


def swap_with(v, axis_name, n, k):
    return lax.ppermute(v, axis_name, [(i, i ^ k) for i in range(n)])


def flip_to(v, axis, n, me):
    shape = v.shape
    bit = 1
    while bit < n:
        split = shape[:axis] + (n // (2 * bit), 2, bit) + shape[axis + 1 :]
        parts = v.reshape(split)
        first = lax.slice_in_dim(parts, 0, 1, axis=axis + 1)
        second = lax.slice_in_dim(parts, 1, 2, axis=axis + 1)
        turned = jnp.concatenate([second, first], axis=axis + 1)
        v = jnp.where((me & bit) != 0, turned, parts).reshape(shape)
        bit *= 2
    return v


class Moves:
    def __init__(self, mesh):
        self.n_dp = mesh.shape["dp"]
        self.n_ctx = mesh.shape["ctx"]
        self.n_tp = mesh.shape["tp"]
        self.n_line = self.n_ctx // 2

    def here(self):
        self.dp = lax.axis_index("dp")
        self.ctx = lax.axis_index("ctx")
        self.tp = lax.axis_index("tp")
        self.line = self.ctx // 2
        self.side = self.ctx % 2

    def halves(self, v):
        half = v.shape[-1] // 2
        turned = jnp.concatenate([v[..., half:], v[..., :half]], axis=-1)
        return jnp.where(self.dp == 0, v, turned)

    def line_gather(self, v):
        blocks = [v] + [swap_with(v, "ctx", self.n_ctx, 2 * k) for k in range(1, self.n_line)]
        return flip_to(jnp.stack(blocks), 0, self.n_line, self.line)

    def line_scatter(self, v):
        total = lax.dynamic_index_in_dim(v, self.line, 0, keepdims=False).astype(F32)
        for k in range(1, self.n_line):
            sent = lax.dynamic_index_in_dim(v, self.line ^ k, 0, keepdims=False)
            total = total + swap_with(sent, "ctx", self.n_ctx, 2 * k).astype(F32)
        return total

    def pair_gather(self, v):
        other = swap_with(v, "ctx", self.n_ctx, 1)
        first = jnp.where(self.side == 0, v, other)
        second = jnp.where(self.side == 0, other, v)
        return jnp.stack([first, second], axis=1).reshape(-1, v.shape[-1])

    def pair_scatter(self, v):
        parts = v.reshape(self.n_line, 2, -1, v.shape[-1])
        sent = lax.dynamic_index_in_dim(parts, 1 - self.side, 1, keepdims=False)
        kept = lax.dynamic_index_in_dim(parts, self.side, 1, keepdims=False)
        got = swap_with(sent, "ctx", self.n_ctx, 1)
        return (kept.astype(F32) + got.astype(F32)).astype(BF16)

    def gather_weights(self, shards):
        gathered = []
        line = strip = None
        for index, v in enumerate(shards):
            if line is not None:
                v, line = lax.optimization_barrier((v, line))
            line = self.line_gather(v)
            if index % 2 == 1:
                if strip is not None:
                    line, strip = lax.optimization_barrier((line, strip))
                lines = [line]
                lines += [swap_with(line, "tp", self.n_tp, r) for r in range(1, self.n_tp)]
                strip = lines[-1]
                blocks = [self.pair_gather(entry) for entry in lines]
            else:
                block = self.pair_gather(line)
                if strip is not None:
                    block, strip = lax.optimization_barrier((block, strip))
                blocks = [block]
                blocks += [swap_with(block, "tp", self.n_tp, r) for r in range(1, self.n_tp)]
                strip = blocks[-1]
            gathered.append(
                [
                    jnp.concatenate([entry, swap_with(entry, "dp", self.n_dp, 1)], axis=0)
                    for entry in blocks
                ]
            )
        return gathered

    def gather_whole(self, v):
        whole = lax.all_gather(v, ("tp", "dp", "ctx"), axis=0, tiled=True)
        whole = whole.reshape(self.n_tp, -1, v.shape[-1])
        return [whole[t] for t in range(self.n_tp)]

    def scatter_whole(self, left, rights):
        parts = jnp.concatenate([dot(left, v, TN).astype(BF16) for v in rights], axis=0)
        shard = lax.psum_scatter(parts, ("tp", "dp", "ctx"), scatter_dimension=0, tiled=True)
        return shard.astype(F32)

    def scatter_weight(self, left, rights, tp_first):
        half = left.shape[1] // 2
        mine, theirs = left[:, :half], left[:, half:]
        blocks = [None] * self.n_tp
        for r in list(range(1, self.n_tp)) + [0]:
            sent = dot(theirs, rights[r], TN).astype(BF16)
            got = swap_with(sent, "dp", self.n_dp, 1)
            total = dot(mine, rights[r], TN) + got.astype(F32)
            if tp_first and r == 0:
                for q in range(1, self.n_tp):
                    total = total + swap_with(blocks[q], "tp", self.n_tp, q).astype(F32)
            blocks[r] = total.astype(BF16)
        if tp_first:
            line = self.pair_scatter(blocks[0])
        else:
            lines = [self.pair_scatter(entry) for entry in blocks]
            total = lines[0].astype(F32)
            for q in range(1, self.n_tp):
                total = total + swap_with(lines[q], "tp", self.n_tp, q).astype(F32)
            line = total.astype(BF16) if self.n_tp > 1 else lines[0]
        return self.line_scatter(line)


def window(head):
    start = head * HEAD_DIM
    return start // LANES * LANES, -(-(start + HEAD_DIM) // LANES) * LANES


def in_head(head, rows, low, high):
    lanes = lax.broadcasted_iota(jnp.int32, (rows, high - low), 1) + low
    return (lanes >= head * HEAD_DIM) & (lanes < (head + 1) * HEAD_DIM)


def spread_parts(x_ref, parts, width):
    for index, part in enumerate(parts):
        padded = part.shape[1]
        if padded != width:
            part[:, padded - LANES :] = jnp.zeros((part.shape[0], LANES), part.dtype)
        part[:, :width] = x_ref[:, index * width : (index + 1) * width]


def same_sequence(rows, stride):
    row = lax.broadcasted_iota(jnp.int32, (rows, rows), 0)
    column = lax.broadcasted_iota(jnp.int32, (rows, rows), 1)
    return lax.rem(row, stride) == lax.rem(column, stride)


def attend_kernel(heads, stride, x_ref, o_ref, lse_ref, q_s, k_s, v_s, o_s):
    rows, width = x_ref.shape[0], heads * HEAD_DIM
    spread_parts(x_ref, (q_s, k_s, v_s), width)
    lane = lax.broadcasted_iota(jnp.int32, (rows, LANES), 1)
    logs = jnp.zeros((rows, LANES), F32)
    if stride > 1:
        allowed = same_sequence(rows, stride)
    for head in range(heads):
        low, high = window(head)
        mask = in_head(head, rows, low, high)
        queries = jnp.where(mask, q_s[:, low:high], jnp.zeros((), BF16))
        scores = dot(queries, k_s[:, low:high], NT) * SCALE
        if stride > 1:
            scores = jnp.where(allowed, scores, -jnp.inf)
        largest = jnp.max(scores, axis=-1, keepdims=True)
        raised = jnp.exp(scores - largest)
        total = jnp.sum(raised, axis=-1, keepdims=True)
        chances = (raised * (1.0 / total)).astype(BF16)
        result = dot(chances, v_s[:, low:high])
        o_s[:, low:high] = jnp.where(mask, result, o_s[:, low:high])
        logs = jnp.where(lane == head, largest + jnp.log(total), logs)
    o_ref[...] = o_s[:, :width].astype(BF16)
    lse_ref[...] = logs


def attend_back_kernel(
    heads, stride, x_ref, g_ref, lse_ref, dx_ref, q_s, k_s, v_s, g_s, dq_s, dk_s, dv_s
):
    rows, width = x_ref.shape[0], heads * HEAD_DIM
    spread_parts(x_ref, (q_s, k_s, v_s), width)
    spread_parts(g_ref, (g_s,), width)
    if stride > 1:
        allowed = same_sequence(rows, stride)
    for head in range(heads):
        low, high = window(head)
        mask = in_head(head, rows, low, high)
        zero = jnp.zeros((), BF16)
        q, k, v, g = q_s[:, low:high], k_s[:, low:high], v_s[:, low:high], g_s[:, low:high]
        scores = dot(jnp.where(mask, q, zero), k, NT) * SCALE
        if stride > 1:
            scores = jnp.where(allowed, scores, -jnp.inf)
        chances = jnp.exp(scores - lse_ref[:, head : head + 1])
        grad_chances = dot(jnp.where(mask, g, zero), v, NT)
        row_dot = jnp.sum(chances * grad_chances, axis=-1, keepdims=True)
        grad_scores = (chances * (grad_chances - row_dot)).astype(BF16)
        dq = dot(grad_scores, k) * SCALE
        dk = dot(grad_scores, q, TN) * SCALE
        dv = dot(chances.astype(BF16), g, TN)
        dq_s[:, low:high] = jnp.where(mask, dq, dq_s[:, low:high])
        dk_s[:, low:high] = jnp.where(mask, dk, dk_s[:, low:high])
        dv_s[:, low:high] = jnp.where(mask, dv, dv_s[:, low:high])
    for index, part in enumerate((dq_s, dk_s, dv_s)):
        dx_ref[:, index * width : (index + 1) * width] = part[:, :width].astype(BF16)


def row_block(rows, columns):
    return pl.BlockSpec((rows, columns), lambda i: (i, 0))


def attend(x, rows, stride):
    count, width = x.shape[0], x.shape[1] // 3
    heads = width // HEAD_DIM
    padded = -(-width // LANES) * LANES
    return pl.pallas_call(
        functools.partial(attend_kernel, heads, stride),
        grid=(count // rows,),
        in_specs=[row_block(rows, 3 * width)],
        out_specs=[row_block(rows, width), row_block(rows, LANES)],
        out_shape=[
            jax.ShapeDtypeStruct((count, width), BF16),
            jax.ShapeDtypeStruct((count, LANES), F32),
        ],
        scratch_shapes=[pltpu.VMEM((rows, padded), BF16)] * 3 + [pltpu.VMEM((rows, padded), F32)],
        cost_estimate=pl.CostEstimate(
            flops=heads * count * rows * 1024,
            bytes_accessed=count * width * 8,
            transcendentals=heads * count * rows,
        ),
        compiler_params=pltpu.CompilerParams(vmem_limit_bytes=32 * 1024 * 1024),
    )(x)


def attend_back(x, grad, lse, rows, stride):
    count, width = grad.shape
    heads = width // HEAD_DIM
    padded = -(-width // LANES) * LANES
    return pl.pallas_call(
        functools.partial(attend_back_kernel, heads, stride),
        grid=(count // rows,),
        in_specs=[row_block(rows, 3 * width), row_block(rows, width), row_block(rows, LANES)],
        out_specs=row_block(rows, 3 * width),
        out_shape=jax.ShapeDtypeStruct((count, 3 * width), BF16),
        scratch_shapes=[pltpu.VMEM((rows, padded), BF16)] * 4
        + [pltpu.VMEM((rows, padded), F32)] * 3,
        cost_estimate=pl.CostEstimate(
            flops=heads * count * rows * 2560,
            bytes_accessed=count * width * 14,
            transcendentals=heads * count * rows,
        ),
        compiler_params=pltpu.CompilerParams(vmem_limit_bytes=32 * 1024 * 1024),
    )(x, grad, lse)


def split_frames(v, frames, width):
    return v.reshape(frames, -1, width // HEAD_DIM, HEAD_DIM)


def attend_shared(x, frames):
    width = x.shape[1] // 3
    shaped = x.reshape(frames, -1, 3, width)
    pairs = lax.all_gather(shaped[:, :, 1:], "tp", axis=1, tiled=True)
    q = split_frames(shaped[:, :, 0], frames, width)
    k = split_frames(pairs[:, :, 0], frames, width)
    v = split_frames(pairs[:, :, 1], frames, width)
    scores = jnp.einsum("bqhe,bkhe->bhqk", q, k, preferred_element_type=F32) * SCALE
    chances = jax.nn.softmax(scores, axis=-1)
    result = jnp.einsum("bhqk,bkhe->bqhe", chances.astype(BF16), v, preferred_element_type=F32)
    return result.reshape(-1, width).astype(BF16), (q, k, v, chances)


def attend_shared_back(saved, grad):
    q, k, v, chances = saved
    frames, width = q.shape[0], grad.shape[1]
    grad = split_frames(grad, frames, width)
    grad_chances = jnp.einsum("bqhe,bkhe->bhqk", grad, v, preferred_element_type=F32)
    row_dot = jnp.sum(chances * grad_chances, axis=-1, keepdims=True)
    grad_scores = (chances * (grad_chances - row_dot)).astype(BF16)
    dq = jnp.einsum("bhqk,bkhe->bqhe", grad_scores, k, preferred_element_type=F32) * SCALE
    dk = jnp.einsum("bhqk,bqhe->bkhe", grad_scores, q, preferred_element_type=F32) * SCALE
    dv = jnp.einsum("bhqk,bqhe->bkhe", chances.astype(BF16), grad, preferred_element_type=F32)
    sums = lax.psum_scatter(jnp.stack([dk, dv], axis=2), "tp", scatter_dimension=1, tiled=True)
    parts = jnp.concatenate([dq[:, :, None], sums], axis=2)
    return parts.reshape(-1, 3 * width).astype(BF16)


def normalise(v):
    centred = v - jnp.mean(v, axis=-1, keepdims=True)
    inverse = lax.rsqrt(jnp.mean(centred * centred, axis=-1, keepdims=True) + EPS)
    return centred * inverse, inverse


def modulate(v, shift, scale):
    return (normalise(v)[0] * (1.0 + scale[:, None]) + shift[:, None]).astype(BF16)


def modulate_back(grad, v, scale):
    normed, inverse = normalise(v)
    shift_grad = jnp.sum(grad, axis=1)
    scale_grad = jnp.sum(grad * normed, axis=1)
    scaled = grad * (1.0 + scale[:, None])
    mean_one = jnp.mean(scaled, axis=-1, keepdims=True)
    mean_two = jnp.mean(scaled * normed, axis=-1, keepdims=True)
    return inverse * (scaled - mean_one - normed * mean_two), shift_grad, scale_grad


def gelu(v):
    return jax.nn.gelu(v, approximate=True)


def gelu_slope(v, grad):
    return jax.vjp(gelu, v)[1](grad)[0]


def local(moves, tokens, condition, micro_ids, w_qkv, w_out, w_up, w_down, w_ada, cotangent):
    moves.here()
    n_dp, n_ctx, n_tp = moves.n_dp, moves.n_ctx, moves.n_tp
    clips, frames_here, patches_here, width = tokens.shape
    rows_here, head_cols = w_qkv.shape[2:]
    whole_frames = frames_here % n_tp == 0
    spread_tp = n_tp if whole_frames else 1
    groups = frames_here // spread_tp
    piece = patches_here // n_ctx

    cond_full = condition.astype(F32)
    cond_low = jax.nn.silu(cond_full).astype(BF16)
    cond_all = jnp.concatenate([cond_low, swap_with(cond_low, "dp", n_dp, 1)], axis=0)
    first_row = (moves.dp * n_ctx + moves.ctx) * rows_here
    cond_rows = lax.dynamic_slice_in_dim(cond_all, first_row, rows_here, axis=1)
    ada_low = w_ada.astype(BF16)
    shares = jnp.stack([dot(cond_rows, ada_low[level]) for level in range(LAYERS)], axis=1)
    sums = shares[:clips] + swap_with(shares[clips:], "dp", n_dp, 1)
    step = 1
    while step < n_ctx:
        sums = sums + swap_with(sums, "ctx", n_ctx, step)
        step *= 2
    strips = [sums] + [swap_with(sums, "tp", n_tp, r) for r in range(1, n_tp)]
    strips = flip_to(jnp.stack(strips, axis=2), 2, n_tp, moves.tp)
    mods = strips.reshape(clips, LAYERS, 6, width)
    mods = [moves.halves(mods[:, 0]), mods[:, 1]]

    pieces = []
    for level in range(LAYERS):
        attention = [w_qkv[level, 0], w_qkv[level, 1], w_qkv[level, 2], w_out[level].T]
        pieces.append(jnp.concatenate(attention, axis=1).astype(BF16))
        pieces.append(w_up[level].astype(BF16))
        pieces.append(w_down[level].T.astype(BF16))
    gathered = moves.gather_weights(pieces[:3])
    later, gathered[0] = lax.optimization_barrier((pieces[3:], gathered[0]))
    gathered += [moves.gather_whole(v) for v in later]

    def to_frames(v):
        v = v.reshape(clips, frames_here, n_ctx, piece, width)
        v = flip_to(v, 2, n_ctx, moves.ctx)
        if spread_tp == 1:
            return v.reshape(clips, groups * patches_here, width)
        v = v.reshape(clips, spread_tp, groups, patches_here, width)
        v = flip_to(v, 1, spread_tp, moves.tp)
        blocks = [v[:, 0]]
        blocks += [swap_with(v[:, r], "tp", n_tp, r) for r in range(1, spread_tp)]
        return jnp.stack(blocks, axis=2).reshape(clips, -1, width)

    def from_frames(v):
        if spread_tp > 1:
            v = v.reshape(clips, groups, spread_tp, patches_here, width)
            blocks = [v[:, :, 0]]
            blocks += [swap_with(v[:, :, r], "tp", n_tp, r) for r in range(1, spread_tp)]
            v = flip_to(jnp.stack(blocks, axis=1), 1, spread_tp, moves.tp)
        v = v.reshape(clips, frames_here, n_ctx, piece, width)
        v = flip_to(v, 2, n_ctx, moves.ctx)
        return v.reshape(clips, frames_here, patches_here, width)

    def trade(get, planes):
        sides = []
        for dx, dr in planes:
            block = get(dx, dr)
            if dx or dr:
                pairs = [
                    (c * n_tp + t, (c ^ dx) * n_tp + (t ^ dr))
                    for c in range(n_ctx)
                    for t in range(n_tp)
                ]
                block = lax.ppermute(block, ("ctx", "tp"), pairs)
            sides.append(block)
        lines = []
        for dz in range(n_ctx // 2):
            block = jnp.stack([v[:, dz] for v in sides], axis=1)
            lines.append(swap_with(block, "ctx", n_ctx, 2 * dz) if dz else block)
        return jnp.stack(lines, axis=1)

    all_planes = [(dx, dr) for dx in range(2) for dr in range(spread_tp)]
    own_planes = [(0, 0), (1, 0)]

    def frames_to_clips(v):
        v = v.reshape(clips, groups, spread_tp, n_ctx // 2, 2, piece, width)
        got = trade(lambda dx, dr: v[:, :, dr, :, dx].swapaxes(1, 2), all_planes)
        return got.reshape(clips, -1, width)

    def clips_to_frames(v):
        v = v.reshape(clips, n_ctx // 2, 2, spread_tp, groups, piece, width)
        got = trade(lambda dx, dr: v[:, :, dx, dr], all_planes)
        got = got.reshape(clips, n_ctx, spread_tp, groups, piece, width)
        return got.transpose(0, 3, 2, 1, 4, 5).reshape(clips, -1, width)

    def here_to_clips(v):
        v = v.reshape(clips, spread_tp, groups, n_ctx, piece, width)
        v = flip_to(flip_to(v, 3, n_ctx, moves.ctx), 1, spread_tp, moves.tp % spread_tp)
        v = v.reshape(clips, spread_tp, groups, n_ctx // 2, 2, piece, width)
        got = trade(lambda dx, dr: v[:, :, :, :, dx].transpose(0, 3, 1, 2, 4, 5), own_planes)
        return got.reshape(clips, -1, width)

    def clips_to_here(v):
        v = v.reshape(clips, n_ctx // 2, 2, spread_tp, groups, piece, width)
        got = trade(lambda dx, dr: v[:, :, dx], own_planes)
        v = got.reshape(clips, n_ctx, spread_tp, groups, piece, width).transpose(0, 2, 3, 1, 4, 5)
        v = flip_to(flip_to(v, 3, n_ctx, moves.ctx), 1, spread_tp, moves.tp % spread_tp)
        return v.reshape(clips, frames_here, patches_here, width)

    def flat(v):
        return v.reshape(-1, v.shape[-1])

    def shaped(v):
        return v.reshape(clips, -1, v.shape[-1])

    residual = to_frames(moves.halves(tokens)).astype(F32)
    qkv_cols = 3 * head_cols
    records = []
    for level in range(LAYERS):
        spatial = level % 2 == 0
        joined, ups, downs = gathered[3 * level : 3 * level + 3]
        qkvs = [v[:, :qkv_cols] for v in joined]
        outs = [v[:, qkv_cols:] for v in joined]
        shift_a, scale_a, gate_a, shift_m, scale_m, gate_m = [mods[level][:, i] for i in range(6)]
        if not spatial:
            residual = frames_to_clips(moves.halves(residual.astype(BF16))).astype(F32)
        block_rows = groups * spread_tp * patches_here if not spatial else spread_tp * patches_here
        block_rows = residual.shape[1] if not spatial else block_rows
        stride = 1 if spatial else piece
        normed = flat(modulate(residual, shift_a, scale_a))
        projected = [dot(normed, v).astype(BF16) for v in qkvs]
        if spatial and not whole_frames:
            attended = [attend_shared(v, clips * frames_here) for v in projected]
        else:
            attended = [attend(v, block_rows, stride) for v in projected]
        results = [entry[0] for entry in attended]
        branch = sum(dot(v, w, NT) for v, w in zip(results, outs))
        branch = shaped(branch)
        middle = residual + gate_a[:, None] * branch
        normed_mlp = flat(modulate(middle, shift_m, scale_m))
        pre_acts = [dot(normed_mlp, w) for w in ups]
        acts = [gelu(v).astype(BF16) for v in pre_acts]
        branch_mlp = shaped(sum(dot(v, w, NT) for v, w in zip(acts, downs)))
        records.append(
            (residual, normed, projected, attended, results, branch, middle, normed_mlp)
            + (pre_acts, acts, branch_mlp, qkvs, outs, ups, downs, block_rows, stride)
        )
        residual = middle + gate_m[:, None] * branch_mlp
    output = clips_to_here(residual.astype(BF16))

    matched = (micro_ids[:, None] == micro_ids[None, :]).astype(F32)
    share = 1.0 / jnp.sum(matched, axis=1)
    gradient = here_to_clips(cotangent).astype(F32) * share[:, None, None]
    grads = [None] * LAYERS
    mod_grads = [None] * LAYERS
    for level in reversed(range(LAYERS)):
        spatial = level % 2 == 0

        def scatter(left, rights, tp_first, level=level):
            if level:
                return moves.scatter_whole(left, rights)
            return moves.scatter_weight(left, rights, tp_first)

        (residual, normed, projected, attended, results, branch, middle, normed_mlp) = records[
            level
        ][:8]
        (pre_acts, acts, branch_mlp, qkvs, outs, ups, downs, block_rows, stride) = records[level][
            8:
        ]
        shift_a, scale_a, gate_a, shift_m, scale_m, gate_m = [mods[level][:, i] for i in range(6)]
        gate_m_grad = jnp.sum(gradient * branch_mlp, axis=1)
        low_grad = flat((gradient * gate_m[:, None]).astype(BF16))
        grad_pre = [
            gelu_slope(u, dot(low_grad, w)).astype(BF16) for u, w in zip(pre_acts, downs)
        ]
        grad_down = scatter(low_grad, acts, True)
        grad_normed = shaped(sum(dot(v, w, NT) for v, w in zip(grad_pre, ups)))
        grad_up = scatter(normed_mlp, grad_pre, False)
        added, shift_m_grad, scale_m_grad = modulate_back(grad_normed, middle, scale_m)
        gradient = gradient + added
        gate_a_grad = jnp.sum(gradient * branch, axis=1)
        low_grad = flat((gradient * gate_a[:, None]).astype(BF16))
        grad_heads = [dot(low_grad, w).astype(BF16) for w in outs]
        grad_out = scatter(low_grad, results, True)
        if spatial and not whole_frames:
            grad_qkv = [attend_shared_back(e[1], g) for e, g in zip(attended, grad_heads)]
        else:
            grad_qkv = [
                attend_back(v, g, e[1], block_rows, stride)
                for v, g, e in zip(projected, grad_heads, attended)
            ]
        grad_normed = shaped(sum(dot(v, w, NT) for v, w in zip(grad_qkv, qkvs)))
        grad_in = scatter(normed, grad_qkv, False)
        added, shift_a_grad, scale_a_grad = modulate_back(grad_normed, residual, scale_a)
        gradient = gradient + added
        if not spatial:
            gradient = moves.halves(clips_to_frames(gradient.astype(BF16))).astype(F32)
        mod_grads[level] = jnp.stack(
            [shift_a_grad, scale_a_grad, gate_a_grad, shift_m_grad, scale_m_grad, gate_m_grad],
            axis=1,
        )
        grads[level] = (
            grad_in.reshape(rows_here, 3, head_cols).transpose(1, 0, 2),
            grad_out.T,
            grad_up,
            grad_down.T,
        )
    grad_tokens = from_frames(moves.halves(gradient.astype(BF16))).astype(F32)

    ada_grads = []
    cond_part = 0.0
    for level in range(LAYERS):
        whole = mod_grads[level] if level else moves.halves(mod_grads[level])
        whole = whole.reshape(clips, n_tp, -1)
        whole = flip_to(whole, 1, n_tp, moves.tp)
        strip = whole[:, 0]
        for r in range(1, n_tp):
            strip = strip + swap_with(whole[:, r], "tp", n_tp, r)
        step = 1
        while step < n_ctx:
            strip = strip + swap_with(strip, "ctx", n_ctx, step)
            step *= 2
        strip = jnp.concatenate([strip, swap_with(strip, "dp", n_dp, 1)], axis=0)
        ada_grads.append(
            lax.dot_general(cond_rows.astype(F32), strip, TN, precision=HIGHEST)
        )
        cond_part = cond_part + lax.dot_general(
            strip, ada_low[level].astype(F32), NT, precision=HIGHEST
        )
    step = 1
    while step < n_tp:
        cond_part = cond_part + swap_with(cond_part, "tp", n_tp, step)
        step *= 2
    cond_grad = jnp.stack(
        [cond_part[:clips], swap_with(cond_part[clips:], "dp", n_dp, 1)], axis=1
    )[:, :, None]
    step = 1
    while step < n_ctx:
        cond_grad = jnp.concatenate(
            [cond_grad, swap_with(cond_grad, "ctx", n_ctx, step)], axis=2
        )
        step *= 2
    cond_grad = flip_to(cond_grad, 2, n_ctx, moves.ctx).reshape(clips, width)
    cond_grad = moves.halves(cond_grad)
    grad_condition = jax.vjp(jax.nn.silu, cond_full)[1](cond_grad)[0]

    stacked = [jnp.stack([grads[level][i] for level in range(LAYERS)]) for i in range(4)]
    return (output, grad_tokens, grad_condition, *stacked, jnp.stack(ada_grads))


def solution(mesh):
    placed = (
        P("dp", "ctx", "tp", None),
        P("dp", None),
        P("dp"),
        P(None, None, ("dp", "ctx"), "tp"),
        P(None, "tp", ("dp", "ctx")),
        P(None, ("dp", "ctx"), "tp"),
        P(None, "tp", ("dp", "ctx")),
        P(None, ("dp", "ctx"), "tp"),
        P("dp", "ctx", "tp", None),
    )
    return jax.shard_map(
        functools.partial(local, Moves(mesh)),
        mesh=mesh,
        in_specs=placed,
        out_specs=(
            P("dp", "ctx", "tp", None),
            P("dp", "ctx", "tp", None),
            P("dp", None),
            P(None, None, ("dp", "ctx"), "tp"),
            P(None, "tp", ("dp", "ctx")),
            P(None, ("dp", "ctx"), "tp"),
            P(None, "tp", ("dp", "ctx")),
            P(None, ("dp", "ctx"), "tp"),
        ),
        check_vma=False,
    )
```

```python
import functools

import jax
import jax.numpy as jnp
from jax import lax
from jax.experimental import pallas as pl
from jax.experimental.pallas import tpu as pltpu
from jax.sharding import PartitionSpec as P

HEAD_DIM = 72
LAYERS = 2
LANES = 128
EPS = 1e-06
SCALE = HEAD_DIM ** (-0.5)
HIGHEST = lax.Precision.HIGHEST
BF16 = jnp.bfloat16
F32 = jnp.float32

NN = (((1,), (0,)), ((), ()))
NT = (((1,), (1,)), ((), ()))
TN = (((0,), (0,)), ((), ()))


def dot(a, b, dims=NN):
    return lax.dot_general(a, b, dims, preferred_element_type=F32)


def swap_with(v, axis_name, n, k):
    return lax.ppermute(v, axis_name, [(i, i ^ k) for i in range(n)])


def flip_to(v, axis, n, me):
    shape = v.shape
    bit = 1
    while bit < n:
        split = shape[:axis] + (n // (2 * bit), 2, bit) + shape[axis + 1 :]
        parts = v.reshape(split)
        first = lax.slice_in_dim(parts, 0, 1, axis=axis + 1)
        second = lax.slice_in_dim(parts, 1, 2, axis=axis + 1)
        turned = jnp.concatenate([second, first], axis=axis + 1)
        v = jnp.where((me & bit) != 0, turned, parts).reshape(shape)
        bit *= 2
    return v


class Moves:
    def __init__(self, mesh):
        self.n_dp = mesh.shape["dp"]
        self.n_ctx = mesh.shape["ctx"]
        self.n_tp = mesh.shape["tp"]
        self.n_line = self.n_ctx // 2

    def here(self):
        self.dp = lax.axis_index("dp")
        self.ctx = lax.axis_index("ctx")
        self.tp = lax.axis_index("tp")
        self.line = self.ctx // 2
        self.side = self.ctx % 2

    def halves(self, v):
        half = v.shape[-1] // 2
        turned = jnp.concatenate([v[..., half:], v[..., :half]], axis=-1)
        return jnp.where(self.dp == 0, v, turned)

    def pair_stack(self, v, other):
        first = jnp.where(self.side == 0, v, other)
        second = jnp.where(self.side == 0, other, v)
        both = jnp.stack([first, second], axis=-3)
        return both.reshape(v.shape[:-3] + (-1, v.shape[-1]))

    def of_side(self, v, side):
        parts = v.reshape(self.n_line, 2, -1, v.shape[-1])
        return lax.dynamic_index_in_dim(parts, side, 1, keepdims=False)

    def over_tp(self, v, r):
        return swap_with(v, "tp", self.n_tp, r)

    def over_side(self, v):
        return swap_with(v, "ctx", self.n_ctx, 1)

    def over_core(self, v):
        return swap_with(v, "dp", self.n_dp, 1)

    def gather_weight(self, v):
        others = range(1, self.n_tp)
        got = [swap_with(v, "ctx", self.n_ctx, 2 * k) for k in range(1, self.n_line)]
        got = yield got
        half = v.shape[1] // 2
        lines = [
            flip_to(jnp.stack([b[:, cut] for b in [v] + got]), 0, self.n_line, self.line)
            for cut in (slice(0, half), slice(half, None))
        ]
        got = self.over_side(lines[0]), [self.over_tp(lines[1], r) for r in others]
        side_got, tp_got = yield got
        block = self.pair_stack(lines[0], side_got)
        strips = jnp.stack([lines[1]] + tp_got)
        got = [self.over_tp(block, r) for r in others], self.over_side(strips)
        tp_got, side_got = yield got
        first = [block] + tp_got
        second = self.pair_stack(strips, side_got)
        mine = jnp.concatenate(
            [part for r in range(self.n_tp) for part in (first[r], second[r])], axis=1
        )
        return mine, self.over_core(mine)

    def scatter_weight(self, left, rights):
        others = range(1, self.n_tp)
        half_width = left.shape[1] // 2
        mine, theirs = left[:, :half_width], left[:, half_width:]
        got = [self.over_core(dot(theirs, v, TN).astype(BF16)) for v in rights]
        got = yield got
        totals = [(dot(mine, v, TN) + g.astype(F32)).astype(BF16) for v, g in zip(rights, got)]
        if len(totals) == 1:
            totals = jnp.split(totals[0], self.n_tp, axis=1)
        columns = totals[0].shape[1]
        half = max(columns // 2 // LANES, 1) * LANES
        firsts = [v[:, :half] for v in totals]
        seconds = jnp.concatenate([v[:, half:] for v in totals], axis=1)
        got = (
            [self.over_tp(firsts[r], r) for r in others],
            self.over_side(self.of_side(seconds, 1 - self.side)),
        )
        tp_got, side_got = yield got
        first = (firsts[0].astype(F32) + sum(v.astype(F32) for v in tp_got)).astype(BF16)
        second = self.of_side(seconds, self.side).astype(F32) + side_got.astype(F32)
        second = jnp.split(second.astype(BF16), self.n_tp, axis=-1)
        got = (
            self.over_side(self.of_side(first, 1 - self.side)),
            [self.over_tp(second[r], r) for r in others],
        )
        side_got, tp_got = yield got
        first = self.of_side(first, self.side).astype(F32) + side_got.astype(F32)
        second = second[0].astype(F32) + sum(v.astype(F32) for v in tp_got)
        line = jnp.concatenate([first, second], axis=-1).astype(BF16)
        got = yield [
            swap_with(
                lax.dynamic_index_in_dim(line, self.line ^ k, 0, keepdims=False),
                "ctx",
                self.n_ctx,
                2 * k,
            )
            for k in range(1, self.n_line)
        ]
        own = lax.dynamic_index_in_dim(line, self.line, 0, keepdims=False)
        return own.astype(F32) + sum(v.astype(F32) for v in got)


class Task:
    def __init__(self, steps):
        self.steps, self.result = steps, None
        self.pending = next(steps)


class Lanes:
    def __init__(self):
        self.tasks = []

    def start(self, steps):
        task = Task(steps)
        self.tasks.append(task)
        return task

    def fence(self, values=()):
        values, pending = lax.optimization_barrier((values, [t.pending for t in self.tasks]))
        going = []
        for task, done in zip(self.tasks, pending):
            try:
                task.pending = task.steps.send(done)
                going.append(task)
            except StopIteration as stop:
                task.result = stop.value
        self.tasks = going
        return values


def window(head):
    start = head * HEAD_DIM
    return start // LANES * LANES, -(-(start + HEAD_DIM) // LANES) * LANES


def in_head(head, rows, low, high):
    lanes = lax.broadcasted_iota(jnp.int32, (rows, high - low), 1) + low
    return (lanes >= head * HEAD_DIM) & (lanes < (head + 1) * HEAD_DIM)


def spread_parts(x_ref, offset, parts, width):
    for index, part in enumerate(parts):
        padded = part.shape[1]
        start = offset + index * width
        if padded != width:
            part[:, padded - LANES :] = jnp.zeros((part.shape[0], LANES), part.dtype)
        part[:, :width] = x_ref[:, start : start + width]


def same_sequence(rows, stride):
    row = lax.broadcasted_iota(jnp.int32, (rows, rows), 0)
    column = lax.broadcasted_iota(jnp.int32, (rows, rows), 1)
    return lax.rem(row, stride) == lax.rem(column, stride)


def attend_kernel(count, width, stride, *refs):
    x_refs, (o_ref, lse_ref, q_s, k_s, v_s, o_s) = refs[:count], refs[count:]
    heads, rows = width // HEAD_DIM, o_ref.shape[0]
    lane = lax.broadcasted_iota(jnp.int32, (rows, LANES), 1)
    logs = jnp.zeros((rows, LANES), F32)
    if stride > 1:
        allowed = same_sequence(rows, stride)
    for index, x_ref in enumerate(x_refs):
        spread_parts(x_ref, 0, (q_s, k_s, v_s), width)
        for head in range(heads):
            low, high = window(head)
            mask = in_head(head, rows, low, high)
            queries = jnp.where(mask, q_s[:, low:high], jnp.zeros((), BF16))
            scores = dot(queries, k_s[:, low:high], NT) * SCALE
            if stride > 1:
                scores = jnp.where(allowed, scores, -jnp.inf)
            largest = jnp.max(scores, axis=-1, keepdims=True)
            raised = jnp.exp(scores - largest)
            total = jnp.sum(raised, axis=-1, keepdims=True)
            chances = (raised * (1.0 / total)).astype(BF16)
            result = dot(chances, v_s[:, low:high])
            o_s[:, low:high] = jnp.where(mask, result, o_s[:, low:high])
            logs = jnp.where(lane == index * heads + head, largest + jnp.log(total), logs)
        o_ref[:, index * width : (index + 1) * width] = o_s[:, :width].astype(BF16)
    lse_ref[...] = logs


def attend_back_kernel(count, width, stride, *refs):
    x_refs, (g_ref, lse_ref), dx_refs = refs[:count], refs[count : count + 2], refs[count + 2 : -7]
    q_s, k_s, v_s, g_s, dq_s, dk_s, dv_s = refs[-7:]
    heads, rows = width // HEAD_DIM, g_ref.shape[0]
    if stride > 1:
        allowed = same_sequence(rows, stride)
    for index, x_ref in enumerate(x_refs):
        spread_parts(x_ref, 0, (q_s, k_s, v_s), width)
        spread_parts(g_ref, index * width, (g_s,), width)
        for head in range(heads):
            low, high = window(head)
            mask = in_head(head, rows, low, high)
            zero = jnp.zeros((), BF16)
            q, k, v, g = q_s[:, low:high], k_s[:, low:high], v_s[:, low:high], g_s[:, low:high]
            scores = dot(jnp.where(mask, q, zero), k, NT) * SCALE
            if stride > 1:
                scores = jnp.where(allowed, scores, -jnp.inf)
            place = index * heads + head
            chances = jnp.exp(scores - lse_ref[:, place : place + 1])
            grad_chances = dot(jnp.where(mask, g, zero), v, NT)
            row_dot = jnp.sum(chances * grad_chances, axis=-1, keepdims=True)
            grad_scores = (chances * (grad_chances - row_dot)).astype(BF16)
            dq = dot(grad_scores, k) * SCALE
            dk = dot(grad_scores, q, TN) * SCALE
            dv = dot(chances.astype(BF16), g, TN)
            dq_s[:, low:high] = jnp.where(mask, dq, dq_s[:, low:high])
            dk_s[:, low:high] = jnp.where(mask, dk, dk_s[:, low:high])
            dv_s[:, low:high] = jnp.where(mask, dv, dv_s[:, low:high])
        for part_index, part in enumerate((dq_s, dk_s, dv_s)):
            start = part_index * width
            dx_refs[index][:, start : start + width] = part[:, :width].astype(BF16)


def row_block(rows, columns):
    return pl.BlockSpec((rows, columns), lambda i: (i, 0))


def attend(xs, rows, stride):
    count, width = xs[0].shape[0], xs[0].shape[1] // 3
    strips = len(xs)
    heads = strips * width // HEAD_DIM
    padded = -(-width // LANES) * LANES
    return pl.pallas_call(
        functools.partial(attend_kernel, strips, width, stride),
        grid=(count // rows,),
        in_specs=[row_block(rows, 3 * width)] * strips,
        out_specs=[row_block(rows, strips * width), row_block(rows, LANES)],
        out_shape=[
            jax.ShapeDtypeStruct((count, strips * width), BF16),
            jax.ShapeDtypeStruct((count, LANES), F32),
        ],
        scratch_shapes=[pltpu.VMEM((rows, padded), BF16)] * 3 + [pltpu.VMEM((rows, padded), F32)],
        cost_estimate=pl.CostEstimate(
            flops=heads * count * rows * 1024,
            bytes_accessed=count * width * strips * 8,
            transcendentals=heads * count * rows,
        ),
        compiler_params=pltpu.CompilerParams(vmem_limit_bytes=32 * 1024 * 1024),
    )(*xs)


def attend_back(xs, grad, lse, rows, stride):
    count, width = xs[0].shape[0], xs[0].shape[1] // 3
    strips = len(xs)
    heads = strips * width // HEAD_DIM
    padded = -(-width // LANES) * LANES
    return pl.pallas_call(
        functools.partial(attend_back_kernel, strips, width, stride),
        grid=(count // rows,),
        in_specs=[row_block(rows, 3 * width)] * strips
        + [row_block(rows, strips * width), row_block(rows, LANES)],
        out_specs=[row_block(rows, 3 * width)] * strips,
        out_shape=[jax.ShapeDtypeStruct((count, 3 * width), BF16)] * strips,
        scratch_shapes=[pltpu.VMEM((rows, padded), BF16)] * 4
        + [pltpu.VMEM((rows, padded), F32)] * 3,
        cost_estimate=pl.CostEstimate(
            flops=heads * count * rows * 2560,
            bytes_accessed=count * width * strips * 14,
            transcendentals=heads * count * rows,
        ),
        compiler_params=pltpu.CompilerParams(vmem_limit_bytes=32 * 1024 * 1024),
    )(*xs, grad, lse)


def split_frames(v, frames, width):
    return v.reshape(frames, -1, width // HEAD_DIM, HEAD_DIM)


def attend_shared(x, frames):
    width = x.shape[1] // 3
    shaped = x.reshape(frames, -1, 3, width)
    pairs = lax.all_gather(shaped[:, :, 1:], "tp", axis=1, tiled=True)
    q = split_frames(shaped[:, :, 0], frames, width)
    k = split_frames(pairs[:, :, 0], frames, width)
    v = split_frames(pairs[:, :, 1], frames, width)
    scores = jnp.einsum("bqhe,bkhe->bhqk", q, k, preferred_element_type=F32) * SCALE
    chances = jax.nn.softmax(scores, axis=-1)
    result = jnp.einsum("bhqk,bkhe->bqhe", chances.astype(BF16), v, preferred_element_type=F32)
    return result.reshape(-1, width).astype(BF16), (q, k, v, chances)


def attend_shared_back(saved, grad):
    q, k, v, chances = saved
    frames, width = q.shape[0], grad.shape[1]
    grad = split_frames(grad, frames, width)
    grad_chances = jnp.einsum("bqhe,bkhe->bhqk", grad, v, preferred_element_type=F32)
    row_dot = jnp.sum(chances * grad_chances, axis=-1, keepdims=True)
    grad_scores = (chances * (grad_chances - row_dot)).astype(BF16)
    dq = jnp.einsum("bhqk,bkhe->bqhe", grad_scores, k, preferred_element_type=F32) * SCALE
    dk = jnp.einsum("bhqk,bqhe->bkhe", grad_scores, q, preferred_element_type=F32) * SCALE
    dv = jnp.einsum("bhqk,bqhe->bkhe", chances.astype(BF16), grad, preferred_element_type=F32)
    sums = lax.psum_scatter(jnp.stack([dk, dv], axis=2), "tp", scatter_dimension=1, tiled=True)
    parts = jnp.concatenate([dq[:, :, None], sums], axis=2)
    return parts.reshape(-1, 3 * width).astype(BF16)


def normalise(v):
    centred = v - jnp.mean(v, axis=-1, keepdims=True)
    inverse = lax.rsqrt(jnp.mean(centred * centred, axis=-1, keepdims=True) + EPS)
    return centred * inverse, inverse


def modulate(v, shift, scale):
    return (normalise(v)[0] * (1.0 + scale[:, None]) + shift[:, None]).astype(BF16)


def modulate_back(grad, v, scale):
    normed, inverse = normalise(v)
    shift_grad = jnp.sum(grad, axis=1)
    scale_grad = jnp.sum(grad * normed, axis=1)
    scaled = grad * (1.0 + scale[:, None])
    mean_one = jnp.mean(scaled, axis=-1, keepdims=True)
    mean_two = jnp.mean(scaled * normed, axis=-1, keepdims=True)
    return inverse * (scaled - mean_one - normed * mean_two), shift_grad, scale_grad


def gelu(v):
    return jax.nn.gelu(v, approximate=True)


def gelu_slope(v, grad):
    return jax.vjp(gelu, v)[1](grad)[0]


def local(moves, tokens, condition, micro_ids, w_qkv, w_out, w_up, w_down, w_ada, cotangent):
    moves.here()
    n_dp, n_ctx, n_tp = moves.n_dp, moves.n_ctx, moves.n_tp
    clips, frames_here, patches_here, width = tokens.shape
    rows_here, head_cols = w_qkv.shape[2:]
    whole_frames = frames_here % n_tp == 0
    spread_tp = n_tp if whole_frames else 1
    groups = frames_here // spread_tp
    piece = patches_here // n_ctx

    cond_full = condition.astype(F32)
    cond_low = jax.nn.silu(cond_full).astype(BF16)
    cond_all = jnp.concatenate([cond_low, swap_with(cond_low, "dp", n_dp, 1)], axis=0)
    first_row = (moves.dp * n_ctx + moves.ctx) * rows_here
    cond_rows = lax.dynamic_slice_in_dim(cond_all, first_row, rows_here, axis=1)
    ada_low = w_ada.astype(BF16)
    shares = jnp.stack([dot(cond_rows, ada_low[level]) for level in range(LAYERS)], axis=1)
    sums = shares[:clips] + swap_with(shares[clips:], "dp", n_dp, 1)
    step = 1
    while step < n_ctx:
        sums = sums + swap_with(sums, "ctx", n_ctx, step)
        step *= 2
    strips = [sums] + [swap_with(sums, "tp", n_tp, r) for r in range(1, n_tp)]
    strips = flip_to(jnp.stack(strips, axis=2), 2, n_tp, moves.tp)
    mods = strips.reshape(clips, LAYERS, 6, width)
    mods = [moves.halves(mods[:, level]) for level in range(LAYERS)]

    def to_frames(v):
        v = v.reshape(clips, frames_here, n_ctx, piece, width)
        v = flip_to(v, 2, n_ctx, moves.ctx)
        if spread_tp == 1:
            yield ()
            return v.reshape(clips, groups * patches_here, width)
        v = v.reshape(clips, spread_tp, groups, patches_here, width)
        v = flip_to(v, 1, spread_tp, moves.tp)
        got = yield [swap_with(v[:, r], "tp", n_tp, r) for r in range(1, spread_tp)]
        return jnp.stack([v[:, 0]] + got, axis=2).reshape(clips, -1, width)

    def from_frames(v):
        if spread_tp > 1:
            v = v.reshape(clips, groups, spread_tp, patches_here, width)
            blocks = [v[:, :, 0]]
            blocks += [swap_with(v[:, :, r], "tp", n_tp, r) for r in range(1, spread_tp)]
            v = flip_to(jnp.stack(blocks, axis=1), 1, spread_tp, moves.tp)
        v = v.reshape(clips, frames_here, n_ctx, piece, width)
        v = flip_to(v, 2, n_ctx, moves.ctx)
        return v.reshape(clips, frames_here, patches_here, width)

    def trade(get, planes):
        sides = []
        for dx, dr in planes:
            block = get(dx, dr)
            if dx or dr:
                pairs = [
                    (c * n_tp + t, (c ^ dx) * n_tp + (t ^ dr))
                    for c in range(n_ctx)
                    for t in range(n_tp)
                ]
                block = lax.ppermute(block, ("ctx", "tp"), pairs)
            sides.append(block)
        sides = sides[:1] + (yield sides[1:])
        lines = [jnp.stack([v[:, dz] for v in sides], axis=1) for dz in range(n_ctx // 2)]
        got = yield [swap_with(v, "ctx", n_ctx, 2 * dz) for dz, v in enumerate(lines) if dz]
        return jnp.stack(lines[:1] + got, axis=1)

    all_planes = [(dx, dr) for dx in range(2) for dr in range(spread_tp)]
    own_planes = [(0, 0), (1, 0)]

    def frames_to_clips(v):
        v = v.reshape(clips, groups, spread_tp, n_ctx // 2, 2, piece, width)
        got = yield from trade(lambda dx, dr: v[:, :, dr, :, dx].swapaxes(1, 2), all_planes)
        return got.reshape(clips, -1, width)

    def clips_to_frames(v):
        v = v.reshape(clips, n_ctx // 2, 2, spread_tp, groups, piece, width)
        got = yield from trade(lambda dx, dr: v[:, :, dx, dr], all_planes)
        got = got.reshape(clips, n_ctx, spread_tp, groups, piece, width)
        return got.transpose(0, 3, 2, 1, 4, 5).reshape(clips, -1, width)

    def here_to_clips(v):
        v = v.reshape(clips, spread_tp, groups, n_ctx, piece, width)
        v = flip_to(flip_to(v, 3, n_ctx, moves.ctx), 1, spread_tp, moves.tp % spread_tp)
        v = v.reshape(clips, spread_tp, groups, n_ctx // 2, 2, piece, width)
        got = yield from trade(lambda dx, dr: v[:, :, :, :, dx].transpose(0, 3, 1, 2, 4, 5), own_planes)
        return got.reshape(clips, -1, width)

    def clips_to_here(v):
        v = v.reshape(clips, n_ctx // 2, 2, spread_tp, groups, piece, width)
        got = yield from trade(lambda dx, dr: v[:, :, dx], own_planes)
        v = got.reshape(clips, n_ctx, spread_tp, groups, piece, width).transpose(0, 2, 3, 1, 4, 5)
        v = flip_to(flip_to(v, 3, n_ctx, moves.ctx), 1, spread_tp, moves.tp % spread_tp)
        return v.reshape(clips, frames_here, patches_here, width)

    def flat(v):
        return v.reshape(-1, v.shape[-1])

    def shaped(v):
        return v.reshape(clips, -1, v.shape[-1])

    shards = []
    for level in range(LAYERS):
        attention = [w_qkv[level, 0], w_qkv[level, 1], w_qkv[level, 2], w_out[level].T]
        shards.append(jnp.concatenate(attention, axis=1).astype(BF16))
        shards.append(w_up[level].astype(BF16))
        shards.append(w_down[level].T.astype(BF16))
    lanes = Lanes()
    gathers = []

    def tick(values=()):
        rest, values = lanes.fence((shards[len(gathers) :], values))
        if rest:
            gathers.append(lanes.start(moves.gather_weight(rest[0])))
        return values

    def whole(index):
        return jnp.concatenate(gathers[index].result, axis=0)

    def attention_weights(index):
        v = whole(index)
        strips = jnp.split(v, n_tp, axis=1)
        cut = 3 * head_cols
        return [w[:, :cut] for w in strips], jnp.concatenate([w[:, cut:] for w in strips], axis=1)

    def modulations(level):
        return [mods[level][:, i] for i in range(6)]

    moved = lanes.start(to_frames(moves.halves(tokens)))
    gathers.append(lanes.start(moves.gather_weight(shards[0])))
    tick()
    residual = moved.result.astype(F32)
    tick()
    tick()
    records = []
    for level in range(LAYERS):
        spatial = level % 2 == 0
        shift_a, scale_a, gate_a, shift_m, scale_m, gate_m = modulations(level)
        normed = flat(modulate(residual, shift_a, scale_a))
        qkvs, outs = attention_weights(3 * level)
        projected = [dot(normed, v).astype(BF16) for v in qkvs]
        rows, stride = (patches_here * spread_tp, 1) if spatial else (residual.shape[1], piece)
        if spatial and not whole_frames:
            saved = [attend_shared(v, clips * frames_here) for v in projected]
            result = jnp.concatenate([entry[0] for entry in saved], axis=1)
            saved = [entry[1] for entry in saved]
        else:
            result, saved = attend(projected, rows, stride)
        result, saved = tick((result, saved))
        branch = shaped(dot(result, outs, NT))
        middle = residual + gate_a[:, None] * branch
        normed_mlp = flat(modulate(middle, shift_m, scale_m))
        up = whole(3 * level + 1)
        pre_act = dot(normed_mlp, up)
        act = gelu(pre_act).astype(BF16)
        act, pre_act = tick((act, pre_act))
        down = whole(3 * level + 2)
        branch_mlp = shaped(dot(act, down, NT))
        records.append(
            (residual, normed, projected, saved, result, branch, middle, normed_mlp)
            + (pre_act, act, branch_mlp, qkvs, outs, up, down, rows, stride)
        )
        residual = middle + gate_m[:, None] * branch_mlp
        if spatial:
            moved = lanes.start(frames_to_clips(residual.astype(BF16)))
            tick()
            turned = lanes.start(here_to_clips(moves.halves(cotangent)))
            tick()
            residual = moved.result.astype(F32)
    matched = (micro_ids[:, None] == micro_ids[None, :]).astype(F32)
    share = 1.0 / jnp.sum(matched, axis=1)
    gradient = turned.result.astype(F32) * share[:, None, None]
    finished = lanes.start(clips_to_here(moves.halves(residual.astype(BF16))))
    scatters = {}
    mod_grads = [None] * LAYERS
    for level in reversed(range(LAYERS)):
        spatial = level % 2 == 0
        (residual, normed, projected, saved, result, branch, middle, normed_mlp) = records[level][
            :8
        ]
        (pre_act, act, branch_mlp, qkvs, outs, up, down, rows, stride) = records[level][8:]
        shift_a, scale_a, gate_a, shift_m, scale_m, gate_m = modulations(level)
        gate_m_grad = jnp.sum(gradient * branch_mlp, axis=1)
        low_grad = flat((gradient * gate_m[:, None]).astype(BF16))
        grad_pre = gelu_slope(pre_act, dot(low_grad, down)).astype(BF16)
        scatters[level, "down"] = lanes.start(moves.scatter_weight(low_grad, [act]))
        grad_pre = lanes.fence(grad_pre)
        grad_normed = shaped(dot(grad_pre, up, NT))
        scatters[level, "up"] = lanes.start(moves.scatter_weight(normed_mlp, [grad_pre]))
        grad_normed = lanes.fence(grad_normed)
        added, shift_m_grad, scale_m_grad = modulate_back(grad_normed, middle, scale_m)
        gradient = gradient + added
        gate_a_grad = jnp.sum(gradient * branch, axis=1)
        low_grad = flat((gradient * gate_a[:, None]).astype(BF16))
        grad_heads = dot(low_grad, outs).astype(BF16)
        scatters[level, "out"] = lanes.start(moves.scatter_weight(low_grad, [result]))
        grad_heads = lanes.fence(grad_heads)
        if spatial and not whole_frames:
            grad_qkv = [
                attend_shared_back(v, g)
                for v, g in zip(saved, jnp.split(grad_heads, n_tp, axis=1))
            ]
        else:
            grad_qkv = attend_back(projected, grad_heads, saved, rows, stride)
        grad_qkv = lanes.fence(grad_qkv)
        scatters[level, "qkv"] = lanes.start(moves.scatter_weight(normed, grad_qkv))
        grad_normed = shaped(sum(dot(v, w, NT) for v, w in zip(grad_qkv, qkvs)))
        added, shift_a_grad, scale_a_grad = modulate_back(grad_normed, residual, scale_a)
        gradient = gradient + added
        mod_grads[level] = jnp.stack(
            [shift_a_grad, scale_a_grad, gate_a_grad, shift_m_grad, scale_m_grad, gate_m_grad],
            axis=1,
        )
        if not spatial:
            moved = lanes.start(clips_to_frames(gradient.astype(BF16)))
            lanes.fence()
            lanes.fence()
            gradient = moved.result.astype(F32)
    grad_tokens = from_frames(moves.halves(gradient.astype(BF16))).astype(F32)
    while lanes.tasks:
        lanes.fence()
    output = finished.result
    grads = [
        (
            scatters[level, "qkv"].result.reshape(rows_here, 3, head_cols).transpose(1, 0, 2),
            scatters[level, "out"].result.T,
            scatters[level, "up"].result,
            scatters[level, "down"].result.T,
        )
        for level in range(LAYERS)
    ]

    ada_grads = []
    cond_part = 0.0
    for level in range(LAYERS):
        strips = moves.halves(mod_grads[level]).reshape(clips, n_tp, -1)
        strips = flip_to(strips, 1, n_tp, moves.tp)
        strip = strips[:, 0]
        for r in range(1, n_tp):
            strip = strip + swap_with(strips[:, r], "tp", n_tp, r)
        step = 1
        while step < n_ctx:
            strip = strip + swap_with(strip, "ctx", n_ctx, step)
            step *= 2
        strip = jnp.concatenate([strip, swap_with(strip, "dp", n_dp, 1)], axis=0)
        ada_grads.append(
            lax.dot_general(cond_rows.astype(F32), strip, TN, precision=HIGHEST)
        )
        cond_part = cond_part + lax.dot_general(
            strip, ada_low[level].astype(F32), NT, precision=HIGHEST
        )
    step = 1
    while step < n_tp:
        cond_part = cond_part + swap_with(cond_part, "tp", n_tp, step)
        step *= 2
    cond_grad = jnp.stack(
        [cond_part[:clips], swap_with(cond_part[clips:], "dp", n_dp, 1)], axis=1
    )[:, :, None]
    step = 1
    while step < n_ctx:
        cond_grad = jnp.concatenate(
            [cond_grad, swap_with(cond_grad, "ctx", n_ctx, step)], axis=2
        )
        step *= 2
    cond_grad = flip_to(cond_grad, 2, n_ctx, moves.ctx).reshape(clips, width)
    cond_grad = moves.halves(cond_grad)
    grad_condition = jax.vjp(jax.nn.silu, cond_full)[1](cond_grad)[0]

    stacked = [jnp.stack([grads[level][i] for level in range(LAYERS)]) for i in range(4)]
    return (output, grad_tokens, grad_condition, *stacked, jnp.stack(ada_grads))


def solution(mesh):
    placed = (
        P("dp", "ctx", "tp", None),
        P("dp", None),
        P("dp"),
        P(None, None, ("dp", "ctx"), "tp"),
        P(None, "tp", ("dp", "ctx")),
        P(None, ("dp", "ctx"), "tp"),
        P(None, "tp", ("dp", "ctx")),
        P(None, ("dp", "ctx"), "tp"),
        P("dp", "ctx", "tp", None),
    )
    return jax.shard_map(
        functools.partial(local, Moves(mesh)),
        mesh=mesh,
        in_specs=placed,
        out_specs=(
            P("dp", "ctx", "tp", None),
            P("dp", "ctx", "tp", None),
            P("dp", None),
            P(None, None, ("dp", "ctx"), "tp"),
            P(None, "tp", ("dp", "ctx")),
            P(None, ("dp", "ctx"), "tp"),
            P(None, "tp", ("dp", "ctx")),
            P(None, ("dp", "ctx"), "tp"),
        ),
        check_vma=False,
    )
```

```python
import functools

import jax
import jax.numpy as jnp
from jax import lax
from jax.experimental import pallas as pl
from jax.experimental.pallas import tpu as pltpu
from jax.sharding import PartitionSpec as P

HEAD_DIM = 72
LAYERS = 2
LANES = 128
EPS = 1e-06
SCALE = HEAD_DIM ** (-0.5)
HIGHEST = lax.Precision.HIGHEST
BF16 = jnp.bfloat16
F32 = jnp.float32

NN = (((1,), (0,)), ((), ()))
NT = (((1,), (1,)), ((), ()))
TN = (((0,), (0,)), ((), ()))


def dot(a, b, dims=NN):
    return lax.dot_general(a, b, dims, preferred_element_type=F32)


def swap_with(v, axis_name, n, k):
    return lax.ppermute(v, axis_name, [(i, i ^ k) for i in range(n)])


def flip_to(v, axis, n, me):
    shape = v.shape
    bit = 1
    while bit < n:
        split = shape[:axis] + (n // (2 * bit), 2, bit) + shape[axis + 1 :]
        parts = v.reshape(split)
        first = lax.slice_in_dim(parts, 0, 1, axis=axis + 1)
        second = lax.slice_in_dim(parts, 1, 2, axis=axis + 1)
        turned = jnp.concatenate([second, first], axis=axis + 1)
        v = jnp.where((me & bit) != 0, turned, parts).reshape(shape)
        bit *= 2
    return v


class Moves:
    def __init__(self, mesh):
        self.n_dp = mesh.shape["dp"]
        self.n_ctx = mesh.shape["ctx"]
        self.n_tp = mesh.shape["tp"]
        self.n_line = self.n_ctx // 2

    def here(self):
        self.dp = lax.axis_index("dp")
        self.ctx = lax.axis_index("ctx")
        self.tp = lax.axis_index("tp")
        self.line = self.ctx // 2
        self.side = self.ctx % 2

    def halves(self, v):
        half = v.shape[-1] // 2
        turned = jnp.concatenate([v[..., half:], v[..., :half]], axis=-1)
        return jnp.where(self.dp == 0, v, turned)

    def pair_stack(self, v, other):
        first = jnp.where(self.side == 0, v, other)
        second = jnp.where(self.side == 0, other, v)
        both = jnp.stack([first, second], axis=-3)
        return both.reshape(v.shape[:-3] + (-1, v.shape[-1]))

    def of_side(self, v, side):
        parts = v.reshape(self.n_line, 2, -1, v.shape[-1])
        return lax.dynamic_index_in_dim(parts, side, 1, keepdims=False)

    def over_tp(self, v, r):
        return swap_with(v, "tp", self.n_tp, r)

    def over_side(self, v):
        return swap_with(v, "ctx", self.n_ctx, 1)

    def over_core(self, v):
        return swap_with(v, "dp", self.n_dp, 1)

    def gather_weight(self, v):
        others = range(1, self.n_tp)
        got = [swap_with(v, "ctx", self.n_ctx, 2 * k) for k in range(1, self.n_line)]
        got = yield got
        half = v.shape[1] // 2
        lines = [
            flip_to(jnp.stack([b[:, cut] for b in [v] + got]), 0, self.n_line, self.line)
            for cut in (slice(0, half), slice(half, None))
        ]
        got = self.over_side(lines[0]), [self.over_tp(lines[1], r) for r in others]
        side_got, tp_got = yield got
        block = self.pair_stack(lines[0], side_got)
        strips = jnp.stack([lines[1]] + tp_got)
        got = [self.over_tp(block, r) for r in others], self.over_side(strips)
        tp_got, side_got = yield got
        first = [block] + tp_got
        second = self.pair_stack(strips, side_got)
        mine = first + [second]
        return mine + [self.over_core(v) for v in mine]

    def scatter_weight(self, left, rights):
        others = range(1, self.n_tp)
        half_width = left.shape[1] // 2
        mine, theirs = left[:, :half_width], left[:, half_width:]
        got = [self.over_core(dot(theirs, v, TN).astype(BF16)) for v in rights]
        got = yield got
        totals = [(dot(mine, v, TN) + g.astype(F32)).astype(BF16) for v, g in zip(rights, got)]
        if len(totals) == 1:
            totals = jnp.split(totals[0], self.n_tp, axis=1)
        columns = totals[0].shape[1]
        half = max(columns // 2 // LANES, 1) * LANES
        firsts = [v[:, :half] for v in totals]
        seconds = jnp.concatenate([v[:, half:] for v in totals], axis=1)
        got = (
            [self.over_tp(firsts[r], r) for r in others],
            self.over_side(self.of_side(seconds, 1 - self.side)),
        )
        tp_got, side_got = yield got
        first = (firsts[0].astype(F32) + sum(v.astype(F32) for v in tp_got)).astype(BF16)
        second = self.of_side(seconds, self.side).astype(F32) + side_got.astype(F32)
        second = jnp.split(second.astype(BF16), self.n_tp, axis=-1)
        got = (
            self.over_side(self.of_side(first, 1 - self.side)),
            [self.over_tp(second[r], r) for r in others],
        )
        side_got, tp_got = yield got
        first = self.of_side(first, self.side).astype(F32) + side_got.astype(F32)
        second = second[0].astype(F32) + sum(v.astype(F32) for v in tp_got)
        line = jnp.concatenate([first, second], axis=-1).astype(BF16)
        got = yield [
            swap_with(
                lax.dynamic_index_in_dim(line, self.line ^ k, 0, keepdims=False),
                "ctx",
                self.n_ctx,
                2 * k,
            )
            for k in range(1, self.n_line)
        ]
        own = lax.dynamic_index_in_dim(line, self.line, 0, keepdims=False)
        return own.astype(F32) + sum(v.astype(F32) for v in got)


class Task:
    def __init__(self, steps):
        self.steps, self.result = steps, None
        self.pending = next(steps)


class Lanes:
    def __init__(self):
        self.tasks = []

    def start(self, steps):
        task = Task(steps)
        self.tasks.append(task)
        return task

    def fence(self, values=(), but=()):
        due = [t for t in self.tasks if t not in but]
        values, pending = lax.optimization_barrier((values, [t.pending for t in due]))
        going = [t for t in self.tasks if t in but]
        for task, done in zip(due, pending):
            try:
                task.pending = task.steps.send(done)
                going.append(task)
            except StopIteration as stop:
                task.result = stop.value
        self.tasks = going
        return values


def window(head):
    start = head * HEAD_DIM
    return start // LANES * LANES, -(-(start + HEAD_DIM) // LANES) * LANES


def in_head(head, rows, low, high):
    lanes = lax.broadcasted_iota(jnp.int32, (rows, high - low), 1) + low
    return (lanes >= head * HEAD_DIM) & (lanes < (head + 1) * HEAD_DIM)


def spread_parts(x_ref, offset, parts, width):
    for index, part in enumerate(parts):
        padded = part.shape[1]
        start = offset + index * width
        if padded != width:
            part[:, padded - LANES :] = jnp.zeros((part.shape[0], LANES), part.dtype)
        part[:, :width] = x_ref[:, start : start + width]


def same_sequence(rows, stride):
    row = lax.broadcasted_iota(jnp.int32, (rows, rows), 0)
    column = lax.broadcasted_iota(jnp.int32, (rows, rows), 1)
    return lax.rem(row, stride) == lax.rem(column, stride)


def attend_kernel(count, width, stride, *refs):
    x_refs, (o_ref, lse_ref, q_s, k_s, v_s, o_s) = refs[:count], refs[count:]
    heads, rows = width // HEAD_DIM, o_ref.shape[0]
    lane = lax.broadcasted_iota(jnp.int32, (rows, LANES), 1)
    logs = jnp.zeros((rows, LANES), F32)
    if stride > 1:
        allowed = same_sequence(rows, stride)
    for index, x_ref in enumerate(x_refs):
        spread_parts(x_ref, 0, (q_s, k_s, v_s), width)
        for head in range(heads):
            low, high = window(head)
            mask = in_head(head, rows, low, high)
            queries = jnp.where(mask, q_s[:, low:high], jnp.zeros((), BF16))
            scores = dot(queries, k_s[:, low:high], NT) * SCALE
            if stride > 1:
                scores = jnp.where(allowed, scores, -jnp.inf)
            largest = jnp.max(scores, axis=-1, keepdims=True)
            raised = jnp.exp(scores - largest)
            total = jnp.sum(raised, axis=-1, keepdims=True)
            chances = (raised * (1.0 / total)).astype(BF16)
            result = dot(chances, v_s[:, low:high])
            o_s[:, low:high] = jnp.where(mask, result, o_s[:, low:high])
            logs = jnp.where(lane == index * heads + head, largest + jnp.log(total), logs)
        o_ref[:, index * width : (index + 1) * width] = o_s[:, :width].astype(BF16)
    lse_ref[...] = logs


def attend_back_kernel(count, width, stride, *refs):
    x_refs, (g_ref, lse_ref), dx_refs = refs[:count], refs[count : count + 2], refs[count + 2 : -7]
    q_s, k_s, v_s, g_s, dq_s, dk_s, dv_s = refs[-7:]
    heads, rows = width // HEAD_DIM, g_ref.shape[0]
    if stride > 1:
        allowed = same_sequence(rows, stride)
    for index, x_ref in enumerate(x_refs):
        spread_parts(x_ref, 0, (q_s, k_s, v_s), width)
        spread_parts(g_ref, index * width, (g_s,), width)
        for head in range(heads):
            low, high = window(head)
            mask = in_head(head, rows, low, high)
            zero = jnp.zeros((), BF16)
            q, k, v, g = q_s[:, low:high], k_s[:, low:high], v_s[:, low:high], g_s[:, low:high]
            scores = dot(jnp.where(mask, q, zero), k, NT) * SCALE
            if stride > 1:
                scores = jnp.where(allowed, scores, -jnp.inf)
            place = index * heads + head
            chances = jnp.exp(scores - lse_ref[:, place : place + 1])
            grad_chances = dot(jnp.where(mask, g, zero), v, NT)
            row_dot = jnp.sum(chances * grad_chances, axis=-1, keepdims=True)
            grad_scores = (chances * (grad_chances - row_dot)).astype(BF16)
            dq = dot(grad_scores, k) * SCALE
            dk = dot(grad_scores, q, TN) * SCALE
            dv = dot(chances.astype(BF16), g, TN)
            dq_s[:, low:high] = jnp.where(mask, dq, dq_s[:, low:high])
            dk_s[:, low:high] = jnp.where(mask, dk, dk_s[:, low:high])
            dv_s[:, low:high] = jnp.where(mask, dv, dv_s[:, low:high])
        for part_index, part in enumerate((dq_s, dk_s, dv_s)):
            start = part_index * width
            dx_refs[index][:, start : start + width] = part[:, :width].astype(BF16)


def row_block(rows, columns):
    return pl.BlockSpec((rows, columns), lambda i: (i, 0))


def attend(xs, rows, stride):
    count, width = xs[0].shape[0], xs[0].shape[1] // 3
    strips = len(xs)
    heads = strips * width // HEAD_DIM
    padded = -(-width // LANES) * LANES
    return pl.pallas_call(
        functools.partial(attend_kernel, strips, width, stride),
        grid=(count // rows,),
        in_specs=[row_block(rows, 3 * width)] * strips,
        out_specs=[row_block(rows, strips * width), row_block(rows, LANES)],
        out_shape=[
            jax.ShapeDtypeStruct((count, strips * width), BF16),
            jax.ShapeDtypeStruct((count, LANES), F32),
        ],
        scratch_shapes=[pltpu.VMEM((rows, padded), BF16)] * 3 + [pltpu.VMEM((rows, padded), F32)],
        cost_estimate=pl.CostEstimate(
            flops=heads * count * rows * 1024,
            bytes_accessed=count * width * strips * 8,
            transcendentals=heads * count * rows,
        ),
        compiler_params=pltpu.CompilerParams(vmem_limit_bytes=32 * 1024 * 1024),
    )(*xs)


def attend_back(xs, grad, lse, rows, stride):
    count, width = xs[0].shape[0], xs[0].shape[1] // 3
    strips = len(xs)
    heads = strips * width // HEAD_DIM
    padded = -(-width // LANES) * LANES
    return pl.pallas_call(
        functools.partial(attend_back_kernel, strips, width, stride),
        grid=(count // rows,),
        in_specs=[row_block(rows, 3 * width)] * strips
        + [row_block(rows, strips * width), row_block(rows, LANES)],
        out_specs=[row_block(rows, 3 * width)] * strips,
        out_shape=[jax.ShapeDtypeStruct((count, 3 * width), BF16)] * strips,
        scratch_shapes=[pltpu.VMEM((rows, padded), BF16)] * 4
        + [pltpu.VMEM((rows, padded), F32)] * 3,
        cost_estimate=pl.CostEstimate(
            flops=heads * count * rows * 2560,
            bytes_accessed=count * width * strips * 14,
            transcendentals=heads * count * rows,
        ),
        compiler_params=pltpu.CompilerParams(vmem_limit_bytes=32 * 1024 * 1024),
    )(*xs, grad, lse)


def weight_specs(pieces):
    return [pl.BlockSpec(memory_space=pl.ANY)] * len(pieces)


def weight_scratch(pieces):
    strips = len(pieces) // 2 - 1
    rows, half = pieces[0].shape
    return [
        pltpu.VMEM((2 * rows, strips * 2 * half), BF16),
        pltpu.SemaphoreType.DMA((2, strips, 2)),
    ]


def weight_copies(refs, w_s, sems):
    count = len(refs) // 2
    copies = [([], []) for _ in range(count - 1)]
    for group in range(2):
        firsts, seconds = refs[group * count : group * count + count - 1], refs[group * count + count - 1]
        for strip, first in enumerate(firsts):
            rows, half = first.shape
            for part, source in enumerate((first, seconds.at[strip])):
                target = w_s.at[pl.ds(group * rows, rows), pl.ds((2 * strip + part) * half, half)]
                copies[strip][part].append(
                    pltpu.make_async_copy(source, target, sems.at[group, strip, part])
                )
    return copies


def start_copies(copies):
    for strip in copies:
        for part in strip:
            for copy in part:
                copy.start()


def await_copies(parts):
    @pl.when(pl.program_id(0) == 0)
    def _():
        for part in parts:
            for copy in part:
                copy.wait()


def turn_copies(parts, w_s, t_s):
    @pl.when(pl.program_id(0) == 0)
    def _():
        low = 0
        for part in parts:
            for copy in part:
                copy.wait()
            size = w_s.shape[1] // len(parts)
            t_s[low : low + size] = w_s[:, low : low + size].T
            low += size


def begin_copies(*many):
    @pl.when(pl.program_id(0) == 0)
    def _():
        for copies in many:
            start_copies(copies)


def row_normal(v):
    centred = v - jnp.mean(v, axis=-1, keepdims=True)
    inverse = lax.rsqrt(jnp.mean(centred * centred, axis=-1, keepdims=True) + EPS)
    return centred * inverse, inverse


def row_back(grad, normed, inverse, scale):
    scaled = grad * (1.0 + scale)
    mean_one = jnp.mean(scaled, axis=-1, keepdims=True)
    mean_two = jnp.mean(scaled * normed, axis=-1, keepdims=True)
    return inverse * (scaled - mean_one - normed * mean_two)


def head_forward(heads, first, rows, allowed, q_s, k_s, v_s, o_s, lane, logs):
    for head in range(heads):
        low, high = window(head)
        mask = in_head(head, rows, low, high)
        queries = jnp.where(mask, q_s[:, low:high], jnp.zeros((), BF16))
        scores = dot(queries, k_s[:, low:high], NT) * SCALE
        if allowed is not None:
            scores = jnp.where(allowed, scores, -jnp.inf)
        largest = jnp.max(scores, axis=-1, keepdims=True)
        raised = jnp.exp(scores - largest)
        total = jnp.sum(raised, axis=-1, keepdims=True)
        chances = (raised * (1.0 / total)).astype(BF16)
        result = dot(chances, v_s[:, low:high])
        o_s[:, low:high] = jnp.where(mask, result, o_s[:, low:high])
        logs = jnp.where(lane == first + head, largest + jnp.log(total), logs)
    return logs


def head_back(heads, first, rows, allowed, q_s, k_s, v_s, g_s, lse_ref, dq_s, dk_s, dv_s):
    zero = jnp.zeros((), BF16)
    for head in range(heads):
        low, high = window(head)
        mask = in_head(head, rows, low, high)
        q, k, v, g = q_s[:, low:high], k_s[:, low:high], v_s[:, low:high], g_s[:, low:high]
        scores = dot(jnp.where(mask, q, zero), k, NT) * SCALE
        if allowed is not None:
            scores = jnp.where(allowed, scores, -jnp.inf)
        place = first + head
        chances = jnp.exp(scores - lse_ref[:, place : place + 1])
        grad_chances = dot(jnp.where(mask, g, zero), v, NT)
        row_dot = jnp.sum(chances * grad_chances, axis=-1, keepdims=True)
        grad_scores = (chances * (grad_chances - row_dot)).astype(BF16)
        dq = dot(grad_scores, k) * SCALE
        dk = dot(grad_scores, q, TN) * SCALE
        dv = dot(chances.astype(BF16), g, TN)
        dq_s[:, low:high] = jnp.where(mask, dq, dq_s[:, low:high])
        dk_s[:, low:high] = jnp.where(mask, dk, dk_s[:, low:high])
        dv_s[:, low:high] = jnp.where(mask, dv, dv_s[:, low:high])


def branch_kernel(strips, stride, x_ref, mod_ref, *refs):
    count = 2 * (strips + 1)
    w_refs = refs[:count]
    h_ref, qkv_ref, lse_ref, o_ref, a_ref, y_ref, g_ref = refs[count : count + 7]
    w_s, sems, p_s, o_s, z_s = refs[count + 7 :]
    rows, width = x_ref.shape
    head_cols = width // strips
    padded = o_s.shape[1]
    spare = padded - head_cols
    columns = w_s.shape[1] // strips
    copies = weight_copies(w_refs, w_s, sems)
    begin_copies(copies)
    x = x_ref[...].astype(F32)
    shift_a, scale_a, gate_a, shift_m, scale_m = [mod_ref[0, i : i + 1, :] for i in range(5)]
    h = (row_normal(x)[0] * (1.0 + scale_a) + shift_a).astype(BF16)
    h_ref[...] = h
    heads = head_cols // HEAD_DIM
    lane = lax.broadcasted_iota(jnp.int32, (rows, LANES), 1)
    logs = jnp.zeros((rows, LANES), F32)
    allowed = same_sequence(rows, stride) if stride > 1 else None
    branch = jnp.zeros((rows, width), F32)
    for strip in range(strips):
        start = strip * columns
        await_copies(copies[strip])
        p_s[...] = dot(h, w_s[:, start : start + p_s.shape[1]]).astype(BF16)
        parts = []
        for index in range(3):
            low = (3 * strip + index) * padded
            if spare:
                qkv_ref[:, low + padded - LANES : low + padded] = jnp.zeros((rows, LANES), BF16)
            qkv_ref[:, low : low + head_cols] = p_s[:, index * head_cols : (index + 1) * head_cols]
            parts.append(qkv_ref.at[:, pl.ds(low, padded)])
        logs = head_forward(heads, strip * heads, rows, allowed, *parts, o_s, lane, logs)
        low = o_s[:, :head_cols].astype(BF16)
        o_ref[:, strip * head_cols : (strip + 1) * head_cols] = low
        if spare:
            z_s[:, :LANES] = jnp.zeros((rows, LANES), BF16)
        z_s[:, spare:] = low
        branch = branch + dot(z_s[...], w_s[:, start + columns - padded : start + columns], NT)
    lse_ref[...] = logs
    a_ref[...] = branch.astype(BF16)
    y = x + gate_a * branch
    y_ref[...] = y
    g_ref[...] = (row_normal(y)[0] * (1.0 + scale_m) + shift_m).astype(BF16)


def branch_back_kernel(strips, stride, x_ref, mod_ref, da_ref, dy_ref, qkv_ref, lse_ref, *refs):
    count = 2 * (strips + 1)
    w_refs = refs[:count]
    dx_ref, sums_ref = refs[count : count + 2]
    out_refs = refs[count + 2 : count + 2 + strips]
    w_s, sems, d_s, g_s, dq_s, dk_s, dv_s = refs[count + 2 + strips :]
    rows, width = x_ref.shape
    head_cols = width // strips
    padded = g_s.shape[1]
    spare = padded - head_cols
    columns = w_s.shape[1] // strips
    copies = weight_copies(w_refs, w_s, sems)
    begin_copies(copies)
    heads = head_cols // HEAD_DIM
    allowed = same_sequence(rows, stride) if stride > 1 else None
    grad = jnp.zeros((rows, width), F32)
    for strip in range(strips):
        start = strip * columns
        await_copies(copies[strip])
        turned = dot(da_ref[...], w_s[:, start + columns - padded : start + columns]).astype(BF16)
        if spare:
            g_s[:, padded - LANES :] = jnp.zeros((rows, LANES), BF16)
        g_s[:, :head_cols] = turned[:, spare:]
        parts = [qkv_ref.at[:, pl.ds((3 * strip + i) * padded, padded)] for i in range(3)]
        head_back(heads, strip * heads, rows, allowed, *parts, g_s, lse_ref, dq_s, dk_s, dv_s)
        if d_s.shape[1] != 3 * head_cols:
            d_s[:, d_s.shape[1] - LANES :] = jnp.zeros((rows, LANES), BF16)
        for index, part in enumerate((dq_s, dk_s, dv_s)):
            d_s[:, index * head_cols : (index + 1) * head_cols] = part[:, :head_cols].astype(BF16)
        out_refs[strip][...] = d_s[:, : 3 * head_cols]
        grad = grad + dot(d_s[...], w_s[:, start : start + d_s.shape[1]], NT)
    scale_a = mod_ref[0, 1:2, :]
    normed, inverse = row_normal(x_ref[...].astype(F32))
    sums_ref[...] = jnp.zeros(sums_ref.shape, F32)
    sums_ref[0, 0:1, :] = jnp.sum(grad, axis=0, keepdims=True)
    sums_ref[0, 1:2, :] = jnp.sum(grad * normed, axis=0, keepdims=True)
    dx_ref[...] = (dy_ref[...] + row_back(grad, normed, inverse, scale_a)).astype(BF16)


GELU_A = 0.7978845608028654
GELU_B = 0.044715


def up_kernel(strips, g_ref, *refs):
    count = 2 * (strips + 1)
    z_ref, slope_ref, w_s, sems = refs[count:]
    copies = weight_copies(refs[:count], w_s, sems)
    begin_copies(copies)
    half = w_s.shape[1] // (2 * strips)
    g = g_ref[...]
    for index in range(2 * strips):
        await_copies([copies[index // 2][index % 2]])
        low = index * half
        u = dot(g, w_s[:, low : low + half])
        square = u * u
        bent = jnp.tanh(u * (GELU_A + GELU_A * GELU_B * square))
        lifted = 0.5 * (1.0 + bent)
        z_ref[:, low : low + half] = (u * lifted).astype(BF16)
        inner = GELU_A + 3.0 * GELU_A * GELU_B * square
        slope = lifted + 0.5 * u * (1.0 - bent * bent) * inner
        slope_ref[:, low : low + half] = slope.astype(BF16)


def down_kernel(strips, z_ref, y_ref, mod_ref, *refs):
    count = 2 * (strips + 1)
    m_ref, x_ref, w_s, sems, t_s = refs[count:]
    copies = weight_copies(refs[:count], w_s, sems)
    begin_copies(copies)
    half = w_s.shape[1] // (2 * strips)
    turn_copies([copies[i // 2][i % 2] for i in range(2 * strips)], w_s, t_s)
    total = dot(z_ref[...], t_s[...])
    m_ref[...] = total.astype(BF16)
    x_ref[...] = (y_ref[...] + mod_ref[0, 5:6, :] * total).astype(BF16)


def mlp_back_kernel(strips, dx_ref, mod_ref, m_ref, slope_ref, y_ref, a_ref, *refs):
    count = 2 * (strips + 1)
    dm_ref, du_ref, dy_ref, da_ref, sums_ref, up_s, up_sems, down_s, down_sems, t_s = refs[2 * count :]
    ups = weight_copies(refs[:count], up_s, up_sems)
    downs = weight_copies(refs[count : 2 * count], down_s, down_sems)
    begin_copies(downs, ups)
    half = up_s.shape[1] // (2 * strips)
    turn_copies([ups[i // 2][i % 2] for i in range(2 * strips)], up_s, t_s)
    scale_m, gate_m, share, gate_a = [mod_ref[0, i : i + 1, :] for i in (4, 5, 6, 2)]
    dx = dx_ref[...].astype(F32) * share
    sums_ref[...] = jnp.zeros(sums_ref.shape, F32)
    sums_ref[0, 5:6, :] = jnp.sum(dx * m_ref[...].astype(F32), axis=0, keepdims=True)
    dm = (gate_m * dx).astype(BF16)
    dm_ref[...] = dm
    grad = jnp.zeros(y_ref.shape, F32)
    for index in range(2 * strips):
        low = index * half
        await_copies([downs[index // 2][index % 2]])
        dz = dot(dm, down_s[:, low : low + half])
        du = (dz * slope_ref[:, low : low + half].astype(F32)).astype(BF16)
        du_ref[:, low : low + half] = du
        grad = grad + dot(du, t_s[low : low + half])
    normed, inverse = row_normal(y_ref[...])
    sums_ref[0, 3:4, :] = jnp.sum(grad, axis=0, keepdims=True)
    sums_ref[0, 4:5, :] = jnp.sum(grad * normed, axis=0, keepdims=True)
    dy = dx + row_back(grad, normed, inverse, scale_m)
    dy_ref[...] = dy
    sums_ref[0, 2:3, :] = jnp.sum(dy * a_ref[...].astype(F32), axis=0, keepdims=True)
    da_ref[...] = (gate_a * dy).astype(BF16)


def shape_of(*dims, dtype=BF16):
    return jax.ShapeDtypeStruct(dims, dtype)


def block_call(kernel, clips, rows, arrays, mods, weights, outs, sums, scratch, flops, order):
    operands, specs = [], []
    for v in order:
        if v is None:
            operands.append(mods)
            specs.append(pl.BlockSpec((1,) + mods.shape[1:], lambda i: (i, 0, 0)))
        else:
            operands.append(arrays[v])
            specs.append(row_block(rows, arrays[v].shape[1]))
    for pieces in weights:
        operands += pieces
        specs += weight_specs(pieces)
    out_specs = [row_block(rows, v.shape[1]) for v in outs]
    out_shape = list(outs)
    if sums is not None:
        width = mods.shape[2]
        out_specs.insert(sums, pl.BlockSpec((1, 8, width), lambda i: (i, 0, 0)))
        out_shape.insert(sums, shape_of(clips, 8, width, dtype=F32))
    held = []
    for pieces in weights:
        held += weight_scratch(pieces)
    moved = sum(v.size * v.dtype.itemsize for v in operands)
    return pl.pallas_call(
        kernel,
        grid=(clips,),
        in_specs=specs,
        out_specs=out_specs,
        out_shape=out_shape,
        scratch_shapes=held + scratch,
        cost_estimate=pl.CostEstimate(flops=flops, bytes_accessed=moved, transcendentals=0),
        compiler_params=pltpu.CompilerParams(vmem_limit_bytes=60 * 1024 * 1024),
    )(*operands)


def padded_to(columns):
    return -(-columns // LANES) * LANES


def fused_branch(x, mods, pieces, clips, stride):
    count, width = x.shape
    rows, strips = count // clips, len(pieces) // 2 - 1
    head_cols = width // strips
    padded = padded_to(head_cols)
    outs = [
        shape_of(count, width),
        shape_of(count, 3 * strips * padded),
        shape_of(count, LANES, dtype=F32),
        shape_of(count, width),
        shape_of(count, width),
        shape_of(count, width, dtype=F32),
        shape_of(count, width),
    ]
    scratch = [
        pltpu.VMEM((rows, padded_to(3 * head_cols)), BF16),
        pltpu.VMEM((rows, padded), F32),
        pltpu.VMEM((rows, padded), BF16),
    ]
    return block_call(
        functools.partial(branch_kernel, strips, stride),
        clips, rows, [x], mods, [pieces], outs, None, scratch,
        12 * count * width * width, [0, None],
    )


def fused_branch_back(x, mods, da, dy, qkv, lse, pieces, clips, stride):
    count, width = x.shape
    rows, strips = count // clips, len(pieces) // 2 - 1
    head_cols = width // strips
    padded = padded_to(head_cols)
    outs = [shape_of(count, width)] + [shape_of(count, 3 * head_cols) for _ in range(strips)]
    scratch = [
        pltpu.VMEM((rows, padded_to(3 * head_cols)), BF16),
        pltpu.VMEM((rows, padded), BF16),
    ] + [pltpu.VMEM((rows, padded), F32)] * 3
    return block_call(
        functools.partial(branch_back_kernel, strips, stride),
        clips, rows, [x, da, dy, qkv, lse], mods, [pieces], outs, 1, scratch,
        16 * count * width * width, [0, None, 1, 2, 3, 4],
    )


def fused_up(g, mods, pieces, clips):
    count, width = g.shape
    rows, strips = count // clips, len(pieces) // 2 - 1
    units = strips * 2 * pieces[0].shape[1]
    outs = [shape_of(count, units), shape_of(count, units)]
    return block_call(
        functools.partial(up_kernel, strips),
        clips, rows, [g], mods, [pieces], outs, None, [], 2 * count * width * units, [0],
    )


def fused_down(z, y, mods, pieces, clips):
    count, width = y.shape
    rows, strips = count // clips, len(pieces) // 2 - 1
    outs = [shape_of(count, width), shape_of(count, width)]
    return block_call(
        functools.partial(down_kernel, strips),
        clips, rows, [z, y], mods, [pieces], outs, None, [pltpu.VMEM((z.shape[1], width), BF16)],
        2 * z.size * width, [0, 1, None],
    )


def fused_mlp_back(dx, mods, m, slope, y, a, ups, downs, clips):
    count, width = y.shape
    rows, strips = count // clips, len(ups) // 2 - 1
    outs = [
        shape_of(count, width),
        shape_of(*slope.shape),
        shape_of(count, width, dtype=F32),
        shape_of(count, width),
    ]
    return block_call(
        functools.partial(mlp_back_kernel, strips),
        clips, rows, [dx, m, slope, y, a], mods, [ups, downs], outs, 4,
        [pltpu.VMEM((slope.shape[1], width), BF16)],
        4 * slope.size * width, [0, None, 1, 2, 3, 4],
    )


def split_frames(v, frames, width):
    return v.reshape(frames, -1, width // HEAD_DIM, HEAD_DIM)


def attend_shared(x, frames):
    width = x.shape[1] // 3
    shaped = x.reshape(frames, -1, 3, width)
    pairs = lax.all_gather(shaped[:, :, 1:], "tp", axis=1, tiled=True)
    q = split_frames(shaped[:, :, 0], frames, width)
    k = split_frames(pairs[:, :, 0], frames, width)
    v = split_frames(pairs[:, :, 1], frames, width)
    scores = jnp.einsum("bqhe,bkhe->bhqk", q, k, preferred_element_type=F32) * SCALE
    chances = jax.nn.softmax(scores, axis=-1)
    result = jnp.einsum("bhqk,bkhe->bqhe", chances.astype(BF16), v, preferred_element_type=F32)
    return result.reshape(-1, width).astype(BF16), (q, k, v, chances)


def attend_shared_back(saved, grad):
    q, k, v, chances = saved
    frames, width = q.shape[0], grad.shape[1]
    grad = split_frames(grad, frames, width)
    grad_chances = jnp.einsum("bqhe,bkhe->bhqk", grad, v, preferred_element_type=F32)
    row_dot = jnp.sum(chances * grad_chances, axis=-1, keepdims=True)
    grad_scores = (chances * (grad_chances - row_dot)).astype(BF16)
    dq = jnp.einsum("bhqk,bkhe->bqhe", grad_scores, k, preferred_element_type=F32) * SCALE
    dk = jnp.einsum("bhqk,bqhe->bkhe", grad_scores, q, preferred_element_type=F32) * SCALE
    dv = jnp.einsum("bhqk,bqhe->bkhe", chances.astype(BF16), grad, preferred_element_type=F32)
    sums = lax.psum_scatter(jnp.stack([dk, dv], axis=2), "tp", scatter_dimension=1, tiled=True)
    parts = jnp.concatenate([dq[:, :, None], sums], axis=2)
    return parts.reshape(-1, 3 * width).astype(BF16)


def normalise(v):
    centred = v - jnp.mean(v, axis=-1, keepdims=True)
    inverse = lax.rsqrt(jnp.mean(centred * centred, axis=-1, keepdims=True) + EPS)
    return centred * inverse, inverse


def modulate(v, shift, scale):
    return (normalise(v)[0] * (1.0 + scale[:, None]) + shift[:, None]).astype(BF16)


def modulate_back(grad, v, scale):
    normed, inverse = normalise(v)
    shift_grad = jnp.sum(grad, axis=1)
    scale_grad = jnp.sum(grad * normed, axis=1)
    scaled = grad * (1.0 + scale[:, None])
    mean_one = jnp.mean(scaled, axis=-1, keepdims=True)
    mean_two = jnp.mean(scaled * normed, axis=-1, keepdims=True)
    return inverse * (scaled - mean_one - normed * mean_two), shift_grad, scale_grad


def gelu(v):
    return jax.nn.gelu(v, approximate=True)


def gelu_slope(v, grad):
    return jax.vjp(gelu, v)[1](grad)[0]


def local(moves, tokens, condition, micro_ids, w_qkv, w_out, w_up, w_down, w_ada, cotangent):
    moves.here()
    n_dp, n_ctx, n_tp = moves.n_dp, moves.n_ctx, moves.n_tp
    clips, frames_here, patches_here, width = tokens.shape
    rows_here, head_cols = w_qkv.shape[2:]
    whole_frames = frames_here % n_tp == 0
    spread_tp = n_tp if whole_frames else 1
    groups = frames_here // spread_tp
    piece = patches_here // n_ctx

    cond_full = condition.astype(F32)
    cond_low = jax.nn.silu(cond_full).astype(BF16)
    cond_all = jnp.concatenate([cond_low, swap_with(cond_low, "dp", n_dp, 1)], axis=0)
    first_row = (moves.dp * n_ctx + moves.ctx) * rows_here
    cond_rows = lax.dynamic_slice_in_dim(cond_all, first_row, rows_here, axis=1)
    ada_low = w_ada.astype(BF16)
    shares = jnp.stack([dot(cond_rows, ada_low[level]) for level in range(LAYERS)], axis=1)
    sums = shares[:clips] + swap_with(shares[clips:], "dp", n_dp, 1)
    step = 1
    while step < n_ctx:
        sums = sums + swap_with(sums, "ctx", n_ctx, step)
        step *= 2
    strips = [sums] + [swap_with(sums, "tp", n_tp, r) for r in range(1, n_tp)]
    strips = flip_to(jnp.stack(strips, axis=2), 2, n_tp, moves.tp)
    mods = strips.reshape(clips, LAYERS, 6, width)
    mods = [moves.halves(mods[:, level]) for level in range(LAYERS)]

    def to_frames(v):
        v = v.reshape(clips, frames_here, n_ctx, piece, width)
        v = flip_to(v, 2, n_ctx, moves.ctx)
        if spread_tp == 1:
            yield ()
            return v.reshape(clips, groups * patches_here, width)
        v = v.reshape(clips, spread_tp, groups, patches_here, width)
        v = flip_to(v, 1, spread_tp, moves.tp)
        got = yield [swap_with(v[:, r], "tp", n_tp, r) for r in range(1, spread_tp)]
        return jnp.stack([v[:, 0]] + got, axis=2).reshape(clips, -1, width)

    def from_frames(v):
        if spread_tp > 1:
            v = v.reshape(clips, groups, spread_tp, patches_here, width)
            blocks = [v[:, :, 0]]
            blocks += [swap_with(v[:, :, r], "tp", n_tp, r) for r in range(1, spread_tp)]
            v = flip_to(jnp.stack(blocks, axis=1), 1, spread_tp, moves.tp)
        v = v.reshape(clips, frames_here, n_ctx, piece, width)
        v = flip_to(v, 2, n_ctx, moves.ctx)
        return v.reshape(clips, frames_here, patches_here, width)

    def trade(get, planes):
        sides = []
        for dx, dr in planes:
            block = get(dx, dr)
            if dx or dr:
                pairs = [
                    (c * n_tp + t, (c ^ dx) * n_tp + (t ^ dr))
                    for c in range(n_ctx)
                    for t in range(n_tp)
                ]
                block = lax.ppermute(block, ("ctx", "tp"), pairs)
            sides.append(block)
        sides = sides[:1] + (yield sides[1:])
        lines = [jnp.stack([v[:, dz] for v in sides], axis=1) for dz in range(n_ctx // 2)]
        got = yield [swap_with(v, "ctx", n_ctx, 2 * dz) for dz, v in enumerate(lines) if dz]
        return jnp.stack(lines[:1] + got, axis=1)

    all_planes = [(dx, dr) for dx in range(2) for dr in range(spread_tp)]
    own_planes = [(0, 0), (1, 0)]

    def frames_to_clips(v):
        v = v.reshape(clips, groups, spread_tp, n_ctx // 2, 2, piece, width)
        got = yield from trade(lambda dx, dr: v[:, :, dr, :, dx].swapaxes(1, 2), all_planes)
        return got.reshape(clips, -1, width)

    def clips_to_frames(v):
        v = v.reshape(clips, n_ctx // 2, 2, spread_tp, groups, piece, width)
        got = yield from trade(lambda dx, dr: v[:, :, dx, dr], all_planes)
        got = got.reshape(clips, n_ctx, spread_tp, groups, piece, width)
        return got.transpose(0, 3, 2, 1, 4, 5).reshape(clips, -1, width)

    def here_to_clips(v):
        v = v.reshape(clips, spread_tp, groups, n_ctx, piece, width)
        v = flip_to(flip_to(v, 3, n_ctx, moves.ctx), 1, spread_tp, moves.tp % spread_tp)
        v = v.reshape(clips, spread_tp, groups, n_ctx // 2, 2, piece, width)
        got = yield from trade(lambda dx, dr: v[:, :, :, :, dx].transpose(0, 3, 1, 2, 4, 5), own_planes)
        return got.reshape(clips, -1, width)

    def clips_to_here(v):
        v = v.reshape(clips, n_ctx // 2, 2, spread_tp, groups, piece, width)
        got = yield from trade(lambda dx, dr: v[:, :, dx], own_planes)
        v = got.reshape(clips, n_ctx, spread_tp, groups, piece, width).transpose(0, 2, 3, 1, 4, 5)
        v = flip_to(flip_to(v, 3, n_ctx, moves.ctx), 1, spread_tp, moves.tp % spread_tp)
        return v.reshape(clips, frames_here, patches_here, width)

    def flat(v):
        return v.reshape(-1, v.shape[-1])

    def shaped(v):
        return v.reshape(clips, -1, v.shape[-1])

    shards = []
    for level in range(LAYERS):
        attention = [w_qkv[level, 0], w_qkv[level, 1], w_qkv[level, 2], w_out[level].T]
        shards.append(jnp.concatenate(attention, axis=1).astype(BF16))
        shards.append(w_up[level].astype(BF16))
        shards.append(w_down[level].T.astype(BF16))
    lanes = Lanes()
    gathers = []

    def tick(values=()):
        rest, values = lanes.fence((shards[len(gathers) :], values))
        if rest:
            gathers.append(lanes.start(moves.gather_weight(rest[0])))
        return values

    def whole(index):
        pieces = gathers[index].result
        count = len(pieces) // 2
        groups = []
        for group in (pieces[:count], pieces[count:]):
            strips = [v for r in range(n_tp) for v in (group[r], group[-1][r])]
            groups.append(jnp.concatenate(strips, axis=1))
        return jnp.concatenate(groups, axis=0)

    def attention_weights(index):
        v = whole(index)
        strips = jnp.split(v, n_tp, axis=1)
        cut = 3 * head_cols
        return [w[:, :cut] for w in strips], jnp.concatenate([w[:, cut:] for w in strips], axis=1)

    def modulations(level):
        return [mods[level][:, i] for i in range(6)]

    moved = lanes.start(to_frames(moves.halves(tokens)))
    gathers.append(lanes.start(moves.gather_weight(shards[0])))
    tick()
    residual = moved.result
    tick()
    tick()
    fused = (
        whole_frames
        and head_cols % 32 == 0
        and w_up.shape[2] % (2 * LANES) == 0
        and 4 * head_cols == w_up.shape[2]
        and width % 32 == 0
    )
    matched = (micro_ids[:, None] == micro_ids[None, :]).astype(F32)
    share = 1.0 / jnp.sum(matched, axis=1)
    scatters = {}
    mod_grads = [None] * LAYERS

    def start_scatter(level, name, left, rights):
        scatters[level, name] = lanes.start(moves.scatter_weight(left, rights))

    def fused_passes(v):
        vectors, saved = [], []
        for level in range(LAYERS):
            last = share if level == LAYERS - 1 else jnp.ones_like(share)
            last = jnp.broadcast_to(last[:, None, None], (clips, 2, width))
            vectors.append(jnp.concatenate([mods[level], last], axis=1))
        v = flat(v)
        for level in range(LAYERS):
            stride = piece if level % 2 else 1
            joined = gathers[3 * level].result
            kept = fused_branch(v, vectors[level], joined, clips, stride)
            normed, qkv, lse, result, branch, middle, normed_mlp = tick(kept)
            up = gathers[3 * level + 1].result
            act, slope = tick(fused_up(normed_mlp, vectors[level], up, clips))
            down = gathers[3 * level + 2].result
            branch_mlp, after = fused_down(act, middle, vectors[level], down, clips)
            saved.append((v, normed, qkv, lse, result, branch, middle, normed_mlp))
            saved[-1] += (act, slope, branch_mlp, joined, up, down, stride)
            v = after
            if level == 0:
                moved = lanes.start(frames_to_clips(shaped(v)))
                tick()
                turned = lanes.start(here_to_clips(moves.halves(cotangent)))
                tick()
                v = flat(moved.result)
        finished = lanes.start(clips_to_here(moves.halves(shaped(v))))
        grad = flat(turned.result)
        for level in reversed(range(LAYERS)):
            v, normed, qkv, lse, result, branch, middle, normed_mlp = saved[level][:8]
            act, slope, branch_mlp, joined, up, down, stride = saved[level][8:]
            back = fused_mlp_back(
                grad, vectors[level], branch_mlp, slope, middle, branch, up, down, clips
            )
            grad_branch, grad_pre, grad_middle, grad_out, sums = lanes.fence(back)
            start_scatter(level, "down", grad_branch, [act])
            if level == 0:
                start_scatter(level, "up", normed_mlp, [grad_pre])
                grad_out = lanes.fence(grad_out)
            back = fused_branch_back(
                v, vectors[level], grad_out, grad_middle, qkv, lse, joined, clips, stride
            )
            grad, more, *grad_qkv = lanes.fence(back)
            mod_grads[level] = (sums + more)[:, :6]
            if level:
                moved = lanes.start(clips_to_frames(shaped(grad)))
                start_scatter(level, "up", normed_mlp, [grad_pre])
                lanes.fence()
                start_scatter(level, "out", grad_out, [result])
                start_scatter(level, "qkv", normed, grad_qkv)
                lanes.fence()
                grad = flat(moved.result)
            else:
                start_scatter(level, "qkv", normed, grad_qkv)
                start_scatter(level, "out", grad_out, [result])
        return finished, shaped(grad)

    def plain_passes(residual):
        residual = residual.astype(F32)
        records = []
        for level in range(LAYERS):
            spatial = level % 2 == 0
            shift_a, scale_a, gate_a, shift_m, scale_m, gate_m = modulations(level)
            normed = flat(modulate(residual, shift_a, scale_a))
            qkvs, outs = attention_weights(3 * level)
            projected = [dot(normed, v).astype(BF16) for v in qkvs]
            rows, stride = (patches_here * spread_tp, 1) if spatial else (residual.shape[1], piece)
            if spatial and not whole_frames:
                saved = [attend_shared(v, clips * frames_here) for v in projected]
                result = jnp.concatenate([entry[0] for entry in saved], axis=1)
                saved = [entry[1] for entry in saved]
            else:
                result, saved = attend(projected, rows, stride)
            result, saved = tick((result, saved))
            branch = shaped(dot(result, outs, NT))
            middle = residual + gate_a[:, None] * branch
            normed_mlp = flat(modulate(middle, shift_m, scale_m))
            up = whole(3 * level + 1)
            pre_act = dot(normed_mlp, up)
            act = gelu(pre_act).astype(BF16)
            act, pre_act = tick((act, pre_act))
            down = whole(3 * level + 2)
            branch_mlp = shaped(dot(act, down, NT))
            records.append(
                (residual, normed, projected, saved, result, branch, middle, normed_mlp)
                + (pre_act, act, branch_mlp, qkvs, outs, up, down, rows, stride)
            )
            residual = middle + gate_m[:, None] * branch_mlp
            if spatial:
                moved = lanes.start(frames_to_clips(residual.astype(BF16)))
                tick()
                turned = lanes.start(here_to_clips(moves.halves(cotangent)))
                tick()
                residual = moved.result.astype(F32)
        gradient = turned.result.astype(F32) * share[:, None, None]
        finished = lanes.start(clips_to_here(moves.halves(residual.astype(BF16))))
        for level in reversed(range(LAYERS)):
            spatial = level % 2 == 0
            (residual, normed, projected, saved, result, branch, middle, normed_mlp) = records[level][
                :8
            ]
            (pre_act, act, branch_mlp, qkvs, outs, up, down, rows, stride) = records[level][8:]
            shift_a, scale_a, gate_a, shift_m, scale_m, gate_m = modulations(level)
            gate_m_grad = jnp.sum(gradient * branch_mlp, axis=1)
            low_grad = flat((gradient * gate_m[:, None]).astype(BF16))
            grad_pre = gelu_slope(pre_act, dot(low_grad, down)).astype(BF16)
            start_scatter(level, "down", low_grad, [act])
            grad_pre = lanes.fence(grad_pre)
            grad_normed = shaped(dot(grad_pre, up, NT))
            start_scatter(level, "up", normed_mlp, [grad_pre])
            grad_normed = lanes.fence(grad_normed)
            added, shift_m_grad, scale_m_grad = modulate_back(grad_normed, middle, scale_m)
            gradient = gradient + added
            gate_a_grad = jnp.sum(gradient * branch, axis=1)
            low_grad = flat((gradient * gate_a[:, None]).astype(BF16))
            grad_heads = dot(low_grad, outs).astype(BF16)
            start_scatter(level, "out", low_grad, [result])
            grad_heads = lanes.fence(grad_heads)
            if spatial and not whole_frames:
                grad_qkv = [
                    attend_shared_back(v, g)
                    for v, g in zip(saved, jnp.split(grad_heads, n_tp, axis=1))
                ]
            else:
                grad_qkv = attend_back(projected, grad_heads, saved, rows, stride)
            grad_qkv = lanes.fence(grad_qkv)
            start_scatter(level, "qkv", normed, grad_qkv)
            grad_normed = shaped(sum(dot(v, w, NT) for v, w in zip(grad_qkv, qkvs)))
            added, shift_a_grad, scale_a_grad = modulate_back(grad_normed, residual, scale_a)
            gradient = gradient + added
            mod_grads[level] = jnp.stack(
                [shift_a_grad, scale_a_grad, gate_a_grad, shift_m_grad, scale_m_grad, gate_m_grad],
                axis=1,
            )
            if not spatial:
                moved = lanes.start(clips_to_frames(gradient.astype(BF16)))
                lanes.fence()
                lanes.fence()
                gradient = moved.result.astype(F32)
        return finished, gradient

    passes = fused_passes if fused else plain_passes
    finished, gradient = passes(residual)
    grad_tokens = from_frames(moves.halves(gradient.astype(BF16))).astype(F32)
    while lanes.tasks:
        lanes.fence()
    output = finished.result
    grads = [
        (
            scatters[level, "qkv"].result.reshape(rows_here, 3, head_cols).transpose(1, 0, 2),
            scatters[level, "out"].result.T,
            scatters[level, "up"].result,
            scatters[level, "down"].result.T,
        )
        for level in range(LAYERS)
    ]

    ada_grads = []
    cond_part = 0.0
    for level in range(LAYERS):
        strips = moves.halves(mod_grads[level]).reshape(clips, n_tp, -1)
        strips = flip_to(strips, 1, n_tp, moves.tp)
        strip = strips[:, 0]
        for r in range(1, n_tp):
            strip = strip + swap_with(strips[:, r], "tp", n_tp, r)
        step = 1
        while step < n_ctx:
            strip = strip + swap_with(strip, "ctx", n_ctx, step)
            step *= 2
        strip = jnp.concatenate([strip, swap_with(strip, "dp", n_dp, 1)], axis=0)
        ada_grads.append(
            lax.dot_general(cond_rows.astype(F32), strip, TN, precision=HIGHEST)
        )
        cond_part = cond_part + lax.dot_general(
            strip, ada_low[level].astype(F32), NT, precision=HIGHEST
        )
    step = 1
    while step < n_tp:
        cond_part = cond_part + swap_with(cond_part, "tp", n_tp, step)
        step *= 2
    cond_grad = jnp.stack(
        [cond_part[:clips], swap_with(cond_part[clips:], "dp", n_dp, 1)], axis=1
    )[:, :, None]
    step = 1
    while step < n_ctx:
        cond_grad = jnp.concatenate(
            [cond_grad, swap_with(cond_grad, "ctx", n_ctx, step)], axis=2
        )
        step *= 2
    cond_grad = flip_to(cond_grad, 2, n_ctx, moves.ctx).reshape(clips, width)
    cond_grad = moves.halves(cond_grad)
    grad_condition = jax.vjp(jax.nn.silu, cond_full)[1](cond_grad)[0]

    stacked = [jnp.stack([grads[level][i] for level in range(LAYERS)]) for i in range(4)]
    return (output, grad_tokens, grad_condition, *stacked, jnp.stack(ada_grads))


def solution(mesh):
    placed = (
        P("dp", "ctx", "tp", None),
        P("dp", None),
        P("dp"),
        P(None, None, ("dp", "ctx"), "tp"),
        P(None, "tp", ("dp", "ctx")),
        P(None, ("dp", "ctx"), "tp"),
        P(None, "tp", ("dp", "ctx")),
        P(None, ("dp", "ctx"), "tp"),
        P("dp", "ctx", "tp", None),
    )
    return jax.shard_map(
        functools.partial(local, Moves(mesh)),
        mesh=mesh,
        in_specs=placed,
        out_specs=(
            P("dp", "ctx", "tp", None),
            P("dp", "ctx", "tp", None),
            P("dp", None),
            P(None, None, ("dp", "ctx"), "tp"),
            P(None, "tp", ("dp", "ctx")),
            P(None, ("dp", "ctx"), "tp"),
            P(None, "tp", ("dp", "ctx")),
            P(None, ("dp", "ctx"), "tp"),
        ),
        check_vma=False,
    )
```

```python
import functools

import jax
import jax.numpy as jnp
from jax import lax
from jax.experimental import pallas as pl
from jax.experimental.pallas import tpu as pltpu
from jax.sharding import PartitionSpec as P

HEAD_DIM = 72
LAYERS = 2
LANES = 128
EPS = 1e-06
SCALE = HEAD_DIM ** (-0.5)
HIGHEST = lax.Precision.HIGHEST
BF16 = jnp.bfloat16
F32 = jnp.float32

NN = (((1,), (0,)), ((), ()))
NT = (((1,), (1,)), ((), ()))
TN = (((0,), (0,)), ((), ()))


def dot(a, b, dims=NN):
    return lax.dot_general(a, b, dims, preferred_element_type=F32)


def swap_with(v, axis_name, n, k):
    return lax.ppermute(v, axis_name, [(i, i ^ k) for i in range(n)])


def flip_to(v, axis, n, me):
    shape = v.shape
    bit = 1
    while bit < n:
        split = shape[:axis] + (n // (2 * bit), 2, bit) + shape[axis + 1 :]
        parts = v.reshape(split)
        first = lax.slice_in_dim(parts, 0, 1, axis=axis + 1)
        second = lax.slice_in_dim(parts, 1, 2, axis=axis + 1)
        turned = jnp.concatenate([second, first], axis=axis + 1)
        v = jnp.where((me & bit) != 0, turned, parts).reshape(shape)
        bit *= 2
    return v


class Moves:
    def __init__(self, mesh):
        self.n_dp = mesh.shape["dp"]
        self.n_ctx = mesh.shape["ctx"]
        self.n_tp = mesh.shape["tp"]
        self.n_line = self.n_ctx // 2

    def here(self):
        self.dp = lax.axis_index("dp")
        self.ctx = lax.axis_index("ctx")
        self.tp = lax.axis_index("tp")
        self.line = self.ctx // 2
        self.side = self.ctx % 2

    def halves(self, v):
        half = v.shape[-1] // 2
        turned = jnp.concatenate([v[..., half:], v[..., :half]], axis=-1)
        return jnp.where(self.dp == 0, v, turned)

    def pair_stack(self, v, other):
        first = jnp.where(self.side == 0, v, other)
        second = jnp.where(self.side == 0, other, v)
        both = jnp.stack([first, second], axis=-3)
        return both.reshape(v.shape[:-3] + (-1, v.shape[-1]))

    def of_side(self, v, side):
        parts = v.reshape(self.n_line, 2, -1, v.shape[-1])
        return lax.dynamic_index_in_dim(parts, side, 1, keepdims=False)

    def over_tp(self, v, r):
        return swap_with(v, "tp", self.n_tp, r)

    def over_side(self, v):
        return swap_with(v, "ctx", self.n_ctx, 1)

    def over_core(self, v):
        return swap_with(v, "dp", self.n_dp, 1)

    def with_core(self, mine, layout):
        return layout, mine + [self.over_core(v) for v in mine]

    def line_gather(self, v):
        return [swap_with(v, "ctx", self.n_ctx, 2 * k) for k in range(1, self.n_line)]

    def line_stack(self, blocks):
        return flip_to(jnp.stack(blocks), 0, self.n_line, self.line)


    def gather_halves(self, v):
        others = range(1, self.n_tp)
        got = yield self.line_gather(v)
        half = v.shape[1] // 2
        lines = [
            self.line_stack([b[:, cut] for b in [v] + got])
            for cut in (slice(0, half), slice(half, None))
        ]
        got = self.over_side(lines[0]), [self.over_tp(lines[1], r) for r in others]
        side_got, tp_got = yield got
        block = self.pair_stack(lines[0], side_got)
        strips = jnp.stack([lines[1]] + tp_got)
        got = [self.over_tp(block, r) for r in others], self.over_side(strips)
        tp_got, side_got = yield got
        mine = [block] + tp_got + [self.pair_stack(strips, side_got)]
        layout = tuple(((r, None, half), (self.n_tp, r, half)) for r in range(self.n_tp))
        return self.with_core(mine, layout)

    def gather_sideways(self, v):
        got = yield self.line_gather(v)
        line = self.line_stack([v] + got)
        got = yield [self.over_tp(line, r) for r in range(1, self.n_tp)]
        strips = jnp.stack([line] + got)
        got = yield self.over_side(strips)
        mine = [self.pair_stack(strips, got)]
        layout = tuple(((0, r, v.shape[1]),) for r in range(self.n_tp))
        return self.with_core(mine, layout)

    def gather_rest(self, block):
        got = yield [self.over_tp(block, r) for r in range(1, self.n_tp)]
        layout = tuple(((r, None, block.shape[1]),) for r in range(self.n_tp))
        return self.with_core([block] + got, layout)

    def scatter_far(self, left, rights):
        others = range(1, self.n_tp)
        half_width = left.shape[1] // 2
        mine, theirs = left[:, :half_width], left[:, half_width:]
        got = [self.over_core(dot(theirs, v, TN).astype(BF16)) for v in rights]
        got = yield got
        totals = [(dot(mine, v, TN) + g.astype(F32)).astype(BF16) for v, g in zip(rights, got)]
        if len(totals) == 1:
            totals = jnp.split(totals[0], self.n_tp, axis=1)
        got = yield [self.over_tp(totals[r], r) for r in others]
        total = (totals[0].astype(F32) + sum(v.astype(F32) for v in got)).astype(BF16)
        return lax.psum_scatter(total, "ctx", scatter_dimension=0, tiled=True).astype(F32)

    def scatter_weight(self, left, rights):
        others = range(1, self.n_tp)
        half_width = left.shape[1] // 2
        mine, theirs = left[:, :half_width], left[:, half_width:]
        got = [self.over_core(dot(theirs, v, TN).astype(BF16)) for v in rights]
        got = yield got
        totals = [(dot(mine, v, TN) + g.astype(F32)).astype(BF16) for v, g in zip(rights, got)]
        if len(totals) == 1:
            totals = jnp.split(totals[0], self.n_tp, axis=1)
        columns = totals[0].shape[1]
        half = max(columns // 2 // LANES, 1) * LANES
        firsts = [v[:, :half] for v in totals]
        seconds = jnp.concatenate([v[:, half:] for v in totals], axis=1)
        got = (
            [self.over_tp(firsts[r], r) for r in others],
            self.over_side(self.of_side(seconds, 1 - self.side)),
        )
        tp_got, side_got = yield got
        first = (firsts[0].astype(F32) + sum(v.astype(F32) for v in tp_got)).astype(BF16)
        second = self.of_side(seconds, self.side).astype(F32) + side_got.astype(F32)
        second = jnp.split(second.astype(BF16), self.n_tp, axis=-1)
        got = (
            self.over_side(self.of_side(first, 1 - self.side)),
            [self.over_tp(second[r], r) for r in others],
        )
        side_got, tp_got = yield got
        first = self.of_side(first, self.side).astype(F32) + side_got.astype(F32)
        second = second[0].astype(F32) + sum(v.astype(F32) for v in tp_got)
        line = jnp.concatenate([first, second], axis=-1).astype(BF16)
        got = yield [
            swap_with(
                lax.dynamic_index_in_dim(line, self.line ^ k, 0, keepdims=False),
                "ctx",
                self.n_ctx,
                2 * k,
            )
            for k in range(1, self.n_line)
        ]
        own = lax.dynamic_index_in_dim(line, self.line, 0, keepdims=False)
        return own.astype(F32) + sum(v.astype(F32) for v in got)


class Task:
    def __init__(self, steps):
        self.steps, self.result = steps, None
        self.pending = next(steps)


def at_once(steps):
    pending = next(steps)
    while True:
        try:
            pending = steps.send(pending)
        except StopIteration as stop:
            return stop.value


class Lanes:
    def __init__(self):
        self.tasks = []

    def start(self, steps):
        task = Task(steps)
        self.tasks.append(task)
        return task

    def fence(self, values=(), but=()):
        due = [t for t in self.tasks if t not in but]
        values, pending = lax.optimization_barrier((values, [t.pending for t in due]))
        going = [t for t in self.tasks if t in but]
        for task, done in zip(due, pending):
            try:
                task.pending = task.steps.send(done)
                going.append(task)
            except StopIteration as stop:
                task.result = stop.value
        self.tasks = going
        return values


def window(head):
    start = head * HEAD_DIM
    return start // LANES * LANES, -(-(start + HEAD_DIM) // LANES) * LANES


def in_head(head, rows, low, high):
    lanes = lax.broadcasted_iota(jnp.int32, (rows, high - low), 1) + low
    return (lanes >= head * HEAD_DIM) & (lanes < (head + 1) * HEAD_DIM)


def spread_parts(x_ref, offset, parts, width):
    for index, part in enumerate(parts):
        padded = part.shape[1]
        start = offset + index * width
        if padded != width:
            part[:, padded - LANES :] = jnp.zeros((part.shape[0], LANES), part.dtype)
        part[:, :width] = x_ref[:, start : start + width]


def same_sequence(rows, stride):
    row = lax.broadcasted_iota(jnp.int32, (rows, rows), 0)
    column = lax.broadcasted_iota(jnp.int32, (rows, rows), 1)
    return lax.rem(row, stride) == lax.rem(column, stride)


def attend_kernel(count, width, stride, *refs):
    x_refs, (o_ref, lse_ref, q_s, k_s, v_s, o_s) = refs[:count], refs[count:]
    heads, rows = width // HEAD_DIM, o_ref.shape[0]
    lane = lax.broadcasted_iota(jnp.int32, (rows, LANES), 1)
    logs = jnp.zeros((rows, LANES), F32)
    if stride > 1:
        allowed = same_sequence(rows, stride)
    for index, x_ref in enumerate(x_refs):
        spread_parts(x_ref, 0, (q_s, k_s, v_s), width)
        for head in range(heads):
            low, high = window(head)
            mask = in_head(head, rows, low, high)
            queries = jnp.where(mask, q_s[:, low:high], jnp.zeros((), BF16))
            scores = dot(queries, k_s[:, low:high], NT) * SCALE
            if stride > 1:
                scores = jnp.where(allowed, scores, -jnp.inf)
            largest = jnp.max(scores, axis=-1, keepdims=True)
            raised = jnp.exp(scores - largest)
            total = jnp.sum(raised, axis=-1, keepdims=True)
            chances = (raised * (1.0 / total)).astype(BF16)
            result = dot(chances, v_s[:, low:high])
            o_s[:, low:high] = jnp.where(mask, result, o_s[:, low:high])
            logs = jnp.where(lane == index * heads + head, largest + jnp.log(total), logs)
        o_ref[:, index * width : (index + 1) * width] = o_s[:, :width].astype(BF16)
    lse_ref[...] = logs


def attend_back_kernel(count, width, stride, *refs):
    x_refs, (g_ref, lse_ref), dx_refs = refs[:count], refs[count : count + 2], refs[count + 2 : -7]
    q_s, k_s, v_s, g_s, dq_s, dk_s, dv_s = refs[-7:]
    heads, rows = width // HEAD_DIM, g_ref.shape[0]
    if stride > 1:
        allowed = same_sequence(rows, stride)
    for index, x_ref in enumerate(x_refs):
        spread_parts(x_ref, 0, (q_s, k_s, v_s), width)
        spread_parts(g_ref, index * width, (g_s,), width)
        for head in range(heads):
            low, high = window(head)
            mask = in_head(head, rows, low, high)
            zero = jnp.zeros((), BF16)
            q, k, v, g = q_s[:, low:high], k_s[:, low:high], v_s[:, low:high], g_s[:, low:high]
            scores = dot(jnp.where(mask, q, zero), k, NT) * SCALE
            if stride > 1:
                scores = jnp.where(allowed, scores, -jnp.inf)
            place = index * heads + head
            chances = jnp.exp(scores - lse_ref[:, place : place + 1])
            grad_chances = dot(jnp.where(mask, g, zero), v, NT)
            row_dot = jnp.sum(chances * grad_chances, axis=-1, keepdims=True)
            grad_scores = (chances * (grad_chances - row_dot)).astype(BF16)
            dq = dot(grad_scores, k) * SCALE
            dk = dot(grad_scores, q, TN) * SCALE
            dv = dot(chances.astype(BF16), g, TN)
            dq_s[:, low:high] = jnp.where(mask, dq, dq_s[:, low:high])
            dk_s[:, low:high] = jnp.where(mask, dk, dk_s[:, low:high])
            dv_s[:, low:high] = jnp.where(mask, dv, dv_s[:, low:high])
        for part_index, part in enumerate((dq_s, dk_s, dv_s)):
            start = part_index * width
            dx_refs[index][:, start : start + width] = part[:, :width].astype(BF16)


def row_block(rows, columns):
    return pl.BlockSpec((rows, columns), lambda i: (i, 0))


def attend(xs, rows, stride):
    count, width = xs[0].shape[0], xs[0].shape[1] // 3
    strips = len(xs)
    heads = strips * width // HEAD_DIM
    padded = -(-width // LANES) * LANES
    return pl.pallas_call(
        functools.partial(attend_kernel, strips, width, stride),
        grid=(count // rows,),
        in_specs=[row_block(rows, 3 * width)] * strips,
        out_specs=[row_block(rows, strips * width), row_block(rows, LANES)],
        out_shape=[
            jax.ShapeDtypeStruct((count, strips * width), BF16),
            jax.ShapeDtypeStruct((count, LANES), F32),
        ],
        scratch_shapes=[pltpu.VMEM((rows, padded), BF16)] * 3 + [pltpu.VMEM((rows, padded), F32)],
        cost_estimate=pl.CostEstimate(
            flops=heads * count * rows * 1024,
            bytes_accessed=count * width * strips * 8,
            transcendentals=heads * count * rows,
        ),
        compiler_params=pltpu.CompilerParams(vmem_limit_bytes=32 * 1024 * 1024),
    )(*xs)


def attend_back(xs, grad, lse, rows, stride):
    count, width = xs[0].shape[0], xs[0].shape[1] // 3
    strips = len(xs)
    heads = strips * width // HEAD_DIM
    padded = -(-width // LANES) * LANES
    return pl.pallas_call(
        functools.partial(attend_back_kernel, strips, width, stride),
        grid=(count // rows,),
        in_specs=[row_block(rows, 3 * width)] * strips
        + [row_block(rows, strips * width), row_block(rows, LANES)],
        out_specs=[row_block(rows, 3 * width)] * strips,
        out_shape=[jax.ShapeDtypeStruct((count, 3 * width), BF16)] * strips,
        scratch_shapes=[pltpu.VMEM((rows, padded), BF16)] * 4
        + [pltpu.VMEM((rows, padded), F32)] * 3,
        cost_estimate=pl.CostEstimate(
            flops=heads * count * rows * 2560,
            bytes_accessed=count * width * strips * 14,
            transcendentals=heads * count * rows,
        ),
        compiler_params=pltpu.CompilerParams(vmem_limit_bytes=32 * 1024 * 1024),
    )(*xs, grad, lse)


def weight_scratch(pieces):
    layout, arrays = pieces
    columns = sum(part[2] for strip in layout for part in strip)
    parts = max(len(strip) for strip in layout)
    return [
        pltpu.VMEM((2 * arrays[0].shape[-2], columns), BF16),
        pltpu.SemaphoreType.DMA((2, len(layout), parts)),
    ]


def weight_copies(layout, refs, w_s, sems):
    count = len(refs) // 2
    rows = w_s.shape[0] // 2
    copies = [[] for _ in layout]
    for group in range(2):
        low = 0
        for strip, parts in enumerate(layout):
            for part, (place, entry, columns) in enumerate(parts):
                source = refs[group * count + place]
                if entry is not None:
                    source = source.at[entry]
                target = w_s.at[pl.ds(group * rows, rows), pl.ds(low, columns)]
                low += columns
                copies[strip].append(
                    pltpu.make_async_copy(source, target, sems.at[group, strip, part])
                )
    return copies


def await_copies(copies):
    @pl.when(pl.program_id(0) == 0)
    def _():
        for copy in copies:
            copy.wait()


def turn_copies(copies, w_s, t_s):
    @pl.when(pl.program_id(0) == 0)
    def _():
        size = w_s.shape[1] // len(copies) // 2
        for strip, waits in enumerate(copies):
            for copy in waits:
                copy.wait()
            for low in (2 * strip * size, (2 * strip + 1) * size):
                t_s[low : low + size] = w_s[:, low : low + size].T


def begin_copies(*many):
    @pl.when(pl.program_id(0) == 0)
    def _():
        for copies in many:
            for strip in copies:
                for copy in strip:
                    copy.start()


def row_normal(v):
    centred = v - jnp.mean(v, axis=-1, keepdims=True)
    inverse = lax.rsqrt(jnp.mean(centred * centred, axis=-1, keepdims=True) + EPS)
    return centred * inverse, inverse


def row_back(grad, normed, inverse, scale):
    scaled = grad * (1.0 + scale)
    mean_one = jnp.mean(scaled, axis=-1, keepdims=True)
    mean_two = jnp.mean(scaled * normed, axis=-1, keepdims=True)
    return inverse * (scaled - mean_one - normed * mean_two)


def head_forward(heads, first, rows, allowed, q_s, k_s, v_s, o_s, lane, logs):
    for head in range(heads):
        low, high = window(head)
        mask = in_head(head, rows, low, high)
        queries = jnp.where(mask, q_s[:, low:high], jnp.zeros((), BF16))
        scores = dot(queries, k_s[:, low:high], NT) * SCALE
        if allowed is not None:
            scores = jnp.where(allowed, scores, -jnp.inf)
        largest = jnp.max(scores, axis=-1, keepdims=True)
        raised = jnp.exp(scores - largest)
        total = jnp.sum(raised, axis=-1, keepdims=True)
        chances = (raised * (1.0 / total)).astype(BF16)
        result = dot(chances, v_s[:, low:high])
        o_s[:, low:high] = jnp.where(mask, result, o_s[:, low:high])
        logs = jnp.where(lane == first + head, largest + jnp.log(total), logs)
    return logs


def head_back(heads, first, rows, allowed, q_s, k_s, v_s, g_s, lse_ref, dq_s, dk_s, dv_s):
    zero = jnp.zeros((), BF16)
    for head in range(heads):
        low, high = window(head)
        mask = in_head(head, rows, low, high)
        q, k, v, g = q_s[:, low:high], k_s[:, low:high], v_s[:, low:high], g_s[:, low:high]
        scores = dot(jnp.where(mask, q, zero), k, NT) * SCALE
        if allowed is not None:
            scores = jnp.where(allowed, scores, -jnp.inf)
        place = first + head
        chances = jnp.exp(scores - lse_ref[:, place : place + 1])
        grad_chances = dot(jnp.where(mask, g, zero), v, NT)
        row_dot = jnp.sum(chances * grad_chances, axis=-1, keepdims=True)
        grad_scores = (chances * (grad_chances - row_dot)).astype(BF16)
        dq = dot(grad_scores, k) * SCALE
        dk = dot(grad_scores, q, TN) * SCALE
        dv = dot(chances.astype(BF16), g, TN)
        dq_s[:, low:high] = jnp.where(mask, dq, dq_s[:, low:high])
        dk_s[:, low:high] = jnp.where(mask, dk, dk_s[:, low:high])
        dv_s[:, low:high] = jnp.where(mask, dv, dv_s[:, low:high])


def branch_kernel(layout, count, stride, x_ref, mod_ref, *refs):
    strips = len(layout)
    w_refs = refs[:count]
    h_ref, qkv_ref, lse_ref, o_ref, a_ref, y_ref, g_ref = refs[count : count + 7]
    w_s, sems, p_s, o_s, z_s = refs[count + 7 :]
    rows, width = x_ref.shape
    head_cols = width // strips
    padded = o_s.shape[1]
    spare = padded - head_cols
    columns = w_s.shape[1] // strips
    copies = weight_copies(layout, w_refs, w_s, sems)
    begin_copies(copies)
    x = x_ref[...].astype(F32)
    shift_a, scale_a, gate_a, shift_m, scale_m = [mod_ref[0, i : i + 1, :] for i in range(5)]
    h = (row_normal(x)[0] * (1.0 + scale_a) + shift_a).astype(BF16)
    h_ref[...] = h
    heads = head_cols // HEAD_DIM
    lane = lax.broadcasted_iota(jnp.int32, (rows, LANES), 1)
    logs = jnp.zeros((rows, LANES), F32)
    allowed = same_sequence(rows, stride) if stride > 1 else None
    branch = jnp.zeros((rows, width), F32)
    for strip in range(strips):
        start = strip * columns
        await_copies(copies[strip])
        p_s[...] = dot(h, w_s[:, start : start + p_s.shape[1]]).astype(BF16)
        parts = []
        for index in range(3):
            low = (3 * strip + index) * padded
            if spare:
                qkv_ref[:, low + padded - LANES : low + padded] = jnp.zeros((rows, LANES), BF16)
            qkv_ref[:, low : low + head_cols] = p_s[:, index * head_cols : (index + 1) * head_cols]
            parts.append(qkv_ref.at[:, pl.ds(low, padded)])
        logs = head_forward(heads, strip * heads, rows, allowed, *parts, o_s, lane, logs)
        low = o_s[:, :head_cols].astype(BF16)
        o_ref[:, strip * head_cols : (strip + 1) * head_cols] = low
        if spare:
            z_s[:, :LANES] = jnp.zeros((rows, LANES), BF16)
        z_s[:, spare:] = low
        branch = branch + dot(z_s[...], w_s[:, start + columns - padded : start + columns], NT)
    lse_ref[...] = logs
    a_ref[...] = branch.astype(BF16)
    y = x + gate_a * branch
    y_ref[...] = y
    g_ref[...] = (row_normal(y)[0] * (1.0 + scale_m) + shift_m).astype(BF16)


def branch_back_kernel(
    layout, count, stride, x_ref, mod_ref, da_ref, dy_ref, qkv_ref, lse_ref, *refs
):
    strips = len(layout)
    w_refs = refs[:count]
    dx_ref, sums_ref = refs[count : count + 2]
    out_refs = refs[count + 2 : count + 2 + strips]
    w_s, sems, d_s, g_s, dq_s, dk_s, dv_s = refs[count + 2 + strips :]
    rows, width = x_ref.shape
    head_cols = width // strips
    padded = g_s.shape[1]
    spare = padded - head_cols
    columns = w_s.shape[1] // strips
    copies = weight_copies(layout, w_refs, w_s, sems)
    begin_copies(copies)
    heads = head_cols // HEAD_DIM
    allowed = same_sequence(rows, stride) if stride > 1 else None
    grad = jnp.zeros((rows, width), F32)
    for strip in range(strips):
        start = strip * columns
        await_copies(copies[strip])
        turned = dot(da_ref[...], w_s[:, start + columns - padded : start + columns]).astype(BF16)
        if spare:
            g_s[:, padded - LANES :] = jnp.zeros((rows, LANES), BF16)
        g_s[:, :head_cols] = turned[:, spare:]
        parts = [qkv_ref.at[:, pl.ds((3 * strip + i) * padded, padded)] for i in range(3)]
        head_back(heads, strip * heads, rows, allowed, *parts, g_s, lse_ref, dq_s, dk_s, dv_s)
        if d_s.shape[1] != 3 * head_cols:
            d_s[:, d_s.shape[1] - LANES :] = jnp.zeros((rows, LANES), BF16)
        for index, part in enumerate((dq_s, dk_s, dv_s)):
            d_s[:, index * head_cols : (index + 1) * head_cols] = part[:, :head_cols].astype(BF16)
        out_refs[strip][...] = d_s[:, : 3 * head_cols]
        grad = grad + dot(d_s[...], w_s[:, start : start + d_s.shape[1]], NT)
    scale_a = mod_ref[0, 1:2, :]
    normed, inverse = row_normal(x_ref[...].astype(F32))
    sums_ref[...] = jnp.zeros(sums_ref.shape, F32)
    sums_ref[0, 0:1, :] = jnp.sum(grad, axis=0, keepdims=True)
    sums_ref[0, 1:2, :] = jnp.sum(grad * normed, axis=0, keepdims=True)
    dx_ref[...] = (dy_ref[...] + row_back(grad, normed, inverse, scale_a)).astype(BF16)


GELU_A = 0.7978845608028654
GELU_B = 0.044715


def up_kernel(layout, count, g_ref, *refs):
    strips = len(layout)
    z_ref, slope_ref, w_s, sems = refs[count:]
    copies = weight_copies(layout, refs[:count], w_s, sems)
    begin_copies(copies)
    half = w_s.shape[1] // (2 * strips)
    g = g_ref[...]
    for index in range(2 * strips):
        if index % 2 == 0:
            await_copies(copies[index // 2])
        low = index * half
        u = dot(g, w_s[:, low : low + half])
        square = u * u
        bent = jnp.tanh(u * (GELU_A + GELU_A * GELU_B * square))
        lifted = 0.5 * (1.0 + bent)
        z_ref[:, low : low + half] = (u * lifted).astype(BF16)
        inner = GELU_A + 3.0 * GELU_A * GELU_B * square
        slope = lifted + 0.5 * u * (1.0 - bent * bent) * inner
        slope_ref[:, low : low + half] = slope.astype(BF16)


def down_kernel(layout, count, z_ref, y_ref, mod_ref, *refs):
    strips = len(layout)
    m_ref, x_ref, w_s, sems, t_s = refs[count:]
    copies = weight_copies(layout, refs[:count], w_s, sems)
    begin_copies(copies)
    turn_copies(copies, w_s, t_s)
    total = dot(z_ref[...], t_s[...])
    m_ref[...] = total.astype(BF16)
    x_ref[...] = (y_ref[...] + mod_ref[0, 5:6, :] * total).astype(BF16)


def mlp_back_kernel(
    up_layout, ups_count, down_layout, count, dx_ref, mod_ref, m_ref, slope_ref, y_ref, a_ref, *refs
):
    strips = len(up_layout)
    (dm_ref, du_ref, dy_ref, da_ref, sums_ref, up_s, up_sems, down_s, down_sems, t_s) = refs[
        ups_count + count :
    ]
    ups = weight_copies(up_layout, refs[:ups_count], up_s, up_sems)
    downs = weight_copies(down_layout, refs[ups_count : ups_count + count], down_s, down_sems)
    begin_copies(downs, ups)
    half = up_s.shape[1] // (2 * strips)
    turn_copies(ups, up_s, t_s)
    scale_m, gate_m, share, gate_a = [mod_ref[0, i : i + 1, :] for i in (4, 5, 6, 2)]
    dx = dx_ref[...].astype(F32) * share
    sums_ref[...] = jnp.zeros(sums_ref.shape, F32)
    sums_ref[0, 5:6, :] = jnp.sum(dx * m_ref[...].astype(F32), axis=0, keepdims=True)
    dm = (gate_m * dx).astype(BF16)
    dm_ref[...] = dm
    grad = jnp.zeros(y_ref.shape, F32)
    for index in range(2 * strips):
        low = index * half
        if index % 2 == 0:
            await_copies(downs[index // 2])
        dz = dot(dm, down_s[:, low : low + half])
        du = (dz * slope_ref[:, low : low + half].astype(F32)).astype(BF16)
        du_ref[:, low : low + half] = du
        grad = grad + dot(du, t_s[low : low + half])
    normed, inverse = row_normal(y_ref[...])
    sums_ref[0, 3:4, :] = jnp.sum(grad, axis=0, keepdims=True)
    sums_ref[0, 4:5, :] = jnp.sum(grad * normed, axis=0, keepdims=True)
    dy = dx + row_back(grad, normed, inverse, scale_m)
    dy_ref[...] = dy
    sums_ref[0, 2:3, :] = jnp.sum(dy * a_ref[...].astype(F32), axis=0, keepdims=True)
    da_ref[...] = (gate_a * dy).astype(BF16)


def shape_of(*dims, dtype=BF16):
    return jax.ShapeDtypeStruct(dims, dtype)


def block_call(kernel, clips, rows, arrays, mods, weights, outs, sums, scratch, flops, order):
    operands, specs = [], []
    for v in order:
        if v is None:
            operands.append(mods)
            specs.append(pl.BlockSpec((1,) + mods.shape[1:], lambda i: (i, 0, 0)))
        else:
            operands.append(arrays[v])
            specs.append(row_block(rows, arrays[v].shape[1]))
    for _, pieces in weights:
        operands += pieces
        specs += [pl.BlockSpec(memory_space=pl.ANY)] * len(pieces)
    out_specs = [row_block(rows, v.shape[1]) for v in outs]
    out_shape = list(outs)
    if sums is not None:
        width = mods.shape[2]
        out_specs.insert(sums, pl.BlockSpec((1, 8, width), lambda i: (i, 0, 0)))
        out_shape.insert(sums, shape_of(clips, 8, width, dtype=F32))
    held = []
    for pieces in weights:
        held += weight_scratch(pieces)
    moved = sum(v.size * v.dtype.itemsize for v in operands)
    return pl.pallas_call(
        kernel,
        grid=(clips,),
        in_specs=specs,
        out_specs=out_specs,
        out_shape=out_shape,
        scratch_shapes=held + scratch,
        cost_estimate=pl.CostEstimate(flops=flops, bytes_accessed=moved, transcendentals=0),
        compiler_params=pltpu.CompilerParams(vmem_limit_bytes=60 * 1024 * 1024),
    )(*operands)


def padded_to(columns):
    return -(-columns // LANES) * LANES


def fused_branch(x, mods, pieces, clips, stride):
    count, width = x.shape
    rows, strips = count // clips, len(pieces[0])
    head_cols = width // strips
    padded = padded_to(head_cols)
    outs = [
        shape_of(count, width),
        shape_of(count, 3 * strips * padded),
        shape_of(count, LANES, dtype=F32),
        shape_of(count, width),
        shape_of(count, width),
        shape_of(count, width, dtype=F32),
        shape_of(count, width),
    ]
    scratch = [
        pltpu.VMEM((rows, padded_to(3 * head_cols)), BF16),
        pltpu.VMEM((rows, padded), F32),
        pltpu.VMEM((rows, padded), BF16),
    ]
    return block_call(
        functools.partial(branch_kernel, pieces[0], len(pieces[1]), stride),
        clips, rows, [x], mods, [pieces], outs, None, scratch,
        12 * count * width * width, [0, None],
    )


def fused_branch_back(x, mods, da, dy, qkv, lse, pieces, clips, stride):
    count, width = x.shape
    rows, strips = count // clips, len(pieces[0])
    head_cols = width // strips
    padded = padded_to(head_cols)
    outs = [shape_of(count, width)] + [shape_of(count, 3 * head_cols) for _ in range(strips)]
    scratch = [
        pltpu.VMEM((rows, padded_to(3 * head_cols)), BF16),
        pltpu.VMEM((rows, padded), BF16),
    ] + [pltpu.VMEM((rows, padded), F32)] * 3
    return block_call(
        functools.partial(branch_back_kernel, pieces[0], len(pieces[1]), stride),
        clips, rows, [x, da, dy, qkv, lse], mods, [pieces], outs, 1, scratch,
        16 * count * width * width, [0, None, 1, 2, 3, 4],
    )


def fused_up(g, mods, pieces, clips):
    count, width = g.shape
    rows, strips = count // clips, len(pieces[0])
    units = sum(part[2] for strip in pieces[0] for part in strip)
    outs = [shape_of(count, units), shape_of(count, units)]
    return block_call(
        functools.partial(up_kernel, pieces[0], len(pieces[1])),
        clips, rows, [g], mods, [pieces], outs, None, [], 2 * count * width * units, [0],
    )


def fused_down(z, y, mods, pieces, clips):
    count, width = y.shape
    rows, strips = count // clips, len(pieces[0])
    outs = [shape_of(count, width), shape_of(count, width)]
    return block_call(
        functools.partial(down_kernel, pieces[0], len(pieces[1])),
        clips, rows, [z, y], mods, [pieces], outs, None, [pltpu.VMEM((z.shape[1], width), BF16)],
        2 * z.size * width, [0, 1, None],
    )


def fused_mlp_back(dx, mods, m, slope, y, a, ups, downs, clips):
    count, width = y.shape
    rows = count // clips
    outs = [
        shape_of(count, width),
        shape_of(*slope.shape),
        shape_of(count, width, dtype=F32),
        shape_of(count, width),
    ]
    return block_call(
        functools.partial(mlp_back_kernel, ups[0], len(ups[1]), downs[0], len(downs[1])),
        clips, rows, [dx, m, slope, y, a], mods, [ups, downs], outs, 4,
        [pltpu.VMEM((slope.shape[1], width), BF16)],
        4 * slope.size * width, [0, None, 1, 2, 3, 4],
    )


def split_frames(v, frames, width):
    return v.reshape(frames, -1, width // HEAD_DIM, HEAD_DIM)


def attend_shared(x, frames):
    width = x.shape[1] // 3
    shaped = x.reshape(frames, -1, 3, width)
    pairs = lax.all_gather(shaped[:, :, 1:], "tp", axis=1, tiled=True)
    q = split_frames(shaped[:, :, 0], frames, width)
    k = split_frames(pairs[:, :, 0], frames, width)
    v = split_frames(pairs[:, :, 1], frames, width)
    scores = jnp.einsum("bqhe,bkhe->bhqk", q, k, preferred_element_type=F32) * SCALE
    chances = jax.nn.softmax(scores, axis=-1)
    result = jnp.einsum("bhqk,bkhe->bqhe", chances.astype(BF16), v, preferred_element_type=F32)
    return result.reshape(-1, width).astype(BF16), (q, k, v, chances)


def attend_shared_back(saved, grad):
    q, k, v, chances = saved
    frames, width = q.shape[0], grad.shape[1]
    grad = split_frames(grad, frames, width)
    grad_chances = jnp.einsum("bqhe,bkhe->bhqk", grad, v, preferred_element_type=F32)
    row_dot = jnp.sum(chances * grad_chances, axis=-1, keepdims=True)
    grad_scores = (chances * (grad_chances - row_dot)).astype(BF16)
    dq = jnp.einsum("bhqk,bkhe->bqhe", grad_scores, k, preferred_element_type=F32) * SCALE
    dk = jnp.einsum("bhqk,bqhe->bkhe", grad_scores, q, preferred_element_type=F32) * SCALE
    dv = jnp.einsum("bhqk,bqhe->bkhe", chances.astype(BF16), grad, preferred_element_type=F32)
    sums = lax.psum_scatter(jnp.stack([dk, dv], axis=2), "tp", scatter_dimension=1, tiled=True)
    parts = jnp.concatenate([dq[:, :, None], sums], axis=2)
    return parts.reshape(-1, 3 * width).astype(BF16)


def normalise(v):
    centred = v - jnp.mean(v, axis=-1, keepdims=True)
    inverse = lax.rsqrt(jnp.mean(centred * centred, axis=-1, keepdims=True) + EPS)
    return centred * inverse, inverse


def modulate(v, shift, scale):
    return (normalise(v)[0] * (1.0 + scale[:, None]) + shift[:, None]).astype(BF16)


def modulate_back(grad, v, scale):
    normed, inverse = normalise(v)
    shift_grad = jnp.sum(grad, axis=1)
    scale_grad = jnp.sum(grad * normed, axis=1)
    scaled = grad * (1.0 + scale[:, None])
    mean_one = jnp.mean(scaled, axis=-1, keepdims=True)
    mean_two = jnp.mean(scaled * normed, axis=-1, keepdims=True)
    return inverse * (scaled - mean_one - normed * mean_two), shift_grad, scale_grad


def gelu(v):
    return jax.nn.gelu(v, approximate=True)


def gelu_slope(v, grad):
    return jax.vjp(gelu, v)[1](grad)[0]


def local(moves, tokens, condition, micro_ids, w_qkv, w_out, w_up, w_down, w_ada, cotangent):
    moves.here()
    n_dp, n_ctx, n_tp = moves.n_dp, moves.n_ctx, moves.n_tp
    clips, frames_here, patches_here, width = tokens.shape
    rows_here, head_cols = w_qkv.shape[2:]
    whole_frames = frames_here % n_tp == 0
    spread_tp = n_tp if whole_frames else 1
    groups = frames_here // spread_tp
    piece = patches_here // n_ctx

    cond_full = condition.astype(F32)
    cond_low = jax.nn.silu(cond_full).astype(BF16)
    cond_all = jnp.concatenate([cond_low, swap_with(cond_low, "dp", n_dp, 1)], axis=0)
    first_row = (moves.dp * n_ctx + moves.ctx) * rows_here
    cond_rows = lax.dynamic_slice_in_dim(cond_all, first_row, rows_here, axis=1)
    ada_low = w_ada.astype(BF16)
    shares = jnp.stack([dot(cond_rows, ada_low[level]) for level in range(LAYERS)], axis=1)

    def total_over_ctx(v):
        got = yield [swap_with(v, "ctx", n_ctx, 2 * k) for k in range(1, n_ctx // 2)]
        return v + sum(got)

    def modulation_vectors():
        sums = shares[:clips] + swap_with(shares[clips:], "dp", n_dp, 1)
        sums = yield from total_over_ctx(sums)
        pairs = [
            [(c * n_tp + t, (c ^ dx) * n_tp + (t ^ r)) for c in range(n_ctx) for t in range(n_tp)]
            for r in range(n_tp)
            for dx in range(2)
        ]
        got = yield [lax.ppermute(sums, ("ctx", "tp"), entry) for entry in pairs[1:]]
        got = [sums] + got
        strips = [got[2 * r] + got[2 * r + 1] for r in range(n_tp)]
        strips = flip_to(jnp.stack(strips, axis=2), 2, n_tp, moves.tp)
        found = strips.reshape(clips, LAYERS, 6, width)
        return [moves.halves(found[:, level]) for level in range(LAYERS)]

    def to_frames(v):
        v = v.reshape(clips, frames_here, n_ctx, piece, width)
        v = flip_to(v, 2, n_ctx, moves.ctx)
        if spread_tp == 1:
            yield ()
            return v.reshape(clips, groups * patches_here, width)
        v = v.reshape(clips, spread_tp, groups, patches_here, width)
        v = flip_to(v, 1, spread_tp, moves.tp)
        got = yield [swap_with(v[:, r], "tp", n_tp, r) for r in range(1, spread_tp)]
        return jnp.stack([v[:, 0]] + got, axis=2).reshape(clips, -1, width)

    def from_frames(v):
        if spread_tp > 1:
            v = v.reshape(clips, groups, spread_tp, patches_here, width)
            blocks = [v[:, :, 0]]
            blocks += [swap_with(v[:, :, r], "tp", n_tp, r) for r in range(1, spread_tp)]
            v = flip_to(jnp.stack(blocks, axis=1), 1, spread_tp, moves.tp)
        v = v.reshape(clips, frames_here, n_ctx, piece, width)
        v = flip_to(v, 2, n_ctx, moves.ctx)
        return v.reshape(clips, frames_here, patches_here, width)

    def trade(get, planes):
        sides = []
        for dx, dr in planes:
            block = get(dx, dr)
            if dx or dr:
                pairs = [
                    (c * n_tp + t, (c ^ dx) * n_tp + (t ^ dr))
                    for c in range(n_ctx)
                    for t in range(n_tp)
                ]
                block = lax.ppermute(block, ("ctx", "tp"), pairs)
            sides.append(block)
        sides = sides[:1] + (yield sides[1:])
        lines = [jnp.stack([v[:, dz] for v in sides], axis=1) for dz in range(n_ctx // 2)]
        got = yield [swap_with(v, "ctx", n_ctx, 2 * dz) for dz, v in enumerate(lines) if dz]
        return jnp.stack(lines[:1] + got, axis=1)

    all_planes = [(dx, dr) for dx in range(2) for dr in range(spread_tp)]
    own_planes = [(0, 0), (1, 0)]

    def frames_to_clips(v):
        v = v.reshape(clips, groups, spread_tp, n_ctx // 2, 2, piece, width)
        got = yield from trade(lambda dx, dr: v[:, :, dr, :, dx].swapaxes(1, 2), all_planes)
        return got.reshape(clips, -1, width)

    def clips_to_frames(v):
        v = v.reshape(clips, n_ctx // 2, 2, spread_tp, groups, piece, width)
        got = yield from trade(lambda dx, dr: v[:, :, dx, dr], all_planes)
        got = got.reshape(clips, n_ctx, spread_tp, groups, piece, width)
        return got.transpose(0, 3, 2, 1, 4, 5).reshape(clips, -1, width)

    def here_to_clips(v):
        v = v.reshape(clips, spread_tp, groups, n_ctx, piece, width)
        v = flip_to(flip_to(v, 3, n_ctx, moves.ctx), 1, spread_tp, moves.tp % spread_tp)
        v = v.reshape(clips, spread_tp, groups, n_ctx // 2, 2, piece, width)
        got = yield from trade(lambda dx, dr: v[:, :, :, :, dx].transpose(0, 3, 1, 2, 4, 5), own_planes)
        return got.reshape(clips, -1, width)

    def clips_to_here(v):
        v = v.reshape(clips, n_ctx // 2, 2, spread_tp, groups, piece, width)
        got = yield from trade(lambda dx, dr: v[:, :, dx], own_planes)
        v = got.reshape(clips, n_ctx, spread_tp, groups, piece, width).transpose(0, 2, 3, 1, 4, 5)
        v = flip_to(flip_to(v, 3, n_ctx, moves.ctx), 1, spread_tp, moves.tp % spread_tp)
        return v.reshape(clips, frames_here, patches_here, width)

    def flat(v):
        return v.reshape(-1, v.shape[-1])

    def shaped(v):
        return v.reshape(clips, -1, v.shape[-1])

    shards = []
    for level in range(LAYERS):
        attention = [w_qkv[level, 0], w_qkv[level, 1], w_qkv[level, 2], w_out[level].T]
        shards.append(jnp.concatenate(attention, axis=1).astype(BF16))
        shards.append(w_up[level].astype(BF16))
        shards.append(w_down[level].T.astype(BF16))
    lanes = Lanes()
    gathers = {}

    shards, blocks = (
        shards,
        {
            index: lax.all_gather(shards[index], "ctx", axis=0, tiled=True)
            for index in range(1, len(shards), 2)
        },
    )

    def set_out(index):
        if index in blocks:
            steps = moves.gather_rest(blocks[index])
        elif index == 0:
            steps = moves.gather_halves(shards[index])
        else:
            steps = moves.gather_sideways(shards[index])
        gathers[index] = lanes.start(steps)

    def tick(values=(), out=()):
        held = {index: blocks.get(index, shards[index]) for index in out}
        held, values = lanes.fence((held, values))
        for index in out:
            if index in blocks:
                blocks[index] = held[index]
            else:
                shards[index] = held[index]
            set_out(index)
        return values

    def whole(index):
        layout, arrays = gathers[index].result
        count = len(arrays) // 2
        groups = []
        for group in (arrays[:count], arrays[count:]):
            parts = [
                group[place] if entry is None else group[place][entry]
                for strip in layout
                for place, entry, _ in strip
            ]
            groups.append(jnp.concatenate(parts, axis=1))
        return jnp.concatenate(groups, axis=0)

    def attention_weights(index):
        v = whole(index)
        strips = jnp.split(v, n_tp, axis=1)
        cut = 3 * head_cols
        return [w[:, :cut] for w in strips], jnp.concatenate([w[:, cut:] for w in strips], axis=1)

    def modulations(level):
        return [mods[level][:, i] for i in range(6)]

    set_out(0)
    moved = lanes.start(to_frames(moves.halves(tokens)))
    vectors_task = lanes.start(modulation_vectors())
    tick(out=(2,))
    residual = moved.result
    tick()
    tick(out=(1,))
    mods = vectors_task.result
    fused = (
        whole_frames
        and head_cols % 32 == 0
        and w_up.shape[2] % (2 * LANES) == 0
        and 4 * head_cols == w_up.shape[2]
        and width % 32 == 0
    )
    matched = (micro_ids[:, None] == micro_ids[None, :]).astype(F32)
    share = 1.0 / jnp.sum(matched, axis=1)
    scatters = {}
    mod_grads = [None] * LAYERS

    def start_scatter(level, name, left, rights):
        far = level and name != "out"
        steps = (moves.scatter_far if far else moves.scatter_weight)(left, rights)
        scatters[level, name] = lanes.start(steps)

    def mod_strip(grads):
        parts = moves.halves(grads).reshape(clips, n_tp, -1)
        parts = flip_to(parts, 1, n_tp, moves.tp)
        got = yield [swap_with(parts[:, r], "tp", n_tp, r) for r in range(1, n_tp)]
        strip = parts[:, 0] + sum(got)
        strip = yield from total_over_ctx(strip)
        got = yield swap_with(strip, "ctx", n_ctx, 1)
        strip = strip + got
        got = yield swap_with(strip, "dp", n_dp, 1)
        return jnp.concatenate([strip, got], axis=0)

    strips = {}

    def fused_passes(v):
        vectors, saved = [], []
        for level in range(LAYERS):
            last = share if level == LAYERS - 1 else jnp.ones_like(share)
            last = jnp.broadcast_to(last[:, None, None], (clips, 2, width))
            vectors.append(jnp.concatenate([mods[level], last], axis=1))
        v = flat(v)
        for level in range(LAYERS):
            stride = piece if level % 2 else 1
            joined = gathers[3 * level].result
            kept = fused_branch(v, vectors[level], joined, clips, stride)
            normed, qkv, lse, result, branch, middle, normed_mlp = tick(kept, (4,) if level == 0 else ())
            up = gathers[3 * level + 1].result
            act, slope = tick(fused_up(normed_mlp, vectors[level], up, clips), (3,) if level == 0 else ())
            down = gathers[3 * level + 2].result
            branch_mlp, after = fused_down(act, middle, vectors[level], down, clips)
            saved.append((v, normed, qkv, lse, result, branch, middle, normed_mlp))
            saved[-1] += (act, slope, branch_mlp, joined, up, down, stride)
            v = after
            if level == 0:
                moved = lanes.start(frames_to_clips(shaped(v)))
                tick(out=(5,))
                late = tick(cotangent)
                turned = lanes.start(here_to_clips(moves.halves(late)))
                v = flat(moved.result)
        finished = lanes.start(clips_to_here(moves.halves(shaped(v))))
        grad = flat(turned.result)
        for level in reversed(range(LAYERS)):
            v, normed, qkv, lse, result, branch, middle, normed_mlp = saved[level][:8]
            act, slope, branch_mlp, joined, up, down, stride = saved[level][8:]
            back = fused_mlp_back(
                grad, vectors[level], branch_mlp, slope, middle, branch, up, down, clips
            )
            grad_branch, grad_pre, grad_middle, grad_out, sums = lanes.fence(back)
            start_scatter(level, "down", grad_branch, [act])
            grad_out = lanes.fence(grad_out, (finished,))
            if level == 0:
                start_scatter(level, "up", normed_mlp, [grad_pre])
                grad_out = lanes.fence(grad_out)
            back = fused_branch_back(
                v, vectors[level], grad_out, grad_middle, qkv, lse, joined, clips, stride
            )
            grad, more, *grad_qkv = lanes.fence(back)
            mod_grads[level] = (sums + more)[:, :6]
            if level:
                moved = lanes.start(clips_to_frames(shaped(grad)))
                start_scatter(level, "up", normed_mlp, [grad_pre])
                lanes.fence()
                start_scatter(level, "qkv", normed, grad_qkv)
                start_scatter(level, "out", grad_out, [result])
                lanes.fence()
                strips[level] = lanes.start(mod_strip(mod_grads[level]))
                grad = flat(moved.result)
            else:
                start_scatter(level, "qkv", normed, grad_qkv)
                start_scatter(level, "out", grad_out, [result])
        return finished, shaped(grad)

    def plain_passes(residual):
        residual = residual.astype(F32)
        records = []
        for level in range(LAYERS):
            spatial = level % 2 == 0
            shift_a, scale_a, gate_a, shift_m, scale_m, gate_m = modulations(level)
            normed = flat(modulate(residual, shift_a, scale_a))
            qkvs, outs = attention_weights(3 * level)
            projected = [dot(normed, v).astype(BF16) for v in qkvs]
            rows, stride = (patches_here * spread_tp, 1) if spatial else (residual.shape[1], piece)
            if spatial and not whole_frames:
                saved = [attend_shared(v, clips * frames_here) for v in projected]
                result = jnp.concatenate([entry[0] for entry in saved], axis=1)
                saved = [entry[1] for entry in saved]
            else:
                result, saved = attend(projected, rows, stride)
            result, saved = tick((result, saved), (4,) if level == 0 else ())
            branch = shaped(dot(result, outs, NT))
            middle = residual + gate_a[:, None] * branch
            normed_mlp = flat(modulate(middle, shift_m, scale_m))
            up = whole(3 * level + 1)
            pre_act = dot(normed_mlp, up)
            act = gelu(pre_act).astype(BF16)
            act, pre_act = tick((act, pre_act), (3,) if level == 0 else ())
            down = whole(3 * level + 2)
            branch_mlp = shaped(dot(act, down, NT))
            records.append(
                (residual, normed, projected, saved, result, branch, middle, normed_mlp)
                + (pre_act, act, branch_mlp, qkvs, outs, up, down, rows, stride)
            )
            residual = middle + gate_m[:, None] * branch_mlp
            if spatial:
                moved = lanes.start(frames_to_clips(residual.astype(BF16)))
                tick(out=(5,))
                turned = lanes.start(here_to_clips(moves.halves(cotangent)))
                tick()
                residual = moved.result.astype(F32)
        gradient = turned.result.astype(F32) * share[:, None, None]
        finished = lanes.start(clips_to_here(moves.halves(residual.astype(BF16))))
        for level in reversed(range(LAYERS)):
            spatial = level % 2 == 0
            (residual, normed, projected, saved, result, branch, middle, normed_mlp) = records[level][
                :8
            ]
            (pre_act, act, branch_mlp, qkvs, outs, up, down, rows, stride) = records[level][8:]
            shift_a, scale_a, gate_a, shift_m, scale_m, gate_m = modulations(level)
            gate_m_grad = jnp.sum(gradient * branch_mlp, axis=1)
            low_grad = flat((gradient * gate_m[:, None]).astype(BF16))
            grad_pre = gelu_slope(pre_act, dot(low_grad, down)).astype(BF16)
            start_scatter(level, "down", low_grad, [act])
            grad_pre = lanes.fence(grad_pre)
            grad_normed = shaped(dot(grad_pre, up, NT))
            start_scatter(level, "up", normed_mlp, [grad_pre])
            grad_normed = lanes.fence(grad_normed)
            added, shift_m_grad, scale_m_grad = modulate_back(grad_normed, middle, scale_m)
            gradient = gradient + added
            gate_a_grad = jnp.sum(gradient * branch, axis=1)
            low_grad = flat((gradient * gate_a[:, None]).astype(BF16))
            grad_heads = dot(low_grad, outs).astype(BF16)
            start_scatter(level, "out", low_grad, [result])
            grad_heads = lanes.fence(grad_heads)
            if spatial and not whole_frames:
                grad_qkv = [
                    attend_shared_back(v, g)
                    for v, g in zip(saved, jnp.split(grad_heads, n_tp, axis=1))
                ]
            else:
                grad_qkv = attend_back(projected, grad_heads, saved, rows, stride)
            grad_qkv = lanes.fence(grad_qkv)
            start_scatter(level, "qkv", normed, grad_qkv)
            grad_normed = shaped(sum(dot(v, w, NT) for v, w in zip(grad_qkv, qkvs)))
            added, shift_a_grad, scale_a_grad = modulate_back(grad_normed, residual, scale_a)
            gradient = gradient + added
            mod_grads[level] = jnp.stack(
                [shift_a_grad, scale_a_grad, gate_a_grad, shift_m_grad, scale_m_grad, gate_m_grad],
                axis=1,
            )
            if not spatial:
                moved = lanes.start(clips_to_frames(gradient.astype(BF16)))
                lanes.fence()
                lanes.fence()
                gradient = moved.result.astype(F32)
        return finished, gradient

    passes = fused_passes if fused else plain_passes
    finished, gradient = passes(residual)
    grad_tokens = from_frames(moves.halves(gradient.astype(BF16))).astype(F32)
    while lanes.tasks:
        lanes.fence()
    output = finished.result
    grads = [
        (
            scatters[level, "qkv"].result.reshape(rows_here, 3, head_cols).transpose(1, 0, 2),
            scatters[level, "out"].result.T,
            scatters[level, "up"].result,
            scatters[level, "down"].result.T,
        )
        for level in range(LAYERS)
    ]

    ada_grads = []
    cond_part = 0.0
    for level in range(LAYERS):
        if level in strips:
            strip = strips[level].result
        else:
            strip = at_once(mod_strip(mod_grads[level]))
        ada_grads.append(
            lax.dot_general(cond_rows.astype(F32), strip, TN, precision=HIGHEST)
        )
        cond_part = cond_part + lax.dot_general(
            strip, ada_low[level].astype(F32), NT, precision=HIGHEST
        )
    step = 1
    while step < n_tp:
        cond_part = cond_part + swap_with(cond_part, "tp", n_tp, step)
        step *= 2
    cond_grad = jnp.stack(
        [cond_part[:clips], swap_with(cond_part[clips:], "dp", n_dp, 1)], axis=1
    )[:, :, None]
    step = 1
    while step < n_ctx:
        cond_grad = jnp.concatenate(
            [cond_grad, swap_with(cond_grad, "ctx", n_ctx, step)], axis=2
        )
        step *= 2
    cond_grad = flip_to(cond_grad, 2, n_ctx, moves.ctx).reshape(clips, width)
    cond_grad = moves.halves(cond_grad)
    grad_condition = jax.vjp(jax.nn.silu, cond_full)[1](cond_grad)[0]

    stacked = [jnp.stack([grads[level][i] for level in range(LAYERS)]) for i in range(4)]
    return (output, grad_tokens, grad_condition, *stacked, jnp.stack(ada_grads))


def solution(mesh):
    placed = (
        P("dp", "ctx", "tp", None),
        P("dp", None),
        P("dp"),
        P(None, None, ("dp", "ctx"), "tp"),
        P(None, "tp", ("dp", "ctx")),
        P(None, ("dp", "ctx"), "tp"),
        P(None, "tp", ("dp", "ctx")),
        P(None, ("dp", "ctx"), "tp"),
        P("dp", "ctx", "tp", None),
    )
    return jax.shard_map(
        functools.partial(local, Moves(mesh)),
        mesh=mesh,
        in_specs=placed,
        out_specs=(
            P("dp", "ctx", "tp", None),
            P("dp", "ctx", "tp", None),
            P("dp", None),
            P(None, None, ("dp", "ctx"), "tp"),
            P(None, "tp", ("dp", "ctx")),
            P(None, ("dp", "ctx"), "tp"),
            P(None, "tp", ("dp", "ctx")),
            P(None, ("dp", "ctx"), "tp"),
        ),
        check_vma=False,
    )
```

```python
import functools

import jax
import jax.numpy as jnp
from jax import lax
from jax.experimental import pallas as pl
from jax.experimental.pallas import tpu as pltpu
from jax.sharding import PartitionSpec as P

HEAD_DIM = 72
LAYERS = 2
LANES = 128
EPS = 1e-06
SCALE = HEAD_DIM ** (-0.5)
HIGHEST = lax.Precision.HIGHEST
BF16 = jnp.bfloat16
F32 = jnp.float32

NN = (((1,), (0,)), ((), ()))
NT = (((1,), (1,)), ((), ()))
TN = (((0,), (0,)), ((), ()))


def dot(a, b, dims=NN):
    return lax.dot_general(a, b, dims, preferred_element_type=F32)


def swap_with(v, axis_name, n, k):
    return lax.ppermute(v, axis_name, [(i, i ^ k) for i in range(n)])


def flip_to(v, axis, n, me):
    shape = v.shape
    bit = 1
    while bit < n:
        split = shape[:axis] + (n // (2 * bit), 2, bit) + shape[axis + 1 :]
        parts = v.reshape(split)
        first = lax.slice_in_dim(parts, 0, 1, axis=axis + 1)
        second = lax.slice_in_dim(parts, 1, 2, axis=axis + 1)
        turned = jnp.concatenate([second, first], axis=axis + 1)
        v = jnp.where((me & bit) != 0, turned, parts).reshape(shape)
        bit *= 2
    return v


class Moves:
    def __init__(self, mesh):
        self.n_dp = mesh.shape["dp"]
        self.n_ctx = mesh.shape["ctx"]
        self.n_tp = mesh.shape["tp"]
        self.n_line = self.n_ctx // 2

    def here(self):
        self.dp = lax.axis_index("dp")
        self.ctx = lax.axis_index("ctx")
        self.tp = lax.axis_index("tp")
        self.line = self.ctx // 2
        self.side = self.ctx % 2

    def halves(self, v):
        half = v.shape[-1] // 2
        turned = jnp.concatenate([v[..., half:], v[..., :half]], axis=-1)
        return jnp.where(self.dp == 0, v, turned)

    def pair_stack(self, v, other):
        first = jnp.where(self.side == 0, v, other)
        second = jnp.where(self.side == 0, other, v)
        both = jnp.stack([first, second], axis=-3)
        return both.reshape(v.shape[:-3] + (-1, v.shape[-1]))

    def of_side(self, v, side):
        parts = v.reshape(self.n_line, 2, -1, v.shape[-1])
        return lax.dynamic_index_in_dim(parts, side, 1, keepdims=False)

    def over_tp(self, v, r):
        return swap_with(v, "tp", self.n_tp, r)

    def over_side(self, v):
        return swap_with(v, "ctx", self.n_ctx, 1)

    def over_core(self, v):
        return swap_with(v, "dp", self.n_dp, 1)

    def with_core(self, mine, layout):
        return layout, mine + [self.over_core(v) for v in mine]

    def line_gather(self, v):
        return [swap_with(v, "ctx", self.n_ctx, 2 * k) for k in range(1, self.n_line)]

    def line_stack(self, blocks):
        return flip_to(jnp.stack(blocks), 0, self.n_line, self.line)


    def gather_halves(self, v):
        others = range(1, self.n_tp)
        got = yield self.line_gather(v)
        half = v.shape[1] // 2
        lines = [
            self.line_stack([b[:, cut] for b in [v] + got])
            for cut in (slice(0, half), slice(half, None))
        ]
        got = self.over_side(lines[0]), [self.over_tp(lines[1], r) for r in others]
        side_got, tp_got = yield got
        block = self.pair_stack(lines[0], side_got)
        strips = jnp.stack([lines[1]] + tp_got)
        got = [self.over_tp(block, r) for r in others], self.over_side(strips)
        tp_got, side_got = yield got
        mine = [block] + tp_got + [self.pair_stack(strips, side_got)]
        layout = tuple(((r, None, half), (self.n_tp, r, half)) for r in range(self.n_tp))
        return self.with_core(mine, layout)

    def gather_rest(self, block):
        got = yield [self.over_tp(block, r) for r in range(1, self.n_tp)]
        layout = tuple(((r, None, block.shape[1]),) for r in range(self.n_tp))
        return self.with_core([block] + got, layout)

    def scatter_far(self, left, rights):
        others = range(1, self.n_tp)
        half_width = left.shape[1] // 2
        mine, theirs = left[:, :half_width], left[:, half_width:]
        got = [self.over_core(dot(theirs, v, TN).astype(BF16)) for v in rights]
        got = yield got
        totals = [(dot(mine, v, TN) + g.astype(F32)).astype(BF16) for v, g in zip(rights, got)]
        if len(totals) == 1:
            totals = jnp.split(totals[0], self.n_tp, axis=1)
        got = yield [self.over_tp(totals[r], r) for r in others]
        total = (totals[0].astype(F32) + sum(v.astype(F32) for v in got)).astype(BF16)
        shard = yield Rest(lax.psum_scatter(total, "ctx", scatter_dimension=0, tiled=True))
        return shard.astype(F32)

    def scatter_weight(self, left, rights):
        others = range(1, self.n_tp)
        half_width = left.shape[1] // 2
        mine, theirs = left[:, :half_width], left[:, half_width:]
        got = [self.over_core(dot(theirs, v, TN).astype(BF16)) for v in rights]
        got = yield got
        totals = [(dot(mine, v, TN) + g.astype(F32)).astype(BF16) for v, g in zip(rights, got)]
        if len(totals) == 1:
            totals = jnp.split(totals[0], self.n_tp, axis=1)
        columns = totals[0].shape[1]
        half = max(columns // 2 // LANES, 1) * LANES
        firsts = [v[:, :half] for v in totals]
        seconds = jnp.concatenate([v[:, half:] for v in totals], axis=1)
        got = (
            [self.over_tp(firsts[r], r) for r in others],
            self.over_side(self.of_side(seconds, 1 - self.side)),
        )
        tp_got, side_got = yield got
        first = (firsts[0].astype(F32) + sum(v.astype(F32) for v in tp_got)).astype(BF16)
        second = self.of_side(seconds, self.side).astype(F32) + side_got.astype(F32)
        second = jnp.split(second.astype(BF16), self.n_tp, axis=-1)
        got = (
            self.over_side(self.of_side(first, 1 - self.side)),
            [self.over_tp(second[r], r) for r in others],
        )
        side_got, tp_got = yield got
        first = self.of_side(first, self.side).astype(F32) + side_got.astype(F32)
        second = second[0].astype(F32) + sum(v.astype(F32) for v in tp_got)
        line = jnp.concatenate([first, second], axis=-1).astype(BF16)
        got = yield [
            swap_with(
                lax.dynamic_index_in_dim(line, self.line ^ k, 0, keepdims=False),
                "ctx",
                self.n_ctx,
                2 * k,
            )
            for k in range(1, self.n_line)
        ]
        own = lax.dynamic_index_in_dim(line, self.line, 0, keepdims=False)
        return own.astype(F32) + sum(v.astype(F32) for v in got)


class Rest:
    def __init__(self, value):
        self.value = value


class Task:
    def __init__(self, steps):
        self.steps, self.result = steps, None
        self.take(next(steps))

    def take(self, pending):
        self.resting = isinstance(pending, Rest)
        self.pending = pending.value if self.resting else pending


def at_once(steps):
    pending = next(steps)
    while True:
        try:
            pending = steps.send(pending)
        except StopIteration as stop:
            return stop.value


class Lanes:
    def __init__(self):
        self.tasks = []

    def start(self, steps):
        task = Task(steps)
        self.tasks.append(task)
        return task

    def fence(self, values=(), but=(), last=False):
        due = [t for t in self.tasks if t not in but and (last or not t.resting)]
        values, pending = lax.optimization_barrier((values, [t.pending for t in due]))
        going = [t for t in self.tasks if t not in due]
        for task, done in zip(due, pending):
            try:
                task.take(task.steps.send(done))
                going.append(task)
            except StopIteration as stop:
                task.result = stop.value
        self.tasks = going
        return values


def window(head):
    start = head * HEAD_DIM
    return start // LANES * LANES, -(-(start + HEAD_DIM) // LANES) * LANES


def in_head(head, rows, low, high):
    lanes = lax.broadcasted_iota(jnp.int32, (rows, high - low), 1) + low
    return (lanes >= head * HEAD_DIM) & (lanes < (head + 1) * HEAD_DIM)


def spread_parts(x_ref, offset, parts, width):
    for index, part in enumerate(parts):
        padded = part.shape[1]
        start = offset + index * width
        if padded != width:
            part[:, padded - LANES :] = jnp.zeros((part.shape[0], LANES), part.dtype)
        part[:, :width] = x_ref[:, start : start + width]


def same_sequence(rows, stride):
    row = lax.broadcasted_iota(jnp.int32, (rows, rows), 0)
    column = lax.broadcasted_iota(jnp.int32, (rows, rows), 1)
    return lax.rem(row, stride) == lax.rem(column, stride)


def attend_kernel(count, width, stride, *refs):
    x_refs, (o_ref, lse_ref, q_s, k_s, v_s, o_s) = refs[:count], refs[count:]
    heads, rows = width // HEAD_DIM, o_ref.shape[0]
    lane = lax.broadcasted_iota(jnp.int32, (rows, LANES), 1)
    logs = jnp.zeros((rows, LANES), F32)
    if stride > 1:
        allowed = same_sequence(rows, stride)
    for index, x_ref in enumerate(x_refs):
        spread_parts(x_ref, 0, (q_s, k_s, v_s), width)
        for head in range(heads):
            low, high = window(head)
            mask = in_head(head, rows, low, high)
            queries = jnp.where(mask, q_s[:, low:high], jnp.zeros((), BF16))
            scores = dot(queries, k_s[:, low:high], NT) * SCALE
            if stride > 1:
                scores = jnp.where(allowed, scores, -jnp.inf)
            largest = jnp.max(scores, axis=-1, keepdims=True)
            raised = jnp.exp(scores - largest)
            total = jnp.sum(raised, axis=-1, keepdims=True)
            chances = (raised * (1.0 / total)).astype(BF16)
            result = dot(chances, v_s[:, low:high])
            o_s[:, low:high] = jnp.where(mask, result, o_s[:, low:high])
            logs = jnp.where(lane == index * heads + head, largest + jnp.log(total), logs)
        o_ref[:, index * width : (index + 1) * width] = o_s[:, :width].astype(BF16)
    lse_ref[...] = logs


def attend_back_kernel(count, width, stride, *refs):
    x_refs, (g_ref, lse_ref), dx_refs = refs[:count], refs[count : count + 2], refs[count + 2 : -7]
    q_s, k_s, v_s, g_s, dq_s, dk_s, dv_s = refs[-7:]
    heads, rows = width // HEAD_DIM, g_ref.shape[0]
    if stride > 1:
        allowed = same_sequence(rows, stride)
    for index, x_ref in enumerate(x_refs):
        spread_parts(x_ref, 0, (q_s, k_s, v_s), width)
        spread_parts(g_ref, index * width, (g_s,), width)
        for head in range(heads):
            low, high = window(head)
            mask = in_head(head, rows, low, high)
            zero = jnp.zeros((), BF16)
            q, k, v, g = q_s[:, low:high], k_s[:, low:high], v_s[:, low:high], g_s[:, low:high]
            scores = dot(jnp.where(mask, q, zero), k, NT) * SCALE
            if stride > 1:
                scores = jnp.where(allowed, scores, -jnp.inf)
            place = index * heads + head
            chances = jnp.exp(scores - lse_ref[:, place : place + 1])
            grad_chances = dot(jnp.where(mask, g, zero), v, NT)
            row_dot = jnp.sum(chances * grad_chances, axis=-1, keepdims=True)
            grad_scores = (chances * (grad_chances - row_dot)).astype(BF16)
            dq = dot(grad_scores, k) * SCALE
            dk = dot(grad_scores, q, TN) * SCALE
            dv = dot(chances.astype(BF16), g, TN)
            dq_s[:, low:high] = jnp.where(mask, dq, dq_s[:, low:high])
            dk_s[:, low:high] = jnp.where(mask, dk, dk_s[:, low:high])
            dv_s[:, low:high] = jnp.where(mask, dv, dv_s[:, low:high])
        for part_index, part in enumerate((dq_s, dk_s, dv_s)):
            start = part_index * width
            dx_refs[index][:, start : start + width] = part[:, :width].astype(BF16)


def row_block(rows, columns):
    return pl.BlockSpec((rows, columns), lambda i: (i, 0))


def attend(xs, rows, stride):
    count, width = xs[0].shape[0], xs[0].shape[1] // 3
    strips = len(xs)
    heads = strips * width // HEAD_DIM
    padded = -(-width // LANES) * LANES
    return pl.pallas_call(
        functools.partial(attend_kernel, strips, width, stride),
        grid=(count // rows,),
        in_specs=[row_block(rows, 3 * width)] * strips,
        out_specs=[row_block(rows, strips * width), row_block(rows, LANES)],
        out_shape=[
            jax.ShapeDtypeStruct((count, strips * width), BF16),
            jax.ShapeDtypeStruct((count, LANES), F32),
        ],
        scratch_shapes=[pltpu.VMEM((rows, padded), BF16)] * 3 + [pltpu.VMEM((rows, padded), F32)],
        cost_estimate=pl.CostEstimate(
            flops=heads * count * rows * 1024,
            bytes_accessed=count * width * strips * 8,
            transcendentals=heads * count * rows,
        ),
        compiler_params=pltpu.CompilerParams(vmem_limit_bytes=32 * 1024 * 1024),
    )(*xs)


def attend_back(xs, grad, lse, rows, stride):
    count, width = xs[0].shape[0], xs[0].shape[1] // 3
    strips = len(xs)
    heads = strips * width // HEAD_DIM
    padded = -(-width // LANES) * LANES
    return pl.pallas_call(
        functools.partial(attend_back_kernel, strips, width, stride),
        grid=(count // rows,),
        in_specs=[row_block(rows, 3 * width)] * strips
        + [row_block(rows, strips * width), row_block(rows, LANES)],
        out_specs=[row_block(rows, 3 * width)] * strips,
        out_shape=[jax.ShapeDtypeStruct((count, 3 * width), BF16)] * strips,
        scratch_shapes=[pltpu.VMEM((rows, padded), BF16)] * 4
        + [pltpu.VMEM((rows, padded), F32)] * 3,
        cost_estimate=pl.CostEstimate(
            flops=heads * count * rows * 2560,
            bytes_accessed=count * width * strips * 14,
            transcendentals=heads * count * rows,
        ),
        compiler_params=pltpu.CompilerParams(vmem_limit_bytes=32 * 1024 * 1024),
    )(*xs, grad, lse)


def weight_scratch(pieces):
    layout, arrays = pieces
    columns = sum(part[2] for strip in layout for part in strip)
    parts = max(len(strip) for strip in layout)
    return [
        pltpu.VMEM((2 * arrays[0].shape[-2], columns), BF16),
        pltpu.SemaphoreType.DMA((2, len(layout), parts)),
    ]


def weight_copies(layout, refs, w_s, sems):
    count = len(refs) // 2
    rows = w_s.shape[0] // 2
    copies = [[] for _ in layout]
    for group in range(2):
        low = 0
        for strip, parts in enumerate(layout):
            for part, (place, entry, columns) in enumerate(parts):
                source = refs[group * count + place]
                if entry is not None:
                    source = source.at[entry]
                target = w_s.at[pl.ds(group * rows, rows), pl.ds(low, columns)]
                low += columns
                copies[strip].append(
                    pltpu.make_async_copy(source, target, sems.at[group, strip, part])
                )
    return copies


def await_copies(copies):
    @pl.when(pl.program_id(0) == 0)
    def _():
        for copy in copies:
            copy.wait()


def turn_copies(copies, w_s, t_s):
    @pl.when(pl.program_id(0) == 0)
    def _():
        size = w_s.shape[1] // len(copies) // 2
        for strip, waits in enumerate(copies):
            for copy in waits:
                copy.wait()
            for low in (2 * strip * size, (2 * strip + 1) * size):
                t_s[low : low + size] = w_s[:, low : low + size].T


def begin_copies(*many):
    @pl.when(pl.program_id(0) == 0)
    def _():
        for copies in many:
            for strip in copies:
                for copy in strip:
                    copy.start()


def row_normal(v):
    centred = v - jnp.mean(v, axis=-1, keepdims=True)
    inverse = lax.rsqrt(jnp.mean(centred * centred, axis=-1, keepdims=True) + EPS)
    return centred * inverse, inverse


def row_back(grad, normed, inverse, scale):
    scaled = grad * (1.0 + scale)
    mean_one = jnp.mean(scaled, axis=-1, keepdims=True)
    mean_two = jnp.mean(scaled * normed, axis=-1, keepdims=True)
    return inverse * (scaled - mean_one - normed * mean_two)


def head_forward(heads, first, rows, allowed, q_s, k_s, v_s, o_s, lane, logs):
    for head in range(heads):
        low, high = window(head)
        mask = in_head(head, rows, low, high)
        queries = jnp.where(mask, q_s[:, low:high], jnp.zeros((), BF16))
        scores = dot(queries, k_s[:, low:high], NT) * SCALE
        if allowed is not None:
            scores = jnp.where(allowed, scores, -jnp.inf)
        largest = jnp.max(scores, axis=-1, keepdims=True)
        raised = jnp.exp(scores - largest)
        total = jnp.sum(raised, axis=-1, keepdims=True)
        chances = (raised * (1.0 / total)).astype(BF16)
        result = dot(chances, v_s[:, low:high])
        o_s[:, low:high] = jnp.where(mask, result, o_s[:, low:high])
        logs = jnp.where(lane == first + head, largest + jnp.log(total), logs)
    return logs


def head_back(heads, first, rows, allowed, q_s, k_s, v_s, g_s, lse_ref, dq_s, dk_s, dv_s):
    zero = jnp.zeros((), BF16)
    for head in range(heads):
        low, high = window(head)
        mask = in_head(head, rows, low, high)
        q, k, v, g = q_s[:, low:high], k_s[:, low:high], v_s[:, low:high], g_s[:, low:high]
        scores = dot(jnp.where(mask, q, zero), k, NT) * SCALE
        if allowed is not None:
            scores = jnp.where(allowed, scores, -jnp.inf)
        place = first + head
        chances = jnp.exp(scores - lse_ref[:, place : place + 1])
        grad_chances = dot(jnp.where(mask, g, zero), v, NT)
        row_dot = jnp.sum(chances * grad_chances, axis=-1, keepdims=True)
        grad_scores = (chances * (grad_chances - row_dot)).astype(BF16)
        dq = dot(grad_scores, k) * SCALE
        dk = dot(grad_scores, q, TN) * SCALE
        dv = dot(chances.astype(BF16), g, TN)
        dq_s[:, low:high] = jnp.where(mask, dq, dq_s[:, low:high])
        dk_s[:, low:high] = jnp.where(mask, dk, dk_s[:, low:high])
        dv_s[:, low:high] = jnp.where(mask, dv, dv_s[:, low:high])


def branch_kernel(layout, count, stride, x_ref, mod_ref, *refs):
    strips = len(layout)
    w_refs = refs[:count]
    h_ref, qkv_ref, lse_ref, o_ref, a_ref, y_ref, g_ref = refs[count : count + 7]
    w_s, sems, p_s, o_s, z_s = refs[count + 7 :]
    rows, width = x_ref.shape
    head_cols = width // strips
    padded = o_s.shape[1]
    spare = padded - head_cols
    columns = w_s.shape[1] // strips
    copies = weight_copies(layout, w_refs, w_s, sems)
    begin_copies(copies)
    x = x_ref[...].astype(F32)
    shift_a, scale_a, gate_a, shift_m, scale_m = [mod_ref[0, i : i + 1, :] for i in range(5)]
    h = (row_normal(x)[0] * (1.0 + scale_a) + shift_a).astype(BF16)
    h_ref[...] = h
    heads = head_cols // HEAD_DIM
    lane = lax.broadcasted_iota(jnp.int32, (rows, LANES), 1)
    logs = jnp.zeros((rows, LANES), F32)
    allowed = same_sequence(rows, stride) if stride > 1 else None
    branch = jnp.zeros((rows, width), F32)
    for strip in range(strips):
        start = strip * columns
        await_copies(copies[strip])
        p_s[...] = dot(h, w_s[:, start : start + p_s.shape[1]]).astype(BF16)
        parts = []
        for index in range(3):
            low = (3 * strip + index) * padded
            if spare:
                qkv_ref[:, low + padded - LANES : low + padded] = jnp.zeros((rows, LANES), BF16)
            qkv_ref[:, low : low + head_cols] = p_s[:, index * head_cols : (index + 1) * head_cols]
            parts.append(qkv_ref.at[:, pl.ds(low, padded)])
        logs = head_forward(heads, strip * heads, rows, allowed, *parts, o_s, lane, logs)
        low = o_s[:, :head_cols].astype(BF16)
        o_ref[:, strip * head_cols : (strip + 1) * head_cols] = low
        if spare:
            z_s[:, :LANES] = jnp.zeros((rows, LANES), BF16)
        z_s[:, spare:] = low
        branch = branch + dot(z_s[...], w_s[:, start + columns - padded : start + columns], NT)
    lse_ref[...] = logs
    a_ref[...] = branch.astype(BF16)
    y = x + gate_a * branch
    y_ref[...] = y
    g_ref[...] = (row_normal(y)[0] * (1.0 + scale_m) + shift_m).astype(BF16)


def branch_back_kernel(
    layout, count, stride, x_ref, mod_ref, da_ref, dy_ref, qkv_ref, lse_ref, *refs
):
    strips = len(layout)
    w_refs = refs[:count]
    dx_ref, sums_ref = refs[count : count + 2]
    out_refs = refs[count + 2 : count + 2 + strips]
    w_s, sems, d_s, g_s, dq_s, dk_s, dv_s = refs[count + 2 + strips :]
    rows, width = x_ref.shape
    head_cols = width // strips
    padded = g_s.shape[1]
    spare = padded - head_cols
    columns = w_s.shape[1] // strips
    copies = weight_copies(layout, w_refs, w_s, sems)
    begin_copies(copies)
    heads = head_cols // HEAD_DIM
    allowed = same_sequence(rows, stride) if stride > 1 else None
    grad = jnp.zeros((rows, width), F32)
    for strip in range(strips):
        start = strip * columns
        await_copies(copies[strip])
        turned = dot(da_ref[...], w_s[:, start + columns - padded : start + columns]).astype(BF16)
        if spare:
            g_s[:, padded - LANES :] = jnp.zeros((rows, LANES), BF16)
        g_s[:, :head_cols] = turned[:, spare:]
        parts = [qkv_ref.at[:, pl.ds((3 * strip + i) * padded, padded)] for i in range(3)]
        head_back(heads, strip * heads, rows, allowed, *parts, g_s, lse_ref, dq_s, dk_s, dv_s)
        if d_s.shape[1] != 3 * head_cols:
            d_s[:, d_s.shape[1] - LANES :] = jnp.zeros((rows, LANES), BF16)
        for index, part in enumerate((dq_s, dk_s, dv_s)):
            d_s[:, index * head_cols : (index + 1) * head_cols] = part[:, :head_cols].astype(BF16)
        out_refs[strip][...] = d_s[:, : 3 * head_cols]
        grad = grad + dot(d_s[...], w_s[:, start : start + d_s.shape[1]], NT)
    scale_a = mod_ref[0, 1:2, :]
    normed, inverse = row_normal(x_ref[...].astype(F32))
    sums_ref[...] = jnp.zeros(sums_ref.shape, F32)
    sums_ref[0, 0:1, :] = jnp.sum(grad, axis=0, keepdims=True)
    sums_ref[0, 1:2, :] = jnp.sum(grad * normed, axis=0, keepdims=True)
    dx_ref[...] = (dy_ref[...] + row_back(grad, normed, inverse, scale_a)).astype(BF16)


GELU_A = 0.7978845608028654
GELU_B = 0.044715


def up_kernel(layout, count, g_ref, *refs):
    strips = len(layout)
    z_ref, slope_ref, w_s, sems = refs[count:]
    copies = weight_copies(layout, refs[:count], w_s, sems)
    begin_copies(copies)
    half = w_s.shape[1] // (2 * strips)
    g = g_ref[...]
    for index in range(2 * strips):
        if index % 2 == 0:
            await_copies(copies[index // 2])
        low = index * half
        u = dot(g, w_s[:, low : low + half])
        square = u * u
        bent = jnp.tanh(u * (GELU_A + GELU_A * GELU_B * square))
        lifted = 0.5 * (1.0 + bent)
        z_ref[:, low : low + half] = (u * lifted).astype(BF16)
        inner = GELU_A + 3.0 * GELU_A * GELU_B * square
        slope = lifted + 0.5 * u * (1.0 - bent * bent) * inner
        slope_ref[:, low : low + half] = slope.astype(BF16)


def down_kernel(layout, count, z_ref, y_ref, mod_ref, *refs):
    strips = len(layout)
    m_ref, x_ref, w_s, sems, t_s = refs[count:]
    copies = weight_copies(layout, refs[:count], w_s, sems)
    begin_copies(copies)
    turn_copies(copies, w_s, t_s)
    total = dot(z_ref[...], t_s[...])
    m_ref[...] = total.astype(BF16)
    x_ref[...] = (y_ref[...] + mod_ref[0, 5:6, :] * total).astype(BF16)


def mlp_back_kernel(
    up_layout, ups_count, down_layout, count, dx_ref, mod_ref, m_ref, slope_ref, y_ref, a_ref, *refs
):
    strips = len(up_layout)
    (dm_ref, du_ref, dy_ref, da_ref, sums_ref, up_s, up_sems, down_s, down_sems, t_s) = refs[
        ups_count + count :
    ]
    ups = weight_copies(up_layout, refs[:ups_count], up_s, up_sems)
    downs = weight_copies(down_layout, refs[ups_count : ups_count + count], down_s, down_sems)
    begin_copies(downs, ups)
    half = up_s.shape[1] // (2 * strips)
    turn_copies(ups, up_s, t_s)
    scale_m, gate_m, share, gate_a = [mod_ref[0, i : i + 1, :] for i in (4, 5, 6, 2)]
    dx = dx_ref[...].astype(F32) * share
    sums_ref[...] = jnp.zeros(sums_ref.shape, F32)
    sums_ref[0, 5:6, :] = jnp.sum(dx * m_ref[...].astype(F32), axis=0, keepdims=True)
    dm = (gate_m * dx).astype(BF16)
    dm_ref[...] = dm
    grad = jnp.zeros(y_ref.shape, F32)
    for index in range(2 * strips):
        low = index * half
        if index % 2 == 0:
            await_copies(downs[index // 2])
        dz = dot(dm, down_s[:, low : low + half])
        du = (dz * slope_ref[:, low : low + half].astype(F32)).astype(BF16)
        du_ref[:, low : low + half] = du
        grad = grad + dot(du, t_s[low : low + half])
    normed, inverse = row_normal(y_ref[...])
    sums_ref[0, 3:4, :] = jnp.sum(grad, axis=0, keepdims=True)
    sums_ref[0, 4:5, :] = jnp.sum(grad * normed, axis=0, keepdims=True)
    dy = dx + row_back(grad, normed, inverse, scale_m)
    dy_ref[...] = dy
    sums_ref[0, 2:3, :] = jnp.sum(dy * a_ref[...].astype(F32), axis=0, keepdims=True)
    da_ref[...] = (gate_a * dy).astype(BF16)


def shape_of(*dims, dtype=BF16):
    return jax.ShapeDtypeStruct(dims, dtype)


def block_call(kernel, clips, rows, arrays, mods, weights, outs, sums, scratch, flops, order):
    operands, specs = [], []
    for v in order:
        if v is None:
            operands.append(mods)
            specs.append(pl.BlockSpec((1,) + mods.shape[1:], lambda i: (i, 0, 0)))
        else:
            operands.append(arrays[v])
            specs.append(row_block(rows, arrays[v].shape[1]))
    for _, pieces in weights:
        operands += pieces
        specs += [pl.BlockSpec(memory_space=pl.ANY)] * len(pieces)
    out_specs = [row_block(rows, v.shape[1]) for v in outs]
    out_shape = list(outs)
    if sums is not None:
        width = mods.shape[2]
        out_specs.insert(sums, pl.BlockSpec((1, 8, width), lambda i: (i, 0, 0)))
        out_shape.insert(sums, shape_of(clips, 8, width, dtype=F32))
    held = []
    for pieces in weights:
        held += weight_scratch(pieces)
    moved = sum(v.size * v.dtype.itemsize for v in operands)
    return pl.pallas_call(
        kernel,
        grid=(clips,),
        in_specs=specs,
        out_specs=out_specs,
        out_shape=out_shape,
        scratch_shapes=held + scratch,
        cost_estimate=pl.CostEstimate(flops=flops, bytes_accessed=moved, transcendentals=0),
        compiler_params=pltpu.CompilerParams(vmem_limit_bytes=60 * 1024 * 1024),
    )(*operands)


def padded_to(columns):
    return -(-columns // LANES) * LANES


def fused_branch(x, mods, pieces, clips, stride):
    count, width = x.shape
    rows, strips = count // clips, len(pieces[0])
    head_cols = width // strips
    padded = padded_to(head_cols)
    outs = [
        shape_of(count, width),
        shape_of(count, 3 * strips * padded),
        shape_of(count, LANES, dtype=F32),
        shape_of(count, width),
        shape_of(count, width),
        shape_of(count, width, dtype=F32),
        shape_of(count, width),
    ]
    scratch = [
        pltpu.VMEM((rows, padded_to(3 * head_cols)), BF16),
        pltpu.VMEM((rows, padded), F32),
        pltpu.VMEM((rows, padded), BF16),
    ]
    return block_call(
        functools.partial(branch_kernel, pieces[0], len(pieces[1]), stride),
        clips, rows, [x], mods, [pieces], outs, None, scratch,
        12 * count * width * width, [0, None],
    )


def fused_branch_back(x, mods, da, dy, qkv, lse, pieces, clips, stride):
    count, width = x.shape
    rows, strips = count // clips, len(pieces[0])
    head_cols = width // strips
    padded = padded_to(head_cols)
    outs = [shape_of(count, width)] + [shape_of(count, 3 * head_cols) for _ in range(strips)]
    scratch = [
        pltpu.VMEM((rows, padded_to(3 * head_cols)), BF16),
        pltpu.VMEM((rows, padded), BF16),
    ] + [pltpu.VMEM((rows, padded), F32)] * 3
    return block_call(
        functools.partial(branch_back_kernel, pieces[0], len(pieces[1]), stride),
        clips, rows, [x, da, dy, qkv, lse], mods, [pieces], outs, 1, scratch,
        16 * count * width * width, [0, None, 1, 2, 3, 4],
    )


def fused_up(g, mods, pieces, clips):
    count, width = g.shape
    rows, strips = count // clips, len(pieces[0])
    units = sum(part[2] for strip in pieces[0] for part in strip)
    outs = [shape_of(count, units), shape_of(count, units)]
    return block_call(
        functools.partial(up_kernel, pieces[0], len(pieces[1])),
        clips, rows, [g], mods, [pieces], outs, None, [], 2 * count * width * units, [0],
    )


def fused_down(z, y, mods, pieces, clips):
    count, width = y.shape
    rows, strips = count // clips, len(pieces[0])
    outs = [shape_of(count, width), shape_of(count, width)]
    return block_call(
        functools.partial(down_kernel, pieces[0], len(pieces[1])),
        clips, rows, [z, y], mods, [pieces], outs, None, [pltpu.VMEM((z.shape[1], width), BF16)],
        2 * z.size * width, [0, 1, None],
    )


def fused_mlp_back(dx, mods, m, slope, y, a, ups, downs, clips):
    count, width = y.shape
    rows = count // clips
    outs = [
        shape_of(count, width),
        shape_of(*slope.shape),
        shape_of(count, width, dtype=F32),
        shape_of(count, width),
    ]
    return block_call(
        functools.partial(mlp_back_kernel, ups[0], len(ups[1]), downs[0], len(downs[1])),
        clips, rows, [dx, m, slope, y, a], mods, [ups, downs], outs, 4,
        [pltpu.VMEM((slope.shape[1], width), BF16)],
        4 * slope.size * width, [0, None, 1, 2, 3, 4],
    )


def split_frames(v, frames, width):
    return v.reshape(frames, -1, width // HEAD_DIM, HEAD_DIM)


def attend_shared(x, frames):
    width = x.shape[1] // 3
    shaped = x.reshape(frames, -1, 3, width)
    pairs = lax.all_gather(shaped[:, :, 1:], "tp", axis=1, tiled=True)
    q = split_frames(shaped[:, :, 0], frames, width)
    k = split_frames(pairs[:, :, 0], frames, width)
    v = split_frames(pairs[:, :, 1], frames, width)
    scores = jnp.einsum("bqhe,bkhe->bhqk", q, k, preferred_element_type=F32) * SCALE
    chances = jax.nn.softmax(scores, axis=-1)
    result = jnp.einsum("bhqk,bkhe->bqhe", chances.astype(BF16), v, preferred_element_type=F32)
    return result.reshape(-1, width).astype(BF16), (q, k, v, chances)


def attend_shared_back(saved, grad):
    q, k, v, chances = saved
    frames, width = q.shape[0], grad.shape[1]
    grad = split_frames(grad, frames, width)
    grad_chances = jnp.einsum("bqhe,bkhe->bhqk", grad, v, preferred_element_type=F32)
    row_dot = jnp.sum(chances * grad_chances, axis=-1, keepdims=True)
    grad_scores = (chances * (grad_chances - row_dot)).astype(BF16)
    dq = jnp.einsum("bhqk,bkhe->bqhe", grad_scores, k, preferred_element_type=F32) * SCALE
    dk = jnp.einsum("bhqk,bqhe->bkhe", grad_scores, q, preferred_element_type=F32) * SCALE
    dv = jnp.einsum("bhqk,bqhe->bkhe", chances.astype(BF16), grad, preferred_element_type=F32)
    sums = lax.psum_scatter(jnp.stack([dk, dv], axis=2), "tp", scatter_dimension=1, tiled=True)
    parts = jnp.concatenate([dq[:, :, None], sums], axis=2)
    return parts.reshape(-1, 3 * width).astype(BF16)


def normalise(v):
    centred = v - jnp.mean(v, axis=-1, keepdims=True)
    inverse = lax.rsqrt(jnp.mean(centred * centred, axis=-1, keepdims=True) + EPS)
    return centred * inverse, inverse


def modulate(v, shift, scale):
    return (normalise(v)[0] * (1.0 + scale[:, None]) + shift[:, None]).astype(BF16)


def modulate_back(grad, v, scale):
    normed, inverse = normalise(v)
    shift_grad = jnp.sum(grad, axis=1)
    scale_grad = jnp.sum(grad * normed, axis=1)
    scaled = grad * (1.0 + scale[:, None])
    mean_one = jnp.mean(scaled, axis=-1, keepdims=True)
    mean_two = jnp.mean(scaled * normed, axis=-1, keepdims=True)
    return inverse * (scaled - mean_one - normed * mean_two), shift_grad, scale_grad


def gelu(v):
    return jax.nn.gelu(v, approximate=True)


def gelu_slope(v, grad):
    return jax.vjp(gelu, v)[1](grad)[0]


def local(moves, tokens, condition, micro_ids, w_qkv, w_out, w_up, w_down, w_ada, cotangent):
    moves.here()
    n_dp, n_ctx, n_tp = moves.n_dp, moves.n_ctx, moves.n_tp
    clips, frames_here, patches_here, width = tokens.shape
    rows_here, head_cols = w_qkv.shape[2:]
    whole_frames = frames_here % n_tp == 0
    spread_tp = n_tp if whole_frames else 1
    groups = frames_here // spread_tp
    piece = patches_here // n_ctx

    cond_full = condition.astype(F32)
    cond_low = jax.nn.silu(cond_full).astype(BF16)
    cond_all = jnp.concatenate([cond_low, swap_with(cond_low, "dp", n_dp, 1)], axis=0)
    first_row = (moves.dp * n_ctx + moves.ctx) * rows_here
    cond_rows = lax.dynamic_slice_in_dim(cond_all, first_row, rows_here, axis=1)
    ada_low = w_ada.astype(BF16)
    shares = jnp.stack([dot(cond_rows, ada_low[level]) for level in range(LAYERS)], axis=1)

    def total_over_ctx(v):
        got = yield [swap_with(v, "ctx", n_ctx, 2 * k) for k in range(1, n_ctx // 2)]
        return v + sum(got)

    def modulation_vectors():
        sums = shares[:clips] + swap_with(shares[clips:], "dp", n_dp, 1)
        sums = yield from total_over_ctx(sums)
        pairs = [
            [(c * n_tp + t, (c ^ dx) * n_tp + (t ^ r)) for c in range(n_ctx) for t in range(n_tp)]
            for r in range(n_tp)
            for dx in range(2)
        ]
        got = yield [lax.ppermute(sums, ("ctx", "tp"), entry) for entry in pairs[1:]]
        got = [sums] + got
        strips = [got[2 * r] + got[2 * r + 1] for r in range(n_tp)]
        strips = flip_to(jnp.stack(strips, axis=2), 2, n_tp, moves.tp)
        found = strips.reshape(clips, LAYERS, 6, width)
        return [moves.halves(found[:, level]) for level in range(LAYERS)]

    def to_frames(v):
        v = v.reshape(clips, frames_here, n_ctx, piece, width)
        v = flip_to(v, 2, n_ctx, moves.ctx)
        if spread_tp == 1:
            yield ()
            return v.reshape(clips, groups * patches_here, width)
        v = v.reshape(clips, spread_tp, groups, patches_here, width)
        v = flip_to(v, 1, spread_tp, moves.tp)
        got = yield [swap_with(v[:, r], "tp", n_tp, r) for r in range(1, spread_tp)]
        return jnp.stack([v[:, 0]] + got, axis=2).reshape(clips, -1, width)

    def from_frames(v):
        if spread_tp > 1:
            v = v.reshape(clips, groups, spread_tp, patches_here, width)
            blocks = [v[:, :, 0]]
            blocks += [swap_with(v[:, :, r], "tp", n_tp, r) for r in range(1, spread_tp)]
            v = flip_to(jnp.stack(blocks, axis=1), 1, spread_tp, moves.tp)
        v = v.reshape(clips, frames_here, n_ctx, piece, width)
        v = flip_to(v, 2, n_ctx, moves.ctx)
        return v.reshape(clips, frames_here, patches_here, width)

    def trade(get, planes):
        sides = []
        for dx, dr in planes:
            block = get(dx, dr)
            if dx or dr:
                pairs = [
                    (c * n_tp + t, (c ^ dx) * n_tp + (t ^ dr))
                    for c in range(n_ctx)
                    for t in range(n_tp)
                ]
                block = lax.ppermute(block, ("ctx", "tp"), pairs)
            sides.append(block)
        sides = sides[:1] + (yield sides[1:])
        lines = [jnp.stack([v[:, dz] for v in sides], axis=1) for dz in range(n_ctx // 2)]
        got = yield [swap_with(v, "ctx", n_ctx, 2 * dz) for dz, v in enumerate(lines) if dz]
        return jnp.stack(lines[:1] + got, axis=1)

    all_planes = [(dx, dr) for dx in range(2) for dr in range(spread_tp)]
    own_planes = [(0, 0), (1, 0)]

    def frames_to_clips(v):
        v = v.reshape(clips, groups, spread_tp, n_ctx // 2, 2, piece, width)
        got = yield from trade(lambda dx, dr: v[:, :, dr, :, dx].swapaxes(1, 2), all_planes)
        return got.reshape(clips, -1, width)

    def clips_to_frames(v):
        v = v.reshape(clips, n_ctx // 2, 2, spread_tp, groups, piece, width)
        got = yield from trade(lambda dx, dr: v[:, :, dx, dr], all_planes)
        got = got.reshape(clips, n_ctx, spread_tp, groups, piece, width)
        return got.transpose(0, 3, 2, 1, 4, 5).reshape(clips, -1, width)

    def here_to_clips(v):
        v = v.reshape(clips, spread_tp, groups, n_ctx, piece, width)
        v = flip_to(flip_to(v, 3, n_ctx, moves.ctx), 1, spread_tp, moves.tp % spread_tp)
        v = v.reshape(clips, spread_tp, groups, n_ctx // 2, 2, piece, width)
        got = yield from trade(lambda dx, dr: v[:, :, :, :, dx].transpose(0, 3, 1, 2, 4, 5), own_planes)
        return got.reshape(clips, -1, width)

    def clips_to_here(v):
        v = v.reshape(clips, n_ctx // 2, 2, spread_tp, groups, piece, width)
        got = yield from trade(lambda dx, dr: v[:, :, dx], own_planes)
        v = got.reshape(clips, n_ctx, spread_tp, groups, piece, width).transpose(0, 2, 3, 1, 4, 5)
        v = flip_to(flip_to(v, 3, n_ctx, moves.ctx), 1, spread_tp, moves.tp % spread_tp)
        return v.reshape(clips, frames_here, patches_here, width)

    def flat(v):
        return v.reshape(-1, v.shape[-1])

    def shaped(v):
        return v.reshape(clips, -1, v.shape[-1])

    shards = []
    for level in range(LAYERS):
        attention = [w_qkv[level, 0], w_qkv[level, 1], w_qkv[level, 2], w_out[level].T]
        shards.append(jnp.concatenate(attention, axis=1).astype(BF16))
        shards.append(w_up[level].astype(BF16))
        shards.append(w_down[level].T.astype(BF16))
    lanes = Lanes()
    gathers = {}

    blocks = {}

    def gather_far(index):
        blocks[index] = lax.all_gather(shards[index], "ctx", axis=0, tiled=True)

    def set_out(index):
        if index in blocks:
            steps = moves.gather_rest(blocks[index])
        else:
            steps = moves.gather_halves(shards[index])
        gathers[index] = lanes.start(steps)

    plan = [
        ((2,), (), ()),
        ((), (2,), ()),
        ((1,), (), ()),
        ((4,), (), (5,)),
        ((3,), (), ()),
        ((), (3,), ()),
        ((5,), (), ()),
        ((), (5,), ()),
        ((), (), ()),
    ]

    def tick(values=()):
        out, but, far = plan.pop(0)
        held = {index: blocks.get(index, shards[index]) for index in out + far}
        held, values = lanes.fence((held, values), [gathers[index] for index in but])
        for index in out + far:
            if index in blocks:
                blocks[index] = held[index]
            else:
                shards[index] = held[index]
        for index in far:
            gather_far(index)
        for index in out:
            set_out(index)
        return values

    def whole(index):
        layout, arrays = gathers[index].result
        count = len(arrays) // 2
        groups = []
        for group in (arrays[:count], arrays[count:]):
            parts = [
                group[place] if entry is None else group[place][entry]
                for strip in layout
                for place, entry, _ in strip
            ]
            groups.append(jnp.concatenate(parts, axis=1))
        return jnp.concatenate(groups, axis=0)

    def attention_weights(index):
        v = whole(index)
        strips = jnp.split(v, n_tp, axis=1)
        cut = 3 * head_cols
        return [w[:, :cut] for w in strips], jnp.concatenate([w[:, cut:] for w in strips], axis=1)

    def modulations(level):
        return [mods[level][:, i] for i in range(6)]

    gather_far(1)
    gather_far(3)
    set_out(0)
    moved = lanes.start(to_frames(moves.halves(tokens)))
    vectors_task = lanes.start(modulation_vectors())
    tick()
    residual = moved.result
    tick()
    tick()
    mods = vectors_task.result
    fused = (
        whole_frames
        and head_cols % 32 == 0
        and w_up.shape[2] % (2 * LANES) == 0
        and 4 * head_cols == w_up.shape[2]
        and width % 32 == 0
    )
    matched = (micro_ids[:, None] == micro_ids[None, :]).astype(F32)
    share = 1.0 / jnp.sum(matched, axis=1)
    scatters = {}
    mod_grads = [None] * LAYERS

    def start_scatter(level, name, left, rights):
        far = level and name != "out"
        steps = (moves.scatter_far if far else moves.scatter_weight)(left, rights)
        scatters[level, name] = lanes.start(steps)

    def mod_strip():
        parts = [moves.halves(v).reshape(clips, n_tp, -1) for v in mod_grads]
        parts = flip_to(jnp.stack(parts, axis=2), 1, n_tp, moves.tp)
        got = yield [swap_with(parts[:, r], "tp", n_tp, r) for r in range(1, n_tp)]
        strip = parts[:, 0] + sum(got)
        strip = yield from total_over_ctx(strip)
        got = yield swap_with(strip, "ctx", n_ctx, 1)
        strip = strip + got
        got = yield swap_with(strip, "dp", n_dp, 1)
        return jnp.concatenate([strip, got], axis=0)

    def fused_passes(v):
        vectors, saved = [], []
        for level in range(LAYERS):
            last = share if level == LAYERS - 1 else jnp.ones_like(share)
            last = jnp.broadcast_to(last[:, None, None], (clips, 2, width))
            vectors.append(jnp.concatenate([mods[level], last], axis=1))
        v = flat(v)
        for level in range(LAYERS):
            stride = piece if level % 2 else 1
            joined = gathers[3 * level].result
            kept = fused_branch(v, vectors[level], joined, clips, stride)
            normed, qkv, lse, result, branch, middle, normed_mlp = tick(kept)
            up = gathers[3 * level + 1].result
            act, slope = tick(fused_up(normed_mlp, vectors[level], up, clips))
            down = gathers[3 * level + 2].result
            branch_mlp, after = fused_down(act, middle, vectors[level], down, clips)
            saved.append((v, normed, qkv, lse, result, branch, middle, normed_mlp))
            saved[-1] += (act, slope, branch_mlp, joined, up, down, stride)
            v = after
            if level == 0:
                moved = lanes.start(frames_to_clips(shaped(v)))
                tick()
                late = tick(cotangent)
                turned = lanes.start(here_to_clips(moves.halves(late)))
                v = flat(moved.result)
        finished = lanes.start(clips_to_here(moves.halves(shaped(v))))
        grad = flat(turned.result)
        for level in reversed(range(LAYERS)):
            v, normed, qkv, lse, result, branch, middle, normed_mlp = saved[level][:8]
            act, slope, branch_mlp, joined, up, down, stride = saved[level][8:]
            back = fused_mlp_back(
                grad, vectors[level], branch_mlp, slope, middle, branch, up, down, clips
            )
            grad_branch, grad_pre, grad_middle, grad_out, sums = lanes.fence(back)
            start_scatter(level, "down", grad_branch, [act])
            late = tuple(scatters[level + 1, n] for n in ("qkv", "out")) if not level else (finished,)
            grad_out = lanes.fence(grad_out, late)
            if level == 0:
                start_scatter(level, "up", normed_mlp, [grad_pre])
                grad_out = lanes.fence(grad_out, (scatters[level, "down"],))
            back = fused_branch_back(
                v, vectors[level], grad_out, grad_middle, qkv, lse, joined, clips, stride
            )
            grad, more, *grad_qkv = lanes.fence(back, (scatters[level, "down"],) if level else ())
            mod_grads[level] = (sums + more)[:, :6]
            if level:
                moved = lanes.start(clips_to_frames(shaped(grad)))
                start_scatter(level, "up", normed_mlp, [grad_pre])
                lanes.fence((), (scatters[level, "down"],))
                start_scatter(level, "qkv", normed, grad_qkv)
                start_scatter(level, "out", grad_out, [result])
                lanes.fence()
                grad = flat(moved.result)
            else:
                start_scatter(level, "qkv", normed, grad_qkv)
                start_scatter(level, "out", grad_out, [result])
        return finished, shaped(grad)

    def plain_passes(residual):
        residual = residual.astype(F32)
        records = []
        for level in range(LAYERS):
            spatial = level % 2 == 0
            shift_a, scale_a, gate_a, shift_m, scale_m, gate_m = modulations(level)
            normed = flat(modulate(residual, shift_a, scale_a))
            qkvs, outs = attention_weights(3 * level)
            projected = [dot(normed, v).astype(BF16) for v in qkvs]
            rows, stride = (patches_here * spread_tp, 1) if spatial else (residual.shape[1], piece)
            if spatial and not whole_frames:
                saved = [attend_shared(v, clips * frames_here) for v in projected]
                result = jnp.concatenate([entry[0] for entry in saved], axis=1)
                saved = [entry[1] for entry in saved]
            else:
                result, saved = attend(projected, rows, stride)
            result, saved = tick((result, saved))
            branch = shaped(dot(result, outs, NT))
            middle = residual + gate_a[:, None] * branch
            normed_mlp = flat(modulate(middle, shift_m, scale_m))
            up = whole(3 * level + 1)
            pre_act = dot(normed_mlp, up)
            act = gelu(pre_act).astype(BF16)
            act, pre_act = tick((act, pre_act))
            down = whole(3 * level + 2)
            branch_mlp = shaped(dot(act, down, NT))
            records.append(
                (residual, normed, projected, saved, result, branch, middle, normed_mlp)
                + (pre_act, act, branch_mlp, qkvs, outs, up, down, rows, stride)
            )
            residual = middle + gate_m[:, None] * branch_mlp
            if spatial:
                moved = lanes.start(frames_to_clips(residual.astype(BF16)))
                tick()
                turned = lanes.start(here_to_clips(moves.halves(cotangent)))
                tick()
                residual = moved.result.astype(F32)
        gradient = turned.result.astype(F32) * share[:, None, None]
        finished = lanes.start(clips_to_here(moves.halves(residual.astype(BF16))))
        for level in reversed(range(LAYERS)):
            spatial = level % 2 == 0
            (residual, normed, projected, saved, result, branch, middle, normed_mlp) = records[level][
                :8
            ]
            (pre_act, act, branch_mlp, qkvs, outs, up, down, rows, stride) = records[level][8:]
            shift_a, scale_a, gate_a, shift_m, scale_m, gate_m = modulations(level)
            gate_m_grad = jnp.sum(gradient * branch_mlp, axis=1)
            low_grad = flat((gradient * gate_m[:, None]).astype(BF16))
            grad_pre = gelu_slope(pre_act, dot(low_grad, down)).astype(BF16)
            start_scatter(level, "down", low_grad, [act])
            grad_pre = lanes.fence(grad_pre)
            grad_normed = shaped(dot(grad_pre, up, NT))
            start_scatter(level, "up", normed_mlp, [grad_pre])
            grad_normed = lanes.fence(grad_normed)
            added, shift_m_grad, scale_m_grad = modulate_back(grad_normed, middle, scale_m)
            gradient = gradient + added
            gate_a_grad = jnp.sum(gradient * branch, axis=1)
            low_grad = flat((gradient * gate_a[:, None]).astype(BF16))
            grad_heads = dot(low_grad, outs).astype(BF16)
            start_scatter(level, "out", low_grad, [result])
            grad_heads = lanes.fence(grad_heads)
            if spatial and not whole_frames:
                grad_qkv = [
                    attend_shared_back(v, g)
                    for v, g in zip(saved, jnp.split(grad_heads, n_tp, axis=1))
                ]
            else:
                grad_qkv = attend_back(projected, grad_heads, saved, rows, stride)
            grad_qkv = lanes.fence(grad_qkv)
            start_scatter(level, "qkv", normed, grad_qkv)
            grad_normed = shaped(sum(dot(v, w, NT) for v, w in zip(grad_qkv, qkvs)))
            added, shift_a_grad, scale_a_grad = modulate_back(grad_normed, residual, scale_a)
            gradient = gradient + added
            mod_grads[level] = jnp.stack(
                [shift_a_grad, scale_a_grad, gate_a_grad, shift_m_grad, scale_m_grad, gate_m_grad],
                axis=1,
            )
            if not spatial:
                moved = lanes.start(clips_to_frames(gradient.astype(BF16)))
                lanes.fence()
                lanes.fence()
                gradient = moved.result.astype(F32)
        return finished, gradient

    passes = fused_passes if fused else plain_passes
    finished, gradient = passes(residual)
    grad_tokens = from_frames(moves.halves(gradient.astype(BF16))).astype(F32)
    lanes.fence()
    while lanes.tasks:
        lanes.fence(last=True)
    output = finished.result
    grads = [
        (
            scatters[level, "qkv"].result.reshape(rows_here, 3, head_cols).transpose(1, 0, 2),
            scatters[level, "out"].result.T,
            scatters[level, "up"].result,
            scatters[level, "down"].result.T,
        )
        for level in range(LAYERS)
    ]

    ada_grads = []
    cond_part = 0.0
    both = at_once(mod_strip())
    for level in range(LAYERS):
        strip = both[:, level]
        ada_grads.append(
            lax.dot_general(cond_rows.astype(F32), strip, TN, precision=HIGHEST)
        )
        cond_part = cond_part + lax.dot_general(
            strip, ada_low[level].astype(F32), NT, precision=HIGHEST
        )
    step = 1
    while step < n_tp:
        cond_part = cond_part + swap_with(cond_part, "tp", n_tp, step)
        step *= 2
    cond_grad = jnp.stack(
        [cond_part[:clips], swap_with(cond_part[clips:], "dp", n_dp, 1)], axis=1
    )[:, :, None]
    step = 1
    while step < n_ctx:
        cond_grad = jnp.concatenate(
            [cond_grad, swap_with(cond_grad, "ctx", n_ctx, step)], axis=2
        )
        step *= 2
    cond_grad = flip_to(cond_grad, 2, n_ctx, moves.ctx).reshape(clips, width)
    cond_grad = moves.halves(cond_grad)
    grad_condition = jax.vjp(jax.nn.silu, cond_full)[1](cond_grad)[0]

    stacked = [jnp.stack([grads[level][i] for level in range(LAYERS)]) for i in range(4)]
    return (output, grad_tokens, grad_condition, *stacked, jnp.stack(ada_grads))


def solution(mesh):
    placed = (
        P("dp", "ctx", "tp", None),
        P("dp", None),
        P("dp"),
        P(None, None, ("dp", "ctx"), "tp"),
        P(None, "tp", ("dp", "ctx")),
        P(None, ("dp", "ctx"), "tp"),
        P(None, "tp", ("dp", "ctx")),
        P(None, ("dp", "ctx"), "tp"),
        P("dp", "ctx", "tp", None),
    )
    return jax.shard_map(
        functools.partial(local, Moves(mesh)),
        mesh=mesh,
        in_specs=placed,
        out_specs=(
            P("dp", "ctx", "tp", None),
            P("dp", "ctx", "tp", None),
            P("dp", None),
            P(None, None, ("dp", "ctx"), "tp"),
            P(None, "tp", ("dp", "ctx")),
            P(None, ("dp", "ctx"), "tp"),
            P(None, "tp", ("dp", "ctx")),
            P(None, ("dp", "ctx"), "tp"),
        ),
        check_vma=False,
    )
```

```python
import functools

import jax
import jax.numpy as jnp
from jax import lax
from jax.experimental import pallas as pl
from jax.experimental.pallas import tpu as pltpu
from jax.sharding import PartitionSpec as P

HEAD_DIM = 72
LAYERS = 2
LANES = 128
EPS = 1e-06
SCALE = HEAD_DIM ** (-0.5)
HIGHEST = lax.Precision.HIGHEST
BF16 = jnp.bfloat16
F32 = jnp.float32

NN = (((1,), (0,)), ((), ()))
NT = (((1,), (1,)), ((), ()))
TN = (((0,), (0,)), ((), ()))


def dot(a, b, dims=NN):
    return lax.dot_general(a, b, dims, preferred_element_type=F32)


def swap_with(v, axis_name, n, k):
    return lax.ppermute(v, axis_name, [(i, i ^ k) for i in range(n)])


def flip_to(v, axis, n, me):
    shape = v.shape
    bit = 1
    while bit < n:
        split = shape[:axis] + (n // (2 * bit), 2, bit) + shape[axis + 1 :]
        parts = v.reshape(split)
        first = lax.slice_in_dim(parts, 0, 1, axis=axis + 1)
        second = lax.slice_in_dim(parts, 1, 2, axis=axis + 1)
        turned = jnp.concatenate([second, first], axis=axis + 1)
        v = jnp.where((me & bit) != 0, turned, parts).reshape(shape)
        bit *= 2
    return v


class Moves:
    def __init__(self, mesh):
        self.n_dp = mesh.shape["dp"]
        self.n_ctx = mesh.shape["ctx"]
        self.n_tp = mesh.shape["tp"]
        self.n_line = self.n_ctx // 2

    def here(self):
        self.dp = lax.axis_index("dp")
        self.ctx = lax.axis_index("ctx")
        self.tp = lax.axis_index("tp")
        self.line = self.ctx // 2
        self.side = self.ctx % 2

    def halves(self, v):
        half = v.shape[-1] // 2
        turned = jnp.concatenate([v[..., half:], v[..., :half]], axis=-1)
        return jnp.where(self.dp == 0, v, turned)

    def pair_stack(self, v, other):
        first = jnp.where(self.side == 0, v, other)
        second = jnp.where(self.side == 0, other, v)
        both = jnp.stack([first, second], axis=-3)
        return both.reshape(v.shape[:-3] + (-1, v.shape[-1]))

    def of_side(self, v, side):
        parts = v.reshape(self.n_line, 2, -1, v.shape[-1])
        return lax.dynamic_index_in_dim(parts, side, 1, keepdims=False)

    def over_tp(self, v, r):
        return swap_with(v, "tp", self.n_tp, r)

    def over_side(self, v):
        return swap_with(v, "ctx", self.n_ctx, 1)

    def over_core(self, v):
        return swap_with(v, "dp", self.n_dp, 1)

    def with_core(self, mine, layout):
        return layout, mine + [self.over_core(v) for v in mine]

    def line_gather(self, v):
        return [swap_with(v, "ctx", self.n_ctx, 2 * k) for k in range(1, self.n_line)]

    def line_stack(self, blocks):
        return flip_to(jnp.stack(blocks), 0, self.n_line, self.line)


    def gather_halves(self, v):
        others = range(1, self.n_tp)
        got = yield self.line_gather(v)
        half = v.shape[1] // 2
        lines = [
            self.line_stack([b[:, cut] for b in [v] + got])
            for cut in (slice(0, half), slice(half, None))
        ]
        got = self.over_side(lines[0]), [self.over_tp(lines[1], r) for r in others]
        side_got, tp_got = yield got
        block = self.pair_stack(lines[0], side_got)
        strips = jnp.stack([lines[1]] + tp_got)
        got = [self.over_tp(block, r) for r in others], self.over_side(strips)
        tp_got, side_got = yield got
        mine = [block] + tp_got + [self.pair_stack(strips, side_got)]
        layout = tuple(((r, None, half), (self.n_tp, r, half)) for r in range(self.n_tp))
        return self.with_core(mine, layout)

    def gather_rest(self, block):
        got = yield [self.over_tp(block, r) for r in range(1, self.n_tp)]
        layout = tuple(((r, None, block.shape[1]),) for r in range(self.n_tp))
        return self.with_core([block] + got, layout)

    def scatter_core(self, groups):
        halves = [(v[:, : v.shape[1] // 2], v[:, v.shape[1] // 2 :]) for v, _ in groups]
        got = yield [
            [self.over_core(dot(theirs, v, TN).astype(BF16)) for v in rights]
            for (_, theirs), (_, rights) in zip(halves, groups)
        ]
        found = []
        for (mine, _), (_, rights), came in zip(halves, groups, got):
            totals = [
                (dot(mine, v, TN) + g.astype(F32)).astype(BF16) for v, g in zip(rights, came)
            ]
            if len(totals) == 1:
                totals = jnp.split(totals[0], self.n_tp, axis=1)
            found.append(totals)
        return found

    def scatter_far(self, groups):
        found = yield from self.scatter_core(groups)
        totals = [
            jnp.concatenate([v[r] for v in found], axis=1) if len(found) > 1 else found[0][r]
            for r in range(self.n_tp)
        ]
        got = yield [self.over_tp(totals[r], r) for r in range(1, self.n_tp)]
        total = (totals[0].astype(F32) + sum(v.astype(F32) for v in got)).astype(BF16)
        shard = yield Rest(lax.psum_scatter(total, "ctx", scatter_dimension=0, tiled=True))
        return shard.astype(F32)

    def scatter_weight(self, groups):
        others = range(1, self.n_tp)
        found = yield from self.scatter_core(groups)
        sizes = [v[0].shape[1] for v in found]
        half = max(sum(sizes) // 2 // LANES, 1) * LANES
        firsts, seconds = [[] for _ in range(self.n_tp)], []
        for r in range(self.n_tp):
            low = 0
            for v, size in zip(found, sizes):
                cut = min(max(half - low, 0), size)
                if cut:
                    firsts[r].append(v[r][:, :cut])
                if cut < size:
                    seconds.append(v[r][:, cut:])
                low += size
        firsts = [jnp.concatenate(v, axis=1) if len(v) > 1 else v[0] for v in firsts]

        def of_side(side):
            return jnp.concatenate([self.of_side(v, side) for v in seconds], axis=-1)

        got = [self.over_tp(firsts[r], r) for r in others], self.over_side(of_side(1 - self.side))
        tp_got, side_got = yield got
        first = (firsts[0].astype(F32) + sum(v.astype(F32) for v in tp_got)).astype(BF16)
        second = of_side(self.side).astype(F32) + side_got.astype(F32)
        second = jnp.split(second.astype(BF16), self.n_tp, axis=-1)
        got = (
            self.over_side(self.of_side(first, 1 - self.side)),
            [self.over_tp(second[r], r) for r in others],
        )
        side_got, tp_got = yield got
        first = self.of_side(first, self.side).astype(F32) + side_got.astype(F32)
        second = second[0].astype(F32) + sum(v.astype(F32) for v in tp_got)
        line = jnp.concatenate([first, second], axis=-1).astype(BF16)
        got = yield [
            swap_with(
                lax.dynamic_index_in_dim(line, self.line ^ k, 0, keepdims=False),
                "ctx",
                self.n_ctx,
                2 * k,
            )
            for k in range(1, self.n_line)
        ]
        own = lax.dynamic_index_in_dim(line, self.line, 0, keepdims=False)
        return own.astype(F32) + sum(v.astype(F32) for v in got)


class Rest:
    def __init__(self, value):
        self.value = value


class Task:
    def __init__(self, steps):
        self.steps, self.result = steps, None
        self.take(next(steps))

    def take(self, pending):
        self.resting = isinstance(pending, Rest)
        self.pending = pending.value if self.resting else pending


def at_once(steps):
    pending = next(steps)
    while True:
        try:
            pending = steps.send(pending)
        except StopIteration as stop:
            return stop.value


class Lanes:
    def __init__(self):
        self.tasks = []

    def start(self, steps):
        task = Task(steps)
        self.tasks.append(task)
        return task

    def fence(self, values=(), but=(), last=False):
        due = [t for t in self.tasks if t not in but and (last or not t.resting)]
        values, pending = lax.optimization_barrier((values, [t.pending for t in due]))
        going = [t for t in self.tasks if t not in due]
        for task, done in zip(due, pending):
            try:
                task.take(task.steps.send(done))
                going.append(task)
            except StopIteration as stop:
                task.result = stop.value
        self.tasks = going
        return values


def window(head):
    start = head * HEAD_DIM
    return start // LANES * LANES, -(-(start + HEAD_DIM) // LANES) * LANES


def in_head(head, rows, low, high):
    lanes = lax.broadcasted_iota(jnp.int32, (rows, high - low), 1) + low
    return (lanes >= head * HEAD_DIM) & (lanes < (head + 1) * HEAD_DIM)


def spread_parts(x_ref, offset, parts, width):
    for index, part in enumerate(parts):
        padded = part.shape[1]
        start = offset + index * width
        if padded != width:
            part[:, padded - LANES :] = jnp.zeros((part.shape[0], LANES), part.dtype)
        part[:, :width] = x_ref[:, start : start + width]


def same_sequence(rows, stride):
    row = lax.broadcasted_iota(jnp.int32, (rows, rows), 0)
    column = lax.broadcasted_iota(jnp.int32, (rows, rows), 1)
    return lax.rem(row, stride) == lax.rem(column, stride)


def attend_kernel(count, width, stride, *refs):
    x_refs, (o_ref, lse_ref, q_s, k_s, v_s, o_s) = refs[:count], refs[count:]
    heads, rows = width // HEAD_DIM, o_ref.shape[0]
    lane = lax.broadcasted_iota(jnp.int32, (rows, LANES), 1)
    logs = jnp.zeros((rows, LANES), F32)
    if stride > 1:
        allowed = same_sequence(rows, stride)
    for index, x_ref in enumerate(x_refs):
        spread_parts(x_ref, 0, (q_s, k_s, v_s), width)
        for head in range(heads):
            low, high = window(head)
            mask = in_head(head, rows, low, high)
            queries = jnp.where(mask, q_s[:, low:high], jnp.zeros((), BF16))
            scores = dot(queries, k_s[:, low:high], NT) * SCALE
            if stride > 1:
                scores = jnp.where(allowed, scores, -jnp.inf)
            largest = jnp.max(scores, axis=-1, keepdims=True)
            raised = jnp.exp(scores - largest)
            total = jnp.sum(raised, axis=-1, keepdims=True)
            chances = (raised * (1.0 / total)).astype(BF16)
            result = dot(chances, v_s[:, low:high])
            o_s[:, low:high] = jnp.where(mask, result, o_s[:, low:high])
            logs = jnp.where(lane == index * heads + head, largest + jnp.log(total), logs)
        o_ref[:, index * width : (index + 1) * width] = o_s[:, :width].astype(BF16)
    lse_ref[...] = logs


def attend_back_kernel(count, width, stride, *refs):
    x_refs, (g_ref, lse_ref), dx_refs = refs[:count], refs[count : count + 2], refs[count + 2 : -7]
    q_s, k_s, v_s, g_s, dq_s, dk_s, dv_s = refs[-7:]
    heads, rows = width // HEAD_DIM, g_ref.shape[0]
    if stride > 1:
        allowed = same_sequence(rows, stride)
    for index, x_ref in enumerate(x_refs):
        spread_parts(x_ref, 0, (q_s, k_s, v_s), width)
        spread_parts(g_ref, index * width, (g_s,), width)
        for head in range(heads):
            low, high = window(head)
            mask = in_head(head, rows, low, high)
            zero = jnp.zeros((), BF16)
            q, k, v, g = q_s[:, low:high], k_s[:, low:high], v_s[:, low:high], g_s[:, low:high]
            scores = dot(jnp.where(mask, q, zero), k, NT) * SCALE
            if stride > 1:
                scores = jnp.where(allowed, scores, -jnp.inf)
            place = index * heads + head
            chances = jnp.exp(scores - lse_ref[:, place : place + 1])
            grad_chances = dot(jnp.where(mask, g, zero), v, NT)
            row_dot = jnp.sum(chances * grad_chances, axis=-1, keepdims=True)
            grad_scores = (chances * (grad_chances - row_dot)).astype(BF16)
            dq = dot(grad_scores, k) * SCALE
            dk = dot(grad_scores, q, TN) * SCALE
            dv = dot(chances.astype(BF16), g, TN)
            dq_s[:, low:high] = jnp.where(mask, dq, dq_s[:, low:high])
            dk_s[:, low:high] = jnp.where(mask, dk, dk_s[:, low:high])
            dv_s[:, low:high] = jnp.where(mask, dv, dv_s[:, low:high])
        for part_index, part in enumerate((dq_s, dk_s, dv_s)):
            start = part_index * width
            dx_refs[index][:, start : start + width] = part[:, :width].astype(BF16)


def row_block(rows, columns):
    return pl.BlockSpec((rows, columns), lambda i: (i, 0))


def attend(xs, rows, stride):
    count, width = xs[0].shape[0], xs[0].shape[1] // 3
    strips = len(xs)
    heads = strips * width // HEAD_DIM
    padded = -(-width // LANES) * LANES
    return pl.pallas_call(
        functools.partial(attend_kernel, strips, width, stride),
        grid=(count // rows,),
        in_specs=[row_block(rows, 3 * width)] * strips,
        out_specs=[row_block(rows, strips * width), row_block(rows, LANES)],
        out_shape=[
            jax.ShapeDtypeStruct((count, strips * width), BF16),
            jax.ShapeDtypeStruct((count, LANES), F32),
        ],
        scratch_shapes=[pltpu.VMEM((rows, padded), BF16)] * 3 + [pltpu.VMEM((rows, padded), F32)],
        cost_estimate=pl.CostEstimate(
            flops=heads * count * rows * 1024,
            bytes_accessed=count * width * strips * 8,
            transcendentals=heads * count * rows,
        ),
        compiler_params=pltpu.CompilerParams(vmem_limit_bytes=32 * 1024 * 1024),
    )(*xs)


def attend_back(xs, grad, lse, rows, stride):
    count, width = xs[0].shape[0], xs[0].shape[1] // 3
    strips = len(xs)
    heads = strips * width // HEAD_DIM
    padded = -(-width // LANES) * LANES
    return pl.pallas_call(
        functools.partial(attend_back_kernel, strips, width, stride),
        grid=(count // rows,),
        in_specs=[row_block(rows, 3 * width)] * strips
        + [row_block(rows, strips * width), row_block(rows, LANES)],
        out_specs=[row_block(rows, 3 * width)] * strips,
        out_shape=[jax.ShapeDtypeStruct((count, 3 * width), BF16)] * strips,
        scratch_shapes=[pltpu.VMEM((rows, padded), BF16)] * 4
        + [pltpu.VMEM((rows, padded), F32)] * 3,
        cost_estimate=pl.CostEstimate(
            flops=heads * count * rows * 2560,
            bytes_accessed=count * width * strips * 14,
            transcendentals=heads * count * rows,
        ),
        compiler_params=pltpu.CompilerParams(vmem_limit_bytes=32 * 1024 * 1024),
    )(*xs, grad, lse)


def weight_scratch(pieces):
    layout, arrays = pieces
    columns = sum(part[2] for strip in layout for part in strip)
    parts = max(len(strip) for strip in layout)
    return [
        pltpu.VMEM((2 * arrays[0].shape[-2], columns), BF16),
        pltpu.SemaphoreType.DMA((2, len(layout), parts)),
    ]


def weight_copies(layout, refs, w_s, sems):
    count = len(refs) // 2
    rows = w_s.shape[0] // 2
    copies = [[] for _ in layout]
    for group in range(2):
        low = 0
        for strip, parts in enumerate(layout):
            for part, (place, entry, columns) in enumerate(parts):
                source = refs[group * count + place]
                if entry is not None:
                    source = source.at[entry]
                target = w_s.at[pl.ds(group * rows, rows), pl.ds(low, columns)]
                low += columns
                copies[strip].append(
                    pltpu.make_async_copy(source, target, sems.at[group, strip, part])
                )
    return copies


def await_copies(copies):
    @pl.when(pl.program_id(0) == 0)
    def _():
        for copy in copies:
            copy.wait()


def turn_copies(copies, w_s, t_s):
    @pl.when(pl.program_id(0) == 0)
    def _():
        size = w_s.shape[1] // len(copies) // 2
        for strip, waits in enumerate(copies):
            for copy in waits:
                copy.wait()
            for low in (2 * strip * size, (2 * strip + 1) * size):
                t_s[low : low + size] = w_s[:, low : low + size].T


def begin_copies(*many):
    @pl.when(pl.program_id(0) == 0)
    def _():
        for copies in many:
            for strip in copies:
                for copy in strip:
                    copy.start()


def row_normal(v):
    centred = v - jnp.mean(v, axis=-1, keepdims=True)
    inverse = lax.rsqrt(jnp.mean(centred * centred, axis=-1, keepdims=True) + EPS)
    return centred * inverse, inverse


def row_back(grad, normed, inverse, scale):
    scaled = grad * (1.0 + scale)
    mean_one = jnp.mean(scaled, axis=-1, keepdims=True)
    mean_two = jnp.mean(scaled * normed, axis=-1, keepdims=True)
    return inverse * (scaled - mean_one - normed * mean_two)


def head_forward(heads, first, rows, allowed, q_s, k_s, v_s, o_s, lane, logs):
    for head in range(heads):
        low, high = window(head)
        mask = in_head(head, rows, low, high)
        queries = jnp.where(mask, q_s[:, low:high], jnp.zeros((), BF16))
        scores = dot(queries, k_s[:, low:high], NT) * SCALE
        if allowed is not None:
            scores = jnp.where(allowed, scores, -jnp.inf)
        largest = jnp.max(scores, axis=-1, keepdims=True)
        raised = jnp.exp(scores - largest)
        total = jnp.sum(raised, axis=-1, keepdims=True)
        chances = (raised * (1.0 / total)).astype(BF16)
        result = dot(chances, v_s[:, low:high])
        o_s[:, low:high] = jnp.where(mask, result, o_s[:, low:high])
        logs = jnp.where(lane == first + head, largest + jnp.log(total), logs)
    return logs


def head_back(heads, first, rows, allowed, q_s, k_s, v_s, g_s, lse_ref, dq_s, dk_s, dv_s):
    zero = jnp.zeros((), BF16)
    for head in range(heads):
        low, high = window(head)
        mask = in_head(head, rows, low, high)
        q, k, v, g = q_s[:, low:high], k_s[:, low:high], v_s[:, low:high], g_s[:, low:high]
        scores = dot(jnp.where(mask, q, zero), k, NT) * SCALE
        if allowed is not None:
            scores = jnp.where(allowed, scores, -jnp.inf)
        place = first + head
        chances = jnp.exp(scores - lse_ref[:, place : place + 1])
        grad_chances = dot(jnp.where(mask, g, zero), v, NT)
        row_dot = jnp.sum(chances * grad_chances, axis=-1, keepdims=True)
        grad_scores = (chances * (grad_chances - row_dot)).astype(BF16)
        dq = dot(grad_scores, k) * SCALE
        dk = dot(grad_scores, q, TN) * SCALE
        dv = dot(chances.astype(BF16), g, TN)
        dq_s[:, low:high] = jnp.where(mask, dq, dq_s[:, low:high])
        dk_s[:, low:high] = jnp.where(mask, dk, dk_s[:, low:high])
        dv_s[:, low:high] = jnp.where(mask, dv, dv_s[:, low:high])


def branch_kernel(layout, count, stride, x_ref, mod_ref, *refs):
    strips = len(layout)
    w_refs = refs[:count]
    h_ref, qkv_ref, lse_ref, o_ref, a_ref, y_ref, g_ref = refs[count : count + 7]
    w_s, sems, p_s, o_s, z_s = refs[count + 7 :]
    rows, width = x_ref.shape
    head_cols = width // strips
    padded = o_s.shape[1]
    spare = padded - head_cols
    columns = w_s.shape[1] // strips
    copies = weight_copies(layout, w_refs, w_s, sems)
    begin_copies(copies)
    x = x_ref[...].astype(F32)
    shift_a, scale_a, gate_a, shift_m, scale_m = [mod_ref[0, i : i + 1, :] for i in range(5)]
    h = (row_normal(x)[0] * (1.0 + scale_a) + shift_a).astype(BF16)
    h_ref[...] = h
    heads = head_cols // HEAD_DIM
    lane = lax.broadcasted_iota(jnp.int32, (rows, LANES), 1)
    logs = jnp.zeros((rows, LANES), F32)
    allowed = same_sequence(rows, stride) if stride > 1 else None
    branch = jnp.zeros((rows, width), F32)
    for strip in range(strips):
        start = strip * columns
        await_copies(copies[strip])
        p_s[...] = dot(h, w_s[:, start : start + p_s.shape[1]]).astype(BF16)
        parts = []
        for index in range(3):
            low = (3 * strip + index) * padded
            if spare:
                qkv_ref[:, low + padded - LANES : low + padded] = jnp.zeros((rows, LANES), BF16)
            qkv_ref[:, low : low + head_cols] = p_s[:, index * head_cols : (index + 1) * head_cols]
            parts.append(qkv_ref.at[:, pl.ds(low, padded)])
        logs = head_forward(heads, strip * heads, rows, allowed, *parts, o_s, lane, logs)
        low = o_s[:, :head_cols].astype(BF16)
        o_ref[:, strip * head_cols : (strip + 1) * head_cols] = low
        if spare:
            z_s[:, :LANES] = jnp.zeros((rows, LANES), BF16)
        z_s[:, spare:] = low
        branch = branch + dot(z_s[...], w_s[:, start + columns - padded : start + columns], NT)
    lse_ref[...] = logs
    a_ref[...] = branch.astype(BF16)
    y = x + gate_a * branch
    y_ref[...] = y
    g_ref[...] = (row_normal(y)[0] * (1.0 + scale_m) + shift_m).astype(BF16)


def branch_back_kernel(
    layout, count, stride, x_ref, mod_ref, da_ref, dy_ref, qkv_ref, lse_ref, *refs
):
    strips = len(layout)
    w_refs = refs[:count]
    dx_ref, sums_ref = refs[count : count + 2]
    out_refs = refs[count + 2 : count + 2 + strips]
    w_s, sems, d_s, g_s, dq_s, dk_s, dv_s = refs[count + 2 + strips :]
    rows, width = x_ref.shape
    head_cols = width // strips
    padded = g_s.shape[1]
    spare = padded - head_cols
    columns = w_s.shape[1] // strips
    copies = weight_copies(layout, w_refs, w_s, sems)
    begin_copies(copies)
    heads = head_cols // HEAD_DIM
    allowed = same_sequence(rows, stride) if stride > 1 else None
    grad = jnp.zeros((rows, width), F32)
    for strip in range(strips):
        start = strip * columns
        await_copies(copies[strip])
        turned = dot(da_ref[...], w_s[:, start + columns - padded : start + columns]).astype(BF16)
        if spare:
            g_s[:, padded - LANES :] = jnp.zeros((rows, LANES), BF16)
        g_s[:, :head_cols] = turned[:, spare:]
        parts = [qkv_ref.at[:, pl.ds((3 * strip + i) * padded, padded)] for i in range(3)]
        head_back(heads, strip * heads, rows, allowed, *parts, g_s, lse_ref, dq_s, dk_s, dv_s)
        if d_s.shape[1] != 3 * head_cols:
            d_s[:, d_s.shape[1] - LANES :] = jnp.zeros((rows, LANES), BF16)
        for index, part in enumerate((dq_s, dk_s, dv_s)):
            d_s[:, index * head_cols : (index + 1) * head_cols] = part[:, :head_cols].astype(BF16)
        out_refs[strip][...] = d_s[:, : 3 * head_cols]
        grad = grad + dot(d_s[...], w_s[:, start : start + d_s.shape[1]], NT)
    scale_a = mod_ref[0, 1:2, :]
    normed, inverse = row_normal(x_ref[...].astype(F32))
    sums_ref[...] = jnp.zeros(sums_ref.shape, F32)
    sums_ref[0, 0:1, :] = jnp.sum(grad, axis=0, keepdims=True)
    sums_ref[0, 1:2, :] = jnp.sum(grad * normed, axis=0, keepdims=True)
    dx_ref[...] = (dy_ref[...] + row_back(grad, normed, inverse, scale_a)).astype(BF16)


GELU_A = 0.7978845608028654
GELU_B = 0.044715


def up_kernel(layout, count, g_ref, *refs):
    strips = len(layout)
    z_ref, slope_ref, w_s, sems = refs[count:]
    copies = weight_copies(layout, refs[:count], w_s, sems)
    begin_copies(copies)
    half = w_s.shape[1] // (2 * strips)
    g = g_ref[...]
    for index in range(2 * strips):
        if index % 2 == 0:
            await_copies(copies[index // 2])
        low = index * half
        u = dot(g, w_s[:, low : low + half])
        square = u * u
        bent = jnp.tanh(u * (GELU_A + GELU_A * GELU_B * square))
        lifted = 0.5 * (1.0 + bent)
        z_ref[:, low : low + half] = (u * lifted).astype(BF16)
        inner = GELU_A + 3.0 * GELU_A * GELU_B * square
        slope = lifted + 0.5 * u * (1.0 - bent * bent) * inner
        slope_ref[:, low : low + half] = slope.astype(BF16)


def down_kernel(layout, count, z_ref, y_ref, mod_ref, *refs):
    strips = len(layout)
    m_ref, x_ref, w_s, sems, t_s = refs[count:]
    copies = weight_copies(layout, refs[:count], w_s, sems)
    begin_copies(copies)
    turn_copies(copies, w_s, t_s)
    total = dot(z_ref[...], t_s[...])
    m_ref[...] = total.astype(BF16)
    x_ref[...] = (y_ref[...] + mod_ref[0, 5:6, :] * total).astype(BF16)


def mlp_back_kernel(
    up_layout, ups_count, down_layout, count, dx_ref, mod_ref, m_ref, slope_ref, y_ref, a_ref, *refs
):
    strips = len(up_layout)
    (dm_ref, du_ref, dy_ref, da_ref, sums_ref, up_s, up_sems, down_s, down_sems, t_s) = refs[
        ups_count + count :
    ]
    ups = weight_copies(up_layout, refs[:ups_count], up_s, up_sems)
    downs = weight_copies(down_layout, refs[ups_count : ups_count + count], down_s, down_sems)
    begin_copies(downs, ups)
    half = up_s.shape[1] // (2 * strips)
    turn_copies(ups, up_s, t_s)
    scale_m, gate_m, share, gate_a = [mod_ref[0, i : i + 1, :] for i in (4, 5, 6, 2)]
    dx = dx_ref[...].astype(F32) * share
    sums_ref[...] = jnp.zeros(sums_ref.shape, F32)
    sums_ref[0, 5:6, :] = jnp.sum(dx * m_ref[...].astype(F32), axis=0, keepdims=True)
    dm = (gate_m * dx).astype(BF16)
    dm_ref[...] = dm
    grad = jnp.zeros(y_ref.shape, F32)
    for index in range(2 * strips):
        low = index * half
        if index % 2 == 0:
            await_copies(downs[index // 2])
        dz = dot(dm, down_s[:, low : low + half])
        du = (dz * slope_ref[:, low : low + half].astype(F32)).astype(BF16)
        du_ref[:, low : low + half] = du
        grad = grad + dot(du, t_s[low : low + half])
    normed, inverse = row_normal(y_ref[...])
    sums_ref[0, 3:4, :] = jnp.sum(grad, axis=0, keepdims=True)
    sums_ref[0, 4:5, :] = jnp.sum(grad * normed, axis=0, keepdims=True)
    dy = dx + row_back(grad, normed, inverse, scale_m)
    dy_ref[...] = dy
    sums_ref[0, 2:3, :] = jnp.sum(dy * a_ref[...].astype(F32), axis=0, keepdims=True)
    da_ref[...] = (gate_a * dy).astype(BF16)


def shape_of(*dims, dtype=BF16):
    return jax.ShapeDtypeStruct(dims, dtype)


def block_call(kernel, clips, rows, arrays, mods, weights, outs, sums, scratch, flops, order):
    operands, specs = [], []
    for v in order:
        if v is None:
            operands.append(mods)
            specs.append(pl.BlockSpec((1,) + mods.shape[1:], lambda i: (i, 0, 0)))
        else:
            operands.append(arrays[v])
            specs.append(row_block(rows, arrays[v].shape[1]))
    for _, pieces in weights:
        operands += pieces
        specs += [pl.BlockSpec(memory_space=pl.ANY)] * len(pieces)
    out_specs = [row_block(rows, v.shape[1]) for v in outs]
    out_shape = list(outs)
    if sums is not None:
        width = mods.shape[2]
        out_specs.insert(sums, pl.BlockSpec((1, 8, width), lambda i: (i, 0, 0)))
        out_shape.insert(sums, shape_of(clips, 8, width, dtype=F32))
    held = []
    for pieces in weights:
        held += weight_scratch(pieces)
    moved = sum(v.size * v.dtype.itemsize for v in operands)
    return pl.pallas_call(
        kernel,
        grid=(clips,),
        in_specs=specs,
        out_specs=out_specs,
        out_shape=out_shape,
        scratch_shapes=held + scratch,
        cost_estimate=pl.CostEstimate(flops=flops, bytes_accessed=moved, transcendentals=0),
        compiler_params=pltpu.CompilerParams(vmem_limit_bytes=60 * 1024 * 1024),
    )(*operands)


def padded_to(columns):
    return -(-columns // LANES) * LANES


def fused_branch(x, mods, pieces, clips, stride):
    count, width = x.shape
    rows, strips = count // clips, len(pieces[0])
    head_cols = width // strips
    padded = padded_to(head_cols)
    outs = [
        shape_of(count, width),
        shape_of(count, 3 * strips * padded),
        shape_of(count, LANES, dtype=F32),
        shape_of(count, width),
        shape_of(count, width),
        shape_of(count, width, dtype=F32),
        shape_of(count, width),
    ]
    scratch = [
        pltpu.VMEM((rows, padded_to(3 * head_cols)), BF16),
        pltpu.VMEM((rows, padded), F32),
        pltpu.VMEM((rows, padded), BF16),
    ]
    return block_call(
        functools.partial(branch_kernel, pieces[0], len(pieces[1]), stride),
        clips, rows, [x], mods, [pieces], outs, None, scratch,
        12 * count * width * width, [0, None],
    )


def fused_branch_back(x, mods, da, dy, qkv, lse, pieces, clips, stride):
    count, width = x.shape
    rows, strips = count // clips, len(pieces[0])
    head_cols = width // strips
    padded = padded_to(head_cols)
    outs = [shape_of(count, width)] + [shape_of(count, 3 * head_cols) for _ in range(strips)]
    scratch = [
        pltpu.VMEM((rows, padded_to(3 * head_cols)), BF16),
        pltpu.VMEM((rows, padded), BF16),
    ] + [pltpu.VMEM((rows, padded), F32)] * 3
    return block_call(
        functools.partial(branch_back_kernel, pieces[0], len(pieces[1]), stride),
        clips, rows, [x, da, dy, qkv, lse], mods, [pieces], outs, 1, scratch,
        16 * count * width * width, [0, None, 1, 2, 3, 4],
    )


def fused_up(g, mods, pieces, clips):
    count, width = g.shape
    rows, strips = count // clips, len(pieces[0])
    units = sum(part[2] for strip in pieces[0] for part in strip)
    outs = [shape_of(count, units), shape_of(count, units)]
    return block_call(
        functools.partial(up_kernel, pieces[0], len(pieces[1])),
        clips, rows, [g], mods, [pieces], outs, None, [], 2 * count * width * units, [0],
    )


def fused_down(z, y, mods, pieces, clips):
    count, width = y.shape
    rows, strips = count // clips, len(pieces[0])
    outs = [shape_of(count, width), shape_of(count, width)]
    return block_call(
        functools.partial(down_kernel, pieces[0], len(pieces[1])),
        clips, rows, [z, y], mods, [pieces], outs, None, [pltpu.VMEM((z.shape[1], width), BF16)],
        2 * z.size * width, [0, 1, None],
    )


def fused_mlp_back(dx, mods, m, slope, y, a, ups, downs, clips):
    count, width = y.shape
    rows = count // clips
    outs = [
        shape_of(count, width),
        shape_of(*slope.shape),
        shape_of(count, width, dtype=F32),
        shape_of(count, width),
    ]
    return block_call(
        functools.partial(mlp_back_kernel, ups[0], len(ups[1]), downs[0], len(downs[1])),
        clips, rows, [dx, m, slope, y, a], mods, [ups, downs], outs, 4,
        [pltpu.VMEM((slope.shape[1], width), BF16)],
        4 * slope.size * width, [0, None, 1, 2, 3, 4],
    )


def split_frames(v, frames, width):
    return v.reshape(frames, -1, width // HEAD_DIM, HEAD_DIM)


def attend_shared(x, frames):
    width = x.shape[1] // 3
    shaped = x.reshape(frames, -1, 3, width)
    pairs = lax.all_gather(shaped[:, :, 1:], "tp", axis=1, tiled=True)
    q = split_frames(shaped[:, :, 0], frames, width)
    k = split_frames(pairs[:, :, 0], frames, width)
    v = split_frames(pairs[:, :, 1], frames, width)
    scores = jnp.einsum("bqhe,bkhe->bhqk", q, k, preferred_element_type=F32) * SCALE
    chances = jax.nn.softmax(scores, axis=-1)
    result = jnp.einsum("bhqk,bkhe->bqhe", chances.astype(BF16), v, preferred_element_type=F32)
    return result.reshape(-1, width).astype(BF16), (q, k, v, chances)


def attend_shared_back(saved, grad):
    q, k, v, chances = saved
    frames, width = q.shape[0], grad.shape[1]
    grad = split_frames(grad, frames, width)
    grad_chances = jnp.einsum("bqhe,bkhe->bhqk", grad, v, preferred_element_type=F32)
    row_dot = jnp.sum(chances * grad_chances, axis=-1, keepdims=True)
    grad_scores = (chances * (grad_chances - row_dot)).astype(BF16)
    dq = jnp.einsum("bhqk,bkhe->bqhe", grad_scores, k, preferred_element_type=F32) * SCALE
    dk = jnp.einsum("bhqk,bqhe->bkhe", grad_scores, q, preferred_element_type=F32) * SCALE
    dv = jnp.einsum("bhqk,bqhe->bkhe", chances.astype(BF16), grad, preferred_element_type=F32)
    sums = lax.psum_scatter(jnp.stack([dk, dv], axis=2), "tp", scatter_dimension=1, tiled=True)
    parts = jnp.concatenate([dq[:, :, None], sums], axis=2)
    return parts.reshape(-1, 3 * width).astype(BF16)


def normalise(v):
    centred = v - jnp.mean(v, axis=-1, keepdims=True)
    inverse = lax.rsqrt(jnp.mean(centred * centred, axis=-1, keepdims=True) + EPS)
    return centred * inverse, inverse


def modulate(v, shift, scale):
    return (normalise(v)[0] * (1.0 + scale[:, None]) + shift[:, None]).astype(BF16)


def modulate_back(grad, v, scale):
    normed, inverse = normalise(v)
    shift_grad = jnp.sum(grad, axis=1)
    scale_grad = jnp.sum(grad * normed, axis=1)
    scaled = grad * (1.0 + scale[:, None])
    mean_one = jnp.mean(scaled, axis=-1, keepdims=True)
    mean_two = jnp.mean(scaled * normed, axis=-1, keepdims=True)
    return inverse * (scaled - mean_one - normed * mean_two), shift_grad, scale_grad


def gelu(v):
    return jax.nn.gelu(v, approximate=True)


def gelu_slope(v, grad):
    return jax.vjp(gelu, v)[1](grad)[0]


def local(moves, tokens, condition, micro_ids, w_qkv, w_out, w_up, w_down, w_ada, cotangent):
    moves.here()
    n_dp, n_ctx, n_tp = moves.n_dp, moves.n_ctx, moves.n_tp
    clips, frames_here, patches_here, width = tokens.shape
    rows_here, head_cols = w_qkv.shape[2:]
    whole_frames = frames_here % n_tp == 0
    spread_tp = n_tp if whole_frames else 1
    groups = frames_here // spread_tp
    piece = patches_here // n_ctx

    cond_full = condition.astype(F32)
    cond_low = jax.nn.silu(cond_full).astype(BF16)
    cond_all = jnp.concatenate([cond_low, swap_with(cond_low, "dp", n_dp, 1)], axis=0)
    first_row = (moves.dp * n_ctx + moves.ctx) * rows_here
    cond_rows = lax.dynamic_slice_in_dim(cond_all, first_row, rows_here, axis=1)
    ada_low = w_ada.astype(BF16)
    shares = jnp.stack([dot(cond_rows, ada_low[level]) for level in range(LAYERS)], axis=1)

    def total_over_ctx(v):
        got = yield [swap_with(v, "ctx", n_ctx, 2 * k) for k in range(1, n_ctx // 2)]
        return v + sum(got)

    def modulation_vectors():
        sums = shares[:clips] + swap_with(shares[clips:], "dp", n_dp, 1)
        sums = yield sums
        sums = yield from total_over_ctx(sums)
        pairs = [
            [(c * n_tp + t, (c ^ dx) * n_tp + (t ^ r)) for c in range(n_ctx) for t in range(n_tp)]
            for r in range(n_tp)
            for dx in range(2)
        ]
        got = yield [lax.ppermute(sums, ("ctx", "tp"), entry) for entry in pairs[1:]]
        got = [sums] + got
        strips = [got[2 * r] + got[2 * r + 1] for r in range(n_tp)]
        strips = flip_to(jnp.stack(strips, axis=2), 2, n_tp, moves.tp)
        found = strips.reshape(clips, LAYERS, 6, width)
        return [moves.halves(found[:, level]) for level in range(LAYERS)]

    def to_frames(v):
        v = v.reshape(clips, frames_here, n_ctx, piece, width)
        v = flip_to(v, 2, n_ctx, moves.ctx)
        if spread_tp == 1:
            yield ()
            return v.reshape(clips, groups * patches_here, width)
        v = v.reshape(clips, spread_tp, groups, patches_here, width)
        v = flip_to(v, 1, spread_tp, moves.tp)
        got = yield [swap_with(v[:, r], "tp", n_tp, r) for r in range(1, spread_tp)]
        return jnp.stack([v[:, 0]] + got, axis=2).reshape(clips, -1, width)

    def from_frames(v):
        got = ()
        if spread_tp > 1:
            v = v.reshape(clips, groups, spread_tp, patches_here, width)
            got = [swap_with(v[:, :, r], "tp", n_tp, r) for r in range(1, spread_tp)]
        got = yield got
        if spread_tp > 1:
            v = flip_to(jnp.stack([v[:, :, 0]] + got, axis=1), 1, spread_tp, moves.tp)
        v = v.reshape(clips, frames_here, n_ctx, piece, width)
        v = flip_to(v, 2, n_ctx, moves.ctx)
        return v.reshape(clips, frames_here, patches_here, width)

    def trade(get, planes):
        sides = []
        for dx, dr in planes:
            block = get(dx, dr)
            if dx or dr:
                pairs = [
                    (c * n_tp + t, (c ^ dx) * n_tp + (t ^ dr))
                    for c in range(n_ctx)
                    for t in range(n_tp)
                ]
                block = lax.ppermute(block, ("ctx", "tp"), pairs)
            sides.append(block)
        sides = sides[:1] + (yield sides[1:])
        lines = [jnp.stack([v[:, dz] for v in sides], axis=1) for dz in range(n_ctx // 2)]
        got = yield [swap_with(v, "ctx", n_ctx, 2 * dz) for dz, v in enumerate(lines) if dz]
        return jnp.stack(lines[:1] + got, axis=1)

    all_planes = [(dx, dr) for dx in range(2) for dr in range(spread_tp)]
    own_planes = [(0, 0), (1, 0)]

    def frames_to_clips(v):
        v = v.reshape(clips, groups, spread_tp, n_ctx // 2, 2, piece, width)
        got = yield from trade(lambda dx, dr: v[:, :, dr, :, dx].swapaxes(1, 2), all_planes)
        return got.reshape(clips, -1, width)

    def clips_to_frames(v):
        v = v.reshape(clips, n_ctx // 2, 2, spread_tp, groups, piece, width)
        got = yield from trade(lambda dx, dr: v[:, :, dx, dr], all_planes)
        got = got.reshape(clips, n_ctx, spread_tp, groups, piece, width)
        return got.transpose(0, 3, 2, 1, 4, 5).reshape(clips, -1, width)

    def here_to_clips(v):
        v = v.reshape(clips, spread_tp, groups, n_ctx, piece, width)
        v = flip_to(flip_to(v, 3, n_ctx, moves.ctx), 1, spread_tp, moves.tp % spread_tp)
        v = v.reshape(clips, spread_tp, groups, n_ctx // 2, 2, piece, width)
        got = yield from trade(lambda dx, dr: v[:, :, :, :, dx].transpose(0, 3, 1, 2, 4, 5), own_planes)
        return got.reshape(clips, -1, width)

    def clips_to_here(v):
        v = v.reshape(clips, n_ctx // 2, 2, spread_tp, groups, piece, width)
        got = yield from trade(lambda dx, dr: v[:, :, dx], own_planes)
        v = got.reshape(clips, n_ctx, spread_tp, groups, piece, width).transpose(0, 2, 3, 1, 4, 5)
        v = flip_to(flip_to(v, 3, n_ctx, moves.ctx), 1, spread_tp, moves.tp % spread_tp)
        return v.reshape(clips, frames_here, patches_here, width)

    def flat(v):
        return v.reshape(-1, v.shape[-1])

    def shaped(v):
        return v.reshape(clips, -1, v.shape[-1])

    shards = []
    for level in range(LAYERS):
        attention = [w_qkv[level, 0], w_qkv[level, 1], w_qkv[level, 2], w_out[level].T]
        shards.append(jnp.concatenate(attention, axis=1).astype(BF16))
        shards.append(w_up[level].astype(BF16))
        shards.append(w_down[level].T.astype(BF16))
    lanes = Lanes()
    gathers = {}

    blocks = {}

    def gather_far(index):
        blocks[index] = lax.all_gather(shards[index], "ctx", axis=0, tiled=True)

    def set_out(index):
        if index in blocks:
            steps = moves.gather_rest(blocks[index])
        else:
            steps = moves.gather_halves(shards[index])
        gathers[index] = lanes.start(steps)

    plan = [
        ((2,), (), ()),
        ((), (2,), ()),
        ((1,), (), ()),
        ((4,), (), (5,)),
        ((3,), (), ()),
        ((), (3, 4), ()),
        ((5,), (), ()),
        ((), (5,), ()),
        ((), (), ()),
    ]

    def tick(values=(), waiting=()):
        out, but, far = plan.pop(0)
        held = {index: blocks.get(index, shards[index]) for index in out + far}
        held, values = lanes.fence((held, values), [gathers[index] for index in but] + list(waiting))
        for index in out + far:
            if index in blocks:
                blocks[index] = held[index]
            else:
                shards[index] = held[index]
        for index in far:
            gather_far(index)
        for index in out:
            set_out(index)
        return values

    def whole(index):
        layout, arrays = gathers[index].result
        count = len(arrays) // 2
        groups = []
        for group in (arrays[:count], arrays[count:]):
            parts = [
                group[place] if entry is None else group[place][entry]
                for strip in layout
                for place, entry, _ in strip
            ]
            groups.append(jnp.concatenate(parts, axis=1))
        return jnp.concatenate(groups, axis=0)

    def attention_weights(index):
        v = whole(index)
        strips = jnp.split(v, n_tp, axis=1)
        cut = 3 * head_cols
        return [w[:, :cut] for w in strips], jnp.concatenate([w[:, cut:] for w in strips], axis=1)

    def modulations(level):
        return [mods[level][:, i] for i in range(6)]

    gather_far(1)
    gather_far(3)
    set_out(0)
    moved = lanes.start(to_frames(moves.halves(tokens)))
    vectors_task = lanes.start(modulation_vectors())
    tick()
    residual = moved.result
    tick()
    tick()
    mods = vectors_task.result
    fused = (
        whole_frames
        and head_cols % 32 == 0
        and w_up.shape[2] % (2 * LANES) == 0
        and 4 * head_cols == w_up.shape[2]
        and width % 32 == 0
    )
    matched = (micro_ids[:, None] == micro_ids[None, :]).astype(F32)
    share = 1.0 / jnp.sum(matched, axis=1)
    scatters = {}
    mod_grads = [None] * LAYERS

    def start_scatter(level, names, *groups):
        steps = (moves.scatter_far if level else moves.scatter_weight)(groups)
        scatters[level, names] = lanes.start(steps)
        return scatters[level, names]

    def scattered(level, name):
        for (at, names), task in scatters.items():
            if at == level and name in names:
                columns = {"qkv": 3 * head_cols, "out": head_cols}
                units = w_up.shape[2]
                low = sum(columns.get(n, units) for n in names[: names.index(name)])
                return task.result[:, low : low + columns.get(name, units)]

    def mod_strip():
        parts = [moves.halves(v).reshape(clips, n_tp, -1) for v in mod_grads]
        parts = flip_to(jnp.stack(parts, axis=2), 1, n_tp, moves.tp)
        got = yield [swap_with(parts[:, r], "tp", n_tp, r) for r in range(1, n_tp)]
        strip = parts[:, 0] + sum(got)
        strip = yield from total_over_ctx(strip)
        got = yield swap_with(strip, "ctx", n_ctx, 1)
        strip = strip + got
        got = yield swap_with(strip, "dp", n_dp, 1)
        return jnp.concatenate([strip, got], axis=0)

    def fused_passes(v):
        vectors, saved = [], []
        for level in range(LAYERS):
            last = share if level == LAYERS - 1 else jnp.ones_like(share)
            last = jnp.broadcast_to(last[:, None, None], (clips, 2, width))
            vectors.append(jnp.concatenate([mods[level], last], axis=1))
        v = flat(v)
        for level in range(LAYERS):
            stride = piece if level % 2 else 1
            joined = gathers[3 * level].result
            kept = fused_branch(v, vectors[level], joined, clips, stride)
            normed, qkv, lse, result, branch, middle, normed_mlp = tick(kept)
            up = gathers[3 * level + 1].result
            waiting = (turned,) if level else ()
            act, slope = tick(fused_up(normed_mlp, vectors[level], up, clips), waiting)
            down = gathers[3 * level + 2].result
            branch_mlp, after = fused_down(act, middle, vectors[level], down, clips)
            saved.append((v, normed, qkv, lse, result, branch, middle, normed_mlp))
            saved[-1] += (act, slope, branch_mlp, joined, up, down, stride)
            v = after
            if level == 0:
                moved = lanes.start(frames_to_clips(shaped(v)))
                tick()
                late = tick(cotangent)
                turned = lanes.start(here_to_clips(moves.halves(late)))
                v = flat(moved.result)
        v = lanes.fence(v)
        finished = lanes.start(clips_to_here(moves.halves(shaped(v))))
        grad = flat(turned.result)
        for level in reversed(range(LAYERS)):
            v, normed, qkv, lse, result, branch, middle, normed_mlp = saved[level][:8]
            act, slope, branch_mlp, joined, up, down, stride = saved[level][8:]
            back = fused_mlp_back(
                grad, vectors[level], branch_mlp, slope, middle, branch, up, down, clips
            )
            grad_branch, grad_pre, grad_middle, grad_out, sums = lanes.fence(back)
            if level:
                waiting = start_scatter(level, ("down",), (grad_branch, [act]))
                grad_out = lanes.fence(grad_out, (finished,))
            else:
                start_scatter(
                    level, ("down", "up"), (grad_branch, [act]), (normed_mlp, [grad_pre])
                )
                grad_out = lanes.fence(grad_out, (scatters[1, ("qkv", "out")],))
            back = fused_branch_back(
                v, vectors[level], grad_out, grad_middle, qkv, lse, joined, clips, stride
            )
            grad, more, *grad_qkv = lanes.fence(back, (waiting,) if level else ())
            mod_grads[level] = (sums + more)[:, :6]
            joint = (normed, grad_qkv), (grad_out, [result])
            if level:
                moved = lanes.start(clips_to_frames(shaped(grad)))
                task = start_scatter(level, ("up",), (normed_mlp, [grad_pre]))
                lanes.fence((), (waiting,))
                start_scatter(level, ("qkv", "out"), *joint)
                lanes.fence((), (task,))
                grad = flat(moved.result)
            else:
                start_scatter(level, ("qkv", "out"), *joint)
        return finished, shaped(grad)

    def plain_passes(residual):
        residual = residual.astype(F32)
        records = []
        for level in range(LAYERS):
            spatial = level % 2 == 0
            shift_a, scale_a, gate_a, shift_m, scale_m, gate_m = modulations(level)
            normed = flat(modulate(residual, shift_a, scale_a))
            qkvs, outs = attention_weights(3 * level)
            projected = [dot(normed, v).astype(BF16) for v in qkvs]
            rows, stride = (patches_here * spread_tp, 1) if spatial else (residual.shape[1], piece)
            if spatial and not whole_frames:
                saved = [attend_shared(v, clips * frames_here) for v in projected]
                result = jnp.concatenate([entry[0] for entry in saved], axis=1)
                saved = [entry[1] for entry in saved]
            else:
                result, saved = attend(projected, rows, stride)
            result, saved = tick((result, saved))
            branch = shaped(dot(result, outs, NT))
            middle = residual + gate_a[:, None] * branch
            normed_mlp = flat(modulate(middle, shift_m, scale_m))
            up = whole(3 * level + 1)
            pre_act = dot(normed_mlp, up)
            act = gelu(pre_act).astype(BF16)
            act, pre_act = tick((act, pre_act))
            down = whole(3 * level + 2)
            branch_mlp = shaped(dot(act, down, NT))
            records.append(
                (residual, normed, projected, saved, result, branch, middle, normed_mlp)
                + (pre_act, act, branch_mlp, qkvs, outs, up, down, rows, stride)
            )
            residual = middle + gate_m[:, None] * branch_mlp
            if spatial:
                moved = lanes.start(frames_to_clips(residual.astype(BF16)))
                tick()
                turned = lanes.start(here_to_clips(moves.halves(cotangent)))
                tick()
                residual = moved.result.astype(F32)
        gradient = turned.result.astype(F32) * share[:, None, None]
        finished = lanes.start(clips_to_here(moves.halves(residual.astype(BF16))))
        for level in reversed(range(LAYERS)):
            spatial = level % 2 == 0
            (residual, normed, projected, saved, result, branch, middle, normed_mlp) = records[level][
                :8
            ]
            (pre_act, act, branch_mlp, qkvs, outs, up, down, rows, stride) = records[level][8:]
            shift_a, scale_a, gate_a, shift_m, scale_m, gate_m = modulations(level)
            gate_m_grad = jnp.sum(gradient * branch_mlp, axis=1)
            low_grad = flat((gradient * gate_m[:, None]).astype(BF16))
            grad_pre = gelu_slope(pre_act, dot(low_grad, down)).astype(BF16)
            start_scatter(level, ("down",), (low_grad, [act]))
            grad_pre = lanes.fence(grad_pre)
            grad_normed = shaped(dot(grad_pre, up, NT))
            start_scatter(level, ("up",), (normed_mlp, [grad_pre]))
            grad_normed = lanes.fence(grad_normed)
            added, shift_m_grad, scale_m_grad = modulate_back(grad_normed, middle, scale_m)
            gradient = gradient + added
            gate_a_grad = jnp.sum(gradient * branch, axis=1)
            low_grad = flat((gradient * gate_a[:, None]).astype(BF16))
            grad_heads = dot(low_grad, outs).astype(BF16)
            start_scatter(level, ("out",), (low_grad, [result]))
            grad_heads = lanes.fence(grad_heads)
            if spatial and not whole_frames:
                grad_qkv = [
                    attend_shared_back(v, g)
                    for v, g in zip(saved, jnp.split(grad_heads, n_tp, axis=1))
                ]
            else:
                grad_qkv = attend_back(projected, grad_heads, saved, rows, stride)
            grad_qkv = lanes.fence(grad_qkv)
            start_scatter(level, ("qkv",), (normed, grad_qkv))
            grad_normed = shaped(sum(dot(v, w, NT) for v, w in zip(grad_qkv, qkvs)))
            added, shift_a_grad, scale_a_grad = modulate_back(grad_normed, residual, scale_a)
            gradient = gradient + added
            mod_grads[level] = jnp.stack(
                [shift_a_grad, scale_a_grad, gate_a_grad, shift_m_grad, scale_m_grad, gate_m_grad],
                axis=1,
            )
            if not spatial:
                moved = lanes.start(clips_to_frames(gradient.astype(BF16)))
                lanes.fence()
                lanes.fence()
                gradient = moved.result.astype(F32)
        return finished, gradient

    passes = fused_passes if fused else plain_passes
    finished, gradient = passes(residual)
    mod_grads, gradient = lanes.fence((mod_grads, gradient))
    hanging = [scatters[key] for key in scatters if key == (0, ("down", "up"))]
    both = at_once(mod_strip())
    lanes.fence((), hanging)
    lanes.fence()
    moved = lanes.start(from_frames(moves.halves(gradient.astype(BF16))))
    while lanes.tasks:
        lanes.fence(last=True)
    grad_tokens = moved.result.astype(F32)
    output = finished.result
    grads = [
        (
            scattered(level, "qkv").reshape(rows_here, 3, head_cols).transpose(1, 0, 2),
            scattered(level, "out").T,
            scattered(level, "up"),
            scattered(level, "down").T,
        )
        for level in range(LAYERS)
    ]

    ada_grads = []
    cond_part = 0.0
    for level in range(LAYERS):
        strip = both[:, level]
        ada_grads.append(
            lax.dot_general(cond_rows.astype(F32), strip, TN, precision=HIGHEST)
        )
        cond_part = cond_part + lax.dot_general(
            strip, ada_low[level].astype(F32), NT, precision=HIGHEST
        )
    step = 1
    while step < n_tp:
        cond_part = cond_part + swap_with(cond_part, "tp", n_tp, step)
        step *= 2
    cond_grad = jnp.stack(
        [cond_part[:clips], swap_with(cond_part[clips:], "dp", n_dp, 1)], axis=1
    )[:, :, None]
    step = 1
    while step < n_ctx:
        cond_grad = jnp.concatenate(
            [cond_grad, swap_with(cond_grad, "ctx", n_ctx, step)], axis=2
        )
        step *= 2
    cond_grad = flip_to(cond_grad, 2, n_ctx, moves.ctx).reshape(clips, width)
    cond_grad = moves.halves(cond_grad)
    grad_condition = jax.vjp(jax.nn.silu, cond_full)[1](cond_grad)[0]

    stacked = [jnp.stack([grads[level][i] for level in range(LAYERS)]) for i in range(4)]
    return (output, grad_tokens, grad_condition, *stacked, jnp.stack(ada_grads))


def solution(mesh):
    placed = (
        P("dp", "ctx", "tp", None),
        P("dp", None),
        P("dp"),
        P(None, None, ("dp", "ctx"), "tp"),
        P(None, "tp", ("dp", "ctx")),
        P(None, ("dp", "ctx"), "tp"),
        P(None, "tp", ("dp", "ctx")),
        P(None, ("dp", "ctx"), "tp"),
        P("dp", "ctx", "tp", None),
    )
    return jax.shard_map(
        functools.partial(local, Moves(mesh)),
        mesh=mesh,
        in_specs=placed,
        out_specs=(
            P("dp", "ctx", "tp", None),
            P("dp", "ctx", "tp", None),
            P("dp", None),
            P(None, None, ("dp", "ctx"), "tp"),
            P(None, "tp", ("dp", "ctx")),
            P(None, ("dp", "ctx"), "tp"),
            P(None, "tp", ("dp", "ctx")),
            P(None, ("dp", "ctx"), "tp"),
        ),
        check_vma=False,
    )
```

```python
import functools

import jax
import jax.numpy as jnp
from jax import lax
from jax.experimental import pallas as pl
from jax.experimental.pallas import tpu as pltpu
from jax.sharding import PartitionSpec as P

HEAD_DIM = 72
LAYERS = 2
LANES = 128
EPS = 1e-06
SCALE = HEAD_DIM ** (-0.5)
HIGHEST = lax.Precision.HIGHEST
BF16 = jnp.bfloat16
F32 = jnp.float32

NN = (((1,), (0,)), ((), ()))
NT = (((1,), (1,)), ((), ()))
TN = (((0,), (0,)), ((), ()))


def dot(a, b, dims=NN):
    return lax.dot_general(a, b, dims, preferred_element_type=F32)


def swap_with(v, axis_name, n, k):
    return lax.ppermute(v, axis_name, [(i, i ^ k) for i in range(n)])


def flip_to(v, axis, n, me):
    shape = v.shape
    bit = 1
    while bit < n:
        split = shape[:axis] + (n // (2 * bit), 2, bit) + shape[axis + 1 :]
        parts = v.reshape(split)
        first = lax.slice_in_dim(parts, 0, 1, axis=axis + 1)
        second = lax.slice_in_dim(parts, 1, 2, axis=axis + 1)
        turned = jnp.concatenate([second, first], axis=axis + 1)
        v = jnp.where((me & bit) != 0, turned, parts).reshape(shape)
        bit *= 2
    return v


class Moves:
    def __init__(self, mesh):
        self.n_dp = mesh.shape["dp"]
        self.n_ctx = mesh.shape["ctx"]
        self.n_tp = mesh.shape["tp"]
        self.n_line = self.n_ctx // 2

    def here(self):
        self.dp = lax.axis_index("dp")
        self.ctx = lax.axis_index("ctx")
        self.tp = lax.axis_index("tp")
        self.line = self.ctx // 2
        self.side = self.ctx % 2

    def halves(self, v):
        half = v.shape[-1] // 2
        turned = jnp.concatenate([v[..., half:], v[..., :half]], axis=-1)
        return jnp.where(self.dp == 0, v, turned)

    def pair_stack(self, v, other):
        first = jnp.where(self.side == 0, v, other)
        second = jnp.where(self.side == 0, other, v)
        both = jnp.stack([first, second], axis=-3)
        return both.reshape(v.shape[:-3] + (-1, v.shape[-1]))

    def of_side(self, v, side):
        parts = v.reshape(self.n_line, 2, -1, v.shape[-1])
        return lax.dynamic_index_in_dim(parts, side, 1, keepdims=False)

    def over_tp(self, v, r):
        return swap_with(v, "tp", self.n_tp, r)

    def over_side(self, v):
        return swap_with(v, "ctx", self.n_ctx, 1)

    def over_core(self, v):
        return swap_with(v, "dp", self.n_dp, 1)

    def with_core(self, mine, layout):
        return layout, mine + [self.over_core(v) for v in mine]

    def line_gather(self, v):
        return [swap_with(v, "ctx", self.n_ctx, 2 * k) for k in range(1, self.n_line)]

    def line_stack(self, blocks):
        return flip_to(jnp.stack(blocks), 0, self.n_line, self.line)


    def gather_halves(self, v):
        others = range(1, self.n_tp)
        got = yield self.line_gather(v)
        half = v.shape[1] // 2
        lines = [
            self.line_stack([b[:, cut] for b in [v] + got])
            for cut in (slice(0, half), slice(half, None))
        ]
        got = self.over_side(lines[0]), [self.over_tp(lines[1], r) for r in others]
        side_got, tp_got = yield got
        block = self.pair_stack(lines[0], side_got)
        strips = jnp.stack([lines[1]] + tp_got)
        got = [self.over_tp(block, r) for r in others], self.over_side(strips)
        tp_got, side_got = yield got
        mine = [block] + tp_got + [self.pair_stack(strips, side_got)]
        layout = tuple(((r, None, half), (self.n_tp, r, half)) for r in range(self.n_tp))
        return self.with_core(mine, layout)

    def gather_rest(self, block):
        got = yield [self.over_tp(block, r) for r in range(1, self.n_tp)]
        layout = tuple(((r, None, block.shape[1]),) for r in range(self.n_tp))
        return self.with_core([block] + got, layout)

    def scatter_core(self, groups):
        halves = [(v[:, : v.shape[1] // 2], v[:, v.shape[1] // 2 :]) for v, _ in groups]
        got = yield [
            [self.over_core(dot(theirs, v, TN).astype(BF16)) for v in rights]
            for (_, theirs), (_, rights) in zip(halves, groups)
        ]
        found = []
        for (mine, _), (_, rights), came in zip(halves, groups, got):
            totals = [
                (dot(mine, v, TN) + g.astype(F32)).astype(BF16) for v, g in zip(rights, came)
            ]
            if len(totals) == 1:
                totals = jnp.split(totals[0], self.n_tp, axis=1)
            found.append(totals)
        return found

    def scatter_far(self, groups):
        found = yield from self.scatter_core(groups)
        totals = [
            jnp.concatenate([v[r] for v in found], axis=1) if len(found) > 1 else found[0][r]
            for r in range(self.n_tp)
        ]
        got = yield [self.over_tp(totals[r], r) for r in range(1, self.n_tp)]
        total = (totals[0].astype(F32) + sum(v.astype(F32) for v in got)).astype(BF16)
        shard = yield Rest(lax.psum_scatter(total, "ctx", scatter_dimension=0, tiled=True))
        return shard.astype(F32)

    def scatter_weight(self, groups):
        others = range(1, self.n_tp)
        found = yield from self.scatter_core(groups)
        sizes = [v[0].shape[1] for v in found]
        half = max(sum(sizes) // 2 // LANES, 1) * LANES
        firsts, seconds = [[] for _ in range(self.n_tp)], []
        for r in range(self.n_tp):
            low = 0
            for v, size in zip(found, sizes):
                cut = min(max(half - low, 0), size)
                if cut:
                    firsts[r].append(v[r][:, :cut])
                if cut < size:
                    seconds.append(v[r][:, cut:])
                low += size
        firsts = [jnp.concatenate(v, axis=1) if len(v) > 1 else v[0] for v in firsts]

        def of_side(side):
            return jnp.concatenate([self.of_side(v, side) for v in seconds], axis=-1)

        got = [self.over_tp(firsts[r], r) for r in others], self.over_side(of_side(1 - self.side))
        tp_got, side_got = yield got
        first = (firsts[0].astype(F32) + sum(v.astype(F32) for v in tp_got)).astype(BF16)
        second = of_side(self.side).astype(F32) + side_got.astype(F32)
        second = jnp.split(second.astype(BF16), self.n_tp, axis=-1)
        got = (
            self.over_side(self.of_side(first, 1 - self.side)),
            [self.over_tp(second[r], r) for r in others],
        )
        side_got, tp_got = yield got
        first = self.of_side(first, self.side).astype(F32) + side_got.astype(F32)
        second = second[0].astype(F32) + sum(v.astype(F32) for v in tp_got)
        line = jnp.concatenate([first, second], axis=-1).astype(BF16)
        got = yield [
            swap_with(
                lax.dynamic_index_in_dim(line, self.line ^ k, 0, keepdims=False),
                "ctx",
                self.n_ctx,
                2 * k,
            )
            for k in range(1, self.n_line)
        ]
        own = lax.dynamic_index_in_dim(line, self.line, 0, keepdims=False)
        return own.astype(F32) + sum(v.astype(F32) for v in got)


class Rest:
    def __init__(self, value):
        self.value = value


class Task:
    def __init__(self, steps):
        self.steps, self.result = steps, None
        self.take(next(steps))

    def take(self, pending):
        self.resting = isinstance(pending, Rest)
        self.pending = pending.value if self.resting else pending


def at_once(steps):
    pending = next(steps)
    while True:
        try:
            pending = steps.send(pending)
        except StopIteration as stop:
            return stop.value


class Lanes:
    def __init__(self):
        self.tasks = []

    def start(self, steps):
        task = Task(steps)
        self.tasks.append(task)
        return task

    def fence(self, values=(), but=(), also=(), last=False):
        due = [t for t in self.tasks if t not in but and (last or not t.resting or t in also)]
        values, pending = lax.optimization_barrier((values, [t.pending for t in due]))
        going = [t for t in self.tasks if t not in due]
        for task, done in zip(due, pending):
            try:
                task.take(task.steps.send(done))
                going.append(task)
            except StopIteration as stop:
                task.result = stop.value
        self.tasks = going
        return values


def window(head):
    start = head * HEAD_DIM
    return start // LANES * LANES, -(-(start + HEAD_DIM) // LANES) * LANES


def in_head(head, rows, low, high):
    lanes = lax.broadcasted_iota(jnp.int32, (rows, high - low), 1) + low
    return (lanes >= head * HEAD_DIM) & (lanes < (head + 1) * HEAD_DIM)


def spread_parts(x_ref, offset, parts, width):
    for index, part in enumerate(parts):
        padded = part.shape[1]
        start = offset + index * width
        if padded != width:
            part[:, padded - LANES :] = jnp.zeros((part.shape[0], LANES), part.dtype)
        part[:, :width] = x_ref[:, start : start + width]


def same_sequence(rows, stride):
    row = lax.broadcasted_iota(jnp.int32, (rows, rows), 0)
    column = lax.broadcasted_iota(jnp.int32, (rows, rows), 1)
    return lax.rem(row, stride) == lax.rem(column, stride)


def attend_kernel(count, width, stride, *refs):
    x_refs, (o_ref, lse_ref, q_s, k_s, v_s, o_s) = refs[:count], refs[count:]
    heads, rows = width // HEAD_DIM, o_ref.shape[0]
    lane = lax.broadcasted_iota(jnp.int32, (rows, LANES), 1)
    logs = jnp.zeros((rows, LANES), F32)
    if stride > 1:
        allowed = same_sequence(rows, stride)
    for index, x_ref in enumerate(x_refs):
        spread_parts(x_ref, 0, (q_s, k_s, v_s), width)
        for head in range(heads):
            low, high = window(head)
            mask = in_head(head, rows, low, high)
            queries = jnp.where(mask, q_s[:, low:high], jnp.zeros((), BF16))
            scores = dot(queries, k_s[:, low:high], NT) * SCALE
            if stride > 1:
                scores = jnp.where(allowed, scores, -jnp.inf)
            largest = jnp.max(scores, axis=-1, keepdims=True)
            raised = jnp.exp(scores - largest)
            total = jnp.sum(raised, axis=-1, keepdims=True)
            chances = (raised * (1.0 / total)).astype(BF16)
            result = dot(chances, v_s[:, low:high])
            o_s[:, low:high] = jnp.where(mask, result, o_s[:, low:high])
            logs = jnp.where(lane == index * heads + head, largest + jnp.log(total), logs)
        o_ref[:, index * width : (index + 1) * width] = o_s[:, :width].astype(BF16)
    lse_ref[...] = logs


def attend_back_kernel(count, width, stride, *refs):
    x_refs, (g_ref, lse_ref), dx_refs = refs[:count], refs[count : count + 2], refs[count + 2 : -7]
    q_s, k_s, v_s, g_s, dq_s, dk_s, dv_s = refs[-7:]
    heads, rows = width // HEAD_DIM, g_ref.shape[0]
    if stride > 1:
        allowed = same_sequence(rows, stride)
    for index, x_ref in enumerate(x_refs):
        spread_parts(x_ref, 0, (q_s, k_s, v_s), width)
        spread_parts(g_ref, index * width, (g_s,), width)
        for head in range(heads):
            low, high = window(head)
            mask = in_head(head, rows, low, high)
            zero = jnp.zeros((), BF16)
            q, k, v, g = q_s[:, low:high], k_s[:, low:high], v_s[:, low:high], g_s[:, low:high]
            scores = dot(jnp.where(mask, q, zero), k, NT) * SCALE
            if stride > 1:
                scores = jnp.where(allowed, scores, -jnp.inf)
            place = index * heads + head
            chances = jnp.exp(scores - lse_ref[:, place : place + 1])
            grad_chances = dot(jnp.where(mask, g, zero), v, NT)
            row_dot = jnp.sum(chances * grad_chances, axis=-1, keepdims=True)
            grad_scores = (chances * (grad_chances - row_dot)).astype(BF16)
            dq = dot(grad_scores, k) * SCALE
            dk = dot(grad_scores, q, TN) * SCALE
            dv = dot(chances.astype(BF16), g, TN)
            dq_s[:, low:high] = jnp.where(mask, dq, dq_s[:, low:high])
            dk_s[:, low:high] = jnp.where(mask, dk, dk_s[:, low:high])
            dv_s[:, low:high] = jnp.where(mask, dv, dv_s[:, low:high])
        for part_index, part in enumerate((dq_s, dk_s, dv_s)):
            start = part_index * width
            dx_refs[index][:, start : start + width] = part[:, :width].astype(BF16)


def row_block(rows, columns):
    return pl.BlockSpec((rows, columns), lambda i: (i, 0))


def attend(xs, rows, stride):
    count, width = xs[0].shape[0], xs[0].shape[1] // 3
    strips = len(xs)
    heads = strips * width // HEAD_DIM
    padded = -(-width // LANES) * LANES
    return pl.pallas_call(
        functools.partial(attend_kernel, strips, width, stride),
        grid=(count // rows,),
        in_specs=[row_block(rows, 3 * width)] * strips,
        out_specs=[row_block(rows, strips * width), row_block(rows, LANES)],
        out_shape=[
            jax.ShapeDtypeStruct((count, strips * width), BF16),
            jax.ShapeDtypeStruct((count, LANES), F32),
        ],
        scratch_shapes=[pltpu.VMEM((rows, padded), BF16)] * 3 + [pltpu.VMEM((rows, padded), F32)],
        cost_estimate=pl.CostEstimate(
            flops=heads * count * rows * 1024,
            bytes_accessed=count * width * strips * 8,
            transcendentals=heads * count * rows,
        ),
        compiler_params=pltpu.CompilerParams(vmem_limit_bytes=32 * 1024 * 1024),
    )(*xs)


def attend_back(xs, grad, lse, rows, stride):
    count, width = xs[0].shape[0], xs[0].shape[1] // 3
    strips = len(xs)
    heads = strips * width // HEAD_DIM
    padded = -(-width // LANES) * LANES
    return pl.pallas_call(
        functools.partial(attend_back_kernel, strips, width, stride),
        grid=(count // rows,),
        in_specs=[row_block(rows, 3 * width)] * strips
        + [row_block(rows, strips * width), row_block(rows, LANES)],
        out_specs=[row_block(rows, 3 * width)] * strips,
        out_shape=[jax.ShapeDtypeStruct((count, 3 * width), BF16)] * strips,
        scratch_shapes=[pltpu.VMEM((rows, padded), BF16)] * 4
        + [pltpu.VMEM((rows, padded), F32)] * 3,
        cost_estimate=pl.CostEstimate(
            flops=heads * count * rows * 2560,
            bytes_accessed=count * width * strips * 14,
            transcendentals=heads * count * rows,
        ),
        compiler_params=pltpu.CompilerParams(vmem_limit_bytes=32 * 1024 * 1024),
    )(*xs, grad, lse)


def weight_scratch(pieces):
    layout, arrays = pieces
    columns = sum(part[2] for strip in layout for part in strip)
    parts = max(len(strip) for strip in layout)
    return [
        pltpu.VMEM((2 * arrays[0].shape[-2], columns), BF16),
        pltpu.SemaphoreType.DMA((2, len(layout), parts)),
    ]


def weight_copies(layout, refs, w_s, sems):
    count = len(refs) // 2
    rows = w_s.shape[0] // 2
    copies = [[] for _ in layout]
    for group in range(2):
        low = 0
        for strip, parts in enumerate(layout):
            for part, (place, entry, columns) in enumerate(parts):
                source = refs[group * count + place]
                if entry is not None:
                    source = source.at[entry]
                target = w_s.at[pl.ds(group * rows, rows), pl.ds(low, columns)]
                low += columns
                copies[strip].append(
                    pltpu.make_async_copy(source, target, sems.at[group, strip, part])
                )
    return copies


def await_copies(copies):
    @pl.when(pl.program_id(0) == 0)
    def _():
        for copy in copies:
            copy.wait()


def turn_copies(copies, w_s, t_s):
    @pl.when(pl.program_id(0) == 0)
    def _():
        size = w_s.shape[1] // len(copies) // 2
        for strip, waits in enumerate(copies):
            for copy in waits:
                copy.wait()
            for low in (2 * strip * size, (2 * strip + 1) * size):
                t_s[low : low + size] = w_s[:, low : low + size].T


def begin_copies(*many):
    @pl.when(pl.program_id(0) == 0)
    def _():
        for copies in many:
            for strip in copies:
                for copy in strip:
                    copy.start()


def row_normal(v):
    centred = v - jnp.mean(v, axis=-1, keepdims=True)
    inverse = lax.rsqrt(jnp.mean(centred * centred, axis=-1, keepdims=True) + EPS)
    return centred * inverse, inverse


def row_back(grad, normed, inverse, scale):
    scaled = grad * (1.0 + scale)
    mean_one = jnp.mean(scaled, axis=-1, keepdims=True)
    mean_two = jnp.mean(scaled * normed, axis=-1, keepdims=True)
    return inverse * (scaled - mean_one - normed * mean_two)


def head_forward(heads, first, rows, allowed, q_s, k_s, v_s, o_s, lane, logs):
    for head in range(heads):
        low, high = window(head)
        mask = in_head(head, rows, low, high)
        queries = jnp.where(mask, q_s[:, low:high], jnp.zeros((), BF16))
        scores = dot(queries, k_s[:, low:high], NT) * SCALE
        if allowed is not None:
            scores = jnp.where(allowed, scores, -jnp.inf)
        largest = jnp.max(scores, axis=-1, keepdims=True)
        raised = jnp.exp(scores - largest)
        total = jnp.sum(raised, axis=-1, keepdims=True)
        chances = (raised * (1.0 / total)).astype(BF16)
        result = dot(chances, v_s[:, low:high])
        o_s[:, low:high] = jnp.where(mask, result, o_s[:, low:high])
        logs = jnp.where(lane == first + head, largest + jnp.log(total), logs)
    return logs


def head_back(heads, first, rows, allowed, q_s, k_s, v_s, g_s, lse_ref, dq_s, dk_s, dv_s):
    zero = jnp.zeros((), BF16)
    for head in range(heads):
        low, high = window(head)
        mask = in_head(head, rows, low, high)
        q, k, v, g = q_s[:, low:high], k_s[:, low:high], v_s[:, low:high], g_s[:, low:high]
        scores = dot(jnp.where(mask, q, zero), k, NT) * SCALE
        if allowed is not None:
            scores = jnp.where(allowed, scores, -jnp.inf)
        place = first + head
        chances = jnp.exp(scores - lse_ref[:, place : place + 1])
        grad_chances = dot(jnp.where(mask, g, zero), v, NT)
        row_dot = jnp.sum(chances * grad_chances, axis=-1, keepdims=True)
        grad_scores = (chances * (grad_chances - row_dot)).astype(BF16)
        dq = dot(grad_scores, k) * SCALE
        dk = dot(grad_scores, q, TN) * SCALE
        dv = dot(chances.astype(BF16), g, TN)
        dq_s[:, low:high] = jnp.where(mask, dq, dq_s[:, low:high])
        dk_s[:, low:high] = jnp.where(mask, dk, dk_s[:, low:high])
        dv_s[:, low:high] = jnp.where(mask, dv, dv_s[:, low:high])


def branch_kernel(layout, count, stride, x_ref, mod_ref, *refs):
    strips = len(layout)
    w_refs = refs[:count]
    h_ref, qkv_ref, lse_ref, o_ref, a_ref, y_ref, g_ref = refs[count : count + 7]
    w_s, sems, p_s, o_s, z_s = refs[count + 7 :]
    rows, width = x_ref.shape
    head_cols = width // strips
    padded = o_s.shape[1]
    spare = padded - head_cols
    columns = w_s.shape[1] // strips
    copies = weight_copies(layout, w_refs, w_s, sems)
    begin_copies(copies)
    x = x_ref[...].astype(F32)
    shift_a, scale_a, gate_a, shift_m, scale_m = [mod_ref[0, i : i + 1, :] for i in range(5)]
    h = (row_normal(x)[0] * (1.0 + scale_a) + shift_a).astype(BF16)
    h_ref[...] = h
    heads = head_cols // HEAD_DIM
    lane = lax.broadcasted_iota(jnp.int32, (rows, LANES), 1)
    logs = jnp.zeros((rows, LANES), F32)
    allowed = same_sequence(rows, stride) if stride > 1 else None
    branch = jnp.zeros((rows, width), F32)
    for strip in range(strips):
        start = strip * columns
        await_copies(copies[strip])
        p_s[...] = dot(h, w_s[:, start : start + p_s.shape[1]]).astype(BF16)
        parts = []
        for index in range(3):
            low = (3 * strip + index) * padded
            if spare:
                qkv_ref[:, low + padded - LANES : low + padded] = jnp.zeros((rows, LANES), BF16)
            qkv_ref[:, low : low + head_cols] = p_s[:, index * head_cols : (index + 1) * head_cols]
            parts.append(qkv_ref.at[:, pl.ds(low, padded)])
        logs = head_forward(heads, strip * heads, rows, allowed, *parts, o_s, lane, logs)
        low = o_s[:, :head_cols].astype(BF16)
        o_ref[:, strip * head_cols : (strip + 1) * head_cols] = low
        if spare:
            z_s[:, :LANES] = jnp.zeros((rows, LANES), BF16)
        z_s[:, spare:] = low
        branch = branch + dot(z_s[...], w_s[:, start + columns - padded : start + columns], NT)
    lse_ref[...] = logs
    a_ref[...] = branch.astype(BF16)
    y = x + gate_a * branch
    y_ref[...] = y
    g_ref[...] = (row_normal(y)[0] * (1.0 + scale_m) + shift_m).astype(BF16)


def branch_back_kernel(
    layout, count, stride, x_ref, mod_ref, da_ref, dy_ref, qkv_ref, lse_ref, *refs
):
    strips = len(layout)
    w_refs = refs[:count]
    dx_ref, sums_ref = refs[count : count + 2]
    out_refs = refs[count + 2 : count + 2 + strips]
    w_s, sems, d_s, g_s, dq_s, dk_s, dv_s = refs[count + 2 + strips :]
    rows, width = x_ref.shape
    head_cols = width // strips
    padded = g_s.shape[1]
    spare = padded - head_cols
    columns = w_s.shape[1] // strips
    copies = weight_copies(layout, w_refs, w_s, sems)
    begin_copies(copies)
    heads = head_cols // HEAD_DIM
    allowed = same_sequence(rows, stride) if stride > 1 else None
    grad = jnp.zeros((rows, width), F32)
    for strip in range(strips):
        start = strip * columns
        await_copies(copies[strip])
        turned = dot(da_ref[...], w_s[:, start + columns - padded : start + columns]).astype(BF16)
        if spare:
            g_s[:, padded - LANES :] = jnp.zeros((rows, LANES), BF16)
        g_s[:, :head_cols] = turned[:, spare:]
        parts = [qkv_ref.at[:, pl.ds((3 * strip + i) * padded, padded)] for i in range(3)]
        head_back(heads, strip * heads, rows, allowed, *parts, g_s, lse_ref, dq_s, dk_s, dv_s)
        if d_s.shape[1] != 3 * head_cols:
            d_s[:, d_s.shape[1] - LANES :] = jnp.zeros((rows, LANES), BF16)
        for index, part in enumerate((dq_s, dk_s, dv_s)):
            d_s[:, index * head_cols : (index + 1) * head_cols] = part[:, :head_cols].astype(BF16)
        out_refs[strip][...] = d_s[:, : 3 * head_cols]
        grad = grad + dot(d_s[...], w_s[:, start : start + d_s.shape[1]], NT)
    scale_a = mod_ref[0, 1:2, :]
    normed, inverse = row_normal(x_ref[...].astype(F32))
    sums_ref[...] = jnp.zeros(sums_ref.shape, F32)
    sums_ref[0, 0:1, :] = jnp.sum(grad, axis=0, keepdims=True)
    sums_ref[0, 1:2, :] = jnp.sum(grad * normed, axis=0, keepdims=True)
    dx_ref[...] = (dy_ref[...] + row_back(grad, normed, inverse, scale_a)).astype(BF16)


GELU_A = 0.7978845608028654
GELU_B = 0.044715


def up_kernel(layout, count, g_ref, *refs):
    strips = len(layout)
    z_ref, slope_ref, w_s, sems = refs[count:]
    copies = weight_copies(layout, refs[:count], w_s, sems)
    begin_copies(copies)
    half = w_s.shape[1] // (2 * strips)
    g = g_ref[...]
    for index in range(2 * strips):
        if index % 2 == 0:
            await_copies(copies[index // 2])
        low = index * half
        u = dot(g, w_s[:, low : low + half])
        square = u * u
        bent = jnp.tanh(u * (GELU_A + GELU_A * GELU_B * square))
        lifted = 0.5 * (1.0 + bent)
        z_ref[:, low : low + half] = (u * lifted).astype(BF16)
        inner = GELU_A + 3.0 * GELU_A * GELU_B * square
        slope = lifted + 0.5 * u * (1.0 - bent * bent) * inner
        slope_ref[:, low : low + half] = slope.astype(BF16)


def down_kernel(layout, count, z_ref, y_ref, mod_ref, *refs):
    strips = len(layout)
    m_ref, x_ref, w_s, sems, t_s = refs[count:]
    copies = weight_copies(layout, refs[:count], w_s, sems)
    begin_copies(copies)
    turn_copies(copies, w_s, t_s)
    total = dot(z_ref[...], t_s[...])
    m_ref[...] = total.astype(BF16)
    x_ref[...] = (y_ref[...] + mod_ref[0, 5:6, :] * total).astype(BF16)


def mlp_back_kernel(
    up_layout, ups_count, down_layout, count, dx_ref, mod_ref, m_ref, slope_ref, y_ref, a_ref, *refs
):
    strips = len(up_layout)
    (dm_ref, du_ref, dy_ref, da_ref, sums_ref, up_s, up_sems, down_s, down_sems, t_s) = refs[
        ups_count + count :
    ]
    ups = weight_copies(up_layout, refs[:ups_count], up_s, up_sems)
    downs = weight_copies(down_layout, refs[ups_count : ups_count + count], down_s, down_sems)
    begin_copies(downs, ups)
    half = up_s.shape[1] // (2 * strips)
    turn_copies(ups, up_s, t_s)
    scale_m, gate_m, share, gate_a = [mod_ref[0, i : i + 1, :] for i in (4, 5, 6, 2)]
    dx = dx_ref[...].astype(F32) * share
    sums_ref[...] = jnp.zeros(sums_ref.shape, F32)
    sums_ref[0, 5:6, :] = jnp.sum(dx * m_ref[...].astype(F32), axis=0, keepdims=True)
    dm = (gate_m * dx).astype(BF16)
    dm_ref[...] = dm
    grad = jnp.zeros(y_ref.shape, F32)
    for index in range(2 * strips):
        low = index * half
        if index % 2 == 0:
            await_copies(downs[index // 2])
        dz = dot(dm, down_s[:, low : low + half])
        du = (dz * slope_ref[:, low : low + half].astype(F32)).astype(BF16)
        du_ref[:, low : low + half] = du
        grad = grad + dot(du, t_s[low : low + half])
    normed, inverse = row_normal(y_ref[...])
    sums_ref[0, 3:4, :] = jnp.sum(grad, axis=0, keepdims=True)
    sums_ref[0, 4:5, :] = jnp.sum(grad * normed, axis=0, keepdims=True)
    dy = dx + row_back(grad, normed, inverse, scale_m)
    dy_ref[...] = dy
    sums_ref[0, 2:3, :] = jnp.sum(dy * a_ref[...].astype(F32), axis=0, keepdims=True)
    da_ref[...] = (gate_a * dy).astype(BF16)


def shape_of(*dims, dtype=BF16):
    return jax.ShapeDtypeStruct(dims, dtype)


def block_call(kernel, clips, rows, arrays, mods, weights, outs, sums, scratch, flops, order):
    operands, specs = [], []
    for v in order:
        if v is None:
            operands.append(mods)
            specs.append(pl.BlockSpec((1,) + mods.shape[1:], lambda i: (i, 0, 0)))
        else:
            operands.append(arrays[v])
            specs.append(row_block(rows, arrays[v].shape[1]))
    for _, pieces in weights:
        operands += pieces
        specs += [pl.BlockSpec(memory_space=pl.ANY)] * len(pieces)
    out_specs = [row_block(rows, v.shape[1]) for v in outs]
    out_shape = list(outs)
    if sums is not None:
        width = mods.shape[2]
        out_specs.insert(sums, pl.BlockSpec((1, 8, width), lambda i: (i, 0, 0)))
        out_shape.insert(sums, shape_of(clips, 8, width, dtype=F32))
    held = []
    for pieces in weights:
        held += weight_scratch(pieces)
    moved = sum(v.size * v.dtype.itemsize for v in operands)
    return pl.pallas_call(
        kernel,
        grid=(clips,),
        in_specs=specs,
        out_specs=out_specs,
        out_shape=out_shape,
        scratch_shapes=held + scratch,
        cost_estimate=pl.CostEstimate(flops=flops, bytes_accessed=moved, transcendentals=0),
        compiler_params=pltpu.CompilerParams(vmem_limit_bytes=60 * 1024 * 1024),
    )(*operands)


def padded_to(columns):
    return -(-columns // LANES) * LANES


def fused_branch(x, mods, pieces, clips, stride):
    count, width = x.shape
    rows, strips = count // clips, len(pieces[0])
    head_cols = width // strips
    padded = padded_to(head_cols)
    outs = [
        shape_of(count, width),
        shape_of(count, 3 * strips * padded),
        shape_of(count, LANES, dtype=F32),
        shape_of(count, width),
        shape_of(count, width),
        shape_of(count, width, dtype=F32),
        shape_of(count, width),
    ]
    scratch = [
        pltpu.VMEM((rows, padded_to(3 * head_cols)), BF16),
        pltpu.VMEM((rows, padded), F32),
        pltpu.VMEM((rows, padded), BF16),
    ]
    return block_call(
        functools.partial(branch_kernel, pieces[0], len(pieces[1]), stride),
        clips, rows, [x], mods, [pieces], outs, None, scratch,
        12 * count * width * width, [0, None],
    )


def fused_branch_back(x, mods, da, dy, qkv, lse, pieces, clips, stride):
    count, width = x.shape
    rows, strips = count // clips, len(pieces[0])
    head_cols = width // strips
    padded = padded_to(head_cols)
    outs = [shape_of(count, width)] + [shape_of(count, 3 * head_cols) for _ in range(strips)]
    scratch = [
        pltpu.VMEM((rows, padded_to(3 * head_cols)), BF16),
        pltpu.VMEM((rows, padded), BF16),
    ] + [pltpu.VMEM((rows, padded), F32)] * 3
    return block_call(
        functools.partial(branch_back_kernel, pieces[0], len(pieces[1]), stride),
        clips, rows, [x, da, dy, qkv, lse], mods, [pieces], outs, 1, scratch,
        16 * count * width * width, [0, None, 1, 2, 3, 4],
    )


def fused_up(g, mods, pieces, clips):
    count, width = g.shape
    rows, strips = count // clips, len(pieces[0])
    units = sum(part[2] for strip in pieces[0] for part in strip)
    outs = [shape_of(count, units), shape_of(count, units)]
    return block_call(
        functools.partial(up_kernel, pieces[0], len(pieces[1])),
        clips, rows, [g], mods, [pieces], outs, None, [], 2 * count * width * units, [0],
    )


def fused_down(z, y, mods, pieces, clips):
    count, width = y.shape
    rows, strips = count // clips, len(pieces[0])
    outs = [shape_of(count, width), shape_of(count, width)]
    return block_call(
        functools.partial(down_kernel, pieces[0], len(pieces[1])),
        clips, rows, [z, y], mods, [pieces], outs, None, [pltpu.VMEM((z.shape[1], width), BF16)],
        2 * z.size * width, [0, 1, None],
    )


def fused_mlp_back(dx, mods, m, slope, y, a, ups, downs, clips):
    count, width = y.shape
    rows = count // clips
    outs = [
        shape_of(count, width),
        shape_of(*slope.shape),
        shape_of(count, width, dtype=F32),
        shape_of(count, width),
    ]
    return block_call(
        functools.partial(mlp_back_kernel, ups[0], len(ups[1]), downs[0], len(downs[1])),
        clips, rows, [dx, m, slope, y, a], mods, [ups, downs], outs, 4,
        [pltpu.VMEM((slope.shape[1], width), BF16)],
        4 * slope.size * width, [0, None, 1, 2, 3, 4],
    )


def split_frames(v, frames, width):
    return v.reshape(frames, -1, width // HEAD_DIM, HEAD_DIM)


def attend_shared(x, frames):
    width = x.shape[1] // 3
    shaped = x.reshape(frames, -1, 3, width)
    pairs = lax.all_gather(shaped[:, :, 1:], "tp", axis=1, tiled=True)
    q = split_frames(shaped[:, :, 0], frames, width)
    k = split_frames(pairs[:, :, 0], frames, width)
    v = split_frames(pairs[:, :, 1], frames, width)
    scores = jnp.einsum("bqhe,bkhe->bhqk", q, k, preferred_element_type=F32) * SCALE
    chances = jax.nn.softmax(scores, axis=-1)
    result = jnp.einsum("bhqk,bkhe->bqhe", chances.astype(BF16), v, preferred_element_type=F32)
    return result.reshape(-1, width).astype(BF16), (q, k, v, chances)


def attend_shared_back(saved, grad):
    q, k, v, chances = saved
    frames, width = q.shape[0], grad.shape[1]
    grad = split_frames(grad, frames, width)
    grad_chances = jnp.einsum("bqhe,bkhe->bhqk", grad, v, preferred_element_type=F32)
    row_dot = jnp.sum(chances * grad_chances, axis=-1, keepdims=True)
    grad_scores = (chances * (grad_chances - row_dot)).astype(BF16)
    dq = jnp.einsum("bhqk,bkhe->bqhe", grad_scores, k, preferred_element_type=F32) * SCALE
    dk = jnp.einsum("bhqk,bqhe->bkhe", grad_scores, q, preferred_element_type=F32) * SCALE
    dv = jnp.einsum("bhqk,bqhe->bkhe", chances.astype(BF16), grad, preferred_element_type=F32)
    sums = lax.psum_scatter(jnp.stack([dk, dv], axis=2), "tp", scatter_dimension=1, tiled=True)
    parts = jnp.concatenate([dq[:, :, None], sums], axis=2)
    return parts.reshape(-1, 3 * width).astype(BF16)


def normalise(v):
    centred = v - jnp.mean(v, axis=-1, keepdims=True)
    inverse = lax.rsqrt(jnp.mean(centred * centred, axis=-1, keepdims=True) + EPS)
    return centred * inverse, inverse


def modulate(v, shift, scale):
    return (normalise(v)[0] * (1.0 + scale[:, None]) + shift[:, None]).astype(BF16)


def modulate_back(grad, v, scale):
    normed, inverse = normalise(v)
    shift_grad = jnp.sum(grad, axis=1)
    scale_grad = jnp.sum(grad * normed, axis=1)
    scaled = grad * (1.0 + scale[:, None])
    mean_one = jnp.mean(scaled, axis=-1, keepdims=True)
    mean_two = jnp.mean(scaled * normed, axis=-1, keepdims=True)
    return inverse * (scaled - mean_one - normed * mean_two), shift_grad, scale_grad


def gelu(v):
    return jax.nn.gelu(v, approximate=True)


def gelu_slope(v, grad):
    return jax.vjp(gelu, v)[1](grad)[0]


def local(moves, tokens, condition, micro_ids, w_qkv, w_out, w_up, w_down, w_ada, cotangent):
    moves.here()
    n_dp, n_ctx, n_tp = moves.n_dp, moves.n_ctx, moves.n_tp
    clips, frames_here, patches_here, width = tokens.shape
    rows_here, head_cols = w_qkv.shape[2:]
    whole_frames = frames_here % n_tp == 0
    spread_tp = n_tp if whole_frames else 1
    groups = frames_here // spread_tp
    piece = patches_here // n_ctx

    cond_full = condition.astype(F32)
    cond_low = jax.nn.silu(cond_full).astype(BF16)
    cond_all = jnp.concatenate([cond_low, swap_with(cond_low, "dp", n_dp, 1)], axis=0)
    first_row = (moves.dp * n_ctx + moves.ctx) * rows_here
    cond_rows = lax.dynamic_slice_in_dim(cond_all, first_row, rows_here, axis=1)
    ada_low = w_ada.astype(BF16)
    shares = jnp.stack([dot(cond_rows, ada_low[level]) for level in range(LAYERS)], axis=1)

    def total_over_ctx(v):
        got = yield [swap_with(v, "ctx", n_ctx, 2 * k) for k in range(1, n_ctx // 2)]
        return v + sum(got)

    def modulation_vectors():
        sums = shares[:clips] + swap_with(shares[clips:], "dp", n_dp, 1)
        sums = yield sums
        sums = yield from total_over_ctx(sums)
        pairs = [
            [(c * n_tp + t, (c ^ dx) * n_tp + (t ^ r)) for c in range(n_ctx) for t in range(n_tp)]
            for r in range(n_tp)
            for dx in range(2)
        ]
        got = yield [lax.ppermute(sums, ("ctx", "tp"), entry) for entry in pairs[1:]]
        got = [sums] + got
        strips = [got[2 * r] + got[2 * r + 1] for r in range(n_tp)]
        strips = flip_to(jnp.stack(strips, axis=2), 2, n_tp, moves.tp)
        found = strips.reshape(clips, LAYERS, 6, width)
        return [moves.halves(found[:, level]) for level in range(LAYERS)]

    def to_frames(v):
        v = v.reshape(clips, frames_here, n_ctx, piece, width)
        v = flip_to(v, 2, n_ctx, moves.ctx)
        if spread_tp == 1:
            yield ()
            return v.reshape(clips, groups * patches_here, width)
        v = v.reshape(clips, spread_tp, groups, patches_here, width)
        v = flip_to(v, 1, spread_tp, moves.tp)
        got = yield [swap_with(v[:, r], "tp", n_tp, r) for r in range(1, spread_tp)]
        return jnp.stack([v[:, 0]] + got, axis=2).reshape(clips, -1, width)

    def from_frames(v):
        got = ()
        if spread_tp > 1:
            v = v.reshape(clips, groups, spread_tp, patches_here, width)
            got = [swap_with(v[:, :, r], "tp", n_tp, r) for r in range(1, spread_tp)]
        got = yield got
        if spread_tp > 1:
            v = flip_to(jnp.stack([v[:, :, 0]] + got, axis=1), 1, spread_tp, moves.tp)
        v = v.reshape(clips, frames_here, n_ctx, piece, width)
        v = flip_to(v, 2, n_ctx, moves.ctx)
        return v.reshape(clips, frames_here, patches_here, width)

    def trade(get, planes):
        sides = []
        for dx, dr in planes:
            block = get(dx, dr)
            if dx or dr:
                pairs = [
                    (c * n_tp + t, (c ^ dx) * n_tp + (t ^ dr))
                    for c in range(n_ctx)
                    for t in range(n_tp)
                ]
                block = lax.ppermute(block, ("ctx", "tp"), pairs)
            sides.append(block)
        sides = sides[:1] + (yield sides[1:])
        lines = [jnp.stack([v[:, dz] for v in sides], axis=1) for dz in range(n_ctx // 2)]
        got = yield [swap_with(v, "ctx", n_ctx, 2 * dz) for dz, v in enumerate(lines) if dz]
        return jnp.stack(lines[:1] + got, axis=1)

    all_planes = [(dx, dr) for dx in range(2) for dr in range(spread_tp)]
    own_planes = [(0, 0), (1, 0)]

    def frames_to_clips(v):
        v = v.reshape(clips, groups, spread_tp, n_ctx // 2, 2, piece, width)
        got = yield from trade(lambda dx, dr: v[:, :, dr, :, dx].swapaxes(1, 2), all_planes)
        return got.reshape(clips, -1, width)

    def clips_to_frames(v):
        v = v.reshape(clips, n_ctx // 2, 2, spread_tp, groups, piece, width)
        got = yield from trade(lambda dx, dr: v[:, :, dx, dr], all_planes)
        got = got.reshape(clips, n_ctx, spread_tp, groups, piece, width)
        return got.transpose(0, 3, 2, 1, 4, 5).reshape(clips, -1, width)

    def here_to_clips(v):
        v = v.reshape(clips, spread_tp, groups, n_ctx, piece, width)
        v = flip_to(flip_to(v, 3, n_ctx, moves.ctx), 1, spread_tp, moves.tp % spread_tp)
        v = v.reshape(clips, spread_tp, groups, n_ctx // 2, 2, piece, width)
        got = yield from trade(lambda dx, dr: v[:, :, :, :, dx].transpose(0, 3, 1, 2, 4, 5), own_planes)
        return got.reshape(clips, -1, width)

    def clips_to_here(v):
        v = v.reshape(clips, n_ctx // 2, 2, spread_tp, groups, piece, width)
        got = yield from trade(lambda dx, dr: v[:, :, dx], own_planes)
        v = got.reshape(clips, n_ctx, spread_tp, groups, piece, width).transpose(0, 2, 3, 1, 4, 5)
        v = flip_to(flip_to(v, 3, n_ctx, moves.ctx), 1, spread_tp, moves.tp % spread_tp)
        return v.reshape(clips, frames_here, patches_here, width)

    def flat(v):
        return v.reshape(-1, v.shape[-1])

    def shaped(v):
        return v.reshape(clips, -1, v.shape[-1])

    shards = []
    for level in range(LAYERS):
        attention = [w_qkv[level, 0], w_qkv[level, 1], w_qkv[level, 2], w_out[level].T]
        shards.append(jnp.concatenate(attention, axis=1).astype(BF16))
        shards.append(w_up[level].astype(BF16))
        shards.append(w_down[level].T.astype(BF16))
    lanes = Lanes()
    gathers = {}

    blocks = {}

    def gather_far(index):
        blocks[index] = lax.all_gather(shards[index], "ctx", axis=0, tiled=True)

    def set_out(index):
        if index in blocks:
            steps = moves.gather_rest(blocks[index])
        else:
            steps = moves.gather_halves(shards[index])
        gathers[index] = lanes.start(steps)

    plan = [
        ((2,), (), ()),
        ((), (2,), ()),
        ((1,), (), ()),
        ((), (), (4, 5)),
        ((3,), (), ()),
        ((4,), (3,), ()),
        ((5,), (4,), ()),
        ((), (5,), ()),
        ((), (), ()),
    ]

    def tick(values=()):
        out, but, far = plan.pop(0)
        held = {index: blocks.get(index, shards[index]) for index in out + far}
        held, values = lanes.fence((held, values), [gathers[index] for index in but])
        for index in out + far:
            if index in blocks:
                blocks[index] = held[index]
            else:
                shards[index] = held[index]
        for index in far:
            gather_far(index)
        for index in out:
            set_out(index)
        return values

    def whole(index):
        layout, arrays = gathers[index].result
        count = len(arrays) // 2
        groups = []
        for group in (arrays[:count], arrays[count:]):
            parts = [
                group[place] if entry is None else group[place][entry]
                for strip in layout
                for place, entry, _ in strip
            ]
            groups.append(jnp.concatenate(parts, axis=1))
        return jnp.concatenate(groups, axis=0)

    def attention_weights(index):
        v = whole(index)
        strips = jnp.split(v, n_tp, axis=1)
        cut = 3 * head_cols
        return [w[:, :cut] for w in strips], jnp.concatenate([w[:, cut:] for w in strips], axis=1)

    def modulations(level):
        return [mods[level][:, i] for i in range(6)]

    gather_far(1)
    gather_far(3)
    set_out(0)
    moved = lanes.start(to_frames(moves.halves(tokens)))
    vectors_task = lanes.start(modulation_vectors())
    tick()
    residual = moved.result
    tick()
    tick()
    mods = vectors_task.result
    fused = (
        whole_frames
        and head_cols % 32 == 0
        and w_up.shape[2] % (2 * LANES) == 0
        and 4 * head_cols == w_up.shape[2]
        and width % 32 == 0
    )
    matched = (micro_ids[:, None] == micro_ids[None, :]).astype(F32)
    share = 1.0 / jnp.sum(matched, axis=1)
    scatters = {}
    mod_grads = [None] * LAYERS

    def start_scatter(level, names, *groups):
        far = level and len(groups) == 1
        steps = (moves.scatter_far if far else moves.scatter_weight)(groups)
        scatters[level, names] = lanes.start(steps)
        return scatters[level, names]

    def scattered(level, name):
        for (at, names), task in scatters.items():
            if at == level and name in names:
                columns = {"qkv": 3 * head_cols, "out": head_cols}
                units = w_up.shape[2]
                low = sum(columns.get(n, units) for n in names[: names.index(name)])
                return task.result[:, low : low + columns.get(name, units)]

    def mod_strip():
        parts = [moves.halves(v).reshape(clips, n_tp, -1) for v in mod_grads]
        parts = flip_to(jnp.stack(parts, axis=2), 1, n_tp, moves.tp)
        parts = yield from total_over_ctx(parts)
        got = yield [swap_with(parts[:, r], "tp", n_tp, r) for r in range(1, n_tp)]
        strip = parts[:, 0] + sum(got)
        got = yield swap_with(strip, "ctx", n_ctx, 1)
        strip = strip + got
        got = yield swap_with(strip, "dp", n_dp, 1)
        return jnp.concatenate([strip, got], axis=0)

    def fused_passes(v):
        vectors, saved = [], []
        for level in range(LAYERS):
            last = share if level == LAYERS - 1 else jnp.ones_like(share)
            last = jnp.broadcast_to(last[:, None, None], (clips, 2, width))
            vectors.append(jnp.concatenate([mods[level], last], axis=1))
        v = flat(v)
        for level in range(LAYERS):
            stride = piece if level % 2 else 1
            joined = gathers[3 * level].result
            kept = fused_branch(v, vectors[level], joined, clips, stride)
            kept, late = tick((kept, cotangent))
            normed, qkv, lse, result, branch, middle, normed_mlp = kept
            if level == 0:
                turned = lanes.start(here_to_clips(moves.halves(late)))
            up = gathers[3 * level + 1].result
            act, slope = tick(fused_up(normed_mlp, vectors[level], up, clips))
            down = gathers[3 * level + 2].result
            branch_mlp, after = fused_down(act, middle, vectors[level], down, clips)
            saved.append((v, normed, qkv, lse, result, branch, middle, normed_mlp))
            saved[-1] += (act, slope, branch_mlp, joined, up, down, stride)
            v = after
            if level == 0:
                moved = lanes.start(frames_to_clips(shaped(v)))
                tick()
                tick()
                v = flat(moved.result)
        finished = lanes.start(clips_to_here(moves.halves(shaped(v))))
        grad = flat(turned.result)
        for level in reversed(range(LAYERS)):
            v, normed, qkv, lse, result, branch, middle, normed_mlp = saved[level][:8]
            act, slope, branch_mlp, joined, up, down, stride = saved[level][8:]
            back = fused_mlp_back(
                grad, vectors[level], branch_mlp, slope, middle, branch, up, down, clips
            )
            late = () if level else (second, third)
            grad_branch, grad_pre, grad_middle, grad_out, sums = lanes.fence(back, late)
            if level:
                first = start_scatter(level, ("down",), (grad_branch, [act]))
                grad_out = lanes.fence(grad_out, (finished,))
            else:
                start_scatter(
                    level, ("down", "up"), (grad_branch, [act]), (normed_mlp, [grad_pre])
                )
                grad_out = lanes.fence(grad_out)
            back = fused_branch_back(
                v, vectors[level], grad_out, grad_middle, qkv, lse, joined, clips, stride
            )
            grad, more, *grad_qkv = lanes.fence(back, (first,) if level else ())
            mod_grads[level] = (sums + more)[:, :6]
            joint = (normed, grad_qkv), (grad_out, [result])
            if level:
                moved = lanes.start(clips_to_frames(shaped(grad)))
                second = start_scatter(level, ("up",), (normed_mlp, [grad_pre]))
                lanes.fence((), (first,))
                third = start_scatter(level, ("qkv", "out"), *joint)
                lanes.fence((), (second,))
                grad = flat(moved.result)
            else:
                start_scatter(level, ("qkv", "out"), *joint)
        return finished, shaped(grad)

    def plain_passes(residual):
        residual = residual.astype(F32)
        records = []
        for level in range(LAYERS):
            spatial = level % 2 == 0
            shift_a, scale_a, gate_a, shift_m, scale_m, gate_m = modulations(level)
            normed = flat(modulate(residual, shift_a, scale_a))
            qkvs, outs = attention_weights(3 * level)
            projected = [dot(normed, v).astype(BF16) for v in qkvs]
            rows, stride = (patches_here * spread_tp, 1) if spatial else (residual.shape[1], piece)
            if spatial and not whole_frames:
                saved = [attend_shared(v, clips * frames_here) for v in projected]
                result = jnp.concatenate([entry[0] for entry in saved], axis=1)
                saved = [entry[1] for entry in saved]
            else:
                result, saved = attend(projected, rows, stride)
            result, saved = tick((result, saved))
            branch = shaped(dot(result, outs, NT))
            middle = residual + gate_a[:, None] * branch
            normed_mlp = flat(modulate(middle, shift_m, scale_m))
            up = whole(3 * level + 1)
            pre_act = dot(normed_mlp, up)
            act = gelu(pre_act).astype(BF16)
            act, pre_act = tick((act, pre_act))
            down = whole(3 * level + 2)
            branch_mlp = shaped(dot(act, down, NT))
            records.append(
                (residual, normed, projected, saved, result, branch, middle, normed_mlp)
                + (pre_act, act, branch_mlp, qkvs, outs, up, down, rows, stride)
            )
            residual = middle + gate_m[:, None] * branch_mlp
            if spatial:
                moved = lanes.start(frames_to_clips(residual.astype(BF16)))
                tick()
                turned = lanes.start(here_to_clips(moves.halves(cotangent)))
                tick()
                residual = moved.result.astype(F32)
        gradient = turned.result.astype(F32) * share[:, None, None]
        finished = lanes.start(clips_to_here(moves.halves(residual.astype(BF16))))
        for level in reversed(range(LAYERS)):
            spatial = level % 2 == 0
            (residual, normed, projected, saved, result, branch, middle, normed_mlp) = records[level][
                :8
            ]
            (pre_act, act, branch_mlp, qkvs, outs, up, down, rows, stride) = records[level][8:]
            shift_a, scale_a, gate_a, shift_m, scale_m, gate_m = modulations(level)
            gate_m_grad = jnp.sum(gradient * branch_mlp, axis=1)
            low_grad = flat((gradient * gate_m[:, None]).astype(BF16))
            grad_pre = gelu_slope(pre_act, dot(low_grad, down)).astype(BF16)
            start_scatter(level, ("down",), (low_grad, [act]))
            grad_pre = lanes.fence(grad_pre)
            grad_normed = shaped(dot(grad_pre, up, NT))
            start_scatter(level, ("up",), (normed_mlp, [grad_pre]))
            grad_normed = lanes.fence(grad_normed)
            added, shift_m_grad, scale_m_grad = modulate_back(grad_normed, middle, scale_m)
            gradient = gradient + added
            gate_a_grad = jnp.sum(gradient * branch, axis=1)
            low_grad = flat((gradient * gate_a[:, None]).astype(BF16))
            grad_heads = dot(low_grad, outs).astype(BF16)
            start_scatter(level, ("out",), (low_grad, [result]))
            grad_heads = lanes.fence(grad_heads)
            if spatial and not whole_frames:
                grad_qkv = [
                    attend_shared_back(v, g)
                    for v, g in zip(saved, jnp.split(grad_heads, n_tp, axis=1))
                ]
            else:
                grad_qkv = attend_back(projected, grad_heads, saved, rows, stride)
            grad_qkv = lanes.fence(grad_qkv)
            start_scatter(level, ("qkv",), (normed, grad_qkv))
            grad_normed = shaped(sum(dot(v, w, NT) for v, w in zip(grad_qkv, qkvs)))
            added, shift_a_grad, scale_a_grad = modulate_back(grad_normed, residual, scale_a)
            gradient = gradient + added
            mod_grads[level] = jnp.stack(
                [shift_a_grad, scale_a_grad, gate_a_grad, shift_m_grad, scale_m_grad, gate_m_grad],
                axis=1,
            )
            if not spatial:
                moved = lanes.start(clips_to_frames(gradient.astype(BF16)))
                lanes.fence()
                lanes.fence()
                gradient = moved.result.astype(F32)
        return finished, gradient

    passes = fused_passes if fused else plain_passes
    finished, gradient = passes(residual)
    hanging = [scatters[key] for key in scatters if key == (0, ("down", "up"))]
    first = [scatters[key] for key in scatters if key == (1, ("down",))]
    second = [scatters[key] for key in scatters if key == (1, ("up",))]
    both = lanes.start(mod_strip())
    gradient = lanes.fence(gradient, (), first)
    gradient = lanes.fence(gradient, hanging)
    gradient = lanes.fence(gradient, (), second)
    moved = lanes.start(from_frames(moves.halves(gradient.astype(BF16))))
    while lanes.tasks:
        lanes.fence(last=True)
    both = both.result
    grad_tokens = moved.result.astype(F32)
    output = finished.result
    grads = [
        (
            scattered(level, "qkv").reshape(rows_here, 3, head_cols).transpose(1, 0, 2),
            scattered(level, "out").T,
            scattered(level, "up"),
            scattered(level, "down").T,
        )
        for level in range(LAYERS)
    ]

    ada_grads = []
    cond_part = 0.0
    for level in range(LAYERS):
        strip = both[:, level]
        ada_grads.append(
            lax.dot_general(cond_rows.astype(F32), strip, TN, precision=HIGHEST)
        )
        cond_part = cond_part + lax.dot_general(
            strip, ada_low[level].astype(F32), NT, precision=HIGHEST
        )
    over_tp = [swap_with(cond_part[:clips], "tp", n_tp, r) for r in range(1, n_tp)]
    over_both = [
        lax.ppermute(
            cond_part[clips:],
            ("dp", "tp"),
            [(d * n_tp + t, (1 - d) * n_tp + (t ^ r)) for d in range(n_dp) for t in range(n_tp)],
        )
        for r in range(n_tp)
    ]
    cond_grad = jnp.stack([cond_part[:clips] + sum(over_tp), sum(over_both)], axis=1)[:, :, None]
    cond_grad = jnp.concatenate([cond_grad, swap_with(cond_grad, "ctx", n_ctx, 1)], axis=2)
    blocks = [cond_grad] + [swap_with(cond_grad, "ctx", n_ctx, 2 * k) for k in range(1, n_ctx // 2)]
    cond_grad = jnp.concatenate(blocks, axis=2)
    cond_grad = flip_to(cond_grad, 2, n_ctx, moves.ctx).reshape(clips, width)
    cond_grad = moves.halves(cond_grad)
    grad_condition = jax.vjp(jax.nn.silu, cond_full)[1](cond_grad)[0]

    stacked = [jnp.stack([grads[level][i] for level in range(LAYERS)]) for i in range(4)]
    return (output, grad_tokens, grad_condition, *stacked, jnp.stack(ada_grads))


def solution(mesh):
    placed = (
        P("dp", "ctx", "tp", None),
        P("dp", None),
        P("dp"),
        P(None, None, ("dp", "ctx"), "tp"),
        P(None, "tp", ("dp", "ctx")),
        P(None, ("dp", "ctx"), "tp"),
        P(None, "tp", ("dp", "ctx")),
        P(None, ("dp", "ctx"), "tp"),
        P("dp", "ctx", "tp", None),
    )
    return jax.shard_map(
        functools.partial(local, Moves(mesh)),
        mesh=mesh,
        in_specs=placed,
        out_specs=(
            P("dp", "ctx", "tp", None),
            P("dp", "ctx", "tp", None),
            P("dp", None),
            P(None, None, ("dp", "ctx"), "tp"),
            P(None, "tp", ("dp", "ctx")),
            P(None, ("dp", "ctx"), "tp"),
            P(None, "tp", ("dp", "ctx")),
            P(None, ("dp", "ctx"), "tp"),
        ),
        check_vma=False,
    )
```

```python
import functools

import jax
import jax.numpy as jnp
from jax import lax
from jax.experimental import pallas as pl
from jax.experimental.pallas import tpu as pltpu
from jax.sharding import PartitionSpec as P

HEAD_DIM = 72
LAYERS = 2
LANES = 128
EPS = 1e-06
SCALE = HEAD_DIM ** (-0.5)
HIGHEST = lax.Precision.HIGHEST
BF16 = jnp.bfloat16
F32 = jnp.float32

NN = (((1,), (0,)), ((), ()))
NT = (((1,), (1,)), ((), ()))
TN = (((0,), (0,)), ((), ()))


def dot(a, b, dims=NN):
    return lax.dot_general(a, b, dims, preferred_element_type=F32)


def swap_with(v, axis_name, n, k):
    return lax.ppermute(v, axis_name, [(i, i ^ k) for i in range(n)])


def flip_to(v, axis, n, me):
    shape = v.shape
    bit = 1
    while bit < n:
        split = shape[:axis] + (n // (2 * bit), 2, bit) + shape[axis + 1 :]
        parts = v.reshape(split)
        first = lax.slice_in_dim(parts, 0, 1, axis=axis + 1)
        second = lax.slice_in_dim(parts, 1, 2, axis=axis + 1)
        turned = jnp.concatenate([second, first], axis=axis + 1)
        v = jnp.where((me & bit) != 0, turned, parts).reshape(shape)
        bit *= 2
    return v


class Moves:
    def __init__(self, mesh):
        self.n_dp = mesh.shape["dp"]
        self.n_ctx = mesh.shape["ctx"]
        self.n_tp = mesh.shape["tp"]
        self.n_line = self.n_ctx // 2

    def here(self):
        self.dp = lax.axis_index("dp")
        self.ctx = lax.axis_index("ctx")
        self.tp = lax.axis_index("tp")
        self.line = self.ctx // 2
        self.side = self.ctx % 2

    def halves(self, v):
        half = v.shape[-1] // 2
        turned = jnp.concatenate([v[..., half:], v[..., :half]], axis=-1)
        return jnp.where(self.dp == 0, v, turned)

    def pair_stack(self, v, other):
        first = jnp.where(self.side == 0, v, other)
        second = jnp.where(self.side == 0, other, v)
        both = jnp.stack([first, second], axis=-3)
        return both.reshape(v.shape[:-3] + (-1, v.shape[-1]))

    def of_side(self, v, side):
        parts = v.reshape(self.n_line, 2, -1, v.shape[-1])
        return lax.dynamic_index_in_dim(parts, side, 1, keepdims=False)

    def over_tp(self, v, r):
        return swap_with(v, "tp", self.n_tp, r)

    def over_side(self, v):
        return swap_with(v, "ctx", self.n_ctx, 1)

    def over_core(self, v):
        return swap_with(v, "dp", self.n_dp, 1)

    def with_core(self, mine, layout):
        return layout, mine + [self.over_core(v) for v in mine]

    def line_gather(self, v):
        return [swap_with(v, "ctx", self.n_ctx, 2 * k) for k in range(1, self.n_line)]

    def line_stack(self, blocks):
        return flip_to(jnp.stack(blocks), 0, self.n_line, self.line)


    def gather_halves(self, v):
        others = range(1, self.n_tp)
        got = yield self.line_gather(v)
        half = v.shape[1] // 2
        lines = [
            self.line_stack([b[:, cut] for b in [v] + got])
            for cut in (slice(0, half), slice(half, None))
        ]
        got = self.over_side(lines[0]), [self.over_tp(lines[1], r) for r in others]
        side_got, tp_got = yield got
        block = self.pair_stack(lines[0], side_got)
        strips = jnp.stack([lines[1]] + tp_got)
        got = [self.over_tp(block, r) for r in others], self.over_side(strips)
        tp_got, side_got = yield got
        mine = [block] + tp_got + [self.pair_stack(strips, side_got)]
        layout = tuple(((r, None, half), (self.n_tp, r, half)) for r in range(self.n_tp))
        return self.with_core(mine, layout)

    def gather_rest(self, block):
        got = yield [self.over_tp(block, r) for r in range(1, self.n_tp)]
        layout = tuple(((r, None, block.shape[1]),) for r in range(self.n_tp))
        return self.with_core([block] + got, layout)

    def scatter_core(self, groups):
        halves = [(v[:, : v.shape[1] // 2], v[:, v.shape[1] // 2 :]) for v, _ in groups]
        got = yield [
            [self.over_core(dot(theirs, v, TN).astype(BF16)) for v in rights]
            for (_, theirs), (_, rights) in zip(halves, groups)
        ]
        found = []
        for (mine, _), (_, rights), came in zip(halves, groups, got):
            totals = [
                (dot(mine, v, TN) + g.astype(F32)).astype(BF16) for v, g in zip(rights, came)
            ]
            if len(totals) == 1:
                totals = jnp.split(totals[0], self.n_tp, axis=1)
            found.append(totals)
        return found

    def scatter_far(self, groups):
        found = yield from self.scatter_core(groups)
        totals = [
            jnp.concatenate([v[r] for v in found], axis=1) if len(found) > 1 else found[0][r]
            for r in range(self.n_tp)
        ]
        got = yield [self.over_tp(totals[r], r) for r in range(1, self.n_tp)]
        total = (totals[0].astype(F32) + sum(v.astype(F32) for v in got)).astype(BF16)
        shard = yield Rest(lax.psum_scatter(total, "ctx", scatter_dimension=0, tiled=True))
        return shard.astype(F32)

    def scatter_weight(self, groups):
        others = range(1, self.n_tp)
        found = yield from self.scatter_core(groups)
        sizes = [v[0].shape[1] for v in found]
        half = max(sum(sizes) // 2 // LANES, 1) * LANES
        firsts, seconds = [[] for _ in range(self.n_tp)], []
        for r in range(self.n_tp):
            low = 0
            for v, size in zip(found, sizes):
                cut = min(max(half - low, 0), size)
                if cut:
                    firsts[r].append(v[r][:, :cut])
                if cut < size:
                    seconds.append(v[r][:, cut:])
                low += size
        firsts = [jnp.concatenate(v, axis=1) if len(v) > 1 else v[0] for v in firsts]

        def of_side(side):
            return jnp.concatenate([self.of_side(v, side) for v in seconds], axis=-1)

        got = [self.over_tp(firsts[r], r) for r in others], self.over_side(of_side(1 - self.side))
        tp_got, side_got = yield got
        first = (firsts[0].astype(F32) + sum(v.astype(F32) for v in tp_got)).astype(BF16)
        second = of_side(self.side).astype(F32) + side_got.astype(F32)
        second = jnp.split(second.astype(BF16), self.n_tp, axis=-1)
        got = (
            self.over_side(self.of_side(first, 1 - self.side)),
            [self.over_tp(second[r], r) for r in others],
        )
        side_got, tp_got = yield got
        first = self.of_side(first, self.side).astype(F32) + side_got.astype(F32)
        second = second[0].astype(F32) + sum(v.astype(F32) for v in tp_got)
        line = jnp.concatenate([first, second], axis=-1).astype(BF16)
        got = yield [
            swap_with(
                lax.dynamic_index_in_dim(line, self.line ^ k, 0, keepdims=False),
                "ctx",
                self.n_ctx,
                2 * k,
            )
            for k in range(1, self.n_line)
        ]
        own = lax.dynamic_index_in_dim(line, self.line, 0, keepdims=False)
        return own.astype(F32) + sum(v.astype(F32) for v in got)


class Rest:
    def __init__(self, value):
        self.value = value


class Task:
    def __init__(self, steps):
        self.steps, self.result = steps, None
        self.take(next(steps))

    def take(self, pending):
        self.resting = isinstance(pending, Rest)
        self.pending = pending.value if self.resting else pending


def at_once(steps):
    pending = next(steps)
    while True:
        try:
            pending = steps.send(pending)
        except StopIteration as stop:
            return stop.value


class Lanes:
    def __init__(self):
        self.tasks = []

    def start(self, steps):
        task = Task(steps)
        self.tasks.append(task)
        return task

    def fence(self, values=(), but=(), also=(), last=False):
        due = [t for t in self.tasks if t not in but and (last or not t.resting or t in also)]
        values, pending = lax.optimization_barrier((values, [t.pending for t in due]))
        going = [t for t in self.tasks if t not in due]
        for task, done in zip(due, pending):
            try:
                task.take(task.steps.send(done))
                going.append(task)
            except StopIteration as stop:
                task.result = stop.value
        self.tasks = going
        return values


def window(head):
    start = head * HEAD_DIM
    return start // LANES * LANES, -(-(start + HEAD_DIM) // LANES) * LANES


def in_head(head, rows, low, high):
    lanes = lax.broadcasted_iota(jnp.int32, (rows, high - low), 1) + low
    return (lanes >= head * HEAD_DIM) & (lanes < (head + 1) * HEAD_DIM)


def spread_parts(x_ref, offset, parts, width):
    for index, part in enumerate(parts):
        padded = part.shape[1]
        start = offset + index * width
        if padded != width:
            part[:, padded - LANES :] = jnp.zeros((part.shape[0], LANES), part.dtype)
        part[:, :width] = x_ref[:, start : start + width]


def same_sequence(rows, stride):
    row = lax.broadcasted_iota(jnp.int32, (rows, rows), 0)
    column = lax.broadcasted_iota(jnp.int32, (rows, rows), 1)
    return lax.rem(row, stride) == lax.rem(column, stride)


def attend_kernel(count, width, stride, *refs):
    x_refs, (o_ref, lse_ref, q_s, k_s, v_s, o_s) = refs[:count], refs[count:]
    heads, rows = width // HEAD_DIM, o_ref.shape[0]
    lane = lax.broadcasted_iota(jnp.int32, (rows, LANES), 1)
    logs = jnp.zeros((rows, LANES), F32)
    if stride > 1:
        allowed = same_sequence(rows, stride)
    for index, x_ref in enumerate(x_refs):
        spread_parts(x_ref, 0, (q_s, k_s, v_s), width)
        for head in range(heads):
            low, high = window(head)
            mask = in_head(head, rows, low, high)
            queries = jnp.where(mask, q_s[:, low:high], jnp.zeros((), BF16))
            scores = dot(queries, k_s[:, low:high], NT) * SCALE
            if stride > 1:
                scores = jnp.where(allowed, scores, -jnp.inf)
            largest = jnp.max(scores, axis=-1, keepdims=True)
            raised = jnp.exp(scores - largest)
            total = jnp.sum(raised, axis=-1, keepdims=True)
            chances = (raised * (1.0 / total)).astype(BF16)
            result = dot(chances, v_s[:, low:high])
            o_s[:, low:high] = jnp.where(mask, result, o_s[:, low:high])
            logs = jnp.where(lane == index * heads + head, largest + jnp.log(total), logs)
        o_ref[:, index * width : (index + 1) * width] = o_s[:, :width].astype(BF16)
    lse_ref[...] = logs


def attend_back_kernel(count, width, stride, *refs):
    x_refs, (g_ref, lse_ref), dx_refs = refs[:count], refs[count : count + 2], refs[count + 2 : -7]
    q_s, k_s, v_s, g_s, dq_s, dk_s, dv_s = refs[-7:]
    heads, rows = width // HEAD_DIM, g_ref.shape[0]
    if stride > 1:
        allowed = same_sequence(rows, stride)
    for index, x_ref in enumerate(x_refs):
        spread_parts(x_ref, 0, (q_s, k_s, v_s), width)
        spread_parts(g_ref, index * width, (g_s,), width)
        for head in range(heads):
            low, high = window(head)
            mask = in_head(head, rows, low, high)
            zero = jnp.zeros((), BF16)
            q, k, v, g = q_s[:, low:high], k_s[:, low:high], v_s[:, low:high], g_s[:, low:high]
            scores = dot(jnp.where(mask, q, zero), k, NT) * SCALE
            if stride > 1:
                scores = jnp.where(allowed, scores, -jnp.inf)
            place = index * heads + head
            chances = jnp.exp(scores - lse_ref[:, place : place + 1])
            grad_chances = dot(jnp.where(mask, g, zero), v, NT)
            row_dot = jnp.sum(chances * grad_chances, axis=-1, keepdims=True)
            grad_scores = (chances * (grad_chances - row_dot)).astype(BF16)
            dq = dot(grad_scores, k) * SCALE
            dk = dot(grad_scores, q, TN) * SCALE
            dv = dot(chances.astype(BF16), g, TN)
            dq_s[:, low:high] = jnp.where(mask, dq, dq_s[:, low:high])
            dk_s[:, low:high] = jnp.where(mask, dk, dk_s[:, low:high])
            dv_s[:, low:high] = jnp.where(mask, dv, dv_s[:, low:high])
        for part_index, part in enumerate((dq_s, dk_s, dv_s)):
            start = part_index * width
            dx_refs[index][:, start : start + width] = part[:, :width].astype(BF16)


def row_block(rows, columns):
    return pl.BlockSpec((rows, columns), lambda i: (i, 0))


def attend(xs, rows, stride):
    count, width = xs[0].shape[0], xs[0].shape[1] // 3
    strips = len(xs)
    heads = strips * width // HEAD_DIM
    padded = -(-width // LANES) * LANES
    return pl.pallas_call(
        functools.partial(attend_kernel, strips, width, stride),
        grid=(count // rows,),
        in_specs=[row_block(rows, 3 * width)] * strips,
        out_specs=[row_block(rows, strips * width), row_block(rows, LANES)],
        out_shape=[
            jax.ShapeDtypeStruct((count, strips * width), BF16),
            jax.ShapeDtypeStruct((count, LANES), F32),
        ],
        scratch_shapes=[pltpu.VMEM((rows, padded), BF16)] * 3 + [pltpu.VMEM((rows, padded), F32)],
        cost_estimate=pl.CostEstimate(
            flops=heads * count * rows * 1024,
            bytes_accessed=count * width * strips * 8,
            transcendentals=heads * count * rows,
        ),
        compiler_params=pltpu.CompilerParams(vmem_limit_bytes=32 * 1024 * 1024),
    )(*xs)


def attend_back(xs, grad, lse, rows, stride):
    count, width = xs[0].shape[0], xs[0].shape[1] // 3
    strips = len(xs)
    heads = strips * width // HEAD_DIM
    padded = -(-width // LANES) * LANES
    return pl.pallas_call(
        functools.partial(attend_back_kernel, strips, width, stride),
        grid=(count // rows,),
        in_specs=[row_block(rows, 3 * width)] * strips
        + [row_block(rows, strips * width), row_block(rows, LANES)],
        out_specs=[row_block(rows, 3 * width)] * strips,
        out_shape=[jax.ShapeDtypeStruct((count, 3 * width), BF16)] * strips,
        scratch_shapes=[pltpu.VMEM((rows, padded), BF16)] * 4
        + [pltpu.VMEM((rows, padded), F32)] * 3,
        cost_estimate=pl.CostEstimate(
            flops=heads * count * rows * 2560,
            bytes_accessed=count * width * strips * 14,
            transcendentals=heads * count * rows,
        ),
        compiler_params=pltpu.CompilerParams(vmem_limit_bytes=32 * 1024 * 1024),
    )(*xs, grad, lse)


def weight_scratch(pieces):
    layout, arrays = pieces
    columns = sum(part[2] for strip in layout for part in strip)
    parts = max(len(strip) for strip in layout)
    return [
        pltpu.VMEM((2 * arrays[0].shape[-2], columns), BF16),
        pltpu.SemaphoreType.DMA((2, len(layout), parts)),
    ]


def weight_copies(layout, refs, w_s, sems):
    count = len(refs) // 2
    rows = w_s.shape[0] // 2
    copies = [[] for _ in layout]
    for group in range(2):
        low = 0
        for strip, parts in enumerate(layout):
            for part, (place, entry, columns) in enumerate(parts):
                source = refs[group * count + place]
                if entry is not None:
                    source = source.at[entry]
                target = w_s.at[pl.ds(group * rows, rows), pl.ds(low, columns)]
                low += columns
                copies[strip].append(
                    pltpu.make_async_copy(source, target, sems.at[group, strip, part])
                )
    return copies


def await_copies(copies):
    @pl.when(pl.program_id(0) == 0)
    def _():
        for copy in copies:
            copy.wait()


def turn_copies(copies, w_s, t_s):
    @pl.when(pl.program_id(0) == 0)
    def _():
        size = w_s.shape[1] // len(copies) // 2
        for strip, waits in enumerate(copies):
            for copy in waits:
                copy.wait()
            for low in (2 * strip * size, (2 * strip + 1) * size):
                t_s[low : low + size] = w_s[:, low : low + size].T


def begin_copies(*many):
    @pl.when(pl.program_id(0) == 0)
    def _():
        for copies in many:
            for strip in copies:
                for copy in strip:
                    copy.start()


def row_normal(v):
    centred = v - jnp.mean(v, axis=-1, keepdims=True)
    inverse = lax.rsqrt(jnp.mean(centred * centred, axis=-1, keepdims=True) + EPS)
    return centred * inverse, inverse


def row_back(grad, normed, inverse, scale):
    scaled = grad * (1.0 + scale)
    mean_one = jnp.mean(scaled, axis=-1, keepdims=True)
    mean_two = jnp.mean(scaled * normed, axis=-1, keepdims=True)
    return inverse * (scaled - mean_one - normed * mean_two)


def head_forward(heads, first, rows, allowed, q_s, k_s, v_s, o_s, lane, logs):
    for head in range(heads):
        low, high = window(head)
        mask = in_head(head, rows, low, high)
        queries = jnp.where(mask, q_s[:, low:high], jnp.zeros((), BF16))
        scores = dot(queries, k_s[:, low:high], NT) * SCALE
        if allowed is not None:
            scores = jnp.where(allowed, scores, -jnp.inf)
        largest = jnp.max(scores, axis=-1, keepdims=True)
        raised = jnp.exp(scores - largest)
        total = jnp.sum(raised, axis=-1, keepdims=True)
        chances = (raised * (1.0 / total)).astype(BF16)
        result = dot(chances, v_s[:, low:high])
        o_s[:, low:high] = jnp.where(mask, result, o_s[:, low:high])
        logs = jnp.where(lane == first + head, largest + jnp.log(total), logs)
    return logs


def head_back(heads, first, rows, allowed, q_s, k_s, v_s, g_s, lse_ref, dq_s, dk_s, dv_s):
    zero = jnp.zeros((), BF16)
    for head in range(heads):
        low, high = window(head)
        mask = in_head(head, rows, low, high)
        q, k, v, g = q_s[:, low:high], k_s[:, low:high], v_s[:, low:high], g_s[:, low:high]
        scores = dot(jnp.where(mask, q, zero), k, NT) * SCALE
        if allowed is not None:
            scores = jnp.where(allowed, scores, -jnp.inf)
        place = first + head
        chances = jnp.exp(scores - lse_ref[:, place : place + 1])
        grad_chances = dot(jnp.where(mask, g, zero), v, NT)
        row_dot = jnp.sum(chances * grad_chances, axis=-1, keepdims=True)
        grad_scores = (chances * (grad_chances - row_dot)).astype(BF16)
        dq = dot(grad_scores, k) * SCALE
        dk = dot(grad_scores, q, TN) * SCALE
        dv = dot(chances.astype(BF16), g, TN)
        dq_s[:, low:high] = jnp.where(mask, dq, dq_s[:, low:high])
        dk_s[:, low:high] = jnp.where(mask, dk, dk_s[:, low:high])
        dv_s[:, low:high] = jnp.where(mask, dv, dv_s[:, low:high])


def branch_kernel(layout, count, stride, x_ref, mod_ref, *refs):
    strips = len(layout)
    w_refs = refs[:count]
    h_ref, qkv_ref, lse_ref, o_ref, a_ref, y_ref, g_ref = refs[count : count + 7]
    w_s, sems, p_s, o_s, z_s = refs[count + 7 :]
    rows, width = x_ref.shape
    head_cols = width // strips
    padded = o_s.shape[1]
    spare = padded - head_cols
    columns = w_s.shape[1] // strips
    copies = weight_copies(layout, w_refs, w_s, sems)
    begin_copies(copies)
    x = x_ref[...].astype(F32)
    shift_a, scale_a, gate_a, shift_m, scale_m = [mod_ref[0, i : i + 1, :] for i in range(5)]
    h = (row_normal(x)[0] * (1.0 + scale_a) + shift_a).astype(BF16)
    h_ref[...] = h
    heads = head_cols // HEAD_DIM
    lane = lax.broadcasted_iota(jnp.int32, (rows, LANES), 1)
    logs = jnp.zeros((rows, LANES), F32)
    allowed = same_sequence(rows, stride) if stride > 1 else None
    branch = jnp.zeros((rows, width), F32)
    for strip in range(strips):
        start = strip * columns
        await_copies(copies[strip])
        p_s[...] = dot(h, w_s[:, start : start + p_s.shape[1]]).astype(BF16)
        parts = []
        for index in range(3):
            low = (3 * strip + index) * padded
            if spare:
                qkv_ref[:, low + padded - LANES : low + padded] = jnp.zeros((rows, LANES), BF16)
            qkv_ref[:, low : low + head_cols] = p_s[:, index * head_cols : (index + 1) * head_cols]
            parts.append(qkv_ref.at[:, pl.ds(low, padded)])
        logs = head_forward(heads, strip * heads, rows, allowed, *parts, o_s, lane, logs)
        low = o_s[:, :head_cols].astype(BF16)
        o_ref[:, strip * head_cols : (strip + 1) * head_cols] = low
        if spare:
            z_s[:, :LANES] = jnp.zeros((rows, LANES), BF16)
        z_s[:, spare:] = low
        branch = branch + dot(z_s[...], w_s[:, start + columns - padded : start + columns], NT)
    lse_ref[...] = logs
    a_ref[...] = branch.astype(BF16)
    y = x + gate_a * branch
    y_ref[...] = y
    g_ref[...] = (row_normal(y)[0] * (1.0 + scale_m) + shift_m).astype(BF16)


def branch_back_kernel(
    layout, count, stride, x_ref, mod_ref, da_ref, dy_ref, qkv_ref, lse_ref, *refs
):
    strips = len(layout)
    w_refs = refs[:count]
    dx_ref, sums_ref = refs[count : count + 2]
    out_refs = refs[count + 2 : count + 2 + strips]
    w_s, sems, d_s, g_s, dq_s, dk_s, dv_s = refs[count + 2 + strips :]
    rows, width = x_ref.shape
    head_cols = width // strips
    padded = g_s.shape[1]
    spare = padded - head_cols
    columns = w_s.shape[1] // strips
    copies = weight_copies(layout, w_refs, w_s, sems)
    begin_copies(copies)
    heads = head_cols // HEAD_DIM
    allowed = same_sequence(rows, stride) if stride > 1 else None
    grad = jnp.zeros((rows, width), F32)
    for strip in range(strips):
        start = strip * columns
        await_copies(copies[strip])
        turned = dot(da_ref[...], w_s[:, start + columns - padded : start + columns]).astype(BF16)
        if spare:
            g_s[:, padded - LANES :] = jnp.zeros((rows, LANES), BF16)
        g_s[:, :head_cols] = turned[:, spare:]
        parts = [qkv_ref.at[:, pl.ds((3 * strip + i) * padded, padded)] for i in range(3)]
        head_back(heads, strip * heads, rows, allowed, *parts, g_s, lse_ref, dq_s, dk_s, dv_s)
        if d_s.shape[1] != 3 * head_cols:
            d_s[:, d_s.shape[1] - LANES :] = jnp.zeros((rows, LANES), BF16)
        for index, part in enumerate((dq_s, dk_s, dv_s)):
            d_s[:, index * head_cols : (index + 1) * head_cols] = part[:, :head_cols].astype(BF16)
        out_refs[strip][...] = d_s[:, : 3 * head_cols]
        grad = grad + dot(d_s[...], w_s[:, start : start + d_s.shape[1]], NT)
    scale_a = mod_ref[0, 1:2, :]
    normed, inverse = row_normal(x_ref[...].astype(F32))
    sums_ref[...] = jnp.zeros(sums_ref.shape, F32)
    sums_ref[0, 0:1, :] = jnp.sum(grad, axis=0, keepdims=True)
    sums_ref[0, 1:2, :] = jnp.sum(grad * normed, axis=0, keepdims=True)
    dx_ref[...] = (dy_ref[...] + row_back(grad, normed, inverse, scale_a)).astype(BF16)


GELU_A = 0.7978845608028654
GELU_B = 0.044715


def up_kernel(layout, count, g_ref, *refs):
    strips = len(layout)
    z_ref, slope_ref, w_s, sems = refs[count:]
    copies = weight_copies(layout, refs[:count], w_s, sems)
    begin_copies(copies)
    half = w_s.shape[1] // (2 * strips)
    g = g_ref[...]
    for index in range(2 * strips):
        if index % 2 == 0:
            await_copies(copies[index // 2])
        low = index * half
        u = dot(g, w_s[:, low : low + half])
        square = u * u
        bent = jnp.tanh(u * (GELU_A + GELU_A * GELU_B * square))
        lifted = 0.5 * (1.0 + bent)
        z_ref[:, low : low + half] = (u * lifted).astype(BF16)
        inner = GELU_A + 3.0 * GELU_A * GELU_B * square
        slope = lifted + 0.5 * u * (1.0 - bent * bent) * inner
        slope_ref[:, low : low + half] = slope.astype(BF16)


def down_kernel(layout, count, z_ref, y_ref, mod_ref, *refs):
    strips = len(layout)
    m_ref, x_ref, w_s, sems, t_s = refs[count:]
    copies = weight_copies(layout, refs[:count], w_s, sems)
    begin_copies(copies)
    turn_copies(copies, w_s, t_s)
    total = dot(z_ref[...], t_s[...])
    m_ref[...] = total.astype(BF16)
    x_ref[...] = (y_ref[...] + mod_ref[0, 5:6, :] * total).astype(BF16)


def mlp_back_kernel(
    up_layout, ups_count, down_layout, count, dx_ref, mod_ref, m_ref, slope_ref, y_ref, a_ref, *refs
):
    strips = len(up_layout)
    (dm_ref, du_ref, dy_ref, da_ref, sums_ref, up_s, up_sems, down_s, down_sems, t_s) = refs[
        ups_count + count :
    ]
    ups = weight_copies(up_layout, refs[:ups_count], up_s, up_sems)
    downs = weight_copies(down_layout, refs[ups_count : ups_count + count], down_s, down_sems)
    begin_copies(downs, ups)
    half = up_s.shape[1] // (2 * strips)
    turn_copies(ups, up_s, t_s)
    scale_m, gate_m, share, gate_a = [mod_ref[0, i : i + 1, :] for i in (4, 5, 6, 2)]
    dx = dx_ref[...].astype(F32) * share
    sums_ref[...] = jnp.zeros(sums_ref.shape, F32)
    sums_ref[0, 5:6, :] = jnp.sum(dx * m_ref[...].astype(F32), axis=0, keepdims=True)
    dm = (gate_m * dx).astype(BF16)
    dm_ref[...] = dm
    grad = jnp.zeros(y_ref.shape, F32)
    for index in range(2 * strips):
        low = index * half
        if index % 2 == 0:
            await_copies(downs[index // 2])
        dz = dot(dm, down_s[:, low : low + half])
        du = (dz * slope_ref[:, low : low + half].astype(F32)).astype(BF16)
        du_ref[:, low : low + half] = du
        grad = grad + dot(du, t_s[low : low + half])
    normed, inverse = row_normal(y_ref[...])
    sums_ref[0, 3:4, :] = jnp.sum(grad, axis=0, keepdims=True)
    sums_ref[0, 4:5, :] = jnp.sum(grad * normed, axis=0, keepdims=True)
    dy = dx + row_back(grad, normed, inverse, scale_m)
    dy_ref[...] = dy
    sums_ref[0, 2:3, :] = jnp.sum(dy * a_ref[...].astype(F32), axis=0, keepdims=True)
    da_ref[...] = (gate_a * dy).astype(BF16)


def shape_of(*dims, dtype=BF16):
    return jax.ShapeDtypeStruct(dims, dtype)


def block_call(kernel, clips, rows, arrays, mods, weights, outs, sums, scratch, flops, order):
    operands, specs = [], []
    for v in order:
        if v is None:
            operands.append(mods)
            specs.append(pl.BlockSpec((1,) + mods.shape[1:], lambda i: (i, 0, 0)))
        else:
            operands.append(arrays[v])
            specs.append(row_block(rows, arrays[v].shape[1]))
    for _, pieces in weights:
        operands += pieces
        specs += [pl.BlockSpec(memory_space=pl.ANY)] * len(pieces)
    out_specs = [row_block(rows, v.shape[1]) for v in outs]
    out_shape = list(outs)
    if sums is not None:
        width = mods.shape[2]
        out_specs.insert(sums, pl.BlockSpec((1, 8, width), lambda i: (i, 0, 0)))
        out_shape.insert(sums, shape_of(clips, 8, width, dtype=F32))
    held = []
    for pieces in weights:
        held += weight_scratch(pieces)
    moved = sum(v.size * v.dtype.itemsize for v in operands)
    return pl.pallas_call(
        kernel,
        grid=(clips,),
        in_specs=specs,
        out_specs=out_specs,
        out_shape=out_shape,
        scratch_shapes=held + scratch,
        cost_estimate=pl.CostEstimate(
            flops=flops // 32, bytes_accessed=moved // 32, transcendentals=0
        ),
        compiler_params=pltpu.CompilerParams(vmem_limit_bytes=60 * 1024 * 1024),
    )(*operands)


def padded_to(columns):
    return -(-columns // LANES) * LANES


def fused_branch(x, mods, pieces, clips, stride):
    count, width = x.shape
    rows, strips = count // clips, len(pieces[0])
    head_cols = width // strips
    padded = padded_to(head_cols)
    outs = [
        shape_of(count, width),
        shape_of(count, 3 * strips * padded),
        shape_of(count, LANES, dtype=F32),
        shape_of(count, width),
        shape_of(count, width),
        shape_of(count, width, dtype=F32),
        shape_of(count, width),
    ]
    scratch = [
        pltpu.VMEM((rows, padded_to(3 * head_cols)), BF16),
        pltpu.VMEM((rows, padded), F32),
        pltpu.VMEM((rows, padded), BF16),
    ]
    return block_call(
        functools.partial(branch_kernel, pieces[0], len(pieces[1]), stride),
        clips, rows, [x], mods, [pieces], outs, None, scratch,
        12 * count * width * width, [0, None],
    )


def fused_branch_back(x, mods, da, dy, qkv, lse, pieces, clips, stride):
    count, width = x.shape
    rows, strips = count // clips, len(pieces[0])
    head_cols = width // strips
    padded = padded_to(head_cols)
    outs = [shape_of(count, width)] + [shape_of(count, 3 * head_cols) for _ in range(strips)]
    scratch = [
        pltpu.VMEM((rows, padded_to(3 * head_cols)), BF16),
        pltpu.VMEM((rows, padded), BF16),
    ] + [pltpu.VMEM((rows, padded), F32)] * 3
    return block_call(
        functools.partial(branch_back_kernel, pieces[0], len(pieces[1]), stride),
        clips, rows, [x, da, dy, qkv, lse], mods, [pieces], outs, 1, scratch,
        16 * count * width * width, [0, None, 1, 2, 3, 4],
    )


def fused_up(g, mods, pieces, clips):
    count, width = g.shape
    rows, strips = count // clips, len(pieces[0])
    units = sum(part[2] for strip in pieces[0] for part in strip)
    outs = [shape_of(count, units), shape_of(count, units)]
    return block_call(
        functools.partial(up_kernel, pieces[0], len(pieces[1])),
        clips, rows, [g], mods, [pieces], outs, None, [], 2 * count * width * units, [0],
    )


def fused_down(z, y, mods, pieces, clips):
    count, width = y.shape
    rows, strips = count // clips, len(pieces[0])
    outs = [shape_of(count, width), shape_of(count, width)]
    return block_call(
        functools.partial(down_kernel, pieces[0], len(pieces[1])),
        clips, rows, [z, y], mods, [pieces], outs, None, [pltpu.VMEM((z.shape[1], width), BF16)],
        2 * z.size * width, [0, 1, None],
    )


def fused_mlp_back(dx, mods, m, slope, y, a, ups, downs, clips):
    count, width = y.shape
    rows = count // clips
    outs = [
        shape_of(count, width),
        shape_of(*slope.shape),
        shape_of(count, width, dtype=F32),
        shape_of(count, width),
    ]
    return block_call(
        functools.partial(mlp_back_kernel, ups[0], len(ups[1]), downs[0], len(downs[1])),
        clips, rows, [dx, m, slope, y, a], mods, [ups, downs], outs, 4,
        [pltpu.VMEM((slope.shape[1], width), BF16)],
        4 * slope.size * width, [0, None, 1, 2, 3, 4],
    )


def split_frames(v, frames, width):
    return v.reshape(frames, -1, width // HEAD_DIM, HEAD_DIM)


def attend_shared(x, frames):
    width = x.shape[1] // 3
    shaped = x.reshape(frames, -1, 3, width)
    pairs = lax.all_gather(shaped[:, :, 1:], "tp", axis=1, tiled=True)
    q = split_frames(shaped[:, :, 0], frames, width)
    k = split_frames(pairs[:, :, 0], frames, width)
    v = split_frames(pairs[:, :, 1], frames, width)
    scores = jnp.einsum("bqhe,bkhe->bhqk", q, k, preferred_element_type=F32) * SCALE
    chances = jax.nn.softmax(scores, axis=-1)
    result = jnp.einsum("bhqk,bkhe->bqhe", chances.astype(BF16), v, preferred_element_type=F32)
    return result.reshape(-1, width).astype(BF16), (q, k, v, chances)


def attend_shared_back(saved, grad):
    q, k, v, chances = saved
    frames, width = q.shape[0], grad.shape[1]
    grad = split_frames(grad, frames, width)
    grad_chances = jnp.einsum("bqhe,bkhe->bhqk", grad, v, preferred_element_type=F32)
    row_dot = jnp.sum(chances * grad_chances, axis=-1, keepdims=True)
    grad_scores = (chances * (grad_chances - row_dot)).astype(BF16)
    dq = jnp.einsum("bhqk,bkhe->bqhe", grad_scores, k, preferred_element_type=F32) * SCALE
    dk = jnp.einsum("bhqk,bqhe->bkhe", grad_scores, q, preferred_element_type=F32) * SCALE
    dv = jnp.einsum("bhqk,bqhe->bkhe", chances.astype(BF16), grad, preferred_element_type=F32)
    sums = lax.psum_scatter(jnp.stack([dk, dv], axis=2), "tp", scatter_dimension=1, tiled=True)
    parts = jnp.concatenate([dq[:, :, None], sums], axis=2)
    return parts.reshape(-1, 3 * width).astype(BF16)


def normalise(v):
    centred = v - jnp.mean(v, axis=-1, keepdims=True)
    inverse = lax.rsqrt(jnp.mean(centred * centred, axis=-1, keepdims=True) + EPS)
    return centred * inverse, inverse


def modulate(v, shift, scale):
    return (normalise(v)[0] * (1.0 + scale[:, None]) + shift[:, None]).astype(BF16)


def modulate_back(grad, v, scale):
    normed, inverse = normalise(v)
    shift_grad = jnp.sum(grad, axis=1)
    scale_grad = jnp.sum(grad * normed, axis=1)
    scaled = grad * (1.0 + scale[:, None])
    mean_one = jnp.mean(scaled, axis=-1, keepdims=True)
    mean_two = jnp.mean(scaled * normed, axis=-1, keepdims=True)
    return inverse * (scaled - mean_one - normed * mean_two), shift_grad, scale_grad


def gelu(v):
    return jax.nn.gelu(v, approximate=True)


def gelu_slope(v, grad):
    return jax.vjp(gelu, v)[1](grad)[0]


def local(moves, tokens, condition, micro_ids, w_qkv, w_out, w_up, w_down, w_ada, cotangent):
    moves.here()
    n_dp, n_ctx, n_tp = moves.n_dp, moves.n_ctx, moves.n_tp
    clips, frames_here, patches_here, width = tokens.shape
    rows_here, head_cols = w_qkv.shape[2:]
    whole_frames = frames_here % n_tp == 0
    spread_tp = n_tp if whole_frames else 1
    groups = frames_here // spread_tp
    piece = patches_here // n_ctx

    cond_full = condition.astype(F32)
    cond_low = jax.nn.silu(cond_full).astype(BF16)
    cond_all = jnp.concatenate([cond_low, swap_with(cond_low, "dp", n_dp, 1)], axis=0)
    first_row = (moves.dp * n_ctx + moves.ctx) * rows_here
    cond_rows = lax.dynamic_slice_in_dim(cond_all, first_row, rows_here, axis=1)
    ada_low = w_ada.astype(BF16)
    shares = jnp.stack([dot(cond_rows, ada_low[level]) for level in range(LAYERS)], axis=1)

    def total_over_ctx(v):
        got = yield [swap_with(v, "ctx", n_ctx, 2 * k) for k in range(1, n_ctx // 2)]
        return v + sum(got)

    def modulation_vectors():
        sums = shares[:clips] + swap_with(shares[clips:], "dp", n_dp, 1)
        sums = yield from total_over_ctx(sums)
        pairs = [
            [(c * n_tp + t, (c ^ dx) * n_tp + (t ^ r)) for c in range(n_ctx) for t in range(n_tp)]
            for r in range(n_tp)
            for dx in range(2)
        ]
        got = yield [lax.ppermute(sums, ("ctx", "tp"), entry) for entry in pairs[1:]]
        got = [sums] + got
        strips = [got[2 * r] + got[2 * r + 1] for r in range(n_tp)]
        strips = flip_to(jnp.stack(strips, axis=2), 2, n_tp, moves.tp)
        found = strips.reshape(clips, LAYERS, 6, width)
        return [moves.halves(found[:, level]) for level in range(LAYERS)]

    def to_frames(v):
        v = v.reshape(clips, frames_here, n_ctx, piece, width)
        v = flip_to(v, 2, n_ctx, moves.ctx)
        if spread_tp == 1:
            yield ()
            return v.reshape(clips, groups * patches_here, width)
        v = v.reshape(clips, spread_tp, groups, patches_here, width)
        v = flip_to(v, 1, spread_tp, moves.tp)
        got = yield [swap_with(v[:, r], "tp", n_tp, r) for r in range(1, spread_tp)]
        return jnp.stack([v[:, 0]] + got, axis=2).reshape(clips, -1, width)

    def from_frames(v):
        got = ()
        if spread_tp > 1:
            v = v.reshape(clips, groups, spread_tp, patches_here, width)
            got = [swap_with(v[:, :, r], "tp", n_tp, r) for r in range(1, spread_tp)]
        got = yield got
        if spread_tp > 1:
            v = flip_to(jnp.stack([v[:, :, 0]] + got, axis=1), 1, spread_tp, moves.tp)
        v = v.reshape(clips, frames_here, n_ctx, piece, width)
        v = flip_to(v, 2, n_ctx, moves.ctx)
        return v.reshape(clips, frames_here, patches_here, width)

    def trade(get, planes):
        sides = []
        for dx, dr in planes:
            block = get(dx, dr)
            if dx or dr:
                pairs = [
                    (c * n_tp + t, (c ^ dx) * n_tp + (t ^ dr))
                    for c in range(n_ctx)
                    for t in range(n_tp)
                ]
                block = lax.ppermute(block, ("ctx", "tp"), pairs)
            sides.append(block)
        sides = sides[:1] + (yield sides[1:])
        lines = [jnp.stack([v[:, dz] for v in sides], axis=1) for dz in range(n_ctx // 2)]
        got = yield [swap_with(v, "ctx", n_ctx, 2 * dz) for dz, v in enumerate(lines) if dz]
        return jnp.stack(lines[:1] + got, axis=1)

    all_planes = [(dx, dr) for dx in range(2) for dr in range(spread_tp)]
    own_planes = [(0, 0), (1, 0)]

    def frames_to_clips(v):
        v = v.reshape(clips, groups, spread_tp, n_ctx // 2, 2, piece, width)
        got = yield from trade(lambda dx, dr: v[:, :, dr, :, dx].swapaxes(1, 2), all_planes)
        return got.reshape(clips, -1, width)

    def clips_to_frames(v):
        v = v.reshape(clips, n_ctx // 2, 2, spread_tp, groups, piece, width)
        got = yield from trade(lambda dx, dr: v[:, :, dx, dr], all_planes)
        got = got.reshape(clips, n_ctx, spread_tp, groups, piece, width)
        return got.transpose(0, 3, 2, 1, 4, 5).reshape(clips, -1, width)

    def here_to_clips(v):
        v = v.reshape(clips, spread_tp, groups, n_ctx, piece, width)
        v = flip_to(flip_to(v, 3, n_ctx, moves.ctx), 1, spread_tp, moves.tp % spread_tp)
        v = v.reshape(clips, spread_tp, groups, n_ctx // 2, 2, piece, width)
        got = yield from trade(lambda dx, dr: v[:, :, :, :, dx].transpose(0, 3, 1, 2, 4, 5), own_planes)
        return got.reshape(clips, -1, width)

    def clips_to_here(v):
        v = v.reshape(clips, n_ctx // 2, 2, spread_tp, groups, piece, width)
        got = yield from trade(lambda dx, dr: v[:, :, dx], own_planes)
        v = got.reshape(clips, n_ctx, spread_tp, groups, piece, width).transpose(0, 2, 3, 1, 4, 5)
        v = flip_to(flip_to(v, 3, n_ctx, moves.ctx), 1, spread_tp, moves.tp % spread_tp)
        return v.reshape(clips, frames_here, patches_here, width)

    def flat(v):
        return v.reshape(-1, v.shape[-1])

    def shaped(v):
        return v.reshape(clips, -1, v.shape[-1])

    shards = []
    for level in range(LAYERS):
        attention = [w_qkv[level, 0], w_qkv[level, 1], w_qkv[level, 2], w_out[level].T]
        shards.append(jnp.concatenate(attention, axis=1).astype(BF16))
        shards.append(w_up[level].astype(BF16))
        shards.append(w_down[level].T.astype(BF16))
    lanes = Lanes()
    gathers = {}

    blocks = {}

    def gather_far(index):
        blocks[index] = lax.all_gather(shards[index], "ctx", axis=0, tiled=True)

    def set_out(index):
        if index in blocks:
            steps = moves.gather_rest(blocks[index])
        else:
            steps = moves.gather_halves(shards[index])
        gathers[index] = lanes.start(steps)

    plan = [
        ((2,), (), ()),
        ((), (2,), ()),
        ((1,), (), ()),
        ((4,), (), (5,)),
        ((3,), (), ()),
        ((), (3,), ()),
        ((5,), (), ()),
        ((), (5,), ()),
        ((), (), ()),
    ]

    def tick(values=()):
        out, but, far = plan.pop(0)
        held = {index: blocks.get(index, shards[index]) for index in out + far}
        held, values = lanes.fence((held, values), [gathers[index] for index in but])
        for index in out + far:
            if index in blocks:
                blocks[index] = held[index]
            else:
                shards[index] = held[index]
        for index in far:
            gather_far(index)
        for index in out:
            set_out(index)
        return values

    def whole(index):
        layout, arrays = gathers[index].result
        count = len(arrays) // 2
        groups = []
        for group in (arrays[:count], arrays[count:]):
            parts = [
                group[place] if entry is None else group[place][entry]
                for strip in layout
                for place, entry, _ in strip
            ]
            groups.append(jnp.concatenate(parts, axis=1))
        return jnp.concatenate(groups, axis=0)

    def attention_weights(index):
        v = whole(index)
        strips = jnp.split(v, n_tp, axis=1)
        cut = 3 * head_cols
        return [w[:, :cut] for w in strips], jnp.concatenate([w[:, cut:] for w in strips], axis=1)

    def modulations(level):
        return [mods[level][:, i] for i in range(6)]

    gather_far(1)
    gather_far(3)
    set_out(0)
    moved = lanes.start(to_frames(moves.halves(tokens)))
    vectors_task = lanes.start(modulation_vectors())
    tick()
    residual = moved.result
    tick()
    tick()
    mods = vectors_task.result
    fused = (
        whole_frames
        and head_cols % 32 == 0
        and w_up.shape[2] % (2 * LANES) == 0
        and 4 * head_cols == w_up.shape[2]
        and width % 32 == 0
    )
    matched = (micro_ids[:, None] == micro_ids[None, :]).astype(F32)
    share = 1.0 / jnp.sum(matched, axis=1)
    scatters = {}
    mod_grads = [None] * LAYERS

    def start_scatter(level, names, *groups):
        far = level and len(groups) == 1
        steps = (moves.scatter_far if far else moves.scatter_weight)(groups)
        scatters[level, names] = lanes.start(steps)
        return scatters[level, names]

    def scattered(level, name):
        for (at, names), task in scatters.items():
            if at == level and name in names:
                columns = {"qkv": 3 * head_cols, "out": head_cols}
                units = w_up.shape[2]
                low = sum(columns.get(n, units) for n in names[: names.index(name)])
                return task.result[:, low : low + columns.get(name, units)]

    def mod_strip():
        parts = [moves.halves(v).reshape(clips, n_tp, -1) for v in mod_grads]
        parts = flip_to(jnp.stack(parts, axis=2), 1, n_tp, moves.tp)
        parts = yield from total_over_ctx(parts)
        got = yield [swap_with(parts[:, r], "tp", n_tp, r) for r in range(1, n_tp)]
        strip = parts[:, 0] + sum(got)
        got = yield swap_with(strip, "ctx", n_ctx, 1)
        strip = strip + got
        got = yield swap_with(strip, "dp", n_dp, 1)
        return jnp.concatenate([strip, got], axis=0)

    def fused_passes(v):
        vectors, saved = [], []
        for level in range(LAYERS):
            last = share if level == LAYERS - 1 else jnp.ones_like(share)
            last = jnp.broadcast_to(last[:, None, None], (clips, 2, width))
            vectors.append(jnp.concatenate([mods[level], last], axis=1))
        v = flat(v)
        for level in range(LAYERS):
            stride = piece if level % 2 else 1
            joined = gathers[3 * level].result
            kept = fused_branch(v, vectors[level], joined, clips, stride)
            normed, qkv, lse, result, branch, middle, normed_mlp = tick(kept)
            up = gathers[3 * level + 1].result
            act, slope = tick(fused_up(normed_mlp, vectors[level], up, clips))
            down = gathers[3 * level + 2].result
            branch_mlp, after = fused_down(act, middle, vectors[level], down, clips)
            saved.append((v, normed, qkv, lse, result, branch, middle, normed_mlp))
            saved[-1] += (act, slope, branch_mlp, joined, up, down, stride)
            v = after
            if level == 0:
                moved = lanes.start(frames_to_clips(shaped(v)))
                tick()
                late = tick(cotangent)
                turned = lanes.start(here_to_clips(moves.halves(late)))
                v = flat(moved.result)
        finished = lanes.start(clips_to_here(moves.halves(shaped(v))))
        grad = flat(turned.result)
        for level in reversed(range(LAYERS)):
            v, normed, qkv, lse, result, branch, middle, normed_mlp = saved[level][:8]
            act, slope, branch_mlp, joined, up, down, stride = saved[level][8:]
            back = fused_mlp_back(
                grad, vectors[level], branch_mlp, slope, middle, branch, up, down, clips
            )
            late = () if level else (second, third)
            grad_branch, grad_pre, grad_middle, grad_out, sums = lanes.fence(back, late)
            if level:
                first = start_scatter(level, ("down",), (grad_branch, [act]))
                grad_out = lanes.fence(grad_out, (finished,))
            else:
                start_scatter(
                    level, ("down", "up"), (grad_branch, [act]), (normed_mlp, [grad_pre])
                )
                grad_out = lanes.fence(grad_out)
            back = fused_branch_back(
                v, vectors[level], grad_out, grad_middle, qkv, lse, joined, clips, stride
            )
            grad, more, *grad_qkv = lanes.fence(back, (first,) if level else ())
            mod_grads[level] = (sums + more)[:, :6]
            joint = (normed, grad_qkv), (grad_out, [result])
            if level:
                moved = lanes.start(clips_to_frames(shaped(grad)))
                second = start_scatter(level, ("up",), (normed_mlp, [grad_pre]))
                lanes.fence((), (first,))
                third = start_scatter(level, ("qkv", "out"), *joint)
                lanes.fence((), (second,))
                grad = flat(moved.result)
            else:
                start_scatter(level, ("qkv", "out"), *joint)
        return finished, shaped(grad)

    def plain_passes(residual):
        residual = residual.astype(F32)
        records = []
        for level in range(LAYERS):
            spatial = level % 2 == 0
            shift_a, scale_a, gate_a, shift_m, scale_m, gate_m = modulations(level)
            normed = flat(modulate(residual, shift_a, scale_a))
            qkvs, outs = attention_weights(3 * level)
            projected = [dot(normed, v).astype(BF16) for v in qkvs]
            rows, stride = (patches_here * spread_tp, 1) if spatial else (residual.shape[1], piece)
            if spatial and not whole_frames:
                saved = [attend_shared(v, clips * frames_here) for v in projected]
                result = jnp.concatenate([entry[0] for entry in saved], axis=1)
                saved = [entry[1] for entry in saved]
            else:
                result, saved = attend(projected, rows, stride)
            result, saved = tick((result, saved))
            branch = shaped(dot(result, outs, NT))
            middle = residual + gate_a[:, None] * branch
            normed_mlp = flat(modulate(middle, shift_m, scale_m))
            up = whole(3 * level + 1)
            pre_act = dot(normed_mlp, up)
            act = gelu(pre_act).astype(BF16)
            act, pre_act = tick((act, pre_act))
            down = whole(3 * level + 2)
            branch_mlp = shaped(dot(act, down, NT))
            records.append(
                (residual, normed, projected, saved, result, branch, middle, normed_mlp)
                + (pre_act, act, branch_mlp, qkvs, outs, up, down, rows, stride)
            )
            residual = middle + gate_m[:, None] * branch_mlp
            if spatial:
                moved = lanes.start(frames_to_clips(residual.astype(BF16)))
                tick()
                turned = lanes.start(here_to_clips(moves.halves(cotangent)))
                tick()
                residual = moved.result.astype(F32)
        gradient = turned.result.astype(F32) * share[:, None, None]
        finished = lanes.start(clips_to_here(moves.halves(residual.astype(BF16))))
        for level in reversed(range(LAYERS)):
            spatial = level % 2 == 0
            (residual, normed, projected, saved, result, branch, middle, normed_mlp) = records[level][
                :8
            ]
            (pre_act, act, branch_mlp, qkvs, outs, up, down, rows, stride) = records[level][8:]
            shift_a, scale_a, gate_a, shift_m, scale_m, gate_m = modulations(level)
            gate_m_grad = jnp.sum(gradient * branch_mlp, axis=1)
            low_grad = flat((gradient * gate_m[:, None]).astype(BF16))
            grad_pre = gelu_slope(pre_act, dot(low_grad, down)).astype(BF16)
            start_scatter(level, ("down",), (low_grad, [act]))
            grad_pre = lanes.fence(grad_pre)
            grad_normed = shaped(dot(grad_pre, up, NT))
            start_scatter(level, ("up",), (normed_mlp, [grad_pre]))
            grad_normed = lanes.fence(grad_normed)
            added, shift_m_grad, scale_m_grad = modulate_back(grad_normed, middle, scale_m)
            gradient = gradient + added
            gate_a_grad = jnp.sum(gradient * branch, axis=1)
            low_grad = flat((gradient * gate_a[:, None]).astype(BF16))
            grad_heads = dot(low_grad, outs).astype(BF16)
            start_scatter(level, ("out",), (low_grad, [result]))
            grad_heads = lanes.fence(grad_heads)
            if spatial and not whole_frames:
                grad_qkv = [
                    attend_shared_back(v, g)
                    for v, g in zip(saved, jnp.split(grad_heads, n_tp, axis=1))
                ]
            else:
                grad_qkv = attend_back(projected, grad_heads, saved, rows, stride)
            grad_qkv = lanes.fence(grad_qkv)
            start_scatter(level, ("qkv",), (normed, grad_qkv))
            grad_normed = shaped(sum(dot(v, w, NT) for v, w in zip(grad_qkv, qkvs)))
            added, shift_a_grad, scale_a_grad = modulate_back(grad_normed, residual, scale_a)
            gradient = gradient + added
            mod_grads[level] = jnp.stack(
                [shift_a_grad, scale_a_grad, gate_a_grad, shift_m_grad, scale_m_grad, gate_m_grad],
                axis=1,
            )
            if not spatial:
                moved = lanes.start(clips_to_frames(gradient.astype(BF16)))
                lanes.fence()
                lanes.fence()
                gradient = moved.result.astype(F32)
        return finished, gradient

    passes = fused_passes if fused else plain_passes
    finished, gradient = passes(residual)
    hanging = [scatters[key] for key in scatters if key == (0, ("down", "up"))]
    first = [scatters[key] for key in scatters if key == (1, ("down",))]
    second = [scatters[key] for key in scatters if key == (1, ("up",))]
    both = lanes.start(mod_strip())
    gradient = lanes.fence(gradient, (), first)
    gradient = lanes.fence(gradient, hanging)
    gradient = lanes.fence(gradient, (), second)
    moved = lanes.start(from_frames(moves.halves(gradient.astype(BF16))))
    while lanes.tasks:
        lanes.fence(last=True)
    both = both.result
    grad_tokens = moved.result.astype(F32)
    output = finished.result
    grads = [
        (
            scattered(level, "qkv").reshape(rows_here, 3, head_cols).transpose(1, 0, 2),
            scattered(level, "out").T,
            scattered(level, "up"),
            scattered(level, "down").T,
        )
        for level in range(LAYERS)
    ]

    ada_grads = []
    cond_part = 0.0
    for level in range(LAYERS):
        strip = both[:, level]
        ada_grads.append(
            lax.dot_general(cond_rows.astype(F32), strip, TN, precision=HIGHEST)
        )
        cond_part = cond_part + lax.dot_general(
            strip, ada_low[level].astype(F32), NT, precision=HIGHEST
        )
    over_tp = [swap_with(cond_part[:clips], "tp", n_tp, r) for r in range(1, n_tp)]
    over_both = [
        lax.ppermute(
            cond_part[clips:],
            ("dp", "tp"),
            [(d * n_tp + t, (1 - d) * n_tp + (t ^ r)) for d in range(n_dp) for t in range(n_tp)],
        )
        for r in range(n_tp)
    ]
    cond_grad = jnp.stack([cond_part[:clips] + sum(over_tp), sum(over_both)], axis=1)[:, :, None]
    cond_grad = jnp.concatenate([cond_grad, swap_with(cond_grad, "ctx", n_ctx, 1)], axis=2)
    blocks = [cond_grad] + [swap_with(cond_grad, "ctx", n_ctx, 2 * k) for k in range(1, n_ctx // 2)]
    cond_grad = jnp.concatenate(blocks, axis=2)
    cond_grad = flip_to(cond_grad, 2, n_ctx, moves.ctx).reshape(clips, width)
    cond_grad = moves.halves(cond_grad)
    grad_condition = jax.vjp(jax.nn.silu, cond_full)[1](cond_grad)[0]

    stacked = [jnp.stack([grads[level][i] for level in range(LAYERS)]) for i in range(4)]
    return (output, grad_tokens, grad_condition, *stacked, jnp.stack(ada_grads))


def solution(mesh):
    placed = (
        P("dp", "ctx", "tp", None),
        P("dp", None),
        P("dp"),
        P(None, None, ("dp", "ctx"), "tp"),
        P(None, "tp", ("dp", "ctx")),
        P(None, ("dp", "ctx"), "tp"),
        P(None, "tp", ("dp", "ctx")),
        P(None, ("dp", "ctx"), "tp"),
        P("dp", "ctx", "tp", None),
    )
    return jax.shard_map(
        functools.partial(local, Moves(mesh)),
        mesh=mesh,
        in_specs=placed,
        out_specs=(
            P("dp", "ctx", "tp", None),
            P("dp", "ctx", "tp", None),
            P("dp", None),
            P(None, None, ("dp", "ctx"), "tp"),
            P(None, "tp", ("dp", "ctx")),
            P(None, ("dp", "ctx"), "tp"),
            P(None, "tp", ("dp", "ctx")),
            P(None, ("dp", "ctx"), "tp"),
        ),
        check_vma=False,
    )
```

```python
import functools

import jax
import jax.numpy as jnp
from jax import lax
from jax.experimental import pallas as pl
from jax.experimental.pallas import tpu as pltpu
from jax.sharding import PartitionSpec as P

HEAD_DIM = 72
LAYERS = 2
LANES = 128
EPS = 1e-06
SCALE = HEAD_DIM ** (-0.5)
HIGHEST = lax.Precision.HIGHEST
BF16 = jnp.bfloat16
F32 = jnp.float32

NN = (((1,), (0,)), ((), ()))
NT = (((1,), (1,)), ((), ()))
TN = (((0,), (0,)), ((), ()))


def dot(a, b, dims=NN):
    return lax.dot_general(a, b, dims, preferred_element_type=F32)


def swap_with(v, axis_name, n, k):
    return lax.ppermute(v, axis_name, [(i, i ^ k) for i in range(n)])


def flip_to(v, axis, n, me):
    shape = v.shape
    bit = 1
    while bit < n:
        split = shape[:axis] + (n // (2 * bit), 2, bit) + shape[axis + 1 :]
        parts = v.reshape(split)
        first = lax.slice_in_dim(parts, 0, 1, axis=axis + 1)
        second = lax.slice_in_dim(parts, 1, 2, axis=axis + 1)
        turned = jnp.concatenate([second, first], axis=axis + 1)
        v = jnp.where((me & bit) != 0, turned, parts).reshape(shape)
        bit *= 2
    return v


class Moves:
    def __init__(self, mesh):
        self.n_dp = mesh.shape["dp"]
        self.n_ctx = mesh.shape["ctx"]
        self.n_tp = mesh.shape["tp"]
        self.n_line = self.n_ctx // 2

    def here(self):
        self.dp = lax.axis_index("dp")
        self.ctx = lax.axis_index("ctx")
        self.tp = lax.axis_index("tp")
        self.line = self.ctx // 2
        self.side = self.ctx % 2

    def halves(self, v):
        half = v.shape[-1] // 2
        turned = jnp.concatenate([v[..., half:], v[..., :half]], axis=-1)
        return jnp.where(self.dp == 0, v, turned)

    def pair_stack(self, v, other):
        first = jnp.where(self.side == 0, v, other)
        second = jnp.where(self.side == 0, other, v)
        both = jnp.stack([first, second], axis=-3)
        return both.reshape(v.shape[:-3] + (-1, v.shape[-1]))

    def of_side(self, v, side):
        parts = v.reshape(self.n_line, 2, -1, v.shape[-1])
        return lax.dynamic_index_in_dim(parts, side, 1, keepdims=False)

    def over_tp(self, v, r):
        return swap_with(v, "tp", self.n_tp, r)

    def over_side(self, v):
        return swap_with(v, "ctx", self.n_ctx, 1)

    def over_core(self, v):
        return swap_with(v, "dp", self.n_dp, 1)

    def with_core(self, mine, layout):
        return layout, mine + [self.over_core(v) for v in mine]

    def line_gather(self, v):
        return [swap_with(v, "ctx", self.n_ctx, 2 * k) for k in range(1, self.n_line)]

    def line_stack(self, blocks):
        return flip_to(jnp.stack(blocks), 0, self.n_line, self.line)


    def gather_halves(self, v):
        others = range(1, self.n_tp)
        got = yield self.line_gather(v)
        half = v.shape[1] // 2
        lines = [
            self.line_stack([b[:, cut] for b in [v] + got])
            for cut in (slice(0, half), slice(half, None))
        ]
        got = self.over_side(lines[0]), [self.over_tp(lines[1], r) for r in others]
        side_got, tp_got = yield got
        block = self.pair_stack(lines[0], side_got)
        strips = jnp.stack([lines[1]] + tp_got)
        got = [self.over_tp(block, r) for r in others], self.over_side(strips)
        tp_got, side_got = yield got
        mine = [block] + tp_got + [self.pair_stack(strips, side_got)]
        layout = tuple(((r, None, half), (self.n_tp, r, half)) for r in range(self.n_tp))
        return self.with_core(mine, layout)

    def gather_rest(self, block):
        got = yield [self.over_tp(block, r) for r in range(1, self.n_tp)]
        layout = tuple(((r, None, block.shape[1]),) for r in range(self.n_tp))
        return self.with_core([block] + got, layout)

    def scatter_core(self, groups):
        halves = [(v[:, : v.shape[1] // 2], v[:, v.shape[1] // 2 :]) for v, _ in groups]
        got = yield [
            [self.over_core(dot(theirs, v, TN).astype(BF16)) for v in rights]
            for (_, theirs), (_, rights) in zip(halves, groups)
        ]
        found = []
        for (mine, _), (_, rights), came in zip(halves, groups, got):
            totals = [
                (dot(mine, v, TN) + g.astype(F32)).astype(BF16) for v, g in zip(rights, came)
            ]
            if len(totals) == 1:
                totals = jnp.split(totals[0], self.n_tp, axis=1)
            found.append(totals)
        return found

    def scatter_far(self, groups):
        found = yield from self.scatter_core(groups)
        totals = [
            jnp.concatenate([v[r] for v in found], axis=1) if len(found) > 1 else found[0][r]
            for r in range(self.n_tp)
        ]
        got = yield [self.over_tp(totals[r], r) for r in range(1, self.n_tp)]
        total = (totals[0].astype(F32) + sum(v.astype(F32) for v in got)).astype(BF16)
        shard = yield Rest(lax.psum_scatter(total, "ctx", scatter_dimension=0, tiled=True))
        return shard.astype(F32)

    def scatter_weight(self, groups):
        others = range(1, self.n_tp)
        found = yield from self.scatter_core(groups)
        sizes = [v[0].shape[1] for v in found]
        half = max(sum(sizes) // 2 // LANES, 1) * LANES
        firsts, seconds = [[] for _ in range(self.n_tp)], []
        for r in range(self.n_tp):
            low = 0
            for v, size in zip(found, sizes):
                cut = min(max(half - low, 0), size)
                if cut:
                    firsts[r].append(v[r][:, :cut])
                if cut < size:
                    seconds.append(v[r][:, cut:])
                low += size
        firsts = [jnp.concatenate(v, axis=1) if len(v) > 1 else v[0] for v in firsts]

        def of_side(side):
            return jnp.concatenate([self.of_side(v, side) for v in seconds], axis=-1)

        got = [self.over_tp(firsts[r], r) for r in others], self.over_side(of_side(1 - self.side))
        tp_got, side_got = yield got
        first = (firsts[0].astype(F32) + sum(v.astype(F32) for v in tp_got)).astype(BF16)
        second = of_side(self.side).astype(F32) + side_got.astype(F32)
        second = jnp.split(second.astype(BF16), self.n_tp, axis=-1)
        got = (
            self.over_side(self.of_side(first, 1 - self.side)),
            [self.over_tp(second[r], r) for r in others],
        )
        side_got, tp_got = yield got
        first = self.of_side(first, self.side).astype(F32) + side_got.astype(F32)
        second = second[0].astype(F32) + sum(v.astype(F32) for v in tp_got)
        line = jnp.concatenate([first, second], axis=-1).astype(BF16)
        got = yield [
            swap_with(
                lax.dynamic_index_in_dim(line, self.line ^ k, 0, keepdims=False),
                "ctx",
                self.n_ctx,
                2 * k,
            )
            for k in range(1, self.n_line)
        ]
        own = lax.dynamic_index_in_dim(line, self.line, 0, keepdims=False)
        return own.astype(F32) + sum(v.astype(F32) for v in got)


class Rest:
    def __init__(self, value):
        self.value = value


class Task:
    def __init__(self, steps):
        self.steps, self.result = steps, None
        self.take(next(steps))

    def take(self, pending):
        self.resting = isinstance(pending, Rest)
        self.pending = pending.value if self.resting else pending


def at_once(steps):
    pending = next(steps)
    while True:
        try:
            pending = steps.send(pending)
        except StopIteration as stop:
            return stop.value


class Lanes:
    def __init__(self):
        self.tasks = []

    def start(self, steps):
        task = Task(steps)
        self.tasks.append(task)
        return task

    def fence(self, values=(), but=(), also=(), last=False):
        due = [t for t in self.tasks if t not in but and (last or not t.resting or t in also)]
        values, pending = lax.optimization_barrier((values, [t.pending for t in due]))
        going = [t for t in self.tasks if t not in due]
        for task, done in zip(due, pending):
            try:
                task.take(task.steps.send(done))
                going.append(task)
            except StopIteration as stop:
                task.result = stop.value
        self.tasks = going
        return values


def window(head):
    start = head * HEAD_DIM
    return start // LANES * LANES, -(-(start + HEAD_DIM) // LANES) * LANES


def in_head(head, rows, low, high):
    lanes = lax.broadcasted_iota(jnp.int32, (rows, high - low), 1) + low
    return (lanes >= head * HEAD_DIM) & (lanes < (head + 1) * HEAD_DIM)


def spread_parts(x_ref, offset, parts, width):
    for index, part in enumerate(parts):
        padded = part.shape[1]
        start = offset + index * width
        if padded != width:
            part[:, padded - LANES :] = jnp.zeros((part.shape[0], LANES), part.dtype)
        part[:, :width] = x_ref[:, start : start + width]


def same_sequence(rows, stride):
    row = lax.broadcasted_iota(jnp.int32, (rows, rows), 0)
    column = lax.broadcasted_iota(jnp.int32, (rows, rows), 1)
    return lax.rem(row, stride) == lax.rem(column, stride)


def attend_kernel(count, width, stride, *refs):
    x_refs, (o_ref, lse_ref, q_s, k_s, v_s, o_s) = refs[:count], refs[count:]
    heads, rows = width // HEAD_DIM, o_ref.shape[0]
    lane = lax.broadcasted_iota(jnp.int32, (rows, LANES), 1)
    logs = jnp.zeros((rows, LANES), F32)
    if stride > 1:
        allowed = same_sequence(rows, stride)
    for index, x_ref in enumerate(x_refs):
        spread_parts(x_ref, 0, (q_s, k_s, v_s), width)
        for head in range(heads):
            low, high = window(head)
            mask = in_head(head, rows, low, high)
            queries = jnp.where(mask, q_s[:, low:high], jnp.zeros((), BF16))
            scores = dot(queries, k_s[:, low:high], NT) * SCALE
            if stride > 1:
                scores = jnp.where(allowed, scores, -jnp.inf)
            largest = jnp.max(scores, axis=-1, keepdims=True)
            raised = jnp.exp(scores - largest)
            total = jnp.sum(raised, axis=-1, keepdims=True)
            chances = (raised * (1.0 / total)).astype(BF16)
            result = dot(chances, v_s[:, low:high])
            o_s[:, low:high] = jnp.where(mask, result, o_s[:, low:high])
            logs = jnp.where(lane == index * heads + head, largest + jnp.log(total), logs)
        o_ref[:, index * width : (index + 1) * width] = o_s[:, :width].astype(BF16)
    lse_ref[...] = logs


def attend_back_kernel(count, width, stride, *refs):
    x_refs, (g_ref, lse_ref), dx_refs = refs[:count], refs[count : count + 2], refs[count + 2 : -7]
    q_s, k_s, v_s, g_s, dq_s, dk_s, dv_s = refs[-7:]
    heads, rows = width // HEAD_DIM, g_ref.shape[0]
    if stride > 1:
        allowed = same_sequence(rows, stride)
    for index, x_ref in enumerate(x_refs):
        spread_parts(x_ref, 0, (q_s, k_s, v_s), width)
        spread_parts(g_ref, index * width, (g_s,), width)
        for head in range(heads):
            low, high = window(head)
            mask = in_head(head, rows, low, high)
            zero = jnp.zeros((), BF16)
            q, k, v, g = q_s[:, low:high], k_s[:, low:high], v_s[:, low:high], g_s[:, low:high]
            scores = dot(jnp.where(mask, q, zero), k, NT) * SCALE
            if stride > 1:
                scores = jnp.where(allowed, scores, -jnp.inf)
            place = index * heads + head
            chances = jnp.exp(scores - lse_ref[:, place : place + 1])
            grad_chances = dot(jnp.where(mask, g, zero), v, NT)
            row_dot = jnp.sum(chances * grad_chances, axis=-1, keepdims=True)
            grad_scores = (chances * (grad_chances - row_dot)).astype(BF16)
            dq = dot(grad_scores, k) * SCALE
            dk = dot(grad_scores, q, TN) * SCALE
            dv = dot(chances.astype(BF16), g, TN)
            dq_s[:, low:high] = jnp.where(mask, dq, dq_s[:, low:high])
            dk_s[:, low:high] = jnp.where(mask, dk, dk_s[:, low:high])
            dv_s[:, low:high] = jnp.where(mask, dv, dv_s[:, low:high])
        for part_index, part in enumerate((dq_s, dk_s, dv_s)):
            start = part_index * width
            dx_refs[index][:, start : start + width] = part[:, :width].astype(BF16)


def row_block(rows, columns):
    return pl.BlockSpec((rows, columns), lambda i: (i, 0))


def attend(xs, rows, stride):
    count, width = xs[0].shape[0], xs[0].shape[1] // 3
    strips = len(xs)
    heads = strips * width // HEAD_DIM
    padded = -(-width // LANES) * LANES
    return pl.pallas_call(
        functools.partial(attend_kernel, strips, width, stride),
        grid=(count // rows,),
        in_specs=[row_block(rows, 3 * width)] * strips,
        out_specs=[row_block(rows, strips * width), row_block(rows, LANES)],
        out_shape=[
            jax.ShapeDtypeStruct((count, strips * width), BF16),
            jax.ShapeDtypeStruct((count, LANES), F32),
        ],
        scratch_shapes=[pltpu.VMEM((rows, padded), BF16)] * 3 + [pltpu.VMEM((rows, padded), F32)],
        cost_estimate=pl.CostEstimate(
            flops=heads * count * rows * 1024,
            bytes_accessed=count * width * strips * 8,
            transcendentals=heads * count * rows,
        ),
        compiler_params=pltpu.CompilerParams(vmem_limit_bytes=32 * 1024 * 1024),
    )(*xs)


def attend_back(xs, grad, lse, rows, stride):
    count, width = xs[0].shape[0], xs[0].shape[1] // 3
    strips = len(xs)
    heads = strips * width // HEAD_DIM
    padded = -(-width // LANES) * LANES
    return pl.pallas_call(
        functools.partial(attend_back_kernel, strips, width, stride),
        grid=(count // rows,),
        in_specs=[row_block(rows, 3 * width)] * strips
        + [row_block(rows, strips * width), row_block(rows, LANES)],
        out_specs=[row_block(rows, 3 * width)] * strips,
        out_shape=[jax.ShapeDtypeStruct((count, 3 * width), BF16)] * strips,
        scratch_shapes=[pltpu.VMEM((rows, padded), BF16)] * 4
        + [pltpu.VMEM((rows, padded), F32)] * 3,
        cost_estimate=pl.CostEstimate(
            flops=heads * count * rows * 2560,
            bytes_accessed=count * width * strips * 14,
            transcendentals=heads * count * rows,
        ),
        compiler_params=pltpu.CompilerParams(vmem_limit_bytes=32 * 1024 * 1024),
    )(*xs, grad, lse)


def weight_scratch(pieces):
    layout, arrays = pieces
    columns = sum(part[2] for strip in layout for part in strip)
    parts = max(len(strip) for strip in layout)
    return [
        pltpu.VMEM((2 * arrays[0].shape[-2], columns), BF16),
        pltpu.SemaphoreType.DMA((2, len(layout), parts)),
    ]


def weight_copies(layout, refs, w_s, sems):
    count = len(refs) // 2
    rows = w_s.shape[0] // 2
    copies = [[] for _ in layout]
    for group in range(2):
        low = 0
        for strip, parts in enumerate(layout):
            for part, (place, entry, columns) in enumerate(parts):
                source = refs[group * count + place]
                if entry is not None:
                    source = source.at[entry]
                target = w_s.at[pl.ds(group * rows, rows), pl.ds(low, columns)]
                low += columns
                copies[strip].append(
                    pltpu.make_async_copy(source, target, sems.at[group, strip, part])
                )
    return copies


def await_copies(copies):
    @pl.when(pl.program_id(0) == 0)
    def _():
        for copy in copies:
            copy.wait()


def turn_copies(copies, w_s, t_s):
    @pl.when(pl.program_id(0) == 0)
    def _():
        size = w_s.shape[1] // len(copies) // 2
        for strip, waits in enumerate(copies):
            for copy in waits:
                copy.wait()
            for low in (2 * strip * size, (2 * strip + 1) * size):
                t_s[low : low + size] = w_s[:, low : low + size].T


def begin_copies(*many):
    @pl.when(pl.program_id(0) == 0)
    def _():
        for copies in many:
            for strip in copies:
                for copy in strip:
                    copy.start()


def row_normal(v):
    centred = v - jnp.mean(v, axis=-1, keepdims=True)
    inverse = lax.rsqrt(jnp.mean(centred * centred, axis=-1, keepdims=True) + EPS)
    return centred * inverse, inverse


def row_back(grad, normed, inverse, scale):
    scaled = grad * (1.0 + scale)
    mean_one = jnp.mean(scaled, axis=-1, keepdims=True)
    mean_two = jnp.mean(scaled * normed, axis=-1, keepdims=True)
    return inverse * (scaled - mean_one - normed * mean_two)


def head_forward(heads, first, rows, allowed, q_s, k_s, v_s, o_s, lane, logs):
    for head in range(heads):
        low, high = window(head)
        mask = in_head(head, rows, low, high)
        queries = jnp.where(mask, q_s[:, low:high], jnp.zeros((), BF16))
        scores = dot(queries, k_s[:, low:high], NT) * SCALE
        if allowed is not None:
            scores = jnp.where(allowed, scores, -jnp.inf)
        largest = jnp.max(scores, axis=-1, keepdims=True)
        raised = jnp.exp(scores - largest)
        total = jnp.sum(raised, axis=-1, keepdims=True)
        chances = (raised * (1.0 / total)).astype(BF16)
        result = dot(chances, v_s[:, low:high])
        o_s[:, low:high] = jnp.where(mask, result, o_s[:, low:high])
        logs = jnp.where(lane == first + head, largest + jnp.log(total), logs)
    return logs


def head_back(heads, first, rows, allowed, q_s, k_s, v_s, g_s, lse_ref, dq_s, dk_s, dv_s):
    zero = jnp.zeros((), BF16)
    for head in range(heads):
        low, high = window(head)
        mask = in_head(head, rows, low, high)
        q, k, v, g = q_s[:, low:high], k_s[:, low:high], v_s[:, low:high], g_s[:, low:high]
        scores = dot(jnp.where(mask, q, zero), k, NT) * SCALE
        if allowed is not None:
            scores = jnp.where(allowed, scores, -jnp.inf)
        place = first + head
        chances = jnp.exp(scores - lse_ref[:, place : place + 1])
        grad_chances = dot(jnp.where(mask, g, zero), v, NT)
        row_dot = jnp.sum(chances * grad_chances, axis=-1, keepdims=True)
        grad_scores = (chances * (grad_chances - row_dot)).astype(BF16)
        dq = dot(grad_scores, k) * SCALE
        dk = dot(grad_scores, q, TN) * SCALE
        dv = dot(chances.astype(BF16), g, TN)
        dq_s[:, low:high] = jnp.where(mask, dq, dq_s[:, low:high])
        dk_s[:, low:high] = jnp.where(mask, dk, dk_s[:, low:high])
        dv_s[:, low:high] = jnp.where(mask, dv, dv_s[:, low:high])


def branch_kernel(layout, count, stride, x_ref, mod_ref, *refs):
    strips = len(layout)
    w_refs = refs[:count]
    h_ref, qkv_ref, lse_ref, o_ref, a_ref, y_ref, g_ref = refs[count : count + 7]
    w_s, sems, p_s, o_s, z_s = refs[count + 7 :]
    rows, width = x_ref.shape
    head_cols = width // strips
    padded = o_s.shape[1]
    spare = padded - head_cols
    columns = w_s.shape[1] // strips
    copies = weight_copies(layout, w_refs, w_s, sems)
    begin_copies(copies)
    x = x_ref[...].astype(F32)
    shift_a, scale_a, gate_a, shift_m, scale_m = [mod_ref[0, i : i + 1, :] for i in range(5)]
    h = (row_normal(x)[0] * (1.0 + scale_a) + shift_a).astype(BF16)
    h_ref[...] = h
    heads = head_cols // HEAD_DIM
    lane = lax.broadcasted_iota(jnp.int32, (rows, LANES), 1)
    logs = jnp.zeros((rows, LANES), F32)
    allowed = same_sequence(rows, stride) if stride > 1 else None
    branch = jnp.zeros((rows, width), F32)
    for strip in range(strips):
        start = strip * columns
        await_copies(copies[strip])
        p_s[...] = dot(h, w_s[:, start : start + p_s.shape[1]]).astype(BF16)
        parts = []
        for index in range(3):
            low = (3 * strip + index) * padded
            if spare:
                qkv_ref[:, low + padded - LANES : low + padded] = jnp.zeros((rows, LANES), BF16)
            qkv_ref[:, low : low + head_cols] = p_s[:, index * head_cols : (index + 1) * head_cols]
            parts.append(qkv_ref.at[:, pl.ds(low, padded)])
        logs = head_forward(heads, strip * heads, rows, allowed, *parts, o_s, lane, logs)
        low = o_s[:, :head_cols].astype(BF16)
        o_ref[:, strip * head_cols : (strip + 1) * head_cols] = low
        if spare:
            z_s[:, :LANES] = jnp.zeros((rows, LANES), BF16)
        z_s[:, spare:] = low
        branch = branch + dot(z_s[...], w_s[:, start + columns - padded : start + columns], NT)
    lse_ref[...] = logs
    a_ref[...] = branch.astype(BF16)
    y = x + gate_a * branch
    y_ref[...] = y
    g_ref[...] = (row_normal(y)[0] * (1.0 + scale_m) + shift_m).astype(BF16)


def branch_back_kernel(
    layout, count, stride, x_ref, mod_ref, da_ref, dy_ref, qkv_ref, lse_ref, *refs
):
    strips = len(layout)
    w_refs = refs[:count]
    dx_ref, sums_ref = refs[count : count + 2]
    out_refs = refs[count + 2 : count + 2 + strips]
    w_s, sems, d_s, g_s, dq_s, dk_s, dv_s = refs[count + 2 + strips :]
    rows, width = x_ref.shape
    head_cols = width // strips
    padded = g_s.shape[1]
    spare = padded - head_cols
    columns = w_s.shape[1] // strips
    copies = weight_copies(layout, w_refs, w_s, sems)
    begin_copies(copies)
    heads = head_cols // HEAD_DIM
    allowed = same_sequence(rows, stride) if stride > 1 else None
    grad = jnp.zeros((rows, width), F32)
    for strip in range(strips):
        start = strip * columns
        await_copies(copies[strip])
        turned = dot(da_ref[...], w_s[:, start + columns - padded : start + columns]).astype(BF16)
        if spare:
            g_s[:, padded - LANES :] = jnp.zeros((rows, LANES), BF16)
        g_s[:, :head_cols] = turned[:, spare:]
        parts = [qkv_ref.at[:, pl.ds((3 * strip + i) * padded, padded)] for i in range(3)]
        head_back(heads, strip * heads, rows, allowed, *parts, g_s, lse_ref, dq_s, dk_s, dv_s)
        if d_s.shape[1] != 3 * head_cols:
            d_s[:, d_s.shape[1] - LANES :] = jnp.zeros((rows, LANES), BF16)
        for index, part in enumerate((dq_s, dk_s, dv_s)):
            d_s[:, index * head_cols : (index + 1) * head_cols] = part[:, :head_cols].astype(BF16)
        out_refs[strip][...] = d_s[:, : 3 * head_cols]
        grad = grad + dot(d_s[...], w_s[:, start : start + d_s.shape[1]], NT)
    scale_a = mod_ref[0, 1:2, :]
    normed, inverse = row_normal(x_ref[...].astype(F32))
    sums_ref[...] = jnp.zeros(sums_ref.shape, F32)
    sums_ref[0, 0:1, :] = jnp.sum(grad, axis=0, keepdims=True)
    sums_ref[0, 1:2, :] = jnp.sum(grad * normed, axis=0, keepdims=True)
    dx_ref[...] = (dy_ref[...] + row_back(grad, normed, inverse, scale_a)).astype(BF16)


GELU_A = 0.7978845608028654
GELU_B = 0.044715


def up_kernel(layout, count, g_ref, *refs):
    strips = len(layout)
    z_ref, slope_ref, w_s, sems = refs[count:]
    copies = weight_copies(layout, refs[:count], w_s, sems)
    begin_copies(copies)
    half = w_s.shape[1] // (2 * strips)
    g = g_ref[...]
    for index in range(2 * strips):
        if index % 2 == 0:
            await_copies(copies[index // 2])
        low = index * half
        u = dot(g, w_s[:, low : low + half])
        square = u * u
        bent = jnp.tanh(u * (GELU_A + GELU_A * GELU_B * square))
        lifted = 0.5 * (1.0 + bent)
        z_ref[:, low : low + half] = (u * lifted).astype(BF16)
        inner = GELU_A + 3.0 * GELU_A * GELU_B * square
        slope = lifted + 0.5 * u * (1.0 - bent * bent) * inner
        slope_ref[:, low : low + half] = slope.astype(BF16)


def down_kernel(layout, count, z_ref, y_ref, mod_ref, *refs):
    strips = len(layout)
    m_ref, x_ref, w_s, sems, t_s = refs[count:]
    copies = weight_copies(layout, refs[:count], w_s, sems)
    begin_copies(copies)
    turn_copies(copies, w_s, t_s)
    total = dot(z_ref[...], t_s[...])
    m_ref[...] = total.astype(BF16)
    x_ref[...] = (y_ref[...] + mod_ref[0, 5:6, :] * total).astype(BF16)


def mlp_back_kernel(
    up_layout, ups_count, down_layout, count, dx_ref, mod_ref, m_ref, slope_ref, y_ref, a_ref, *refs
):
    strips = len(up_layout)
    (dm_ref, du_ref, dy_ref, da_ref, sums_ref, up_s, up_sems, down_s, down_sems, t_s) = refs[
        ups_count + count :
    ]
    ups = weight_copies(up_layout, refs[:ups_count], up_s, up_sems)
    downs = weight_copies(down_layout, refs[ups_count : ups_count + count], down_s, down_sems)
    begin_copies(downs, ups)
    half = up_s.shape[1] // (2 * strips)
    turn_copies(ups, up_s, t_s)
    scale_m, gate_m, share, gate_a = [mod_ref[0, i : i + 1, :] for i in (4, 5, 6, 2)]
    dx = dx_ref[...].astype(F32) * share
    sums_ref[...] = jnp.zeros(sums_ref.shape, F32)
    sums_ref[0, 5:6, :] = jnp.sum(dx * m_ref[...].astype(F32), axis=0, keepdims=True)
    dm = (gate_m * dx).astype(BF16)
    dm_ref[...] = dm
    grad = jnp.zeros(y_ref.shape, F32)
    for index in range(2 * strips):
        low = index * half
        if index % 2 == 0:
            await_copies(downs[index // 2])
        dz = dot(dm, down_s[:, low : low + half])
        du = (dz * slope_ref[:, low : low + half].astype(F32)).astype(BF16)
        du_ref[:, low : low + half] = du
        grad = grad + dot(du, t_s[low : low + half])
    normed, inverse = row_normal(y_ref[...])
    sums_ref[0, 3:4, :] = jnp.sum(grad, axis=0, keepdims=True)
    sums_ref[0, 4:5, :] = jnp.sum(grad * normed, axis=0, keepdims=True)
    dy = dx + row_back(grad, normed, inverse, scale_m)
    dy_ref[...] = dy
    sums_ref[0, 2:3, :] = jnp.sum(dy * a_ref[...].astype(F32), axis=0, keepdims=True)
    da_ref[...] = (gate_a * dy).astype(BF16)


def shape_of(*dims, dtype=BF16):
    return jax.ShapeDtypeStruct(dims, dtype)


def block_call(kernel, clips, rows, arrays, mods, weights, outs, sums, scratch, flops, order):
    operands, specs = [], []
    for v in order:
        if v is None:
            operands.append(mods)
            specs.append(pl.BlockSpec((1,) + mods.shape[1:], lambda i: (i, 0, 0)))
        else:
            operands.append(arrays[v])
            specs.append(row_block(rows, arrays[v].shape[1]))
    for _, pieces in weights:
        operands += pieces
        specs += [pl.BlockSpec(memory_space=pl.ANY)] * len(pieces)
    out_specs = [row_block(rows, v.shape[1]) for v in outs]
    out_shape = list(outs)
    if sums is not None:
        width = mods.shape[2]
        out_specs.insert(sums, pl.BlockSpec((1, 8, width), lambda i: (i, 0, 0)))
        out_shape.insert(sums, shape_of(clips, 8, width, dtype=F32))
    held = []
    for pieces in weights:
        held += weight_scratch(pieces)
    moved = sum(v.size * v.dtype.itemsize for v in operands)
    return pl.pallas_call(
        kernel,
        grid=(clips,),
        in_specs=specs,
        out_specs=out_specs,
        out_shape=out_shape,
        scratch_shapes=held + scratch,
        cost_estimate=pl.CostEstimate(
            flops=flops // 32, bytes_accessed=moved // 32, transcendentals=0
        ),
        compiler_params=pltpu.CompilerParams(vmem_limit_bytes=60 * 1024 * 1024),
    )(*operands)


def padded_to(columns):
    return -(-columns // LANES) * LANES


def fused_branch(x, mods, pieces, clips, stride):
    count, width = x.shape
    rows, strips = count // clips, len(pieces[0])
    head_cols = width // strips
    padded = padded_to(head_cols)
    outs = [
        shape_of(count, width),
        shape_of(count, 3 * strips * padded),
        shape_of(count, LANES, dtype=F32),
        shape_of(count, width),
        shape_of(count, width),
        shape_of(count, width, dtype=F32),
        shape_of(count, width),
    ]
    scratch = [
        pltpu.VMEM((rows, padded_to(3 * head_cols)), BF16),
        pltpu.VMEM((rows, padded), F32),
        pltpu.VMEM((rows, padded), BF16),
    ]
    return block_call(
        functools.partial(branch_kernel, pieces[0], len(pieces[1]), stride),
        clips, rows, [x], mods, [pieces], outs, None, scratch,
        12 * count * width * width, [0, None],
    )


def fused_branch_back(x, mods, da, dy, qkv, lse, pieces, clips, stride):
    count, width = x.shape
    rows, strips = count // clips, len(pieces[0])
    head_cols = width // strips
    padded = padded_to(head_cols)
    outs = [shape_of(count, width)] + [shape_of(count, 3 * head_cols) for _ in range(strips)]
    scratch = [
        pltpu.VMEM((rows, padded_to(3 * head_cols)), BF16),
        pltpu.VMEM((rows, padded), BF16),
    ] + [pltpu.VMEM((rows, padded), F32)] * 3
    return block_call(
        functools.partial(branch_back_kernel, pieces[0], len(pieces[1]), stride),
        clips, rows, [x, da, dy, qkv, lse], mods, [pieces], outs, 1, scratch,
        16 * count * width * width, [0, None, 1, 2, 3, 4],
    )


def fused_up(g, mods, pieces, clips):
    count, width = g.shape
    rows, strips = count // clips, len(pieces[0])
    units = sum(part[2] for strip in pieces[0] for part in strip)
    outs = [shape_of(count, units), shape_of(count, units)]
    return block_call(
        functools.partial(up_kernel, pieces[0], len(pieces[1])),
        clips, rows, [g], mods, [pieces], outs, None, [], 2 * count * width * units, [0],
    )


def fused_down(z, y, mods, pieces, clips):
    count, width = y.shape
    rows, strips = count // clips, len(pieces[0])
    outs = [shape_of(count, width), shape_of(count, width)]
    return block_call(
        functools.partial(down_kernel, pieces[0], len(pieces[1])),
        clips, rows, [z, y], mods, [pieces], outs, None, [pltpu.VMEM((z.shape[1], width), BF16)],
        2 * z.size * width, [0, 1, None],
    )


def fused_mlp_back(dx, mods, m, slope, y, a, ups, downs, clips):
    count, width = y.shape
    rows = count // clips
    outs = [
        shape_of(count, width),
        shape_of(*slope.shape),
        shape_of(count, width, dtype=F32),
        shape_of(count, width),
    ]
    return block_call(
        functools.partial(mlp_back_kernel, ups[0], len(ups[1]), downs[0], len(downs[1])),
        clips, rows, [dx, m, slope, y, a], mods, [ups, downs], outs, 4,
        [pltpu.VMEM((slope.shape[1], width), BF16)],
        4 * slope.size * width, [0, None, 1, 2, 3, 4],
    )


def split_frames(v, frames, width):
    return v.reshape(frames, -1, width // HEAD_DIM, HEAD_DIM)


def attend_shared(x, frames):
    width = x.shape[1] // 3
    shaped = x.reshape(frames, -1, 3, width)
    pairs = lax.all_gather(shaped[:, :, 1:], "tp", axis=1, tiled=True)
    q = split_frames(shaped[:, :, 0], frames, width)
    k = split_frames(pairs[:, :, 0], frames, width)
    v = split_frames(pairs[:, :, 1], frames, width)
    scores = jnp.einsum("bqhe,bkhe->bhqk", q, k, preferred_element_type=F32) * SCALE
    chances = jax.nn.softmax(scores, axis=-1)
    result = jnp.einsum("bhqk,bkhe->bqhe", chances.astype(BF16), v, preferred_element_type=F32)
    return result.reshape(-1, width).astype(BF16), (q, k, v, chances)


def attend_shared_back(saved, grad):
    q, k, v, chances = saved
    frames, width = q.shape[0], grad.shape[1]
    grad = split_frames(grad, frames, width)
    grad_chances = jnp.einsum("bqhe,bkhe->bhqk", grad, v, preferred_element_type=F32)
    row_dot = jnp.sum(chances * grad_chances, axis=-1, keepdims=True)
    grad_scores = (chances * (grad_chances - row_dot)).astype(BF16)
    dq = jnp.einsum("bhqk,bkhe->bqhe", grad_scores, k, preferred_element_type=F32) * SCALE
    dk = jnp.einsum("bhqk,bqhe->bkhe", grad_scores, q, preferred_element_type=F32) * SCALE
    dv = jnp.einsum("bhqk,bqhe->bkhe", chances.astype(BF16), grad, preferred_element_type=F32)
    sums = lax.psum_scatter(jnp.stack([dk, dv], axis=2), "tp", scatter_dimension=1, tiled=True)
    parts = jnp.concatenate([dq[:, :, None], sums], axis=2)
    return parts.reshape(-1, 3 * width).astype(BF16)


def normalise(v):
    centred = v - jnp.mean(v, axis=-1, keepdims=True)
    inverse = lax.rsqrt(jnp.mean(centred * centred, axis=-1, keepdims=True) + EPS)
    return centred * inverse, inverse


def modulate(v, shift, scale):
    return (normalise(v)[0] * (1.0 + scale[:, None]) + shift[:, None]).astype(BF16)


def modulate_back(grad, v, scale):
    normed, inverse = normalise(v)
    shift_grad = jnp.sum(grad, axis=1)
    scale_grad = jnp.sum(grad * normed, axis=1)
    scaled = grad * (1.0 + scale[:, None])
    mean_one = jnp.mean(scaled, axis=-1, keepdims=True)
    mean_two = jnp.mean(scaled * normed, axis=-1, keepdims=True)
    return inverse * (scaled - mean_one - normed * mean_two), shift_grad, scale_grad


def gelu(v):
    return jax.nn.gelu(v, approximate=True)


def gelu_slope(v, grad):
    return jax.vjp(gelu, v)[1](grad)[0]


def local(moves, tokens, condition, micro_ids, w_qkv, w_out, w_up, w_down, w_ada, cotangent):
    moves.here()
    n_dp, n_ctx, n_tp = moves.n_dp, moves.n_ctx, moves.n_tp
    clips, frames_here, patches_here, width = tokens.shape
    rows_here, head_cols = w_qkv.shape[2:]
    whole_frames = frames_here % n_tp == 0
    spread_tp = n_tp if whole_frames else 1
    groups = frames_here // spread_tp
    piece = patches_here // n_ctx

    cond_full = condition.astype(F32)
    cond_low = jax.nn.silu(cond_full).astype(BF16)
    cond_all = jnp.concatenate([cond_low, swap_with(cond_low, "dp", n_dp, 1)], axis=0)
    first_row = (moves.dp * n_ctx + moves.ctx) * rows_here
    cond_rows = lax.dynamic_slice_in_dim(cond_all, first_row, rows_here, axis=1)
    ada_low = w_ada.astype(BF16)
    shares = jnp.stack([dot(cond_rows, ada_low[level]) for level in range(LAYERS)], axis=1)

    def total_over_ctx(v):
        got = yield [swap_with(v, "ctx", n_ctx, 2 * k) for k in range(1, n_ctx // 2)]
        return v + sum(got)

    def modulation_vectors():
        sums = shares[:clips] + swap_with(shares[clips:], "dp", n_dp, 1)
        sums = yield from total_over_ctx(sums)
        pairs = [
            [(c * n_tp + t, (c ^ dx) * n_tp + (t ^ r)) for c in range(n_ctx) for t in range(n_tp)]
            for r in range(n_tp)
            for dx in range(2)
        ]
        got = yield [lax.ppermute(sums, ("ctx", "tp"), entry) for entry in pairs[1:]]
        got = [sums] + got
        strips = [got[2 * r] + got[2 * r + 1] for r in range(n_tp)]
        strips = flip_to(jnp.stack(strips, axis=2), 2, n_tp, moves.tp)
        found = strips.reshape(clips, LAYERS, 6, width)
        return [moves.halves(found[:, level]) for level in range(LAYERS)]

    def to_frames(v):
        v = v.reshape(clips, frames_here, n_ctx, piece, width)
        v = flip_to(v, 2, n_ctx, moves.ctx)
        if spread_tp == 1:
            yield ()
            return v.reshape(clips, groups * patches_here, width)
        v = v.reshape(clips, spread_tp, groups, patches_here, width)
        v = flip_to(v, 1, spread_tp, moves.tp)
        got = yield [swap_with(v[:, r], "tp", n_tp, r) for r in range(1, spread_tp)]
        return jnp.stack([v[:, 0]] + got, axis=2).reshape(clips, -1, width)

    def from_frames(v):
        got = ()
        if spread_tp > 1:
            v = v.reshape(clips, groups, spread_tp, patches_here, width)
            got = [swap_with(v[:, :, r], "tp", n_tp, r) for r in range(1, spread_tp)]
        got = yield got
        if spread_tp > 1:
            v = flip_to(jnp.stack([v[:, :, 0]] + got, axis=1), 1, spread_tp, moves.tp)
        v = v.reshape(clips, frames_here, n_ctx, piece, width)
        v = flip_to(v, 2, n_ctx, moves.ctx)
        return v.reshape(clips, frames_here, patches_here, width)

    def trade(get, planes):
        sides = []
        for dx, dr in planes:
            block = get(dx, dr)
            if dx or dr:
                pairs = [
                    (c * n_tp + t, (c ^ dx) * n_tp + (t ^ dr))
                    for c in range(n_ctx)
                    for t in range(n_tp)
                ]
                block = lax.ppermute(block, ("ctx", "tp"), pairs)
            sides.append(block)
        sides = sides[:1] + (yield sides[1:])
        lines = [jnp.stack([v[:, dz] for v in sides], axis=1) for dz in range(n_ctx // 2)]
        got = yield [swap_with(v, "ctx", n_ctx, 2 * dz) for dz, v in enumerate(lines) if dz]
        return jnp.stack(lines[:1] + got, axis=1)

    all_planes = [(dx, dr) for dx in range(2) for dr in range(spread_tp)]
    own_planes = [(0, 0), (1, 0)]

    def frames_to_clips(v):
        v = v.reshape(clips, groups, spread_tp, n_ctx // 2, 2, piece, width)
        got = yield from trade(lambda dx, dr: v[:, :, dr, :, dx].swapaxes(1, 2), all_planes)
        return got.reshape(clips, -1, width)

    def clips_to_frames(v):
        v = v.reshape(clips, n_ctx // 2, 2, spread_tp, groups, piece, width)
        got = yield from trade(lambda dx, dr: v[:, :, dx, dr], all_planes)
        got = got.reshape(clips, n_ctx, spread_tp, groups, piece, width)
        return got.transpose(0, 3, 2, 1, 4, 5).reshape(clips, -1, width)

    def here_to_clips(v):
        v = v.reshape(clips, spread_tp, groups, n_ctx, piece, width)
        v = flip_to(flip_to(v, 3, n_ctx, moves.ctx), 1, spread_tp, moves.tp % spread_tp)
        v = v.reshape(clips, spread_tp, groups, n_ctx // 2, 2, piece, width)
        got = yield from trade(lambda dx, dr: v[:, :, :, :, dx].transpose(0, 3, 1, 2, 4, 5), own_planes)
        return got.reshape(clips, -1, width)

    def clips_to_here(v):
        v = v.reshape(clips, n_ctx // 2, 2, spread_tp, groups, piece, width)
        got = yield from trade(lambda dx, dr: v[:, :, dx], own_planes)
        v = got.reshape(clips, n_ctx, spread_tp, groups, piece, width).transpose(0, 2, 3, 1, 4, 5)
        v = flip_to(flip_to(v, 3, n_ctx, moves.ctx), 1, spread_tp, moves.tp % spread_tp)
        return v.reshape(clips, frames_here, patches_here, width)

    def flat(v):
        return v.reshape(-1, v.shape[-1])

    def shaped(v):
        return v.reshape(clips, -1, v.shape[-1])

    shards = []
    for level in range(LAYERS):
        attention = [w_qkv[level, 0], w_qkv[level, 1], w_qkv[level, 2], w_out[level].T]
        shards.append(jnp.concatenate(attention, axis=1).astype(BF16))
        shards.append(w_up[level].astype(BF16))
        shards.append(w_down[level].T.astype(BF16))
    lanes = Lanes()
    gathers = {}

    blocks = {}

    def gather_far(index):
        blocks[index] = lax.all_gather(shards[index], "ctx", axis=0, tiled=True)

    def set_out(index):
        if index in blocks:
            steps = moves.gather_rest(blocks[index])
        else:
            steps = moves.gather_halves(shards[index])
        gathers[index] = lanes.start(steps)

    plan = [
        ((2,), (), ()),
        ((), (2,), ()),
        ((1,), (), ()),
        ((4,), (), (5,)),
        ((3,), (), ()),
        ((), (3,), ()),
        ((5,), (), ()),
        ((), (5,), ()),
        ((), (), ()),
    ]

    def tick(values=()):
        out, but, far = plan.pop(0)
        held = {index: blocks.get(index, shards[index]) for index in out + far}
        held, values = lanes.fence((held, values), [gathers[index] for index in but])
        for index in out + far:
            if index in blocks:
                blocks[index] = held[index]
            else:
                shards[index] = held[index]
        for index in far:
            gather_far(index)
        for index in out:
            set_out(index)
        return values

    def whole(index):
        layout, arrays = gathers[index].result
        count = len(arrays) // 2
        groups = []
        for group in (arrays[:count], arrays[count:]):
            parts = [
                group[place] if entry is None else group[place][entry]
                for strip in layout
                for place, entry, _ in strip
            ]
            groups.append(jnp.concatenate(parts, axis=1))
        return jnp.concatenate(groups, axis=0)

    def attention_weights(index):
        v = whole(index)
        strips = jnp.split(v, n_tp, axis=1)
        cut = 3 * head_cols
        return [w[:, :cut] for w in strips], jnp.concatenate([w[:, cut:] for w in strips], axis=1)

    def modulations(level):
        return [mods[level][:, i] for i in range(6)]

    gather_far(1)
    gather_far(3)
    set_out(0)
    moved = lanes.start(to_frames(moves.halves(tokens)))
    vectors_task = lanes.start(modulation_vectors())
    tick()
    residual = moved.result
    tick()
    tick()
    mods = vectors_task.result
    fused = (
        whole_frames
        and head_cols % 32 == 0
        and w_up.shape[2] % (2 * LANES) == 0
        and 4 * head_cols == w_up.shape[2]
        and width % 32 == 0
    )
    matched = (micro_ids[:, None] == micro_ids[None, :]).astype(F32)
    share = 1.0 / jnp.sum(matched, axis=1)
    scatters = {}
    mod_grads = [None] * LAYERS

    def start_scatter(level, names, *groups):
        far = level and len(groups) == 1
        steps = (moves.scatter_far if far else moves.scatter_weight)(groups)
        scatters[level, names] = lanes.start(steps)
        return scatters[level, names]

    def scattered(level, name):
        for (at, names), task in scatters.items():
            if at == level and name in names:
                columns = {"qkv": 3 * head_cols, "out": head_cols}
                units = w_up.shape[2]
                low = sum(columns.get(n, units) for n in names[: names.index(name)])
                return task.result[:, low : low + columns.get(name, units)]

    def mod_strip():
        parts = [moves.halves(v).reshape(clips, n_tp, -1) for v in mod_grads]
        parts = flip_to(jnp.stack(parts, axis=2), 1, n_tp, moves.tp)
        parts = yield from total_over_ctx(parts)
        got = yield [swap_with(parts[:, r], "tp", n_tp, r) for r in range(1, n_tp)]
        strip = parts[:, 0] + sum(got)
        got = yield swap_with(strip, "ctx", n_ctx, 1)
        strip = strip + got
        got = yield swap_with(strip, "dp", n_dp, 1)
        return jnp.concatenate([strip, got], axis=0)

    def fused_passes(v):
        vectors, saved = [], []
        for level in range(LAYERS):
            last = share if level == LAYERS - 1 else jnp.ones_like(share)
            last = jnp.broadcast_to(last[:, None, None], (clips, 2, width))
            vectors.append(jnp.concatenate([mods[level], last], axis=1))
        v = flat(v)
        for level in range(LAYERS):
            stride = piece if level % 2 else 1
            joined = gathers[3 * level].result
            kept = fused_branch(v, vectors[level], joined, clips, stride)
            normed, qkv, lse, result, branch, middle, normed_mlp = tick(kept)
            up = gathers[3 * level + 1].result
            act, slope = tick(fused_up(normed_mlp, vectors[level], up, clips))
            down = gathers[3 * level + 2].result
            branch_mlp, after = fused_down(act, middle, vectors[level], down, clips)
            saved.append((v, normed, qkv, lse, result, branch, middle, normed_mlp))
            saved[-1] += (act, slope, branch_mlp, joined, up, down, stride)
            v = after
            if level == 0:
                moved = lanes.start(frames_to_clips(shaped(v)))
                tick()
                late = tick(cotangent)
                turned = lanes.start(here_to_clips(moves.halves(late)))
                v = flat(moved.result)
        finished = lanes.start(clips_to_here(moves.halves(shaped(v))))
        grad = flat(turned.result)
        for level in reversed(range(LAYERS)):
            v, normed, qkv, lse, result, branch, middle, normed_mlp = saved[level][:8]
            act, slope, branch_mlp, joined, up, down, stride = saved[level][8:]
            back = fused_mlp_back(
                grad, vectors[level], branch_mlp, slope, middle, branch, up, down, clips
            )
            grad_branch, grad_pre, grad_middle, grad_out, sums = lanes.fence(back)
            if level:
                first = start_scatter(level, ("down",), (grad_branch, [act]))
                grad_out = lanes.fence(grad_out, (finished,))
            else:
                start_scatter(
                    level, ("down", "up"), (grad_branch, [act]), (normed_mlp, [grad_pre])
                )
                grad_out = lanes.fence(grad_out)
            back = fused_branch_back(
                v, vectors[level], grad_out, grad_middle, qkv, lse, joined, clips, stride
            )
            grad, more, *grad_qkv = lanes.fence(back)
            mod_grads[level] = (sums + more)[:, :6]
            joint = (normed, grad_qkv), (grad_out, [result])
            if level:
                moved = lanes.start(clips_to_frames(shaped(grad)))
                second = start_scatter(level, ("up",), (normed_mlp, [grad_pre]))
                lanes.fence()
                third = start_scatter(level, ("qkv", "out"), *joint)
                lanes.fence()
                grad = flat(moved.result)
            else:
                start_scatter(level, ("qkv", "out"), *joint)
        return finished, shaped(grad)

    def plain_passes(residual):
        residual = residual.astype(F32)
        records = []
        for level in range(LAYERS):
            spatial = level % 2 == 0
            shift_a, scale_a, gate_a, shift_m, scale_m, gate_m = modulations(level)
            normed = flat(modulate(residual, shift_a, scale_a))
            qkvs, outs = attention_weights(3 * level)
            projected = [dot(normed, v).astype(BF16) for v in qkvs]
            rows, stride = (patches_here * spread_tp, 1) if spatial else (residual.shape[1], piece)
            if spatial and not whole_frames:
                saved = [attend_shared(v, clips * frames_here) for v in projected]
                result = jnp.concatenate([entry[0] for entry in saved], axis=1)
                saved = [entry[1] for entry in saved]
            else:
                result, saved = attend(projected, rows, stride)
            result, saved = tick((result, saved))
            branch = shaped(dot(result, outs, NT))
            middle = residual + gate_a[:, None] * branch
            normed_mlp = flat(modulate(middle, shift_m, scale_m))
            up = whole(3 * level + 1)
            pre_act = dot(normed_mlp, up)
            act = gelu(pre_act).astype(BF16)
            act, pre_act = tick((act, pre_act))
            down = whole(3 * level + 2)
            branch_mlp = shaped(dot(act, down, NT))
            records.append(
                (residual, normed, projected, saved, result, branch, middle, normed_mlp)
                + (pre_act, act, branch_mlp, qkvs, outs, up, down, rows, stride)
            )
            residual = middle + gate_m[:, None] * branch_mlp
            if spatial:
                moved = lanes.start(frames_to_clips(residual.astype(BF16)))
                tick()
                turned = lanes.start(here_to_clips(moves.halves(cotangent)))
                tick()
                residual = moved.result.astype(F32)
        gradient = turned.result.astype(F32) * share[:, None, None]
        finished = lanes.start(clips_to_here(moves.halves(residual.astype(BF16))))
        for level in reversed(range(LAYERS)):
            spatial = level % 2 == 0
            (residual, normed, projected, saved, result, branch, middle, normed_mlp) = records[level][
                :8
            ]
            (pre_act, act, branch_mlp, qkvs, outs, up, down, rows, stride) = records[level][8:]
            shift_a, scale_a, gate_a, shift_m, scale_m, gate_m = modulations(level)
            gate_m_grad = jnp.sum(gradient * branch_mlp, axis=1)
            low_grad = flat((gradient * gate_m[:, None]).astype(BF16))
            grad_pre = gelu_slope(pre_act, dot(low_grad, down)).astype(BF16)
            start_scatter(level, ("down",), (low_grad, [act]))
            grad_pre = lanes.fence(grad_pre)
            grad_normed = shaped(dot(grad_pre, up, NT))
            start_scatter(level, ("up",), (normed_mlp, [grad_pre]))
            grad_normed = lanes.fence(grad_normed)
            added, shift_m_grad, scale_m_grad = modulate_back(grad_normed, middle, scale_m)
            gradient = gradient + added
            gate_a_grad = jnp.sum(gradient * branch, axis=1)
            low_grad = flat((gradient * gate_a[:, None]).astype(BF16))
            grad_heads = dot(low_grad, outs).astype(BF16)
            start_scatter(level, ("out",), (low_grad, [result]))
            grad_heads = lanes.fence(grad_heads)
            if spatial and not whole_frames:
                grad_qkv = [
                    attend_shared_back(v, g)
                    for v, g in zip(saved, jnp.split(grad_heads, n_tp, axis=1))
                ]
            else:
                grad_qkv = attend_back(projected, grad_heads, saved, rows, stride)
            grad_qkv = lanes.fence(grad_qkv)
            start_scatter(level, ("qkv",), (normed, grad_qkv))
            grad_normed = shaped(sum(dot(v, w, NT) for v, w in zip(grad_qkv, qkvs)))
            added, shift_a_grad, scale_a_grad = modulate_back(grad_normed, residual, scale_a)
            gradient = gradient + added
            mod_grads[level] = jnp.stack(
                [shift_a_grad, scale_a_grad, gate_a_grad, shift_m_grad, scale_m_grad, gate_m_grad],
                axis=1,
            )
            if not spatial:
                moved = lanes.start(clips_to_frames(gradient.astype(BF16)))
                lanes.fence()
                lanes.fence()
                gradient = moved.result.astype(F32)
        return finished, gradient

    passes = fused_passes if fused else plain_passes
    finished, gradient = passes(residual)
    hanging = [scatters[key] for key in scatters if key == (0, ("down", "up"))]
    first = [scatters[key] for key in scatters if key == (1, ("down",))]
    second = [scatters[key] for key in scatters if key == (1, ("up",))]
    both = lanes.start(mod_strip())
    gradient = lanes.fence(gradient, (), first)
    gradient = lanes.fence(gradient, hanging)
    gradient = lanes.fence(gradient, (), second)
    moved = lanes.start(from_frames(moves.halves(gradient.astype(BF16))))
    while lanes.tasks:
        lanes.fence(last=True)
    both = both.result
    grad_tokens = moved.result.astype(F32)
    output = finished.result
    grads = [
        (
            scattered(level, "qkv").reshape(rows_here, 3, head_cols).transpose(1, 0, 2),
            scattered(level, "out").T,
            scattered(level, "up"),
            scattered(level, "down").T,
        )
        for level in range(LAYERS)
    ]

    ada_grads = []
    cond_part = 0.0
    for level in range(LAYERS):
        strip = both[:, level]
        ada_grads.append(
            lax.dot_general(cond_rows.astype(F32), strip, TN, precision=HIGHEST)
        )
        cond_part = cond_part + lax.dot_general(
            strip, ada_low[level].astype(F32), NT, precision=HIGHEST
        )
    over_tp = [swap_with(cond_part[:clips], "tp", n_tp, r) for r in range(1, n_tp)]
    over_both = [
        lax.ppermute(
            cond_part[clips:],
            ("dp", "tp"),
            [(d * n_tp + t, (1 - d) * n_tp + (t ^ r)) for d in range(n_dp) for t in range(n_tp)],
        )
        for r in range(n_tp)
    ]
    cond_grad = jnp.stack([cond_part[:clips] + sum(over_tp), sum(over_both)], axis=1)[:, :, None]
    cond_grad = jnp.concatenate([cond_grad, swap_with(cond_grad, "ctx", n_ctx, 1)], axis=2)
    blocks = [cond_grad] + [swap_with(cond_grad, "ctx", n_ctx, 2 * k) for k in range(1, n_ctx // 2)]
    cond_grad = jnp.concatenate(blocks, axis=2)
    cond_grad = flip_to(cond_grad, 2, n_ctx, moves.ctx).reshape(clips, width)
    cond_grad = moves.halves(cond_grad)
    grad_condition = jax.vjp(jax.nn.silu, cond_full)[1](cond_grad)[0]

    stacked = [jnp.stack([grads[level][i] for level in range(LAYERS)]) for i in range(4)]
    return (output, grad_tokens, grad_condition, *stacked, jnp.stack(ada_grads))


def solution(mesh):
    placed = (
        P("dp", "ctx", "tp", None),
        P("dp", None),
        P("dp"),
        P(None, None, ("dp", "ctx"), "tp"),
        P(None, "tp", ("dp", "ctx")),
        P(None, ("dp", "ctx"), "tp"),
        P(None, "tp", ("dp", "ctx")),
        P(None, ("dp", "ctx"), "tp"),
        P("dp", "ctx", "tp", None),
    )
    return jax.shard_map(
        functools.partial(local, Moves(mesh)),
        mesh=mesh,
        in_specs=placed,
        out_specs=(
            P("dp", "ctx", "tp", None),
            P("dp", "ctx", "tp", None),
            P("dp", None),
            P(None, None, ("dp", "ctx"), "tp"),
            P(None, "tp", ("dp", "ctx")),
            P(None, ("dp", "ctx"), "tp"),
            P(None, "tp", ("dp", "ctx")),
            P(None, ("dp", "ctx"), "tp"),
        ),
        check_vma=False,
    )
```
